32 devices in a mesh: section: 2 (over x), tensor: 2 (over y), wide: 8 (over z, core).
Axes of the slice: x: 2, y: 2, z: 4, core: 2. Of those that a mesh axis runs over, the one named last changes fastest.
Arguments:
- block_input: bfloat16 [4, 2048, 1024], P(None, ('wide', 'tensor')), may hold values from -6 to 6
- doc_lengths: int32 [4, 8], replicated, may hold values from 1 to 1536, 2048 in all within a row
- norm_gain: float32 [2, 2, 1024], P('section'), may hold values from 0.5 to 1.5
- norm_bias: float32 [2, 2, 1024], P('section'), may hold values from -1.8 to 1.8
- qkv_weight: bfloat16 [2, 1024, 3072], P('section', None, 'tensor'), may hold values from -0.1875 to 0.1875
- qkv_bias: float32 [2, 3072], P('section', 'tensor'), may hold values from -1.8 to 1.8
- dense_weight: bfloat16 [2, 1024, 1024], P('section', 'tensor'), may hold values from -0.75 to 0.75
- dense_bias: float32 [2, 1024], P('section'), may hold values from -1.8 to 1.8
- up_weight: bfloat16 [2, 1024, 4096], P('section', None, 'tensor'), may hold values from -0.1875 to 0.1875
- up_bias: float32 [2, 4096], P('section', 'tensor'), may hold values from -3 to 3
- down_weight: bfloat16 [2, 4096, 1024], P('section', 'tensor'), may hold values from -0.09375 to 0.09375
- down_bias: float32 [2, 1024], P('section'), may hold values from -1.8 to 1.8
- cotangent: float32 [4, 2048, 1024], P(None, ('wide', 'tensor')), may hold values from -9 to 9
Outputs:
- layer_out: bfloat16 [2, 4, 2048, 1024], P('section', None, ('wide', 'tensor'))
- input_grad: float32 [2, 4, 2048, 1024], P('section', None, ('wide', 'tensor'))
- norm_gain_grad: float32 [2, 2, 1024], P('section')
- norm_bias_grad: float32 [2, 2, 1024], P('section')
- qkv_weight_grad: float32 [2, 1024, 3072], P('section', None, 'tensor')
- qkv_bias_grad: float32 [2, 3072], P('section', 'tensor')
- dense_weight_grad: float32 [2, 1024, 1024], P('section', 'tensor')
- dense_bias_grad: float32 [2, 1024], P('section')
- up_weight_grad: float32 [2, 1024, 4096], P('section', None, 'tensor')
- up_bias_grad: float32 [2, 4096], P('section', 'tensor')
- down_weight_grad: float32 [2, 4096, 1024], P('section', 'tensor')
- down_bias_grad: float32 [2, 1024], P('section')
The draws below stay inside these ranges and needn't reach their ends.
Inputs may be any that keep to these rules, and one draw needn't show every extreme that they name: `doc_lengths`: row s holds, in order, the lengths of the 8 documents packed in sequence s; each row sums to 2048, and in each row one document has exactly 1536 tokens.
All inputs are finite; a program needn't handle non-finite values.
Results may differ from the reference program's by a relative error of at most 0.018.
Values may be sent and summed in bfloat16 or wider, within the bound.
A program may use at most 192 MiB of HBM per device.

```python
import math
import jax
import jax.numpy as jnp
import numpy as np
from jax import lax

D = 1024
HEADS = 16
HEAD_DIM = 64
ROT = 16
FF = 4096
MICRO = 4
SEQ = 2048
NDOC = 8
N_SECTION = 2


def draw_cotangent(key, part):
    key = jax.random.fold_in(key, 11)
    first_key = jax.random.fold_in(key, 0)
    ramp = jnp.arange(SEQ, dtype=jnp.float32) / SEQ
    noise = jnp.clip(jax.random.normal(first_key, (MICRO, SEQ, D), jnp.float32), -6.0, 6.0)
    return noise * (0.5 + ramp)[None, :, None]


def level_of(rng, dims, shards, smallest, largest):
    level, own = 1.0, jax.random.fold_in(rng, 6)
    for axis_at, shards_of in shards:
        steps = jnp.exp(jax.random.uniform(jax.random.fold_in(own, axis_at), (shards_of,), jnp.float32, smallest / len(shards), largest / len(shards)))
        level = level * jnp.repeat(steps, dims[axis_at] // shards_of).reshape([-1 if axis == axis_at else 1 for axis in range(len(dims))])
    return level


def split_up(number_of, total, most, skew):
    weights = [(1 << 20) // math.isqrt(grade ** skew) + 1 for grade in range(2, number_of + 1)]
    spare, given = total - most - (number_of - 1), [1] * (number_of - 1)
    while spare > 0:
        free = [i for i in range(number_of - 1) if given[i] < most]
        pool, remaining = sum([weights[i] for i in free]), spare
        for i in free:
            more = min(most - given[i], max(1, remaining * weights[i] // pool), spare)
            given[i] = given[i] + more
            spare = spare - more
    return np.array([most] + given)


def ragged_sizes(key, amount, total, limit, slope):
    if amount == 2:
        one = jax.random.randint(key, (), max(1, total - limit), min(limit, total - 1) + 1)
        return jnp.stack([one, total - one])
    sizes = jnp.asarray(split_up(amount, total, limit, slope), jnp.int32)
    pairs = (amount - 1) // 2
    source_of, sink = sizes[1:1 + 2 * pairs:2], sizes[2:2 + 2 * pairs:2]
    room = jnp.minimum(source_of - 1, limit - sink)
    passed = jax.random.randint(jax.random.fold_in(key, 1), (pairs,), 0, 1 << 20) % (room + 1)
    sizes = sizes.at[1:1 + 2 * pairs:2].set(source_of - passed).at[2:2 + 2 * pairs:2].set(sink + passed)
    return sizes[jax.random.permutation(jax.random.fold_in(key, 2), amount)]


def normal_values(key, dims, deviation, limit, cuts=(), kind=jnp.bfloat16):
    level = level_of(key, dims, cuts, -0.22, 0.18) if cuts else 1.0
    entries = jax.random.normal(key, dims, jnp.float32) * deviation * level
    return jnp.minimum(jnp.maximum(entries, -limit), limit).astype(kind)


def setup_inputs(seed: int = 0) -> dict:
    key_of = jax.random.split(jax.random.key(seed), 14)
    return {
        "block_input": normal_values(key_of[0], (MICRO, SEQ, D), 1.0, 6.0, ((1, 16),)),
        "doc_lengths": jax.vmap(lambda own: ragged_sizes(own, NDOC, SEQ, 3 * SEQ // 4, 2))(jax.random.split(key_of[1], MICRO)).reshape((MICRO, NDOC)).astype(jnp.int32),
        "norm_gain": jnp.clip(1.0 + 0.1 * jax.random.normal(key_of[2], (N_SECTION, 2, D), jnp.float32), 0.5, 1.5),
        "norm_bias": normal_values(key_of[3], (N_SECTION, 2, D), 0.3, 1.8, ((0, 2),), jnp.float32),
        "qkv_weight": normal_values(key_of[4], (N_SECTION, D, 3 * D), D ** -0.5, 0.1875, ((0, 2), (2, 2))),
        "qkv_bias": normal_values(key_of[5], (N_SECTION, 3 * D), 0.3, 1.8, ((0, 2), (1, 2)), jnp.float32),
        "dense_weight": normal_values(key_of[6], (N_SECTION, D, D), (D // 16) ** -0.5, 0.75, ((0, 2), (1, 2))),
        "dense_bias": normal_values(key_of[7], (N_SECTION, D), 0.3, 1.8, ((0, 2),), jnp.float32),
        "up_weight": normal_values(key_of[8], (N_SECTION, D, FF), D ** -0.5, 0.1875, ((0, 2), (2, 2))),
        "up_bias": normal_values(key_of[9], (N_SECTION, FF), 0.5, 3.0, ((0, 2), (1, 2)), jnp.float32),
        "down_weight": normal_values(key_of[10], (N_SECTION, FF, D), FF ** -0.5, 0.09375, ((0, 2), (1, 2))),
        "down_bias": normal_values(key_of[11], (N_SECTION, D), 0.3, 1.8, ((0, 2),), jnp.float32),
        "cotangent": draw_cotangent(jax.random.fold_in(key_of[13], 71), 0),
    }


EPSILON = 1e-05
ROPE_BASE = 10000.0
HIGH = lax.Precision.HIGHEST

@jax.custom_vjp
def low(v):
    return lax.optimization_barrier(v.astype(jnp.bfloat16)).astype(jnp.float32)

@jax.custom_vjp
def low_back(v):
    return v

def low_keep(v):
    return (low(v), None)

def low_pass(kept, grad):
    return (grad,)

def back_keep(v):
    return (v, None)

def back_low(kept, grad):
    return (low(grad),)
low.defvjp(low_keep, low_pass)
low_back.defvjp(back_keep, back_low)

def layer_norm(values, gain, shift):
    center = lax.optimization_barrier(jnp.mean(values, axis=-1, keepdims=True))
    centred = values - center
    spread = lax.optimization_barrier(jnp.mean(centred * centred, axis=-1, keepdims=True))
    return centred * lax.rsqrt(spread + EPSILON) * gain + shift

def doc_layout(lengths, tok_index):
    ends = jnp.cumsum(lengths).astype(jnp.int32)
    starts = (ends - lengths).astype(jnp.int32)
    doc_ids = lax.optimization_barrier(jnp.sum((tok_index[:, None] >= ends[None, :]).astype(jnp.int32), axis=1)).astype(jnp.int32)
    numbers = jnp.arange(lengths.shape[0], dtype=jnp.int32)
    picked = doc_ids[:, None] == numbers[None, :]
    begins = lax.optimization_barrier(jnp.sum(jnp.where(picked, starts[None, :], 0), axis=1)).astype(jnp.int32)
    return (doc_ids, (tok_index - begins).astype(jnp.int32))

def rope_tables(offsets):
    half = ROT // 2
    freqs = ROPE_BASE ** (-2.0 * jnp.arange(half, dtype=jnp.float32) / ROT)
    angle = offsets.astype(jnp.float32)[:, None] * freqs[None, :]
    return (jnp.cos(angle)[:, None, :], jnp.sin(angle)[:, None, :])

def rotate(values, cos_table, sin_table):
    half = ROT // 2
    front = values[..., :half]
    back = values[..., half:ROT]
    turned = [front * cos_table - back * sin_table, back * cos_table + front * sin_table, values[..., ROT:]]
    return jnp.concatenate(turned, axis=-1)

def attention(queries, keys, values, doc_ids, tok_index):
    block = min(512, SEQ)
    count = SEQ // block
    factor = 1.0 / math.sqrt(HEAD_DIM)
    query_blocks = queries.reshape(count, block, HEADS, HEAD_DIM)
    doc_blocks = doc_ids.reshape(count, block)
    index_blocks = tok_index.reshape(count, block)

    @jax.checkpoint
    def one_block(items):
        query_part, doc_part, index_part = items
        raw_scores = low_back(jnp.einsum('qhd,khd->qhk', query_part, keys, precision=HIGH))
        allowed = (doc_part[:, None] == doc_ids[None, :]) & (tok_index[None, :] <= index_part[:, None])
        scores = jnp.where(allowed[:, None, :], raw_scores * factor, -jnp.inf)
        row_max = lax.optimization_barrier(jnp.max(scores, axis=-1, keepdims=True))
        log_total = row_max + jnp.log(lax.optimization_barrier(jnp.sum(jnp.exp(scores - row_max), axis=-1, keepdims=True)))
        probs_low = low(jnp.exp(scores - log_total))
        return jnp.einsum('qhk,khd->qhd', probs_low, values, precision=HIGH)
    mixed = lax.map(one_block, (query_blocks, doc_blocks, index_blocks))
    return mixed.reshape(SEQ, HEADS * HEAD_DIM)

def layer(values, lengths, params):
    norm_gain, norm_bias, qkv_weight, qkv_bias, dense_weight, dense_bias, up_weight, up_bias, down_weight, down_bias = params
    norm_first = low(layer_norm(values, norm_gain[0], norm_bias[0]))
    norm_second = low(layer_norm(values, norm_gain[1], norm_bias[1]))
    packed = low_back(jnp.dot(norm_first, qkv_weight, precision=HIGH) + qkv_bias)
    packed = packed.reshape(SEQ, HEADS, 3, HEAD_DIM)
    tok_index = jnp.arange(SEQ, dtype=jnp.int32)
    doc_ids, offsets = doc_layout(lengths, tok_index)
    cos_table, sin_table = rope_tables(offsets)
    queries = low(rotate(packed[:, :, 0], cos_table, sin_table))
    keys = low(rotate(packed[:, :, 1], cos_table, sin_table))
    vals = low(packed[:, :, 2])
    mixed = attention(queries, keys, vals, doc_ids, tok_index)
    mixed = low(low_back(mixed))
    up_pre = low_back(jnp.dot(norm_second, up_weight, precision=HIGH) + up_bias)
    hidden = low(jax.nn.gelu(up_pre, approximate=False))
    branch = jnp.dot(mixed, dense_weight, precision=HIGH) + dense_bias
    branch = branch + jnp.dot(hidden, down_weight, precision=HIGH) + down_bias
    branch = low_back(branch)
    return low(values + branch)

def reference(block_input, doc_lengths, norm_gain, norm_bias, qkv_weight, qkv_bias, dense_weight, dense_bias, up_weight, up_bias, down_weight, down_bias, cotangent):
    params = tuple((array.astype(jnp.float32) for array in (norm_gain, norm_bias, qkv_weight, qkv_bias, dense_weight, dense_bias, up_weight, up_bias, down_weight, down_bias)))
    first_input = block_input.astype(jnp.float32)
    extras = jnp.zeros((N_SECTION, MICRO, SEQ, D), jnp.float32)

    def forward(start_values, extra_values, *weights):

        def per_sequence(carry, items):
            values, extra_rows, lengths = items
            current = values
            results = []
            for depth in range(N_SECTION):
                current = layer(current + extra_rows[depth], lengths, tuple((weight[depth] for weight in weights)))
                results.append(current)
            return (carry, jnp.stack(results))
        moved = jnp.moveaxis(extra_values, 0, 1)
        unused, stacked = lax.scan(per_sequence, jnp.zeros((), jnp.float32), (start_values, moved, doc_lengths))
        return jnp.moveaxis(stacked, 1, 0)
    outputs, pullback = jax.vjp(forward, first_input, extras, *params)
    seeds = jnp.zeros_like(outputs).at[N_SECTION - 1].set(cotangent.astype(jnp.float32))
    grads = pullback(seeds)
    return (outputs.astype(jnp.bfloat16), grads[1], grads[2], grads[3], grads[4], grads[5], grads[6], grads[7], grads[8], grads[9], grads[10], grads[11])
```

```python
import functools
import math

import jax
import jax.numpy as jnp
from jax import lax
from jax.experimental import pallas as pl
from jax.experimental.pallas import tpu as pltpu
from jax.sharding import PartitionSpec as P

HEAD_DIM = 64
ROT = 16
SEQ = 2048


EPSILON = 1e-05
ROPE_BASE = 10000.0

MESH = pl.DeviceIdType.MESH
F32 = jnp.float32
BF16 = jnp.bfloat16
LANES = 128
BLOCK = 512
COLS = 512
NEG = -1e30
SCORE_SCALE = math.log2(math.e) / math.sqrt(HEAD_DIM)


def dot(a, b):
    return jnp.dot(a, b, preferred_element_type=F32)


def dot_t(a, b):
    return lax.dot_general(a, b, (((1,), (1,)), ((), ())), preferred_element_type=F32)


def t_dot(a, b):
    return lax.dot_general(a, b, (((0,), (0,)), ((), ())), preferred_element_type=F32)


def lane_low(rows):
    return lax.broadcasted_iota(jnp.int32, (rows, LANES), 1) < HEAD_DIM


def turn(values):
    return pltpu.roll(values, HEAD_DIM, 1)


def rotary(values, cos_ref, front_ref, back_ref, seq, sign):
    cos, front, back = cos_ref[seq], front_ref[seq], back_ref[seq]
    ahead = pltpu.roll(values, LANES - ROT // 2, 1)
    behind = pltpu.roll(values, ROT // 2, 1)
    return values * cos + sign * (ahead * front + behind * back)


def pair_up(first, second, low):
    half = first.shape[0]
    top = jnp.where(low, first, turn(second))
    bottom = jnp.where(low, turn(first), second)
    del half
    return top, bottom


def relay_kernel(
    dims,
    ends,
    x_hbm,
    cot_hbm,
    gain,
    shift,
    qkv_b,
    up_b,
    out_b,
    wqkv_hbm,
    wdense_hbm,
    wup_hbm,
    wdown_hbm,
    cos,
    front,
    back,
    out_hbm,
    ig_hbm,
    norm_hbm,
    g_hbm,
    mixed_hbm,
    hid_hbm,
    dpre_hbm,
    dpk_hbm,
    small,
    wqkv,
    wdense,
    wup,
    wdown,
    xfull,
    gfull,
    cot,
    qkv_r,
    mix_r,
    do_r,
    dqkv_r,
    rsf_r,
    rsb_r,
    qkv_st,
    o_st,
    do_st,
    dqkv_st,
    rsf_st,
    rsb_st,
    out_st,
    gx_st,
    ig_st,
    norm_st,
    mixed_st,
    hid_st,
    dpre_st,
    dpk_st,
    slope,
    part,
    dn1,
    qm,
    kr,
    vx,
    dox,
    dq,
    lse,
    delta,
    scores,
    peak,
    acc,
    wsem,
    ownx_sem,
    yx_s,
    yx_r,
    owng_sem,
    yg_s,
    yg_r,
    qkv_ss,
    qkv_rs,
    o_ss,
    o_rs,
    do_ss,
    do_rs,
    dqkv_ss,
    dqkv_rs,
    rsf_ss,
    rsf_rs,
    rsb_ss,
    rsb_rs,
    xs_ss,
    gs_ss,
    store_sem,
):
    micro, rows, group, wide, heads, d_model, ff = dims
    sect = lax.axis_index("section")
    tens = lax.axis_index("tensor")
    me = lax.axis_index("wide")
    pairs = heads // 2
    per_source = group + group // 2
    half = group // 2
    q_blocks = SEQ // BLOCK
    sources = BLOCK // group
    my_rows = pl.ds(pl.multiple_of(tens * rows, rows), rows)
    his_rows = pl.ds(pl.multiple_of((1 - tens) * rows, rows), rows)
    x_dev = {"section": 1 - sect}
    y_dev = {"tensor": 1 - tens}
    low_half = lane_low(half)
    low_group = lane_low(group)

    def remote(src, dst, ss, rs, dev):
        return pltpu.make_async_remote_copy(
            src_ref=src, dst_ref=dst, send_sem=ss, recv_sem=rs, device_id=dev, device_id_type=MESH
        )

    def arrived(ref, sem):
        pltpu.make_async_copy(ref, ref, sem).wait()

    def y_send_x(s):
        own = xfull.at[s, my_rows]
        return remote(own, own, yx_s.at[s], yx_r.at[s], y_dev)

    def y_send_g(s):
        own = gfull.at[s, my_rows]
        return remote(own, own, yg_s.at[s], yg_r.at[s], y_dev)

    def spread(stage, target, seq, dest, ss, rs):
        @pl.when(dest == me)
        def _():
            pltpu.make_async_copy(stage, target.at[seq, me], rs).start()

        @pl.when(dest != me)
        def _():
            remote(stage, target.at[seq, me], ss, rs, {"wide": dest}).start()

    loads = [
        pltpu.make_async_copy(source, target, wsem.at[i])
        for i, (source, target) in enumerate(
            ((wqkv_hbm, wqkv), (wup_hbm, wup), (wdown_hbm, wdown), (wdense_hbm, wdense))
        )
    ]

    barrier = pltpu.get_barrier_semaphore()
    for dev in [x_dev, y_dev] + [{"wide": lax.rem(me + k, wide)} for k in range(1, wide)]:
        pl.semaphore_signal(barrier, inc=1, device_id=dev, device_id_type=MESH)

    @pl.when(sect == 0)
    def _():
        for s in range(micro):
            pltpu.make_async_copy(x_hbm.at[s], xfull.at[s, my_rows], ownx_sem.at[s]).start()

    for load in loads:
        load.start()

    @pl.when(sect == 1)
    def _():
        for s in range(micro):
            pltpu.make_async_copy(cot_hbm.at[s], cot.at[s], owng_sem.at[s]).start()

    small[...] = jnp.zeros_like(small)
    pl.semaphore_wait(barrier, wide + 1)

    @pl.when(sect == 0)
    def _():
        for s in range(micro):
            arrived(xfull.at[s, my_rows], ownx_sem.at[s])
            y_send_x(s).start()

    @pl.when(sect == 1)
    def _():
        for s in range(micro):
            arrived(cot.at[s], owng_sem.at[s])

            def chunk(i, carry, s=s):
                at = pl.ds(pl.multiple_of(i * 32, 32), 32)
                there = pl.ds(pl.multiple_of(tens * rows + i * 32, 32), 32)
                gfull[s, there, :] = cot[s, at, :].astype(BF16)
                return carry

            lax.fori_loop(0, rows // 32, chunk, 0)
            y_send_g(s).start()

    for load in loads:
        load.wait()

    def normed_rows(values):
        center = jnp.mean(values, axis=-1, keepdims=True)
        centred = values - center
        spread_of = jnp.mean(centred * centred, axis=-1, keepdims=True)
        inv = lax.rsqrt(spread_of + EPSILON)
        return centred * inv, inv

    def starts_of(s, tokens):
        found = jnp.zeros_like(tokens)
        for j in range(ends.shape[1]):
            end = ends[s, j]
            found = jnp.where(tokens >= end, end, found)
        return found

    def unpack_heads(s):
        def step(src, carry):
            qk = qkv_r[s, src, 0:group, :].astype(F32)
            at = pl.multiple_of(src * group, group)
            qm[pl.ds(at, group), :] = jnp.where(low_group, qk, 0.0).astype(BF16)
            kr[pl.ds(at, group), :] = turn(qk).astype(BF16)
            packed_v = qkv_r[s, src, group:per_source, :].astype(F32)
            ones = jnp.where(
                lax.broadcasted_iota(jnp.int32, (half, LANES), 1) == HEAD_DIM, 1.0, 0.0
            )
            vx[pl.ds(at, half), :] = jnp.where(low_half, packed_v, ones).astype(BF16)
            vx[pl.ds(pl.multiple_of(at + half, half), half), :] = jnp.where(
                low_half, turn(packed_v), ones
            ).astype(BF16)
            return carry

        lax.fori_loop(0, wide, step, 0)

    def forward(s):
        @pl.when(sect == 1)
        def _():
            arrived(xfull.at[s, my_rows], ownx_sem.at[s])
            y_send_x(s).start()

        arrived(xfull.at[s, his_rows], yx_r.at[s])

        def norm_step(i, carry):
            at = pl.ds(pl.multiple_of(i * 32, 32), 32)
            a, _ = normed_rows(xfull[s, at, :].astype(F32))
            norm_st[0, at, :] = (a * gain[0:1, :] + shift[0:1, :]).astype(BF16)
            norm_st[1, at, :] = (a * gain[1:2, :] + shift[1:2, :]).astype(BF16)
            return carry

        lax.fori_loop(0, group // 32, norm_step, 0)
        pltpu.make_async_copy(norm_st.at[0], norm_hbm.at[0, s], store_sem.at[0]).start()
        pltpu.make_async_copy(norm_st.at[1], norm_hbm.at[1, s], store_sem.at[1]).start()

        def qkv_step(k, carry):
            pair = lax.rem(me // 2 + 1 + k, pairs)
            cols = pl.ds(pl.multiple_of(pair * 3 * LANES, LANES), 3 * LANES)
            packed = dot(norm_st[0], wqkv[:, cols]) + qkv_b[:, cols]
            first, middle, last = (packed[:, i * LANES : (i + 1) * LANES] for i in range(3))
            qk0 = rotary(first, cos, front, back, s, 1.0)
            qk1 = rotary(
                turn(jnp.where(low_group, last, middle)), cos, front, back, s, 1.0
            )
            vv = jnp.where(low_group, middle, last)
            v0 = jnp.where(low_half, vv[:half], turn(vv[half:]))
            v1 = jnp.where(low_half, turn(vv[:half]), vv[half:])
            for i, (qk, v) in enumerate(((qk0, v0), (qk1, v1))):
                qkv_st[2 * pair + i, 0:group, :] = qk.astype(BF16)
                qkv_st[2 * pair + i, group:per_source, :] = v.astype(BF16)
            for i in range(2):
                dest = 2 * pair + i
                spread(qkv_st.at[dest], qkv_r, s, dest, qkv_ss.at[0], qkv_rs.at[s])
            return carry

        lax.fori_loop(0, pairs, qkv_step, 0)

    def forward_ff(s):
        def ff_step(j, carry):
            cols = pl.ds(pl.multiple_of(j * COLS, COLS), COLS)
            pre = dot(norm_st[1], wup[:, cols]) + up_b[:, cols]
            cumul = 0.5 * (1.0 + lax.erf(pre * (1.0 / math.sqrt(2.0))))
            density = jnp.exp(-0.5 * pre * pre) * (1.0 / math.sqrt(2.0 * math.pi))
            hid = (pre * cumul).astype(BF16)
            hid_st[:, cols] = hid
            slope[s, :, cols] = (cumul + pre * density).astype(BF16)
            term = dot(hid, wdown[cols, :])

            @pl.when(j == 0)
            def _():
                part[...] = term

            @pl.when(j > 0)
            def _():
                part[...] += term

            return carry

        lax.fori_loop(0, ff // COLS, ff_step, 0)
        pltpu.make_async_copy(hid_st, hid_hbm.at[s], store_sem.at[2]).start()

    def forward_attention(s):
        arrived(qkv_r.at[s], qkv_rs.at[s])
        arrived(qkv_st.at[pl.ds(0, wide - 1)], qkv_ss.at[0])
        unpack_heads(s)

        def q_step(i, carry):
            q_at = pl.ds(pl.multiple_of(i * BLOCK, BLOCK), BLOCK)
            tokens = i * BLOCK + lax.broadcasted_iota(jnp.int32, (BLOCK, LANES), 0)
            begin = starts_of(s, tokens)[:, 0:1]
            token = tokens[:, 0:1]
            peak[...] = jnp.full(peak.shape, NEG, F32)

            def score_step(j, inner):
                k_at = pl.ds(pl.multiple_of(j * BLOCK, BLOCK), BLOCK)
                raw = dot_t(qm[q_at, :], kr[k_at, :])
                u = j * BLOCK + lax.broadcasted_iota(jnp.int32, (BLOCK, BLOCK), 1)
                raw = jnp.where((u >= begin) & (u <= token), raw, NEG)
                scores[:, k_at] = raw
                best = peak[...]
                for k in range(BLOCK // LANES):
                    best = jnp.maximum(best, raw[:, k * LANES : (k + 1) * LANES])
                peak[...] = best
                return inner

            lax.fori_loop(0, i + 1, score_step, 0)
            top = jnp.max(peak[...], axis=1, keepdims=True) * SCORE_SCALE
            acc[...] = jnp.zeros_like(acc)

            def value_step(j, inner):
                k_at = pl.ds(pl.multiple_of(j * BLOCK, BLOCK), BLOCK)
                probs = jnp.exp2(scores[:, k_at] * SCORE_SCALE - top)
                acc[...] += dot(probs.astype(BF16), vx[k_at, :])
                return inner

            lax.fori_loop(0, i + 1, value_step, 0)
            total = acc[:, HEAD_DIM : HEAD_DIM + 1]
            out = acc[...] / total
            log_total = top + jnp.log2(total)
            lse[s, i] = jnp.broadcast_to(log_total, (BLOCK, LANES)).T[0:8, :]
            for k in range(sources):
                first = out[k * group : k * group + half]
                second = out[k * group + half : (k + 1) * group]
                source = i * sources + k
                o_st[s, source] = jnp.where(low_half, first, turn(second)).astype(BF16)
                spread(o_st.at[s, source], mix_r, s, source, o_ss.at[s], o_rs.at[s])
            return carry

        lax.fori_loop(0, q_blocks, q_step, 0)

    def forward_out(s):
        arrived(mix_r.at[s], o_rs.at[s])
        arrived(o_st.at[s, pl.ds(0, wide - 1)], o_ss.at[s])
        for pair in range(pairs):
            top, bottom = pair_up(
                mix_r[s, 2 * pair].astype(F32), mix_r[s, 2 * pair + 1].astype(F32), low_half
            )
            mixed_st[0:half, pair * LANES : (pair + 1) * LANES] = top.astype(BF16)
            mixed_st[half:group, pair * LANES : (pair + 1) * LANES] = bottom.astype(BF16)
        pltpu.make_async_copy(mixed_st, mixed_hbm.at[s], store_sem.at[3]).start()
        part[...] += dot(mixed_st[...], wdense[...])
        rsf_st[...] = part[his_rows, :].astype(BF16)
        remote(rsf_st, rsf_r.at[s], rsf_ss.at[0], rsf_rs.at[s], y_dev).start()

    def forward_end(s):
        arrived(rsf_r.at[s], rsf_rs.at[s])

        def out_step(i, carry):
            at = pl.ds(pl.multiple_of(i * 32, 32), 32)
            there = pl.ds(pl.multiple_of(tens * rows + i * 32, 32), 32)
            branch = part[there, :] + rsf_r[s, at, :].astype(F32) + out_b[...]
            out_st[s, at, :] = (xfull[s, there, :].astype(F32) + branch).astype(BF16)
            return carry

        lax.fori_loop(0, rows // 32, out_step, 0)

        @pl.when(sect == 0)
        def _():
            remote(
                out_st.at[s], xfull.at[s, my_rows], xs_ss.at[s], ownx_sem.at[s], x_dev
            ).start()

        pltpu.make_async_copy(out_st.at[s], out_hbm.at[s], store_sem.at[4]).start()
        arrived(rsf_st, rsf_ss.at[0])
        arrived(norm_st.at[0], store_sem.at[0])
        arrived(norm_st.at[1], store_sem.at[1])
        arrived(hid_st, store_sem.at[2])
        arrived(mixed_st, store_sem.at[3])
        arrived(out_st.at[s], store_sem.at[4])

    def backward(s):
        @pl.when(sect == 0)
        def _():
            arrived(gfull.at[s, my_rows], owng_sem.at[s])
            y_send_g(s).start()

        arrived(gfull.at[s, his_rows], yg_r.at[s])
        pltpu.make_async_copy(gfull.at[s], g_hbm.at[s], store_sem.at[5]).start()

        def mixed_step(k, carry):
            pair = lax.rem(me // 2 + 1 + k, pairs)
            at = pl.ds(pl.multiple_of(pair * LANES, LANES), LANES)
            both = dot_t(gfull[s], wdense[at, :])
            first = jnp.where(low_half, both[:half], turn(both[half:]))
            second = jnp.where(low_half, turn(both[:half]), both[half:])
            do_st[2 * pair] = first.astype(BF16)
            do_st[2 * pair + 1] = second.astype(BF16)
            for i in range(2):
                dest = 2 * pair + i
                spread(do_st.at[dest], do_r, s, dest, do_ss.at[0], do_rs.at[s])
            return carry

        lax.fori_loop(0, pairs, mixed_step, 0)

    def backward_ff(s):
        def ff_step(j, carry):
            cols = pl.ds(pl.multiple_of(j * COLS, COLS), COLS)
            grad = dot_t(gfull[s], wdown[cols, :])
            grad = (grad * slope[s, :, cols].astype(F32)).astype(BF16)
            dpre_st[:, cols] = grad
            term = dot_t(grad, wup[:, cols])

            @pl.when(j == 0)
            def _():
                dn1[...] = term

            @pl.when(j > 0)
            def _():
                dn1[...] += term

            return carry

        lax.fori_loop(0, ff // COLS, ff_step, 0)
        pltpu.make_async_copy(dpre_st, dpre_hbm.at[s], store_sem.at[6]).start()

    def backward_attention(s):
        arrived(do_r.at[s], do_rs.at[s])
        arrived(do_st.at[pl.ds(0, wide - 1)], do_ss.at[0])
        unpack_heads(s)

        def unpack_step(src, carry):
            at = pl.multiple_of(src * group, group)
            grad = do_r[s, src].astype(F32)
            dox[pl.ds(at, half), :] = jnp.where(low_half, grad, 0.0).astype(BF16)
            dox[pl.ds(pl.multiple_of(at + half, half), half), :] = jnp.where(
                low_half, turn(grad), 0.0
            ).astype(BF16)
            product = grad * o_st[s, src].astype(F32)
            left = jnp.sum(jnp.where(low_half, product, 0.0), axis=1, keepdims=True)
            right = jnp.sum(jnp.where(low_half, 0.0, product), axis=1, keepdims=True)
            delta[src, :, 0:half] = jnp.broadcast_to(left, (half, LANES)).T[0:8, :]
            delta[src, :, half:group] = jnp.broadcast_to(right, (half, LANES)).T[0:8, :]
            return carry

        lax.fori_loop(0, wide, unpack_step, 0)
        dq[...] = jnp.zeros_like(dq)

        def k_step(j, carry):
            k_at = pl.ds(pl.multiple_of(j * BLOCK, BLOCK), BLOCK)
            acc[...] = jnp.zeros_like(acc)
            peak[...] = jnp.zeros_like(peak)

            def q_step(i, inner):
                q_at = pl.ds(pl.multiple_of(i * BLOCK, BLOCK), BLOCK)
                tokens = i * BLOCK + lax.broadcasted_iota(jnp.int32, (8, BLOCK), 1)
                begin = starts_of(s, tokens)[0:1, :]
                token = tokens[0:1, :]
                raw = dot_t(kr[k_at, :], qm[q_at, :])
                u = j * BLOCK + lax.broadcasted_iota(jnp.int32, (BLOCK, BLOCK), 0)
                probs = jnp.exp2(raw * SCORE_SCALE - lse[s, i, 0:1, :])
                probs = jnp.where((u >= begin) & (u <= token), probs, 0.0)
                probs_grad = dot_t(vx[k_at, :], dox[q_at, :])
                inner_sum = jnp.concatenate(
                    [delta[i * sources + k, 0:1, :] for k in range(sources)], axis=1
                )
                score_grad = (
                    probs * (probs_grad - inner_sum) * (1.0 / math.sqrt(HEAD_DIM))
                ).astype(BF16)
                acc[...] += dot(probs.astype(BF16), dox[q_at, :])
                peak[...] += dot(score_grad, qm_turned[q_at, :])
                dq[q_at, :] += t_dot(score_grad, kr[k_at, :])
                return inner

            qm_turned = kr
            lax.fori_loop(j, q_blocks, q_step, 0)
            for k in range(sources):
                source = j * sources + k
                mine = slice(k * group, (k + 1) * group)
                at = pl.ds(pl.multiple_of(source * group, group), group)
                both = jnp.where(low_group, dq[at, :], peak[mine, :])
                value = acc[mine, :]
                value = jnp.where(low_half, value[:half], turn(value[half:]))
                dqkv_st[source, 0:group, :] = both.astype(BF16)
                dqkv_st[source, group:per_source, :] = value.astype(BF16)
                spread(dqkv_st.at[source], dqkv_r, s, source, dqkv_ss.at[0], dqkv_rs.at[s])
            return carry

        lax.fori_loop(0, q_blocks, k_step, 0)

    def backward_norm(s):
        arrived(dqkv_r.at[s], dqkv_rs.at[s])
        arrived(dqkv_st.at[pl.ds(0, wide - 1)], dqkv_ss.at[0])

        def pair_step(pair, carry):
            qk0 = rotary(
                dqkv_r[s, 2 * pair, 0:group, :].astype(F32), cos, front, back, s, -1.0
            )
            qk1 = turn(
                rotary(
                    dqkv_r[s, 2 * pair + 1, 0:group, :].astype(F32), cos, front, back, s, -1.0
                )
            )
            top, bottom = pair_up(
                dqkv_r[s, 2 * pair, group:per_source, :].astype(F32),
                dqkv_r[s, 2 * pair + 1, group:per_source, :].astype(F32),
                low_half,
            )
            vv = jnp.concatenate([top, bottom], axis=0)
            at = pl.multiple_of(pair * 3 * LANES, LANES)
            dpk_st[:, pl.ds(at, LANES)] = qk0.astype(BF16)
            dpk_st[:, pl.ds(pl.multiple_of(at + LANES, LANES), LANES)] = jnp.where(
                low_group, vv, qk1
            ).astype(BF16)
            dpk_st[:, pl.ds(pl.multiple_of(at + 2 * LANES, LANES), LANES)] = jnp.where(
                low_group, qk1, vv
            ).astype(BF16)
            return carry

        lax.fori_loop(0, pairs, pair_step, 0)
        pltpu.make_async_copy(dpk_st, dpk_hbm.at[s], store_sem.at[7]).start()
        part[...] = dot_t(dpk_st[...], wqkv[...])

        def fold(values):
            total = values[0:8]
            for k in range(1, values.shape[0] // 8):
                total = total + values[k * 8 : (k + 1) * 8]
            return total

        def e_step(i, carry):
            at = pl.ds(pl.multiple_of(i * 32, 32), 32)
            a, _ = normed_rows(xfull[s, at, :].astype(F32))
            first = part[at, :]
            second = dn1[at, :]
            small[0] += fold(first * a)
            small[1] += fold(second * a)
            small[2] += fold(first)
            small[3] += fold(second)
            part[at, :] = first * gain[0:1, :] + second * gain[1:2, :]
            return carry

        lax.fori_loop(0, group // 32, e_step, 0)
        rsb_st[...] = part[his_rows, :].astype(BF16)
        remote(rsb_st, rsb_r.at[s], rsb_ss.at[0], rsb_rs.at[s], y_dev).start()

    def backward_end(s):
        def fold(values):
            total = values[0:8]
            for k in range(1, values.shape[0] // 8):
                total = total + values[k * 8 : (k + 1) * 8]
            return total

        arrived(rsb_r.at[s], rsb_rs.at[s])

        def in_step(i, carry):
            at = pl.ds(pl.multiple_of(i * 32, 32), 32)
            there = pl.ds(pl.multiple_of(tens * rows + i * 32, 32), 32)
            a, inv = normed_rows(xfull[s, there, :].astype(F32))
            e = part[there, :] + rsb_r[s, at, :].astype(F32)
            mean_e = jnp.mean(e, axis=-1, keepdims=True)
            cross = jnp.mean(e * a, axis=-1, keepdims=True)
            g_low = gfull[s, there, :].astype(F32)
            small[4] += fold(g_low)
            g = jnp.where(sect == 1, cot[s, at, :], g_low)
            grad = g + inv * (e - mean_e - a * cross)
            ig_st[at, :] = grad
            gx_st[s, at, :] = grad.astype(BF16)
            return carry

        lax.fori_loop(0, rows // 32, in_step, 0)

        @pl.when(sect == 1)
        def _():
            remote(
                gx_st.at[s], gfull.at[s, my_rows], gs_ss.at[s], owng_sem.at[s], x_dev
            ).start()

        pltpu.make_async_copy(ig_st, ig_hbm.at[s], store_sem.at[8]).start()
        arrived(rsb_st, rsb_ss.at[0])
        arrived(gfull.at[s], store_sem.at[5])
        arrived(dpre_st, store_sem.at[6])
        arrived(dpk_st, store_sem.at[7])
        arrived(ig_st, store_sem.at[8])

    def tick(step, carry):
        f_seq = step - sect
        b_seq = step - (3 - sect)
        f_on = (f_seq >= 0) & (f_seq < micro)
        b_on = (b_seq >= 0) & (b_seq < micro)
        pl.when(f_on)(lambda: forward(f_seq))
        pl.when(b_on)(lambda: backward(b_seq))
        pl.when(f_on)(lambda: forward_ff(f_seq))
        pl.when(b_on)(lambda: backward_ff(b_seq))
        pl.when(f_on)(lambda: forward_attention(f_seq))
        pl.when(b_on)(lambda: backward_attention(b_seq))

        @pl.when(f_on)
        def _():
            forward_out(f_seq)
            forward_end(f_seq)

        @pl.when(b_on)
        def _():
            backward_norm(b_seq)
            backward_end(b_seq)

        return carry

    lax.fori_loop(0, micro + 3, tick, 0)

    for s in range(micro):
        arrived(xfull.at[s, my_rows], yx_s.at[s])
        arrived(gfull.at[s, my_rows], yg_s.at[s])

    @pl.when(sect == 0)
    def _():
        for s in range(micro):
            arrived(out_st.at[s], xs_ss.at[s])

    @pl.when(sect == 1)
    def _():
        for s in range(micro):
            arrived(gx_st.at[s], gs_ss.at[s])


def rotary_tables(doc_lengths, tokens):
    ends = jnp.cumsum(doc_lengths, axis=1)
    starts = ends - doc_lengths
    inside = (tokens[None, :, None] >= starts[:, None, :]) & (
        tokens[None, :, None] < ends[:, None, :]
    )
    begins = jnp.sum(jnp.where(inside, starts[:, None, :], 0), axis=2)
    offsets = (tokens[None, :] - begins).astype(F32)
    part_of = ROT // 2
    freqs = ROPE_BASE ** (-2.0 * jnp.arange(part_of, dtype=F32) / ROT)
    angle = offsets[:, :, None] * freqs
    cos, sin = jnp.cos(angle), jnp.sin(angle)
    ones = jnp.ones(offsets.shape + (HEAD_DIM - ROT,), F32)
    zeros = jnp.zeros_like(sin)

    def lanes(parts):
        return jnp.concatenate(parts + parts, axis=2)

    return (
        ends.astype(jnp.int32),
        lanes([cos, cos, ones]),
        lanes([-sin, zeros, 0.0 * ones]),
        lanes([zeros, sin, 0.0 * ones]),
    )


def relay(dims, doc_lengths, block_input, cotangent, weights, collective_id):
    micro, rows, group, wide, heads, d_model, ff = dims
    (
        norm_gain,
        norm_bias,
        qkv_weight,
        qkv_bias,
        dense_weight,
        dense_bias,
        up_weight,
        up_bias,
        down_weight,
        down_bias,
    ) = weights
    tokens = lax.axis_index("wide") * group + jnp.arange(group, dtype=jnp.int32)
    ends, cos, front, back = rotary_tables(doc_lengths, tokens)
    inner = heads * HEAD_DIM
    per_source = group + group // 2
    anywhere = pl.BlockSpec(memory_space=pl.ANY)
    local = pl.BlockSpec(memory_space=pltpu.VMEM)
    scalars = pl.BlockSpec(memory_space=pltpu.SMEM)
    dma = pltpu.SemaphoreType.DMA
    vmem = pltpu.VMEM
    outs = [
        jax.ShapeDtypeStruct((micro, rows, d_model), BF16),
        jax.ShapeDtypeStruct((micro, rows, d_model), F32),
        jax.ShapeDtypeStruct((2, micro, group, d_model), BF16),
        jax.ShapeDtypeStruct((micro, group, d_model), BF16),
        jax.ShapeDtypeStruct((micro, group, inner), BF16),
        jax.ShapeDtypeStruct((micro, group, ff), BF16),
        jax.ShapeDtypeStruct((micro, group, ff), BF16),
        jax.ShapeDtypeStruct((micro, group, 3 * inner), BF16),
        jax.ShapeDtypeStruct((5, 8, d_model), F32),
    ]
    scratch = [
        vmem(qkv_weight.shape, BF16),
        vmem(dense_weight.shape, BF16),
        vmem(up_weight.shape, BF16),
        vmem(down_weight.shape, BF16),
        vmem((micro, group, d_model), BF16),
        vmem((micro, group, d_model), BF16),
        vmem((micro, rows, d_model), F32),
        vmem((micro, wide, per_source, LANES), BF16),
        vmem((micro, wide, group // 2, LANES), BF16),
        vmem((micro, wide, group // 2, LANES), BF16),
        vmem((micro, wide, per_source, LANES), BF16),
        vmem((micro, rows, d_model), BF16),
        vmem((micro, rows, d_model), BF16),
        vmem((wide, per_source, LANES), BF16),
        vmem((micro, wide, group // 2, LANES), BF16),
        vmem((wide, group // 2, LANES), BF16),
        vmem((wide, per_source, LANES), BF16),
        vmem((rows, d_model), BF16),
        vmem((rows, d_model), BF16),
        vmem((micro, rows, d_model), BF16),
        vmem((micro, rows, d_model), BF16),
        vmem((rows, d_model), F32),
        vmem((2, group, d_model), BF16),
        vmem((group, inner), BF16),
        vmem((group, ff), BF16),
        vmem((group, ff), BF16),
        vmem((group, 3 * inner), BF16),
        vmem((micro, group, ff), BF16),
        vmem((group, d_model), F32),
        vmem((group, d_model), F32),
        vmem((SEQ, LANES), BF16),
        vmem((SEQ, LANES), BF16),
        vmem((SEQ, LANES), BF16),
        vmem((SEQ, LANES), BF16),
        vmem((SEQ, LANES), F32),
        vmem((micro, SEQ // BLOCK, 8, BLOCK), F32),
        vmem((wide, 8, group), F32),
        vmem((BLOCK, SEQ), F32),
        vmem((BLOCK, LANES), F32),
        vmem((BLOCK, LANES), F32),
        dma((4,)),
        dma((micro,)),
        dma((micro,)),
        dma((micro,)),
        dma((micro,)),
        dma((micro,)),
        dma((micro,)),
        dma((1,)),
        dma((micro,)),
        dma((micro,)),
        dma((micro,)),
        dma((1,)),
        dma((micro,)),
        dma((1,)),
        dma((micro,)),
        dma((1,)),
        dma((micro,)),
        dma((1,)),
        dma((micro,)),
        dma((micro,)),
        dma((micro,)),
        dma((9,)),
    ]
    return pl.pallas_call(
        functools.partial(relay_kernel, dims),
        out_shape=outs,
        in_specs=[scalars, anywhere, anywhere]
        + [local] * 5
        + [anywhere] * 4
        + [local] * 3,
        out_specs=[anywhere] * 8 + [local],
        scratch_shapes=scratch,
        compiler_params=pltpu.CompilerParams(
            collective_id=collective_id, has_side_effects=True, vmem_limit_bytes=63 << 20
        ),
        name="relay",
    )(
        ends,
        block_input,
        cotangent,
        norm_gain,
        norm_bias,
        qkv_bias[None],
        up_bias[None],
        (dense_bias + down_bias)[None],
        qkv_weight,
        dense_weight,
        up_weight,
        down_weight,
        cos,
        front,
        back,
    )


def token_sum(left, right):
    return lax.dot_general(left, right, (((0,), (0,)), ((), ())), preferred_element_type=F32)


def relay_shards(
    block_input,
    doc_lengths,
    norm_gain,
    norm_bias,
    qkv_weight,
    qkv_bias,
    dense_weight,
    dense_bias,
    up_weight,
    up_bias,
    down_weight,
    down_bias,
    cotangent,
):
    weights = tuple(
        array[0]
        for array in (
            norm_gain,
            norm_bias,
            qkv_weight,
            qkv_bias,
            dense_weight,
            dense_bias,
            up_weight,
            up_bias,
            down_weight,
            down_bias,
        )
    )
    micro, rows, d_model = block_input.shape
    group = rows * lax.axis_size("tensor")
    wide = lax.axis_size("wide")
    heads = qkv_weight.shape[2] // (3 * HEAD_DIM)
    ff = up_weight.shape[2]
    dims = (micro, rows, group, wide, heads, d_model, ff)
    out, input_grad, normed, g_low, mixed, hidden, d_pre, d_packed, small = relay(
        dims, doc_lengths, block_input, cotangent, weights, 1
    )
    count = micro * group
    normed = normed.reshape(2, count, d_model)
    g_low = g_low.reshape(count, d_model)
    mixed = mixed.reshape(count, -1)
    hidden = hidden.reshape(count, -1)
    d_pre = d_pre.reshape(count, -1)
    d_packed = d_packed.reshape(count, -1)
    grads = (
        token_sum(normed[0], d_packed),
        token_sum(mixed, g_low),
        token_sum(normed[1], d_pre),
        token_sum(hidden, g_low),
    )
    qkv_grad, dense_grad, up_grad, down_grad = (
        lax.psum(grad.astype(BF16), "wide").astype(F32)[None] for grad in grads
    )
    biases = jnp.concatenate(
        [jnp.sum(d_packed.astype(F32), axis=0), jnp.sum(d_pre.astype(F32), axis=0)]
    )
    biases = lax.psum(biases, "wide")
    small = lax.psum(jnp.sum(small, axis=1), ("tensor", "wide"))
    qkv_width = d_packed.shape[1]
    return (
        out[None],
        input_grad[None],
        small[0:2][None],
        small[2:4][None],
        qkv_grad,
        biases[:qkv_width][None],
        dense_grad,
        small[4][None],
        up_grad,
        biases[qkv_width:][None],
        down_grad,
        small[4][None],
    )


def shortened(shard):

    def short(part):
        return part.astype(jnp.bfloat16) if part.dtype == jnp.float32 else part

    return jax.tree.map(short, shard)


def from_behind(block, axis, distance):
    devices = range(lax.axis_size(axis))
    route = [(i - distance, i) for i in devices if i - distance in devices]
    return lax.ppermute(block, axis, route)


def norm_parts(values, gain, shift):
    center = jnp.mean(values, axis=-1, keepdims=True)
    centred = values - center
    spread = jnp.mean(centred * centred, axis=-1, keepdims=True)
    inv_scale = lax.rsqrt(spread + EPSILON)
    normed = centred * inv_scale
    return (normed * gain + shift, normed, inv_scale)


def norm_back(grad, normed, inv_scale, gain):
    scaled = grad * gain
    inner_mean = jnp.mean(scaled, axis=-1, keepdims=True)
    cross_mean = jnp.mean(scaled * normed, axis=-1, keepdims=True)
    return inv_scale * (scaled - inner_mean - normed * cross_mean)


def doc_layout(lengths, tok_index):
    ends = jnp.cumsum(lengths)
    starts = ends - lengths
    doc_ids = jnp.sum((tok_index[:, None] >= ends[None, :]).astype(jnp.int32), axis=1)
    numbers = jnp.arange(lengths.shape[0], dtype=jnp.int32)
    picked = doc_ids[:, None] == numbers[None, :]
    begins = jnp.sum(jnp.where(picked, starts[None, :], 0), axis=1)
    return (doc_ids, tok_index - begins)


def rope_tables(offsets):
    half = ROT // 2
    freqs = ROPE_BASE ** (-2.0 * jnp.arange(half, dtype=jnp.float32) / ROT)
    angle = offsets.astype(jnp.float32)[:, None] * freqs[None, :]
    return (jnp.cos(angle)[:, None, :], jnp.sin(angle)[:, None, :])


def rotate(values, cos_table, sin_table):
    half = ROT // 2
    front = values[..., :half]
    back = values[..., half:ROT]
    turned = [
        front * cos_table - back * sin_table,
        back * cos_table + front * sin_table,
        values[..., ROT:],
    ]
    return jnp.concatenate(turned, axis=-1)


def unrotate(values, cos_table, sin_table):
    half = ROT // 2
    front = values[..., :half]
    back = values[..., half:ROT]
    turned = [
        front * cos_table + back * sin_table,
        back * cos_table - front * sin_table,
        values[..., ROT:],
    ]
    return jnp.concatenate(turned, axis=-1)


def gelu_parts(pre_act):
    cumul = 0.5 * (1.0 + lax.erf(pre_act * (1.0 / math.sqrt(2.0))))
    density = jnp.exp(-0.5 * pre_act * pre_act) * (1.0 / math.sqrt(2.0 * math.pi))
    return (pre_act * cumul, cumul + pre_act * density)


def store_slot(buffer, update, slot_here, is_valid):
    previous = lax.dynamic_index_in_dim(buffer, slot_here, 0, keepdims=False)
    return lax.dynamic_update_index_in_dim(
        buffer, jnp.where(is_valid, update, previous), slot_here, 0
    )


def gather_keys(key_rows, value_rows):
    return (
        lax.all_gather(key_rows, "wide", axis=0, tiled=True),
        lax.all_gather(value_rows, "wide", axis=0, tiled=True),
    )


def forward_parts(inputs, lengths, weights, with_output):
    (
        norm_gain,
        norm_bias,
        qkv_weight,
        qkv_bias,
        dense_weight,
        dense_bias,
        up_weight,
        up_bias,
        down_weight,
        down_bias,
    ) = weights
    seq_len = SEQ
    group = inputs.shape[0] * lax.axis_size("tensor")
    head_count = qkv_weight.shape[1] // (3 * HEAD_DIM)
    factor = 1.0 / math.sqrt(HEAD_DIM)
    values = inputs.astype(jnp.float32)
    norm_first, normed_first, scale_first = norm_parts(values, norm_gain[0], norm_bias[0])
    norm_second, normed_second, scale_second = norm_parts(values, norm_gain[1], norm_bias[1])
    full_first, full_second = (
        lax.all_gather(norm_first.astype(jnp.bfloat16), "tensor", axis=0, tiled=True),
        lax.all_gather(norm_second.astype(jnp.bfloat16), "tensor", axis=0, tiled=True),
    )
    tok_index = lax.axis_index("wide") * group + jnp.arange(group, dtype=jnp.int32)
    doc_ids, offsets = doc_layout(lengths, tok_index)
    all_index = jnp.arange(seq_len, dtype=jnp.int32)
    all_docs = doc_layout(lengths, all_index)[0]
    cos_table, sin_table = rope_tables(offsets)
    packed = jnp.dot(full_first, qkv_weight, preferred_element_type=jnp.float32) + qkv_bias
    packed = packed.reshape(group, head_count, 3, HEAD_DIM)
    queries = rotate(packed[:, :, 0], cos_table, sin_table).astype(jnp.bfloat16)
    key_here = rotate(packed[:, :, 1], cos_table, sin_table).astype(jnp.bfloat16)
    value_here = packed[:, :, 2].astype(jnp.bfloat16)
    key_all, value_all = gather_keys(key_here.reshape(group, -1), value_here.reshape(group, -1))
    key_heads = key_all.reshape(seq_len, head_count, HEAD_DIM)
    value_heads = value_all.reshape(seq_len, head_count, HEAD_DIM)
    allowed = (doc_ids[:, None] == all_docs[None, :]) & (all_index[None, :] <= tok_index[:, None])
    raw_scores = jnp.einsum("qhd,khd->qhk", queries, key_heads, preferred_element_type=jnp.float32)
    scores = jnp.where(allowed[:, None, :], raw_scores * factor, -jnp.inf)
    row_max = jnp.max(scores, axis=-1, keepdims=True)
    log_total = row_max + jnp.log(jnp.sum(jnp.exp(scores - row_max), axis=-1, keepdims=True))
    attn_probs = jnp.exp(scores - log_total)
    probs_low = attn_probs.astype(jnp.bfloat16)
    mixed_out = jnp.einsum(
        "qhk,khd->qhd", probs_low, value_heads, preferred_element_type=jnp.float32
    )
    mixed_out = mixed_out.reshape(group, -1).astype(jnp.bfloat16)
    up_pre = jnp.dot(full_second, up_weight, preferred_element_type=jnp.float32) + up_bias
    up_act, gelu_slope = gelu_parts(up_pre)
    hidden = up_act.astype(jnp.bfloat16)
    output = None
    if with_output:
        partial_value = jnp.dot(mixed_out, dense_weight, preferred_element_type=jnp.float32)
        partial_value = partial_value + jnp.dot(
            hidden, down_weight, preferred_element_type=jnp.float32
        )
        branch = (
            lax.psum_scatter(
                partial_value.astype(jnp.bfloat16), "tensor", scatter_dimension=0, tiled=True
            ).astype(jnp.float32)
            + dense_bias
            + down_bias
        )
        output = (values + branch).astype(jnp.bfloat16)
    return dict(
        output=output,
        normed_first=normed_first,
        scale_first=scale_first,
        normed_second=normed_second,
        scale_second=scale_second,
        full_first=full_first,
        full_second=full_second,
        tok_index=tok_index,
        doc_ids=doc_ids,
        all_index=all_index,
        all_docs=all_docs,
        cos_table=cos_table,
        sin_table=sin_table,
        queries=queries,
        key_here=key_here,
        value_here=value_here,
        key_all=key_all,
        value_all=value_all,
        key_heads=key_heads,
        value_heads=value_heads,
        attn_probs=attn_probs,
        probs_low=probs_low,
        log_total=log_total,
        mixed_out=mixed_out,
        gelu_slope=gelu_slope,
        hidden=hidden,
    )


def backward_parts(inputs, grad_out, lengths, weights):
    (
        norm_gain,
        norm_bias,
        qkv_weight,
        qkv_bias,
        dense_weight,
        dense_bias,
        up_weight,
        up_bias,
        down_weight,
        down_bias,
    ) = weights
    parts = forward_parts(inputs, lengths, weights, False)
    seq_len = SEQ
    group = inputs.shape[0] * lax.axis_size("tensor")
    head_count = qkv_weight.shape[1] // (3 * HEAD_DIM)
    factor = 1.0 / math.sqrt(HEAD_DIM)
    cos_table = parts["cos_table"]
    sin_table = parts["sin_table"]
    grad_low = grad_out.astype(jnp.bfloat16)
    grad_rows = grad_low.astype(jnp.float32)
    grad_full = lax.all_gather(grad_low, "tensor", axis=0, tiled=True)
    dense_grad = jnp.einsum(
        "cf,cd->fd", parts["mixed_out"], grad_full, preferred_element_type=jnp.float32
    )
    down_grad = jnp.einsum(
        "cf,cd->fd", parts["hidden"], grad_full, preferred_element_type=jnp.float32
    )
    hidden_grad = jnp.einsum(
        "cd,fd->cf", grad_full, down_weight, preferred_element_type=jnp.float32
    )
    pre_grad = (hidden_grad * parts["gelu_slope"]).astype(jnp.bfloat16)
    up_grad = jnp.einsum(
        "cd,cf->df", parts["full_second"], pre_grad, preferred_element_type=jnp.float32
    )
    up_bias_grad = jnp.sum(pre_grad.astype(jnp.float32), axis=0)
    second_grad = jnp.einsum("cf,df->cd", pre_grad, up_weight, preferred_element_type=jnp.float32)
    mixed_grad = jnp.einsum(
        "cd,fd->cf", grad_full, dense_weight, preferred_element_type=jnp.float32
    )
    mixed_grad = mixed_grad.astype(jnp.bfloat16).reshape(group, head_count, HEAD_DIM)
    attn_probs = parts["attn_probs"]
    probs_grad = jnp.einsum(
        "qhd,khd->qhk", mixed_grad, parts["value_heads"], preferred_element_type=jnp.float32
    )
    inner = jnp.sum(attn_probs * probs_grad, axis=-1, keepdims=True)
    score_grad = (attn_probs * (probs_grad - inner) * factor).astype(jnp.bfloat16)
    query_grad = jnp.einsum(
        "qhk,khd->qhd", score_grad, parts["key_heads"], preferred_element_type=jnp.float32
    )
    key_sums = jnp.einsum(
        "qhk,qhd->khd", score_grad, parts["queries"], preferred_element_type=jnp.float32
    )
    value_sums = jnp.einsum(
        "qhk,qhd->khd", parts["probs_low"], mixed_grad, preferred_element_type=jnp.float32
    )
    key_flat, value_flat = (
        lax.psum_scatter(
            key_sums.reshape(seq_len, -1).astype(jnp.bfloat16),
            "wide",
            scatter_dimension=0,
            tiled=True,
        ).astype(jnp.float32),
        lax.psum_scatter(
            value_sums.reshape(seq_len, -1).astype(jnp.bfloat16),
            "wide",
            scatter_dimension=0,
            tiled=True,
        ).astype(jnp.float32),
    )
    key_grad = key_flat.reshape(group, head_count, HEAD_DIM)
    value_grad = value_flat.reshape(group, head_count, HEAD_DIM)
    query_back = unrotate(query_grad, cos_table, sin_table)
    key_back = unrotate(key_grad, cos_table, sin_table)
    packed_grad = (
        jnp.stack([query_back, key_back, value_grad], axis=2)
        .reshape(group, -1)
        .astype(jnp.bfloat16)
    )
    qkv_grad = jnp.einsum(
        "cd,cf->df", parts["full_first"], packed_grad, preferred_element_type=jnp.float32
    )
    qkv_bias_grad = jnp.sum(packed_grad.astype(jnp.float32), axis=0)
    first_grad = jnp.einsum(
        "cf,df->cd", packed_grad, qkv_weight, preferred_element_type=jnp.float32
    )
    norm_first_grad, norm_second_grad = (
        lax.psum_scatter(
            first_grad.astype(jnp.bfloat16), "tensor", scatter_dimension=0, tiled=True
        ).astype(jnp.float32),
        lax.psum_scatter(
            second_grad.astype(jnp.bfloat16), "tensor", scatter_dimension=0, tiled=True
        ).astype(jnp.float32),
    )
    gain_grad = jnp.stack(
        [
            jnp.sum(norm_first_grad * parts["normed_first"], axis=0),
            jnp.sum(norm_second_grad * parts["normed_second"], axis=0),
        ]
    )
    shift_grad = jnp.stack([jnp.sum(norm_first_grad, axis=0), jnp.sum(norm_second_grad, axis=0)])
    input_grad = grad_out + norm_back(
        norm_first_grad, parts["normed_first"], parts["scale_first"], norm_gain[0]
    )
    input_grad = input_grad + norm_back(
        norm_second_grad, parts["normed_second"], parts["scale_second"], norm_gain[1]
    )
    bias_rows = jnp.sum(grad_rows, axis=0)
    terms = (
        gain_grad,
        shift_grad,
        qkv_grad,
        qkv_bias_grad,
        dense_grad,
        bias_rows,
        up_grad,
        up_bias_grad,
        down_grad,
        bias_rows,
    )
    return (input_grad, terms)


def general_shards(
    block_input,
    doc_lengths,
    norm_gain,
    norm_bias,
    qkv_weight,
    qkv_bias,
    dense_weight,
    dense_bias,
    up_weight,
    up_bias,
    down_weight,
    down_bias,
    cotangent,
):
    weights = (
        norm_gain[0],
        norm_bias[0],
        qkv_weight[0],
        qkv_bias[0],
        dense_weight[0],
        dense_bias[0],
        up_weight[0],
        up_bias[0],
        down_weight[0],
        down_bias[0],
    )
    section_index = lax.axis_index("section")
    last_section = lax.axis_size("section") - 1
    micro_count = block_input.shape[0]
    row_count = block_input.shape[1]
    tick_count = micro_count + last_section

    def forward_tick(carry, tick_index):
        incoming, kept_inputs, outputs, kept_pairs = carry
        slot_raw = tick_index - section_index
        is_valid = (slot_raw >= 0) & (slot_raw < micro_count)
        slot_here = jnp.clip(slot_raw, 0, micro_count - 1)
        fresh = lax.dynamic_index_in_dim(
            block_input, jnp.clip(tick_index, 0, micro_count - 1), 0, keepdims=False
        )
        inputs = jnp.where(section_index == 0, fresh, incoming)
        lengths = lax.dynamic_index_in_dim(doc_lengths, slot_here, 0, keepdims=False)
        parts = forward_parts(inputs, lengths, weights, True)
        output = parts["output"]
        kept_inputs = store_slot(kept_inputs, inputs, slot_here, is_valid)
        outputs = store_slot(outputs, output, slot_here, is_valid)
        incoming = jax.tree.map(
            lambda part, own: part.astype(own.dtype),
            from_behind(shortened(output), "section", 1),
            output,
        )
        return ((incoming, kept_inputs, outputs, kept_pairs), None)

    pair_init = (jnp.zeros((1,), jnp.bfloat16), jnp.zeros((1,), jnp.bfloat16))
    zero_rows = jnp.zeros((row_count, block_input.shape[2]), jnp.bfloat16)
    zero_stack = jnp.zeros(block_input.shape, jnp.bfloat16)
    forward_init = (zero_rows, zero_stack, zero_stack, pair_init)
    forward_done = lax.scan(forward_tick, forward_init, jnp.arange(tick_count, dtype=jnp.int32))[0]
    kept_inputs = forward_done[1]
    outputs = forward_done[2]
    kept_pairs = forward_done[3]

    def add_masked(total, term, scale_mask):
        return total + scale_mask * term

    def backward_tick(carry, tick_index):
        incoming, grads, input_grads = carry
        slot_raw = tick_index - (last_section - section_index)
        is_valid = (slot_raw >= 0) & (slot_raw < micro_count)
        slot_here = jnp.clip(slot_raw, 0, micro_count - 1)
        top_grad = lax.dynamic_index_in_dim(cotangent, slot_here, 0, keepdims=False)
        grad_out = jnp.where(section_index == last_section, top_grad, incoming)
        inputs = lax.dynamic_index_in_dim(kept_inputs, slot_here, 0, keepdims=False)
        lengths = lax.dynamic_index_in_dim(doc_lengths, slot_here, 0, keepdims=False)
        input_grad, terms = backward_parts(inputs, grad_out, lengths, weights)
        scale_mask = is_valid.astype(jnp.float32)
        grads = tuple((add_masked(total, term, scale_mask) for total, term in zip(grads, terms)))
        input_grads = store_slot(input_grads, input_grad, slot_here, is_valid)
        incoming = from_behind(shortened(input_grad), "section", -1).astype(input_grad.dtype)
        return ((incoming, grads, input_grads), None)

    grad_init = tuple((jnp.zeros(weight.shape, jnp.float32) for weight in weights))
    backward_init = (
        jnp.zeros((row_count, block_input.shape[2]), jnp.float32),
        grad_init,
        jnp.zeros(block_input.shape, jnp.float32),
    )
    backward_done = lax.scan(backward_tick, backward_init, jnp.arange(tick_count, dtype=jnp.int32))[
        0
    ]
    grads = backward_done[1]
    input_grads = backward_done[2]
    wide_sums = (
        lax.psum(grads[2].astype(jnp.bfloat16), "wide").astype(jnp.float32),
        lax.psum(grads[3].astype(jnp.bfloat16), "wide").astype(jnp.float32),
        lax.psum(grads[4].astype(jnp.bfloat16), "wide").astype(jnp.float32),
        lax.psum(grads[6].astype(jnp.bfloat16), "wide").astype(jnp.float32),
        lax.psum(grads[7].astype(jnp.bfloat16), "wide").astype(jnp.float32),
        lax.psum(grads[8].astype(jnp.bfloat16), "wide").astype(jnp.float32),
    )
    shared = lax.psum((grads[0], grads[1], grads[5], grads[9]), ("tensor", "wide"))
    return (
        outputs[None],
        input_grads[None],
        shared[0][None],
        shared[1][None],
        wide_sums[0][None],
        wide_sums[1][None],
        wide_sums[2][None],
        shared[2][None],
        wide_sums[3][None],
        wide_sums[4][None],
        wide_sums[5][None],
        shared[3][None],
    )


def solution(mesh):
    placed = (
        P(None, ("wide", "tensor"), None),
        P(),
        P("section", None, None),
        P("section", None, None),
        P("section", None, "tensor"),
        P("section", "tensor"),
        P("section", "tensor", None),
        P("section", None),
        P("section", None, "tensor"),
        P("section", "tensor"),
        P("section", "tensor", None),
        P("section", None),
        P(None, ("wide", "tensor"), None),
    )
    results = (
        P("section", None, ("wide", "tensor"), None),
        P("section", None, ("wide", "tensor"), None),
        P("section", None, None),
        P("section", None, None),
        P("section", None, "tensor"),
        P("section", "tensor"),
        P("section", "tensor", None),
        P("section", None),
        P("section", None, "tensor"),
        P("section", "tensor"),
        P("section", "tensor", None),
        P("section", None),
    )

    def program(*args):
        heads = args[4].shape[2] // (3 * HEAD_DIM * mesh.shape["tensor"])
        one_head_each = heads == mesh.shape["wide"] and heads % 2 == 0
        two_by_two = mesh.shape["section"] == 2 and mesh.shape["tensor"] == 2
        body = relay_shards if one_head_each and two_by_two else general_shards
        return jax.shard_map(
            body, mesh=mesh, in_specs=placed, out_specs=results, check_vma=False
        )(*args)

    return program
```

```python
import functools
import math

import jax
import jax.numpy as jnp
from jax import lax
from jax.experimental import pallas as pl
from jax.experimental.pallas import tpu as pltpu
from jax.sharding import PartitionSpec as P

HEAD_DIM = 64
ROT = 16
SEQ = 2048


EPSILON = 1e-05
ROPE_BASE = 10000.0

MESH = pl.DeviceIdType.MESH
F32 = jnp.float32
BF16 = jnp.bfloat16
LANES = 128
BLOCK = 512
COLS = 512
NEG = -1e30
SCORE_SCALE = math.log2(math.e) / math.sqrt(HEAD_DIM)


def dot(a, b):
    return jnp.dot(a, b, preferred_element_type=F32)


def dot_t(a, b):
    return lax.dot_general(a, b, (((1,), (1,)), ((), ())), preferred_element_type=F32)


def t_dot(a, b):
    return lax.dot_general(a, b, (((0,), (0,)), ((), ())), preferred_element_type=F32)


def lane_low(rows):
    return lax.broadcasted_iota(jnp.int32, (rows, LANES), 1) < HEAD_DIM


def turn(values):
    return pltpu.roll(values, HEAD_DIM, 1)


def rotary(values, cos_ref, front_ref, back_ref, seq, sign):
    cos, front, back = cos_ref[seq], front_ref[seq], back_ref[seq]
    ahead = pltpu.roll(values, LANES - ROT // 2, 1)
    behind = pltpu.roll(values, ROT // 2, 1)
    return values * cos + sign * (ahead * front + behind * back)


def pair_up(first, second, low):
    return jnp.where(low, first, turn(second)), jnp.where(low, turn(first), second)


def relay_kernel(
    dims,
    ends,
    x_hbm,
    cot_hbm,
    gain,
    shift,
    qkv_b,
    up_b,
    out_b,
    wqkv_hbm,
    wdense_hbm,
    wup_hbm,
    wdown_hbm,
    cos,
    front,
    back,
    out_hbm,
    ig_hbm,
    norm_hbm,
    g_hbm,
    mixed_hbm,
    hid_hbm,
    dpre_hbm,
    dpk_hbm,
    small,
    bias_sums,
    wqkv,
    wdense,
    wup,
    wdown,
    xfull,
    gfull,
    cot,
    qkv_r,
    mix_r,
    do_r,
    dqkv_r,
    rsf_r,
    rsb_r,
    qkv_st,
    o_st,
    do_st,
    dqkv_st,
    rsf_st,
    rsb_st,
    out_st,
    gx_st,
    ig_st,
    norm_st,
    mixed_st,
    hid_st,
    dpre_st,
    dpk_st,
    slope,
    part,
    dn1,
    qm,
    kr,
    vx,
    dox,
    dq,
    lse,
    delta,
    scores,
    peak,
    acc,
    wsem,
    ownx_sem,
    yx_s,
    yx_r,
    owng_sem,
    yg_s,
    yg_r,
    qkv_ss,
    qkv_rs,
    o_ss,
    o_rs,
    do_ss,
    do_rs,
    dqkv_ss,
    dqkv_rs,
    rsf_ss,
    rsf_rs,
    rsb_ss,
    rsb_rs,
    xs_ss,
    gs_ss,
    store_sem,
):
    micro, rows, group, wide, heads, d_model, ff = dims
    sect = lax.axis_index("section")
    tens = lax.axis_index("tensor")
    me = lax.axis_index("wide")
    pairs = heads // 2
    per_source = group + group // 2
    half = group // 2
    q_blocks = SEQ // BLOCK
    sources = BLOCK // group
    my_rows = pl.ds(pl.multiple_of(tens * rows, rows), rows)
    his_rows = pl.ds(pl.multiple_of((1 - tens) * rows, rows), rows)
    x_dev = {"section": 1 - sect}
    y_dev = {"tensor": 1 - tens}
    low_half = lane_low(half)
    low_group = lane_low(group)

    def remote(src, dst, ss, rs, dev):
        return pltpu.make_async_remote_copy(
            src_ref=src, dst_ref=dst, send_sem=ss, recv_sem=rs, device_id=dev, device_id_type=MESH
        )

    def arrived(ref, sem):
        pltpu.make_async_copy(ref, ref, sem).wait()

    def tokens_of(s):
        return pl.ds(pl.multiple_of(s * group, group), group)

    def y_send_x(s):
        own = xfull.at[s, my_rows]
        return remote(own, own, yx_s.at[s], yx_r.at[s], y_dev)

    def y_send_g(s):
        own = gfull.at[s, my_rows]
        return remote(own, own, yg_s.at[s], yg_r.at[s], y_dev)

    def spread(stage, target, seq, dest, ss, rs):
        @pl.when(dest == me)
        def _():
            pltpu.make_async_copy(stage, target.at[seq, me], rs).start()

        @pl.when(dest != me)
        def _():
            remote(stage, target.at[seq, me], ss, rs, {"wide": dest}).start()

    loads = [
        pltpu.make_async_copy(source, target, wsem.at[i])
        for i, (source, target) in enumerate(
            ((wqkv_hbm, wqkv), (wup_hbm, wup), (wdown_hbm, wdown), (wdense_hbm, wdense))
        )
    ]

    barrier = pltpu.get_barrier_semaphore()
    for dev in [x_dev, y_dev] + [{"wide": lax.rem(me + k, wide)} for k in range(1, wide)]:
        pl.semaphore_signal(barrier, inc=1, device_id=dev, device_id_type=MESH)

    @pl.when(sect == 0)
    def _():
        for s in range(micro):
            pltpu.make_async_copy(x_hbm.at[s], xfull.at[s, my_rows], ownx_sem.at[s]).start()

    for load in loads:
        load.start()

    @pl.when(sect == 1)
    def _():
        for s in range(micro):
            pltpu.make_async_copy(cot_hbm.at[s], cot.at[s], owng_sem.at[s]).start()

    small[...] = jnp.zeros_like(small)
    bias_sums[...] = jnp.zeros_like(bias_sums)
    pl.semaphore_wait(barrier, wide + 1)

    @pl.when(sect == 0)
    def _():
        for s in range(micro):
            arrived(xfull.at[s, my_rows], ownx_sem.at[s])
            y_send_x(s).start()

    @pl.when(sect == 1)
    def _():
        for s in range(micro):
            arrived(cot.at[s], owng_sem.at[s])

            def chunk(i, carry, s=s):
                at = pl.ds(pl.multiple_of(i * 32, 32), 32)
                there = pl.ds(pl.multiple_of(tens * rows + i * 32, 32), 32)
                gfull[s, there, :] = cot[s, at, :].astype(BF16)
                return carry

            lax.fori_loop(0, rows // 32, chunk, 0)
            y_send_g(s).start()

    for load in loads:
        load.wait()

    def fold(values):
        total = values[0:8]
        for k in range(1, values.shape[0] // 8):
            total = total + values[k * 8 : (k + 1) * 8]
        return total

    def normed_rows(values):
        center = jnp.mean(values, axis=-1, keepdims=True)
        centred = values - center
        spread_of = jnp.mean(centred * centred, axis=-1, keepdims=True)
        inv = lax.rsqrt(spread_of + EPSILON)
        return centred * inv, inv

    def starts_of(s, tokens):
        found = jnp.zeros_like(tokens)
        for j in range(ends.shape[1]):
            end = ends[s, j]
            found = jnp.where(tokens >= end, end, found)
        return found

    def unpack_heads(s):
        def step(src, carry):
            qk = qkv_r[s, src, 0:group, :].astype(F32)
            at = pl.multiple_of(src * group, group)
            qm[pl.ds(at, group), :] = jnp.where(low_group, qk, 0.0).astype(BF16)
            kr[pl.ds(at, group), :] = turn(qk).astype(BF16)
            packed_v = qkv_r[s, src, group:per_source, :].astype(F32)
            ones = jnp.where(
                lax.broadcasted_iota(jnp.int32, (half, LANES), 1) == HEAD_DIM, 1.0, 0.0
            )
            vx[pl.ds(at, half), :] = jnp.where(low_half, packed_v, ones).astype(BF16)
            vx[pl.ds(pl.multiple_of(at + half, half), half), :] = jnp.where(
                low_half, turn(packed_v), ones
            ).astype(BF16)
            return carry

        lax.fori_loop(0, wide, step, 0)

    def forward(s):
        @pl.when(sect == 1)
        def _():
            arrived(xfull.at[s, my_rows], ownx_sem.at[s])
            y_send_x(s).start()

        arrived(xfull.at[s, his_rows], yx_r.at[s])

        def norm_step(i, carry):
            at = pl.ds(pl.multiple_of(i * 32, 32), 32)
            a, _ = normed_rows(xfull[s, at, :].astype(F32))
            norm_st[0, at, :] = (a * gain[0:1, :] + shift[0:1, :]).astype(BF16)
            norm_st[1, at, :] = (a * gain[1:2, :] + shift[1:2, :]).astype(BF16)
            return carry

        lax.fori_loop(0, group // 32, norm_step, 0)
        pltpu.make_async_copy(norm_st.at[0], norm_hbm.at[0, tokens_of(s)], store_sem.at[0]).start()
        pltpu.make_async_copy(norm_st.at[1], norm_hbm.at[1, tokens_of(s)], store_sem.at[1]).start()

        def qkv_step(k, carry):
            pair = lax.rem(me // 2 + 1 + k, pairs)
            cols = pl.ds(pl.multiple_of(pair * 3 * LANES, LANES), 3 * LANES)
            packed = dot(norm_st[0], wqkv[:, cols]) + qkv_b[:, cols]
            first, middle, last = (packed[:, i * LANES : (i + 1) * LANES] for i in range(3))
            qk0 = rotary(first, cos, front, back, s, 1.0)
            qk1 = rotary(
                turn(jnp.where(low_group, last, middle)), cos, front, back, s, 1.0
            )
            vv = jnp.where(low_group, middle, last)
            v0 = jnp.where(low_half, vv[:half], turn(vv[half:]))
            v1 = jnp.where(low_half, turn(vv[:half]), vv[half:])
            for i, (qk, v) in enumerate(((qk0, v0), (qk1, v1))):
                qkv_st[2 * pair + i, 0:group, :] = qk.astype(BF16)
                qkv_st[2 * pair + i, group:per_source, :] = v.astype(BF16)
            for i in range(2):
                dest = 2 * pair + i
                spread(qkv_st.at[dest], qkv_r, s, dest, qkv_ss.at[0], qkv_rs.at[s])
            return carry

        lax.fori_loop(0, pairs, qkv_step, 0)

    def forward_ff(s):
        def ff_step(j, carry):
            cols = pl.ds(pl.multiple_of(j * COLS, COLS), COLS)
            pre = dot(norm_st[1], wup[:, cols]) + up_b[:, cols]
            cumul = 0.5 * (1.0 + lax.erf(pre * (1.0 / math.sqrt(2.0))))
            density = jnp.exp(-0.5 * pre * pre) * (1.0 / math.sqrt(2.0 * math.pi))
            hid = (pre * cumul).astype(BF16)
            hid_st[:, cols] = hid
            slope[s, :, cols] = (cumul + pre * density).astype(BF16)
            term = dot(hid, wdown[cols, :])

            @pl.when(j == 0)
            def _():
                part[...] = term

            @pl.when(j > 0)
            def _():
                part[...] += term

            return carry

        lax.fori_loop(0, ff // COLS, ff_step, 0)
        pltpu.make_async_copy(hid_st, hid_hbm.at[tokens_of(s)], store_sem.at[2]).start()

    def forward_attention(s):
        arrived(qkv_r.at[s], qkv_rs.at[s])
        arrived(qkv_st.at[pl.ds(0, wide - 1)], qkv_ss.at[0])
        unpack_heads(s)

        def q_step(i, carry):
            q_at = pl.ds(pl.multiple_of(i * BLOCK, BLOCK), BLOCK)
            tokens = i * BLOCK + lax.broadcasted_iota(jnp.int32, (BLOCK, LANES), 0)
            begin = starts_of(s, tokens)[:, 0:1]
            token = tokens[:, 0:1]
            peak[...] = jnp.full(peak.shape, NEG, F32)

            def score_step(j, inner):
                k_at = pl.ds(pl.multiple_of(j * BLOCK, BLOCK), BLOCK)
                raw = dot_t(qm[q_at, :], kr[k_at, :])
                u = j * BLOCK + lax.broadcasted_iota(jnp.int32, (BLOCK, BLOCK), 1)
                raw = jnp.where((u >= begin) & (u <= token), raw, NEG)
                scores[:, k_at] = raw
                best = peak[...]
                for k in range(BLOCK // LANES):
                    best = jnp.maximum(best, raw[:, k * LANES : (k + 1) * LANES])
                peak[...] = best
                return inner

            lax.fori_loop(0, i + 1, score_step, 0)
            top = jnp.max(peak[...], axis=1, keepdims=True) * SCORE_SCALE
            acc[...] = jnp.zeros_like(acc)

            def value_step(j, inner):
                k_at = pl.ds(pl.multiple_of(j * BLOCK, BLOCK), BLOCK)
                probs = jnp.exp2(scores[:, k_at] * SCORE_SCALE - top)
                acc[...] += dot(probs.astype(BF16), vx[k_at, :])
                return inner

            lax.fori_loop(0, i + 1, value_step, 0)
            total = acc[:, HEAD_DIM : HEAD_DIM + 1]
            out = acc[...] / total
            log_total = top + jnp.log2(total)
            lse[s, i] = jnp.broadcast_to(log_total, (BLOCK, LANES)).T[0:8, :]
            for k in range(sources):
                first = out[k * group : k * group + half]
                second = out[k * group + half : (k + 1) * group]
                source = i * sources + k
                o_st[s, source] = jnp.where(low_half, first, turn(second)).astype(BF16)
                spread(o_st.at[s, source], mix_r, s, source, o_ss.at[s], o_rs.at[s])
            return carry

        lax.fori_loop(0, q_blocks, q_step, 0)

    def forward_out(s):
        arrived(mix_r.at[s], o_rs.at[s])
        arrived(o_st.at[s, pl.ds(0, wide - 1)], o_ss.at[s])
        for pair in range(pairs):
            top, bottom = pair_up(
                mix_r[s, 2 * pair].astype(F32), mix_r[s, 2 * pair + 1].astype(F32), low_half
            )
            mixed_st[0:half, pair * LANES : (pair + 1) * LANES] = top.astype(BF16)
            mixed_st[half:group, pair * LANES : (pair + 1) * LANES] = bottom.astype(BF16)
        pltpu.make_async_copy(mixed_st, mixed_hbm.at[tokens_of(s)], store_sem.at[3]).start()
        part[...] += dot(mixed_st[...], wdense[...])
        rsf_st[...] = part[his_rows, :].astype(BF16)
        remote(rsf_st, rsf_r.at[s], rsf_ss.at[0], rsf_rs.at[s], y_dev).start()

    def forward_end(s):
        arrived(rsf_r.at[s], rsf_rs.at[s])

        def out_step(i, carry):
            at = pl.ds(pl.multiple_of(i * 32, 32), 32)
            there = pl.ds(pl.multiple_of(tens * rows + i * 32, 32), 32)
            branch = part[there, :] + rsf_r[s, at, :].astype(F32) + out_b[...]
            out_st[s, at, :] = (xfull[s, there, :].astype(F32) + branch).astype(BF16)
            return carry

        lax.fori_loop(0, rows // 32, out_step, 0)

        @pl.when(sect == 0)
        def _():
            remote(
                out_st.at[s], xfull.at[s, my_rows], xs_ss.at[s], ownx_sem.at[s], x_dev
            ).start()

        pltpu.make_async_copy(out_st.at[s], out_hbm.at[s], store_sem.at[4]).start()
        arrived(rsf_st, rsf_ss.at[0])
        arrived(norm_st.at[0], store_sem.at[0])
        arrived(norm_st.at[1], store_sem.at[1])
        arrived(hid_st, store_sem.at[2])
        arrived(mixed_st, store_sem.at[3])
        arrived(out_st.at[s], store_sem.at[4])

    def backward(s):
        @pl.when(sect == 0)
        def _():
            arrived(gfull.at[s, my_rows], owng_sem.at[s])
            y_send_g(s).start()

        arrived(gfull.at[s, his_rows], yg_r.at[s])
        pltpu.make_async_copy(gfull.at[s], g_hbm.at[tokens_of(s)], store_sem.at[5]).start()

        def mixed_step(k, carry):
            pair = lax.rem(me // 2 + 1 + k, pairs)
            at = pl.ds(pl.multiple_of(pair * LANES, LANES), LANES)
            both = dot_t(gfull[s], wdense[at, :])
            first = jnp.where(low_half, both[:half], turn(both[half:]))
            second = jnp.where(low_half, turn(both[:half]), both[half:])
            do_st[2 * pair] = first.astype(BF16)
            do_st[2 * pair + 1] = second.astype(BF16)
            for i in range(2):
                dest = 2 * pair + i
                spread(do_st.at[dest], do_r, s, dest, do_ss.at[0], do_rs.at[s])
            return carry

        lax.fori_loop(0, pairs, mixed_step, 0)

    def backward_ff(s):
        def ff_step(j, carry):
            cols = pl.ds(pl.multiple_of(j * COLS, COLS), COLS)
            grad = dot_t(gfull[s], wdown[cols, :])
            grad = (grad * slope[s, :, cols].astype(F32)).astype(BF16)
            dpre_st[:, cols] = grad
            sums_at = pl.ds(pl.multiple_of(3 * heads * HEAD_DIM + j * COLS, COLS), COLS)
            bias_sums[:, sums_at] += fold(grad.astype(F32))
            term = dot_t(grad, wup[:, cols])

            @pl.when(j == 0)
            def _():
                dn1[...] = term

            @pl.when(j > 0)
            def _():
                dn1[...] += term

            return carry

        lax.fori_loop(0, ff // COLS, ff_step, 0)
        pltpu.make_async_copy(dpre_st, dpre_hbm.at[tokens_of(s)], store_sem.at[6]).start()

    def backward_attention(s):
        arrived(do_r.at[s], do_rs.at[s])
        arrived(do_st.at[pl.ds(0, wide - 1)], do_ss.at[0])
        unpack_heads(s)

        def unpack_step(src, carry):
            at = pl.multiple_of(src * group, group)
            grad = do_r[s, src].astype(F32)
            dox[pl.ds(at, half), :] = jnp.where(low_half, grad, 0.0).astype(BF16)
            dox[pl.ds(pl.multiple_of(at + half, half), half), :] = jnp.where(
                low_half, turn(grad), 0.0
            ).astype(BF16)
            product = grad * o_st[s, src].astype(F32)
            left = jnp.sum(jnp.where(low_half, product, 0.0), axis=1, keepdims=True)
            right = jnp.sum(jnp.where(low_half, 0.0, product), axis=1, keepdims=True)
            delta[src, :, 0:half] = jnp.broadcast_to(left, (half, LANES)).T[0:8, :]
            delta[src, :, half:group] = jnp.broadcast_to(right, (half, LANES)).T[0:8, :]
            return carry

        lax.fori_loop(0, wide, unpack_step, 0)
        dq[...] = jnp.zeros_like(dq)

        def k_step(j, carry):
            k_at = pl.ds(pl.multiple_of(j * BLOCK, BLOCK), BLOCK)
            acc[...] = jnp.zeros_like(acc)
            peak[...] = jnp.zeros_like(peak)

            def q_step(i, inner):
                q_at = pl.ds(pl.multiple_of(i * BLOCK, BLOCK), BLOCK)
                tokens = i * BLOCK + lax.broadcasted_iota(jnp.int32, (8, BLOCK), 1)
                begin = starts_of(s, tokens)[0:1, :]
                token = tokens[0:1, :]
                raw = dot_t(kr[k_at, :], qm[q_at, :])
                u = j * BLOCK + lax.broadcasted_iota(jnp.int32, (BLOCK, BLOCK), 0)
                probs = jnp.exp2(raw * SCORE_SCALE - lse[s, i, 0:1, :])
                probs = jnp.where((u >= begin) & (u <= token), probs, 0.0)
                probs_grad = dot_t(vx[k_at, :], dox[q_at, :])
                inner_sum = jnp.concatenate(
                    [delta[i * sources + k, 0:1, :] for k in range(sources)], axis=1
                )
                score_grad = (
                    probs * (probs_grad - inner_sum) * (1.0 / math.sqrt(HEAD_DIM))
                ).astype(BF16)
                acc[...] += dot(probs.astype(BF16), dox[q_at, :])
                peak[...] += dot(score_grad, qm_turned[q_at, :])
                dq[q_at, :] += t_dot(score_grad, kr[k_at, :])
                return inner

            qm_turned = kr
            lax.fori_loop(j, q_blocks, q_step, 0)
            for k in range(sources):
                source = j * sources + k
                mine = slice(k * group, (k + 1) * group)
                at = pl.ds(pl.multiple_of(source * group, group), group)
                both = jnp.where(low_group, dq[at, :], peak[mine, :])
                value = acc[mine, :]
                value = jnp.where(low_half, value[:half], turn(value[half:]))
                dqkv_st[source, 0:group, :] = both.astype(BF16)
                dqkv_st[source, group:per_source, :] = value.astype(BF16)
                spread(dqkv_st.at[source], dqkv_r, s, source, dqkv_ss.at[0], dqkv_rs.at[s])
            return carry

        lax.fori_loop(0, q_blocks, k_step, 0)

    def backward_norm(s):
        arrived(dqkv_r.at[s], dqkv_rs.at[s])
        arrived(dqkv_st.at[pl.ds(0, wide - 1)], dqkv_ss.at[0])

        def pair_step(pair, carry):
            qk0 = rotary(
                dqkv_r[s, 2 * pair, 0:group, :].astype(F32), cos, front, back, s, -1.0
            )
            qk1 = turn(
                rotary(
                    dqkv_r[s, 2 * pair + 1, 0:group, :].astype(F32), cos, front, back, s, -1.0
                )
            )
            top, bottom = pair_up(
                dqkv_r[s, 2 * pair, group:per_source, :].astype(F32),
                dqkv_r[s, 2 * pair + 1, group:per_source, :].astype(F32),
                low_half,
            )
            vv = jnp.concatenate([top, bottom], axis=0)
            columns = (qk0, jnp.where(low_group, vv, qk1), jnp.where(low_group, qk1, vv))
            for k, column in enumerate(columns):
                at = pl.ds(pl.multiple_of((pair * 3 + k) * LANES, LANES), LANES)
                column = column.astype(BF16)
                dpk_st[:, at] = column
                bias_sums[:, at] += fold(column.astype(F32))
            return carry

        lax.fori_loop(0, pairs, pair_step, 0)
        pltpu.make_async_copy(dpk_st, dpk_hbm.at[tokens_of(s)], store_sem.at[7]).start()
        part[...] = dot_t(dpk_st[...], wqkv[...])

        def e_step(i, carry):
            at = pl.ds(pl.multiple_of(i * 32, 32), 32)
            a, _ = normed_rows(xfull[s, at, :].astype(F32))
            first = part[at, :]
            second = dn1[at, :]
            small[0] += fold(first * a)
            small[1] += fold(second * a)
            small[2] += fold(first)
            small[3] += fold(second)
            part[at, :] = first * gain[0:1, :] + second * gain[1:2, :]
            return carry

        lax.fori_loop(0, group // 32, e_step, 0)
        rsb_st[...] = part[his_rows, :].astype(BF16)
        remote(rsb_st, rsb_r.at[s], rsb_ss.at[0], rsb_rs.at[s], y_dev).start()

    def backward_end(s):
        arrived(rsb_r.at[s], rsb_rs.at[s])

        def in_step(i, carry):
            at = pl.ds(pl.multiple_of(i * 32, 32), 32)
            there = pl.ds(pl.multiple_of(tens * rows + i * 32, 32), 32)
            a, inv = normed_rows(xfull[s, there, :].astype(F32))
            e = part[there, :] + rsb_r[s, at, :].astype(F32)
            mean_e = jnp.mean(e, axis=-1, keepdims=True)
            cross = jnp.mean(e * a, axis=-1, keepdims=True)
            g_low = gfull[s, there, :].astype(F32)
            small[4] += fold(g_low)
            g = jnp.where(sect == 1, cot[s, at, :], g_low)
            grad = g + inv * (e - mean_e - a * cross)
            ig_st[at, :] = grad
            gx_st[s, at, :] = grad.astype(BF16)
            return carry

        lax.fori_loop(0, rows // 32, in_step, 0)

        @pl.when(sect == 1)
        def _():
            remote(
                gx_st.at[s], gfull.at[s, my_rows], gs_ss.at[s], owng_sem.at[s], x_dev
            ).start()

        pltpu.make_async_copy(ig_st, ig_hbm.at[s], store_sem.at[8]).start()
        arrived(rsb_st, rsb_ss.at[0])
        arrived(gfull.at[s], store_sem.at[5])
        arrived(dpre_st, store_sem.at[6])
        arrived(dpk_st, store_sem.at[7])
        arrived(ig_st, store_sem.at[8])

    def tick(step, carry):
        f_seq = step - sect
        b_seq = step - (3 - sect)
        f_on = (f_seq >= 0) & (f_seq < micro)
        b_on = (b_seq >= 0) & (b_seq < micro)
        pl.when(f_on)(lambda: forward(f_seq))
        pl.when(b_on)(lambda: backward(b_seq))
        pl.when(f_on)(lambda: forward_ff(f_seq))
        pl.when(b_on)(lambda: backward_ff(b_seq))
        pl.when(f_on)(lambda: forward_attention(f_seq))
        pl.when(b_on)(lambda: backward_attention(b_seq))

        @pl.when(f_on)
        def _():
            forward_out(f_seq)
            forward_end(f_seq)

        @pl.when(b_on)
        def _():
            backward_norm(b_seq)
            backward_end(b_seq)

        return carry

    lax.fori_loop(0, micro + 3, tick, 0)

    for s in range(micro):
        arrived(xfull.at[s, my_rows], yx_s.at[s])
        arrived(gfull.at[s, my_rows], yg_s.at[s])

    @pl.when(sect == 0)
    def _():
        for s in range(micro):
            arrived(out_st.at[s], xs_ss.at[s])

    @pl.when(sect == 1)
    def _():
        for s in range(micro):
            arrived(gx_st.at[s], gs_ss.at[s])


def rotary_tables(doc_lengths, tokens):
    ends = jnp.cumsum(doc_lengths, axis=1)
    starts = ends - doc_lengths
    inside = (tokens[None, :, None] >= starts[:, None, :]) & (
        tokens[None, :, None] < ends[:, None, :]
    )
    begins = jnp.sum(jnp.where(inside, starts[:, None, :], 0), axis=2)
    offsets = (tokens[None, :] - begins).astype(F32)
    part_of = ROT // 2
    freqs = ROPE_BASE ** (-2.0 * jnp.arange(part_of, dtype=F32) / ROT)
    angle = offsets[:, :, None] * freqs
    cos, sin = jnp.cos(angle), jnp.sin(angle)
    ones = jnp.ones(offsets.shape + (HEAD_DIM - ROT,), F32)
    zeros = jnp.zeros_like(sin)

    def lanes(parts):
        return jnp.concatenate(parts + parts, axis=2)

    return (
        ends.astype(jnp.int32),
        lanes([cos, cos, ones]),
        lanes([-sin, zeros, 0.0 * ones]),
        lanes([zeros, sin, 0.0 * ones]),
    )


def relay(dims, doc_lengths, block_input, cotangent, weights, collective_id):
    micro, rows, group, wide, heads, d_model, ff = dims
    (
        norm_gain,
        norm_bias,
        qkv_weight,
        qkv_bias,
        dense_weight,
        dense_bias,
        up_weight,
        up_bias,
        down_weight,
        down_bias,
    ) = weights
    tokens = lax.axis_index("wide") * group + jnp.arange(group, dtype=jnp.int32)
    ends, cos, front, back = rotary_tables(doc_lengths, tokens)
    inner = heads * HEAD_DIM
    per_source = group + group // 2
    anywhere = pl.BlockSpec(memory_space=pl.ANY)
    local = pl.BlockSpec(memory_space=pltpu.VMEM)
    scalars = pl.BlockSpec(memory_space=pltpu.SMEM)
    dma = pltpu.SemaphoreType.DMA
    vmem = pltpu.VMEM
    outs = [
        jax.ShapeDtypeStruct((micro, rows, d_model), BF16),
        jax.ShapeDtypeStruct((micro, rows, d_model), F32),
        jax.ShapeDtypeStruct((2, micro * group, d_model), BF16),
        jax.ShapeDtypeStruct((micro * group, d_model), BF16),
        jax.ShapeDtypeStruct((micro * group, inner), BF16),
        jax.ShapeDtypeStruct((micro * group, ff), BF16),
        jax.ShapeDtypeStruct((micro * group, ff), BF16),
        jax.ShapeDtypeStruct((micro * group, 3 * inner), BF16),
        jax.ShapeDtypeStruct((5, 8, d_model), F32),
        jax.ShapeDtypeStruct((8, 3 * inner + ff), F32),
    ]
    scratch = [
        vmem(qkv_weight.shape, BF16),
        vmem(dense_weight.shape, BF16),
        vmem(up_weight.shape, BF16),
        vmem(down_weight.shape, BF16),
        vmem((micro, group, d_model), BF16),
        vmem((micro, group, d_model), BF16),
        vmem((micro, rows, d_model), F32),
        vmem((micro, wide, per_source, LANES), BF16),
        vmem((micro, wide, group // 2, LANES), BF16),
        vmem((micro, wide, group // 2, LANES), BF16),
        vmem((micro, wide, per_source, LANES), BF16),
        vmem((micro, rows, d_model), BF16),
        vmem((micro, rows, d_model), BF16),
        vmem((wide, per_source, LANES), BF16),
        vmem((micro, wide, group // 2, LANES), BF16),
        vmem((wide, group // 2, LANES), BF16),
        vmem((wide, per_source, LANES), BF16),
        vmem((rows, d_model), BF16),
        vmem((rows, d_model), BF16),
        vmem((micro, rows, d_model), BF16),
        vmem((micro, rows, d_model), BF16),
        vmem((rows, d_model), F32),
        vmem((2, group, d_model), BF16),
        vmem((group, inner), BF16),
        vmem((group, ff), BF16),
        vmem((group, ff), BF16),
        vmem((group, 3 * inner), BF16),
        vmem((micro, group, ff), BF16),
        vmem((group, d_model), F32),
        vmem((group, d_model), F32),
        vmem((SEQ, LANES), BF16),
        vmem((SEQ, LANES), BF16),
        vmem((SEQ, LANES), BF16),
        vmem((SEQ, LANES), BF16),
        vmem((SEQ, LANES), F32),
        vmem((micro, SEQ // BLOCK, 8, BLOCK), F32),
        vmem((wide, 8, group), F32),
        vmem((BLOCK, SEQ), F32),
        vmem((BLOCK, LANES), F32),
        vmem((BLOCK, LANES), F32),
        dma((4,)),
        dma((micro,)),
        dma((micro,)),
        dma((micro,)),
        dma((micro,)),
        dma((micro,)),
        dma((micro,)),
        dma((1,)),
        dma((micro,)),
        dma((micro,)),
        dma((micro,)),
        dma((1,)),
        dma((micro,)),
        dma((1,)),
        dma((micro,)),
        dma((1,)),
        dma((micro,)),
        dma((1,)),
        dma((micro,)),
        dma((micro,)),
        dma((micro,)),
        dma((9,)),
    ]
    return pl.pallas_call(
        functools.partial(relay_kernel, dims),
        out_shape=outs,
        in_specs=[scalars, anywhere, anywhere]
        + [local] * 5
        + [anywhere] * 4
        + [local] * 3,
        out_specs=[anywhere] * 8 + [local] * 2,
        scratch_shapes=scratch,
        compiler_params=pltpu.CompilerParams(
            collective_id=collective_id, has_side_effects=True, vmem_limit_bytes=63 << 20
        ),
        name="relay",
    )(
        ends,
        block_input,
        cotangent,
        norm_gain,
        norm_bias,
        qkv_bias[None],
        up_bias[None],
        (dense_bias + down_bias)[None],
        qkv_weight,
        dense_weight,
        up_weight,
        down_weight,
        cos,
        front,
        back,
    )


TILE = 256
RING = 8
TOTALS = 4


def gradient_kinds(d_model, inner, ff):
    return ((d_model, ff), (ff, d_model), (inner, d_model), (d_model, 3 * inner))


def gradient_kernel(
    dims,
    norm_hbm,
    g_hbm,
    mixed_hbm,
    hid_hbm,
    dpre_hbm,
    dpk_hbm,
    small,
    biases,
    up_out,
    down_out,
    dense_out,
    qkv_out,
    sums,
    left_op,
    right_op,
    own,
    core_r,
    outer_r,
    inner_r,
    core_st,
    red_st,
    tot,
    sums_r,
    op_sem,
    core_ss,
    core_rs,
    outer_rs,
    inner_rs,
    red_ss,
    bc_rs,
    tot_ss,
    fwd_ss,
    share_ss,
    fin_rs,
    sum_ss,
    sum_rs,
    core_free,
    outer_free,
    inner_free,
):
    micro, rows, group, wide, heads, d_model, ff = dims
    tens = lax.axis_index("tensor")
    me = lax.axis_index("wide")
    chip, core = me // 2, lax.rem(me, 2)
    partner = {"wide": me + 1 - 2 * core}
    up_dev = {"wide": lax.rem(me + 2, wide)}
    down_dev = {"wide": lax.rem(me + wide - 2, wide)}
    at_bottom, at_top = chip == 0, chip == wide // 2 - 1
    at_end = at_bottom | at_top
    middle = jnp.logical_not(at_end)
    lower = chip == 1
    outer_of = {"wide": jnp.where(lower, me - 2, lax.rem(me + 2, wide))}
    inner_of = {"wide": jnp.where(lower, me + 2, lax.rem(me + wide - 2, wide))}
    end_of = {"wide": jnp.where(at_bottom, me + 2, lax.rem(me + wide - 2, wide))}
    inner = heads * HEAD_DIM
    kinds = gradient_kinds(d_model, inner, ff)
    targets = (up_out, down_out, dense_out, qkv_out)
    operands = (
        (norm_hbm.at[1], dpre_hbm),
        (hid_hbm, g_hbm),
        (mixed_hbm, g_hbm),
        (norm_hbm.at[0], dpk_hbm),
    )
    ranges, first = [], 0
    for height, width in kinds:
        count = (height // TILE) * (width // (2 * TILE))
        ranges.append((first, first + count, width // (2 * TILE)))
        first += count
    steps = first

    def remote(src, dst, ss, rs, dev):
        return pltpu.make_async_remote_copy(
            src_ref=src, dst_ref=dst, send_sem=ss, recv_sem=rs, device_id=dev, device_id_type=MESH
        )

    def arrived(ref, sem):
        pltpu.make_async_copy(ref, ref, sem).wait()

    tile_ref = tot.at[0]

    def by_kind(m, body):
        for kind, (low, high, across) in enumerate(ranges):

            @pl.when((m >= low) & (m < high))
            def _(kind=kind, low=low, across=across):
                at = m - low
                body(kind, at // across, lax.rem(at, across))

    def tile_of(kind, row, col, which):
        return targets[kind].at[
            pl.ds(pl.multiple_of(row * TILE, TILE), TILE),
            pl.ds(pl.multiple_of((2 * col + which) * TILE, TILE), TILE),
        ]

    def fetch(m):
        def body(kind, row, col):
            left, right = operands[kind]
            slot = lax.rem(m, 2)
            pltpu.make_async_copy(
                left.at[:, pl.ds(pl.multiple_of(row * TILE, TILE), TILE)],
                left_op.at[slot],
                op_sem.at[0, slot],
            ).start()
            pltpu.make_async_copy(
                right.at[:, pl.ds(pl.multiple_of(col * 2 * TILE, 2 * TILE), 2 * TILE)],
                right_op.at[slot],
                op_sem.at[1, slot],
            ).start()

        by_kind(m, body)

    def is_root(m):
        return middle & (chip == 1 + lax.rem(m, 2))

    def products(m):
        slot, ring = lax.rem(m, 2), lax.rem(m, RING)
        arrived(left_op.at[slot], op_sem.at[0, slot])
        arrived(right_op.at[slot], op_sem.at[1, slot])
        left = left_op[slot]
        mine = pl.ds(pl.multiple_of(core * TILE, TILE), TILE)
        other = pl.ds(pl.multiple_of((1 - core) * TILE, TILE), TILE)

        @pl.when(m >= RING)
        def _():
            arrived(tile_ref, core_ss.at[ring])
            pl.semaphore_wait(core_free, 1)

        core_st[ring] = t_dot(left, right_op[slot, :, other]).astype(BF16)
        remote(
            core_st.at[ring], core_r.at[ring], core_ss.at[ring], core_rs.at[ring], partner
        ).start()
        own[ring] = t_dot(left, right_op[slot, :, mine])

    def send_red(m, value, target, sem, dev, free):
        ring = lax.rem(m, RING)

        @pl.when(m >= RING)
        def _():
            pl.semaphore_wait(free, 1)

        red_st[ring] = value.astype(BF16)
        remote(red_st.at[ring], target.at[ring], red_ss.at[ring], sem.at[ring], dev).start()

    def chip_sum(m):
        ring = lax.rem(m, RING)
        arrived(tile_ref, core_rs.at[ring])
        total = own[ring] + core_r[ring].astype(F32)

        @pl.when(m + RING < steps)
        def _():
            pl.semaphore_signal(core_free, inc=1, device_id=partner, device_id_type=MESH)

        @pl.when(at_end)
        def _():
            @pl.when(m >= RING)
            def _():
                arrived(tile_ref, red_ss.at[ring])

            send_red(m, total, outer_r, outer_rs, end_of, outer_free.at[lax.rem(m, 2)])

        @pl.when(middle)
        def _():
            own[ring] = total

    def take_outer(m):
        ring = lax.rem(m, RING)
        arrived(tile_ref, outer_rs.at[ring])
        total = own[ring] + outer_r[ring].astype(F32)

        @pl.when(m + RING < steps)
        def _():
            pl.semaphore_signal(
                outer_free.at[lax.rem(m, 2)], inc=1, device_id=outer_of, device_id_type=MESH
            )

        return total

    def pass_in(m):
        ring = lax.rem(m, RING)
        total = take_outer(m)

        @pl.when(m >= RING)
        def _():
            arrived(tile_ref, red_ss.at[ring])

        send_red(m, total, inner_r, inner_rs, inner_of, inner_free)

    def finish(m):
        ring = lax.rem(m, RING)
        slot = lax.rem(m // 2, TOTALS)
        total = take_outer(m)
        arrived(tile_ref, inner_rs.at[ring])
        total = total + inner_r[ring].astype(F32)

        @pl.when(m + RING < steps)
        def _():
            pl.semaphore_signal(inner_free, inc=1, device_id=inner_of, device_id_type=MESH)

        @pl.when(m >= 2 * TOTALS)
        def _():
            for k in range(4):
                arrived(tile_ref, tot_ss.at[k, slot])

        tot[slot] = total.astype(BF16)

        def body(kind, row, col):
            here = tile_of(kind, row, col, core)
            remote(tot.at[slot], here, tot_ss.at[0, slot], bc_rs.at[m], outer_of).start()
            remote(tot.at[slot], here, tot_ss.at[1, slot], bc_rs.at[m], inner_of).start()
            remote(tot.at[slot], here, tot_ss.at[2, slot], fin_rs.at[kind], partner).start()
            pltpu.make_async_copy(tot.at[slot], here, tot_ss.at[3, slot]).start()

        by_kind(m, body)

    def hand_on(m):
        arrived(tile_ref, bc_rs.at[m])

        def body(kind, row, col):
            here = tile_of(kind, row, col, core)

            @pl.when(middle)
            def _():
                remote(here, here, fwd_ss.at[m], bc_rs.at[m], outer_of).start()

            remote(here, here, share_ss.at[m], fin_rs.at[kind], partner).start()

        by_kind(m, body)

    exchanges = (
        {"tensor": 1 - tens},
        partner,
        {"wide": me + 2 - 4 * lax.rem(chip, 2)},
        {"wide": me + 4 - 8 * (chip // 2)},
    )

    barrier = pltpu.get_barrier_semaphore()
    for dev in exchanges:
        pl.semaphore_signal(barrier, inc=1, device_id=dev, device_id_type=MESH)

    @pl.when(middle)
    def _():
        pl.semaphore_signal(barrier, inc=1, device_id=inner_of, device_id_type=MESH)

    fetch(jnp.int32(0))
    sums[:, 0:d_model] = jnp.concatenate(
        [jnp.sum(small[k], axis=0, keepdims=True) for k in range(5)]
        + [jnp.zeros((3, d_model), F32)],
        axis=0,
    )
    total = jnp.sum(biases[...], axis=0, keepdims=True)
    lines = [total[:, k * COLS : (k + 1) * COLS] for k in range(total.shape[1] // COLS)]
    lines.append(jnp.zeros((8 - len(lines), COLS), F32))
    sums[:, d_model:] = jnp.concatenate(lines, axis=0)
    pl.when(middle)(lambda: pl.semaphore_wait(barrier, len(exchanges) + 1))
    pl.when(at_end)(lambda: pl.semaphore_wait(barrier, len(exchanges)))

    def exchange_start(k):
        if k > 0:
            arrived(sums, sum_ss.at[0])
        sums_r[0] = sums[...]
        remote(sums_r.at[0], sums_r.at[k + 1], sum_ss.at[0], sum_rs.at[k], exchanges[k]).start()

    def exchange_end(k):
        arrived(sums, sum_rs.at[k])
        if k == 0:
            sums[:, 0:d_model] += sums_r[1, :, 0:d_model]
        else:
            sums[...] += sums_r[k + 1]

    def step(i, carry):
        pl.when(i + 1 < steps)(lambda: fetch(i + 1))
        pl.when(i < steps)(lambda: products(i))
        for k in range(4):
            pl.when(i == 4 * k + 2)(lambda k=k: exchange_start(k))
            pl.when(i == 4 * k + 5)(lambda k=k: exchange_end(k))

        def at(lag, allowed, body):
            m = i - lag
            pl.when((m >= 0) & (m < steps) & allowed(m))(lambda: body(m))

        at(1, lambda m: m >= 0, chip_sum)
        at(3, lambda m: middle & jnp.logical_not(is_root(m)), pass_in)
        at(5, is_root, finish)
        at(8, lambda m: middle & jnp.logical_not(is_root(m)), hand_on)
        at(10, lambda m: at_end, hand_on)
        return carry

    lax.fori_loop(0, steps + 10, step, 0)

    arrived(sums, sum_ss.at[0])
    for ring in range(RING):
        arrived(tile_ref, core_ss.at[ring])

    def drain(m, carry):
        ring = lax.rem(m, RING)
        root = is_root(m)
        last = m + RING >= steps
        pl.when(at_end & last)(lambda: arrived(tile_ref, red_ss.at[ring]))
        pl.when(middle & jnp.logical_not(root) & last)(
            lambda: arrived(tile_ref, red_ss.at[ring])
        )

        @pl.when(root & (m + 2 * TOTALS >= steps))
        def _():
            for k in range(4):
                arrived(tile_ref, tot_ss.at[k, lax.rem(m // 2, TOTALS)])

        @pl.when(middle & jnp.logical_not(root))
        def _():
            arrived(tile_ref, fwd_ss.at[m])

        pl.when(jnp.logical_not(root))(lambda: arrived(tile_ref, share_ss.at[m]))
        return carry

    lax.fori_loop(0, steps, drain, 0)
    for kind, (height, width) in enumerate(kinds):
        arrived(targets[kind].at[pl.ds(0, height // 2)], fin_rs.at[kind])


def gradient_sums(dims, operands, small, biases, collective_id):
    micro, rows, group, wide, heads, d_model, ff = dims
    inner = heads * HEAD_DIM
    kinds = gradient_kinds(d_model, inner, ff)
    steps = sum((height // TILE) * (width // (2 * TILE)) for height, width in kinds)
    count = micro * group
    anywhere = pl.BlockSpec(memory_space=pl.ANY)
    local = pl.BlockSpec(memory_space=pltpu.VMEM)
    dma = pltpu.SemaphoreType.DMA
    regular = pltpu.SemaphoreType.REGULAR
    vmem = pltpu.VMEM
    width = d_model + COLS
    return pl.pallas_call(
        functools.partial(gradient_kernel, dims),
        out_shape=[jax.ShapeDtypeStruct(kind, BF16) for kind in kinds]
        + [jax.ShapeDtypeStruct((8, width), F32)],
        in_specs=[anywhere] * 6 + [local] * 2,
        out_specs=[anywhere] * 4 + [local],
        scratch_shapes=[
            vmem((2, count, TILE), BF16),
            vmem((2, count, 2 * TILE), BF16),
            vmem((RING, TILE, TILE), F32),
            vmem((RING, TILE, TILE), BF16),
            vmem((RING, TILE, TILE), BF16),
            vmem((RING, TILE, TILE), BF16),
            vmem((RING, TILE, TILE), BF16),
            vmem((RING, TILE, TILE), BF16),
            vmem((TOTALS, TILE, TILE), BF16),
            vmem((5, 8, width), F32),
            dma((2, 2)),
            dma((RING,)),
            dma((RING,)),
            dma((RING,)),
            dma((RING,)),
            dma((RING,)),
            dma((steps,)),
            dma((4, TOTALS)),
            dma((steps,)),
            dma((steps,)),
            dma((4,)),
            dma((1,)),
            dma((4,)),
            regular,
            regular((2,)),
            regular,
        ],
        compiler_params=pltpu.CompilerParams(
            collective_id=collective_id, has_side_effects=True, vmem_limit_bytes=40 << 20
        ),
        name="gradient_sums",
    )(*operands, small, biases)


def relay_shards(
    block_input,
    doc_lengths,
    norm_gain,
    norm_bias,
    qkv_weight,
    qkv_bias,
    dense_weight,
    dense_bias,
    up_weight,
    up_bias,
    down_weight,
    down_bias,
    cotangent,
):
    weights = tuple(
        array[0]
        for array in (
            norm_gain,
            norm_bias,
            qkv_weight,
            qkv_bias,
            dense_weight,
            dense_bias,
            up_weight,
            up_bias,
            down_weight,
            down_bias,
        )
    )
    micro, rows, d_model = block_input.shape
    group = rows * lax.axis_size("tensor")
    wide = lax.axis_size("wide")
    heads = qkv_weight.shape[2] // (3 * HEAD_DIM)
    ff = up_weight.shape[2]
    dims = (micro, rows, group, wide, heads, d_model, ff)
    out, input_grad, *operands, small, bias_sums = relay(
        dims, doc_lengths, block_input, cotangent, weights, 1
    )
    up_grad, down_grad, dense_grad, qkv_grad, sums = gradient_sums(
        dims, operands, small, bias_sums, 2
    )
    up_grad, down_grad, dense_grad, qkv_grad = (
        grad.astype(F32)[None] for grad in (up_grad, down_grad, dense_grad, qkv_grad)
    )
    biases = sums[:, d_model:].reshape(1, -1)
    qkv_width = qkv_weight.shape[2]
    out_bias_grad = sums[4:5, :d_model]
    return (
        out[None],
        input_grad[None],
        sums[None, 0:2, :d_model],
        sums[None, 2:4, :d_model],
        qkv_grad,
        biases[:, :qkv_width],
        dense_grad,
        out_bias_grad,
        up_grad,
        biases[:, qkv_width : qkv_width + ff],
        down_grad,
        out_bias_grad,
    )


def shortened(shard):

    def short(part):
        return part.astype(jnp.bfloat16) if part.dtype == jnp.float32 else part

    return jax.tree.map(short, shard)


def from_behind(block, axis, distance):
    devices = range(lax.axis_size(axis))
    route = [(i - distance, i) for i in devices if i - distance in devices]
    return lax.ppermute(block, axis, route)


def norm_parts(values, gain, shift):
    center = jnp.mean(values, axis=-1, keepdims=True)
    centred = values - center
    spread = jnp.mean(centred * centred, axis=-1, keepdims=True)
    inv_scale = lax.rsqrt(spread + EPSILON)
    normed = centred * inv_scale
    return (normed * gain + shift, normed, inv_scale)


def norm_back(grad, normed, inv_scale, gain):
    scaled = grad * gain
    inner_mean = jnp.mean(scaled, axis=-1, keepdims=True)
    cross_mean = jnp.mean(scaled * normed, axis=-1, keepdims=True)
    return inv_scale * (scaled - inner_mean - normed * cross_mean)


def doc_layout(lengths, tok_index):
    ends = jnp.cumsum(lengths)
    starts = ends - lengths
    doc_ids = jnp.sum((tok_index[:, None] >= ends[None, :]).astype(jnp.int32), axis=1)
    numbers = jnp.arange(lengths.shape[0], dtype=jnp.int32)
    picked = doc_ids[:, None] == numbers[None, :]
    begins = jnp.sum(jnp.where(picked, starts[None, :], 0), axis=1)
    return (doc_ids, tok_index - begins)


def rope_tables(offsets):
    half = ROT // 2
    freqs = ROPE_BASE ** (-2.0 * jnp.arange(half, dtype=jnp.float32) / ROT)
    angle = offsets.astype(jnp.float32)[:, None] * freqs[None, :]
    return (jnp.cos(angle)[:, None, :], jnp.sin(angle)[:, None, :])


def rotate(values, cos_table, sin_table):
    half = ROT // 2
    front = values[..., :half]
    back = values[..., half:ROT]
    turned = [
        front * cos_table - back * sin_table,
        back * cos_table + front * sin_table,
        values[..., ROT:],
    ]
    return jnp.concatenate(turned, axis=-1)


def unrotate(values, cos_table, sin_table):
    half = ROT // 2
    front = values[..., :half]
    back = values[..., half:ROT]
    turned = [
        front * cos_table + back * sin_table,
        back * cos_table - front * sin_table,
        values[..., ROT:],
    ]
    return jnp.concatenate(turned, axis=-1)


def gelu_parts(pre_act):
    cumul = 0.5 * (1.0 + lax.erf(pre_act * (1.0 / math.sqrt(2.0))))
    density = jnp.exp(-0.5 * pre_act * pre_act) * (1.0 / math.sqrt(2.0 * math.pi))
    return (pre_act * cumul, cumul + pre_act * density)


def store_slot(buffer, update, slot_here, is_valid):
    previous = lax.dynamic_index_in_dim(buffer, slot_here, 0, keepdims=False)
    return lax.dynamic_update_index_in_dim(
        buffer, jnp.where(is_valid, update, previous), slot_here, 0
    )


def gather_keys(key_rows, value_rows):
    return (
        lax.all_gather(key_rows, "wide", axis=0, tiled=True),
        lax.all_gather(value_rows, "wide", axis=0, tiled=True),
    )


def forward_parts(inputs, lengths, weights, with_output):
    (
        norm_gain,
        norm_bias,
        qkv_weight,
        qkv_bias,
        dense_weight,
        dense_bias,
        up_weight,
        up_bias,
        down_weight,
        down_bias,
    ) = weights
    seq_len = SEQ
    group = inputs.shape[0] * lax.axis_size("tensor")
    head_count = qkv_weight.shape[1] // (3 * HEAD_DIM)
    factor = 1.0 / math.sqrt(HEAD_DIM)
    values = inputs.astype(jnp.float32)
    norm_first, normed_first, scale_first = norm_parts(values, norm_gain[0], norm_bias[0])
    norm_second, normed_second, scale_second = norm_parts(values, norm_gain[1], norm_bias[1])
    full_first, full_second = (
        lax.all_gather(norm_first.astype(jnp.bfloat16), "tensor", axis=0, tiled=True),
        lax.all_gather(norm_second.astype(jnp.bfloat16), "tensor", axis=0, tiled=True),
    )
    tok_index = lax.axis_index("wide") * group + jnp.arange(group, dtype=jnp.int32)
    doc_ids, offsets = doc_layout(lengths, tok_index)
    all_index = jnp.arange(seq_len, dtype=jnp.int32)
    all_docs = doc_layout(lengths, all_index)[0]
    cos_table, sin_table = rope_tables(offsets)
    packed = jnp.dot(full_first, qkv_weight, preferred_element_type=jnp.float32) + qkv_bias
    packed = packed.reshape(group, head_count, 3, HEAD_DIM)
    queries = rotate(packed[:, :, 0], cos_table, sin_table).astype(jnp.bfloat16)
    key_here = rotate(packed[:, :, 1], cos_table, sin_table).astype(jnp.bfloat16)
    value_here = packed[:, :, 2].astype(jnp.bfloat16)
    key_all, value_all = gather_keys(key_here.reshape(group, -1), value_here.reshape(group, -1))
    key_heads = key_all.reshape(seq_len, head_count, HEAD_DIM)
    value_heads = value_all.reshape(seq_len, head_count, HEAD_DIM)
    allowed = (doc_ids[:, None] == all_docs[None, :]) & (all_index[None, :] <= tok_index[:, None])
    raw_scores = jnp.einsum("qhd,khd->qhk", queries, key_heads, preferred_element_type=jnp.float32)
    scores = jnp.where(allowed[:, None, :], raw_scores * factor, -jnp.inf)
    row_max = jnp.max(scores, axis=-1, keepdims=True)
    log_total = row_max + jnp.log(jnp.sum(jnp.exp(scores - row_max), axis=-1, keepdims=True))
    attn_probs = jnp.exp(scores - log_total)
    probs_low = attn_probs.astype(jnp.bfloat16)
    mixed_out = jnp.einsum(
        "qhk,khd->qhd", probs_low, value_heads, preferred_element_type=jnp.float32
    )
    mixed_out = mixed_out.reshape(group, -1).astype(jnp.bfloat16)
    up_pre = jnp.dot(full_second, up_weight, preferred_element_type=jnp.float32) + up_bias
    up_act, gelu_slope = gelu_parts(up_pre)
    hidden = up_act.astype(jnp.bfloat16)
    output = None
    if with_output:
        partial_value = jnp.dot(mixed_out, dense_weight, preferred_element_type=jnp.float32)
        partial_value = partial_value + jnp.dot(
            hidden, down_weight, preferred_element_type=jnp.float32
        )
        branch = (
            lax.psum_scatter(
                partial_value.astype(jnp.bfloat16), "tensor", scatter_dimension=0, tiled=True
            ).astype(jnp.float32)
            + dense_bias
            + down_bias
        )
        output = (values + branch).astype(jnp.bfloat16)
    return dict(
        output=output,
        normed_first=normed_first,
        scale_first=scale_first,
        normed_second=normed_second,
        scale_second=scale_second,
        full_first=full_first,
        full_second=full_second,
        tok_index=tok_index,
        doc_ids=doc_ids,
        all_index=all_index,
        all_docs=all_docs,
        cos_table=cos_table,
        sin_table=sin_table,
        queries=queries,
        key_here=key_here,
        value_here=value_here,
        key_all=key_all,
        value_all=value_all,
        key_heads=key_heads,
        value_heads=value_heads,
        attn_probs=attn_probs,
        probs_low=probs_low,
        log_total=log_total,
        mixed_out=mixed_out,
        gelu_slope=gelu_slope,
        hidden=hidden,
    )


def backward_parts(inputs, grad_out, lengths, weights):
    (
        norm_gain,
        norm_bias,
        qkv_weight,
        qkv_bias,
        dense_weight,
        dense_bias,
        up_weight,
        up_bias,
        down_weight,
        down_bias,
    ) = weights
    parts = forward_parts(inputs, lengths, weights, False)
    seq_len = SEQ
    group = inputs.shape[0] * lax.axis_size("tensor")
    head_count = qkv_weight.shape[1] // (3 * HEAD_DIM)
    factor = 1.0 / math.sqrt(HEAD_DIM)
    cos_table = parts["cos_table"]
    sin_table = parts["sin_table"]
    grad_low = grad_out.astype(jnp.bfloat16)
    grad_rows = grad_low.astype(jnp.float32)
    grad_full = lax.all_gather(grad_low, "tensor", axis=0, tiled=True)
    dense_grad = jnp.einsum(
        "cf,cd->fd", parts["mixed_out"], grad_full, preferred_element_type=jnp.float32
    )
    down_grad = jnp.einsum(
        "cf,cd->fd", parts["hidden"], grad_full, preferred_element_type=jnp.float32
    )
    hidden_grad = jnp.einsum(
        "cd,fd->cf", grad_full, down_weight, preferred_element_type=jnp.float32
    )
    pre_grad = (hidden_grad * parts["gelu_slope"]).astype(jnp.bfloat16)
    up_grad = jnp.einsum(
        "cd,cf->df", parts["full_second"], pre_grad, preferred_element_type=jnp.float32
    )
    up_bias_grad = jnp.sum(pre_grad.astype(jnp.float32), axis=0)
    second_grad = jnp.einsum("cf,df->cd", pre_grad, up_weight, preferred_element_type=jnp.float32)
    mixed_grad = jnp.einsum(
        "cd,fd->cf", grad_full, dense_weight, preferred_element_type=jnp.float32
    )
    mixed_grad = mixed_grad.astype(jnp.bfloat16).reshape(group, head_count, HEAD_DIM)
    attn_probs = parts["attn_probs"]
    probs_grad = jnp.einsum(
        "qhd,khd->qhk", mixed_grad, parts["value_heads"], preferred_element_type=jnp.float32
    )
    inner = jnp.sum(attn_probs * probs_grad, axis=-1, keepdims=True)
    score_grad = (attn_probs * (probs_grad - inner) * factor).astype(jnp.bfloat16)
    query_grad = jnp.einsum(
        "qhk,khd->qhd", score_grad, parts["key_heads"], preferred_element_type=jnp.float32
    )
    key_sums = jnp.einsum(
        "qhk,qhd->khd", score_grad, parts["queries"], preferred_element_type=jnp.float32
    )
    value_sums = jnp.einsum(
        "qhk,qhd->khd", parts["probs_low"], mixed_grad, preferred_element_type=jnp.float32
    )
    key_flat, value_flat = (
        lax.psum_scatter(
            key_sums.reshape(seq_len, -1).astype(jnp.bfloat16),
            "wide",
            scatter_dimension=0,
            tiled=True,
        ).astype(jnp.float32),
        lax.psum_scatter(
            value_sums.reshape(seq_len, -1).astype(jnp.bfloat16),
            "wide",
            scatter_dimension=0,
            tiled=True,
        ).astype(jnp.float32),
    )
    key_grad = key_flat.reshape(group, head_count, HEAD_DIM)
    value_grad = value_flat.reshape(group, head_count, HEAD_DIM)
    query_back = unrotate(query_grad, cos_table, sin_table)
    key_back = unrotate(key_grad, cos_table, sin_table)
    packed_grad = (
        jnp.stack([query_back, key_back, value_grad], axis=2)
        .reshape(group, -1)
        .astype(jnp.bfloat16)
    )
    qkv_grad = jnp.einsum(
        "cd,cf->df", parts["full_first"], packed_grad, preferred_element_type=jnp.float32
    )
    qkv_bias_grad = jnp.sum(packed_grad.astype(jnp.float32), axis=0)
    first_grad = jnp.einsum(
        "cf,df->cd", packed_grad, qkv_weight, preferred_element_type=jnp.float32
    )
    norm_first_grad, norm_second_grad = (
        lax.psum_scatter(
            first_grad.astype(jnp.bfloat16), "tensor", scatter_dimension=0, tiled=True
        ).astype(jnp.float32),
        lax.psum_scatter(
            second_grad.astype(jnp.bfloat16), "tensor", scatter_dimension=0, tiled=True
        ).astype(jnp.float32),
    )
    gain_grad = jnp.stack(
        [
            jnp.sum(norm_first_grad * parts["normed_first"], axis=0),
            jnp.sum(norm_second_grad * parts["normed_second"], axis=0),
        ]
    )
    shift_grad = jnp.stack([jnp.sum(norm_first_grad, axis=0), jnp.sum(norm_second_grad, axis=0)])
    input_grad = grad_out + norm_back(
        norm_first_grad, parts["normed_first"], parts["scale_first"], norm_gain[0]
    )
    input_grad = input_grad + norm_back(
        norm_second_grad, parts["normed_second"], parts["scale_second"], norm_gain[1]
    )
    bias_rows = jnp.sum(grad_rows, axis=0)
    terms = (
        gain_grad,
        shift_grad,
        qkv_grad,
        qkv_bias_grad,
        dense_grad,
        bias_rows,
        up_grad,
        up_bias_grad,
        down_grad,
        bias_rows,
    )
    return (input_grad, terms)


def general_shards(
    block_input,
    doc_lengths,
    norm_gain,
    norm_bias,
    qkv_weight,
    qkv_bias,
    dense_weight,
    dense_bias,
    up_weight,
    up_bias,
    down_weight,
    down_bias,
    cotangent,
):
    weights = (
        norm_gain[0],
        norm_bias[0],
        qkv_weight[0],
        qkv_bias[0],
        dense_weight[0],
        dense_bias[0],
        up_weight[0],
        up_bias[0],
        down_weight[0],
        down_bias[0],
    )
    section_index = lax.axis_index("section")
    last_section = lax.axis_size("section") - 1
    micro_count = block_input.shape[0]
    row_count = block_input.shape[1]
    tick_count = micro_count + last_section

    def forward_tick(carry, tick_index):
        incoming, kept_inputs, outputs, kept_pairs = carry
        slot_raw = tick_index - section_index
        is_valid = (slot_raw >= 0) & (slot_raw < micro_count)
        slot_here = jnp.clip(slot_raw, 0, micro_count - 1)
        fresh = lax.dynamic_index_in_dim(
            block_input, jnp.clip(tick_index, 0, micro_count - 1), 0, keepdims=False
        )
        inputs = jnp.where(section_index == 0, fresh, incoming)
        lengths = lax.dynamic_index_in_dim(doc_lengths, slot_here, 0, keepdims=False)
        parts = forward_parts(inputs, lengths, weights, True)
        output = parts["output"]
        kept_inputs = store_slot(kept_inputs, inputs, slot_here, is_valid)
        outputs = store_slot(outputs, output, slot_here, is_valid)
        incoming = jax.tree.map(
            lambda part, own: part.astype(own.dtype),
            from_behind(shortened(output), "section", 1),
            output,
        )
        return ((incoming, kept_inputs, outputs, kept_pairs), None)

    pair_init = (jnp.zeros((1,), jnp.bfloat16), jnp.zeros((1,), jnp.bfloat16))
    zero_rows = jnp.zeros((row_count, block_input.shape[2]), jnp.bfloat16)
    zero_stack = jnp.zeros(block_input.shape, jnp.bfloat16)
    forward_init = (zero_rows, zero_stack, zero_stack, pair_init)
    forward_done = lax.scan(forward_tick, forward_init, jnp.arange(tick_count, dtype=jnp.int32))[0]
    kept_inputs = forward_done[1]
    outputs = forward_done[2]
    kept_pairs = forward_done[3]

    def add_masked(total, term, scale_mask):
        return total + scale_mask * term

    def backward_tick(carry, tick_index):
        incoming, grads, input_grads = carry
        slot_raw = tick_index - (last_section - section_index)
        is_valid = (slot_raw >= 0) & (slot_raw < micro_count)
        slot_here = jnp.clip(slot_raw, 0, micro_count - 1)
        top_grad = lax.dynamic_index_in_dim(cotangent, slot_here, 0, keepdims=False)
        grad_out = jnp.where(section_index == last_section, top_grad, incoming)
        inputs = lax.dynamic_index_in_dim(kept_inputs, slot_here, 0, keepdims=False)
        lengths = lax.dynamic_index_in_dim(doc_lengths, slot_here, 0, keepdims=False)
        input_grad, terms = backward_parts(inputs, grad_out, lengths, weights)
        scale_mask = is_valid.astype(jnp.float32)
        grads = tuple((add_masked(total, term, scale_mask) for total, term in zip(grads, terms)))
        input_grads = store_slot(input_grads, input_grad, slot_here, is_valid)
        incoming = from_behind(shortened(input_grad), "section", -1).astype(input_grad.dtype)
        return ((incoming, grads, input_grads), None)

    grad_init = tuple((jnp.zeros(weight.shape, jnp.float32) for weight in weights))
    backward_init = (
        jnp.zeros((row_count, block_input.shape[2]), jnp.float32),
        grad_init,
        jnp.zeros(block_input.shape, jnp.float32),
    )
    backward_done = lax.scan(backward_tick, backward_init, jnp.arange(tick_count, dtype=jnp.int32))[
        0
    ]
    grads = backward_done[1]
    input_grads = backward_done[2]
    wide_sums = (
        lax.psum(grads[2].astype(jnp.bfloat16), "wide").astype(jnp.float32),
        lax.psum(grads[3].astype(jnp.bfloat16), "wide").astype(jnp.float32),
        lax.psum(grads[4].astype(jnp.bfloat16), "wide").astype(jnp.float32),
        lax.psum(grads[6].astype(jnp.bfloat16), "wide").astype(jnp.float32),
        lax.psum(grads[7].astype(jnp.bfloat16), "wide").astype(jnp.float32),
        lax.psum(grads[8].astype(jnp.bfloat16), "wide").astype(jnp.float32),
    )
    shared = lax.psum((grads[0], grads[1], grads[5], grads[9]), ("tensor", "wide"))
    return (
        outputs[None],
        input_grads[None],
        shared[0][None],
        shared[1][None],
        wide_sums[0][None],
        wide_sums[1][None],
        wide_sums[2][None],
        shared[2][None],
        wide_sums[3][None],
        wide_sums[4][None],
        wide_sums[5][None],
        shared[3][None],
    )


def solution(mesh):
    placed = (
        P(None, ("wide", "tensor"), None),
        P(),
        P("section", None, None),
        P("section", None, None),
        P("section", None, "tensor"),
        P("section", "tensor"),
        P("section", "tensor", None),
        P("section", None),
        P("section", None, "tensor"),
        P("section", "tensor"),
        P("section", "tensor", None),
        P("section", None),
        P(None, ("wide", "tensor"), None),
    )
    results = (
        P("section", None, ("wide", "tensor"), None),
        P("section", None, ("wide", "tensor"), None),
        P("section", None, None),
        P("section", None, None),
        P("section", None, "tensor"),
        P("section", "tensor"),
        P("section", "tensor", None),
        P("section", None),
        P("section", None, "tensor"),
        P("section", "tensor"),
        P("section", "tensor", None),
        P("section", None),
    )

    def program(*args):
        heads = args[4].shape[2] // (3 * HEAD_DIM * mesh.shape["tensor"])
        one_head_each = heads == mesh.shape["wide"] and heads % 2 == 0
        two_by_two = mesh.shape["section"] == 2 and mesh.shape["tensor"] == 2
        body = relay_shards if one_head_each and two_by_two else general_shards
        return jax.shard_map(
            body, mesh=mesh, in_specs=placed, out_specs=results, check_vma=False
        )(*args)

    return program
```

```python
import functools
import math

import jax
import jax.numpy as jnp
from jax import lax
from jax.experimental import pallas as pl
from jax.experimental.pallas import tpu as pltpu
from jax.sharding import PartitionSpec as P

HEAD_DIM = 64
ROT = 16
SEQ = 2048


EPSILON = 1e-05
ROPE_BASE = 10000.0

MESH = pl.DeviceIdType.MESH
F32 = jnp.float32
BF16 = jnp.bfloat16
LANES = 128
BLOCK = 512
COLS = 512
NEG = -1e30
SCORE_SCALE = math.log2(math.e) / math.sqrt(HEAD_DIM)


def dot(a, b):
    return jnp.dot(a, b, preferred_element_type=F32)


def dot_t(a, b):
    return lax.dot_general(a, b, (((1,), (1,)), ((), ())), preferred_element_type=F32)


def t_dot(a, b):
    return lax.dot_general(a, b, (((0,), (0,)), ((), ())), preferred_element_type=F32)


def lane_low(rows):
    return lax.broadcasted_iota(jnp.int32, (rows, LANES), 1) < HEAD_DIM


def turn(values):
    return pltpu.roll(values, HEAD_DIM, 1)


def rotary(values, cos_ref, front_ref, back_ref, seq, sign):
    cos, front, back = cos_ref[seq], front_ref[seq], back_ref[seq]
    ahead = pltpu.roll(values, LANES - ROT // 2, 1)
    behind = pltpu.roll(values, ROT // 2, 1)
    return values * cos + sign * (ahead * front + behind * back)


def pair_up(first, second, low):
    return jnp.where(low, first, turn(second)), jnp.where(low, turn(first), second)


def relay_kernel(
    dims,
    ends,
    x_hbm,
    cot_hbm,
    gain,
    shift,
    qkv_b,
    up_b,
    out_b,
    wqkv_hbm,
    wdense_hbm,
    wup_hbm,
    wdown_hbm,
    cos,
    front,
    back,
    out_hbm,
    ig_hbm,
    norm_hbm,
    g_hbm,
    mixed_hbm,
    hid_hbm,
    dpre_hbm,
    dpk_hbm,
    small,
    bias_sums,
    wqkv,
    wdense,
    wup,
    wdown,
    xfull,
    gfull,
    cot,
    qkv_r,
    mix_r,
    do_r,
    dqkv_r,
    rsf_r,
    rsb_r,
    qkv_st,
    o_st,
    do_st,
    dqkv_st,
    rsf_st,
    rsb_st,
    out_st,
    gx_st,
    ig_st,
    norm_st,
    mixed_st,
    hid_st,
    dpre_st,
    dpk_st,
    slope,
    part,
    part_b,
    dn1,
    qm,
    kr,
    vx,
    dox,
    dq,
    lse,
    delta,
    scores,
    peak,
    acc,
    wsem,
    ownx_sem,
    yx_s,
    yx_r,
    owng_sem,
    yg_s,
    yg_r,
    qkv_ss,
    qkv_rs,
    o_ss,
    o_rs,
    do_ss,
    do_rs,
    dqkv_ss,
    dqkv_rs,
    rsf_ss,
    rsf_rs,
    rsb_ss,
    rsb_rs,
    xs_ss,
    gs_ss,
    store_sem,
    g_store,
):
    micro, rows, group, wide, heads, d_model, ff = dims
    sect = lax.axis_index("section")
    tens = lax.axis_index("tensor")
    me = lax.axis_index("wide")
    pairs = heads // 2
    per_source = group + group // 2
    half = group // 2
    q_blocks = SEQ // BLOCK
    sources = BLOCK // group
    my_rows = pl.ds(pl.multiple_of(tens * rows, rows), rows)
    his_rows = pl.ds(pl.multiple_of((1 - tens) * rows, rows), rows)
    x_dev = {"section": 1 - sect}
    y_dev = {"tensor": 1 - tens}
    low_half = lane_low(half)
    low_group = lane_low(group)

    def remote(src, dst, ss, rs, dev):
        return pltpu.make_async_remote_copy(
            src_ref=src, dst_ref=dst, send_sem=ss, recv_sem=rs, device_id=dev, device_id_type=MESH
        )

    def arrived(ref, sem):
        pltpu.make_async_copy(ref, ref, sem).wait()

    def tokens_of(s):
        return pl.ds(pl.multiple_of(s * group, group), group)

    def y_send_x(s):
        own = xfull.at[s, my_rows]
        return remote(own, own, yx_s.at[s], yx_r.at[s], y_dev)

    def y_send_g(s):
        own = gfull.at[s, my_rows]
        return remote(own, own, yg_s.at[s], yg_r.at[s], y_dev)

    def spread(stage, target, seq, dest, ss, rs):
        @pl.when(dest == me)
        def _():
            pltpu.make_async_copy(stage, target.at[seq, me], rs).start()

        @pl.when(dest != me)
        def _():
            remote(stage, target.at[seq, me], ss, rs, {"wide": dest}).start()

    loads = [
        pltpu.make_async_copy(source, target, wsem.at[i])
        for i, (source, target) in enumerate(
            ((wqkv_hbm, wqkv), (wup_hbm, wup), (wdown_hbm, wdown), (wdense_hbm, wdense))
        )
    ]

    barrier = pltpu.get_barrier_semaphore()
    for dev in [x_dev, y_dev] + [{"wide": lax.rem(me + k, wide)} for k in range(1, wide)]:
        pl.semaphore_signal(barrier, inc=1, device_id=dev, device_id_type=MESH)

    @pl.when(sect == 0)
    def _():
        for s in range(micro):
            pltpu.make_async_copy(x_hbm.at[s], xfull.at[s, my_rows], ownx_sem.at[s]).start()

    for load in loads:
        load.start()

    @pl.when(sect == 1)
    def _():
        for s in range(micro):
            pltpu.make_async_copy(cot_hbm.at[s], cot.at[s], owng_sem.at[s]).start()

    small[...] = jnp.zeros_like(small)
    bias_sums[...] = jnp.zeros_like(bias_sums)
    pl.semaphore_wait(barrier, wide + 1)

    @pl.when(sect == 0)
    def _():
        for s in range(micro):
            arrived(xfull.at[s, my_rows], ownx_sem.at[s])
            y_send_x(s).start()

    @pl.when(sect == 1)
    def _():
        for s in range(micro):
            arrived(cot.at[s], owng_sem.at[s])

            def chunk(i, carry, s=s):
                at = pl.ds(pl.multiple_of(i * 32, 32), 32)
                there = pl.ds(pl.multiple_of(tens * rows + i * 32, 32), 32)
                gfull[s, there, :] = cot[s, at, :].astype(BF16)
                return carry

            lax.fori_loop(0, rows // 32, chunk, 0)
            y_send_g(s).start()

    def fold(values):
        total = values[0:8]
        for k in range(1, values.shape[0] // 8):
            total = total + values[k * 8 : (k + 1) * 8]
        return total

    def normed_rows(values):
        center = jnp.mean(values, axis=-1, keepdims=True)
        centred = values - center
        spread_of = jnp.mean(centred * centred, axis=-1, keepdims=True)
        inv = lax.rsqrt(spread_of + EPSILON)
        return centred * inv, inv

    def starts_of(s, tokens):
        found = jnp.zeros_like(tokens)
        for j in range(ends.shape[1]):
            end = ends[s, j]
            found = jnp.where(tokens >= end, end, found)
        return found

    def unpack_heads(s):
        def step(src, carry):
            qk = qkv_r[s, src, 0:group, :].astype(F32)
            at = pl.multiple_of(src * group, group)
            qm[pl.ds(at, group), :] = jnp.where(low_group, qk, 0.0).astype(BF16)
            kr[pl.ds(at, group), :] = turn(qk).astype(BF16)
            packed_v = qkv_r[s, src, group:per_source, :].astype(F32)
            ones = jnp.where(
                lax.broadcasted_iota(jnp.int32, (half, LANES), 1) == HEAD_DIM, 1.0, 0.0
            )
            vx[pl.ds(at, half), :] = jnp.where(low_half, packed_v, ones).astype(BF16)
            vx[pl.ds(pl.multiple_of(at + half, half), half), :] = jnp.where(
                low_half, turn(packed_v), ones
            ).astype(BF16)
            return carry

        lax.fori_loop(0, wide, step, 0)

    def forward(s):
        @pl.when(sect == 1)
        def _():
            arrived(xfull.at[s, my_rows], ownx_sem.at[s])
            y_send_x(s).start()

        arrived(xfull.at[s, his_rows], yx_r.at[s])

        def norm_step(i, carry):
            at = pl.ds(pl.multiple_of(i * 32, 32), 32)
            a, _ = normed_rows(xfull[s, at, :].astype(F32))
            norm_st[0, at, :] = (a * gain[0:1, :] + shift[0:1, :]).astype(BF16)
            norm_st[1, at, :] = (a * gain[1:2, :] + shift[1:2, :]).astype(BF16)
            return carry

        @pl.when(s > 0)
        def _():
            arrived(norm_st.at[0], store_sem.at[0])
            arrived(norm_st.at[1], store_sem.at[1])

        lax.fori_loop(0, group // 32, norm_step, 0)
        pltpu.make_async_copy(norm_st.at[0], norm_hbm.at[0, tokens_of(s)], store_sem.at[0]).start()
        pltpu.make_async_copy(norm_st.at[1], norm_hbm.at[1, tokens_of(s)], store_sem.at[1]).start()

        def qkv_step(k, carry):
            pair = lax.rem(me // 2 + 1 + k, pairs)
            cols = pl.ds(pl.multiple_of(pair * 3 * LANES, LANES), 3 * LANES)
            packed = dot(norm_st[0], wqkv[:, cols]) + qkv_b[:, cols]
            first, middle, last = (packed[:, i * LANES : (i + 1) * LANES] for i in range(3))
            qk0 = rotary(first, cos, front, back, s, 1.0)
            qk1 = rotary(
                turn(jnp.where(low_group, last, middle)), cos, front, back, s, 1.0
            )
            vv = jnp.where(low_group, middle, last)
            v0 = jnp.where(low_half, vv[:half], turn(vv[half:]))
            v1 = jnp.where(low_half, turn(vv[:half]), vv[half:])
            for i, (qk, v) in enumerate(((qk0, v0), (qk1, v1))):
                qkv_st[2 * pair + i, 0:group, :] = qk.astype(BF16)
                qkv_st[2 * pair + i, group:per_source, :] = v.astype(BF16)
            for i in range(2):
                dest = 2 * pair + i
                spread(qkv_st.at[dest], qkv_r, s, dest, qkv_ss.at[0], qkv_rs.at[s])
            return carry

        pl.when(s == 0)(loads[0].wait)
        lax.fori_loop(0, pairs, qkv_step, 0)

    def forward_ff(s):
        @pl.when(s == 0)
        def _():
            loads[1].wait()
            loads[2].wait()

        @pl.when(s > 0)
        def _():
            arrived(hid_st, store_sem.at[2])

        def ff_step(j, carry):
            cols = pl.ds(pl.multiple_of(j * COLS, COLS), COLS)
            pre = dot(norm_st[1], wup[:, cols]) + up_b[:, cols]
            cumul = 0.5 * (1.0 + lax.erf(pre * (1.0 / math.sqrt(2.0))))
            density = jnp.exp(-0.5 * pre * pre) * (1.0 / math.sqrt(2.0 * math.pi))
            hid = (pre * cumul).astype(BF16)
            hid_st[:, cols] = hid
            slope[s, :, cols] = (cumul + pre * density).astype(BF16)
            term = dot(hid, wdown[cols, :])

            @pl.when(j == 0)
            def _():
                part[...] = term

            @pl.when(j > 0)
            def _():
                part[...] += term

            return carry

        lax.fori_loop(0, ff // COLS, ff_step, 0)
        pltpu.make_async_copy(hid_st, hid_hbm.at[tokens_of(s)], store_sem.at[2]).start()

    def forward_attention(s):
        arrived(qkv_r.at[s], qkv_rs.at[s])
        arrived(qkv_st.at[pl.ds(0, wide - 1)], qkv_ss.at[0])
        unpack_heads(s)

        def q_step(i, carry):
            q_at = pl.ds(pl.multiple_of(i * BLOCK, BLOCK), BLOCK)
            tokens = i * BLOCK + lax.broadcasted_iota(jnp.int32, (BLOCK, LANES), 0)
            begin = starts_of(s, tokens)[:, 0:1]
            token = tokens[:, 0:1]
            peak[...] = jnp.full(peak.shape, NEG, F32)

            def score_step(j, inner):
                k_at = pl.ds(pl.multiple_of(j * BLOCK, BLOCK), BLOCK)
                raw = dot_t(qm[q_at, :], kr[k_at, :])
                u = j * BLOCK + lax.broadcasted_iota(jnp.int32, (BLOCK, BLOCK), 1)
                raw = jnp.where((u >= begin) & (u <= token), raw, NEG)
                scores[:, k_at] = raw
                best = peak[...]
                for k in range(BLOCK // LANES):
                    best = jnp.maximum(best, raw[:, k * LANES : (k + 1) * LANES])
                peak[...] = best
                return inner

            lax.fori_loop(0, i + 1, score_step, 0)
            top = jnp.max(peak[...], axis=1, keepdims=True) * SCORE_SCALE
            acc[...] = jnp.zeros_like(acc)

            def value_step(j, inner):
                k_at = pl.ds(pl.multiple_of(j * BLOCK, BLOCK), BLOCK)
                probs = jnp.exp2(scores[:, k_at] * SCORE_SCALE - top)
                acc[...] += dot(probs.astype(BF16), vx[k_at, :])
                return inner

            lax.fori_loop(0, i + 1, value_step, 0)
            total = acc[:, HEAD_DIM : HEAD_DIM + 1]
            out = acc[...] / total
            log_total = top + jnp.log2(total)
            lse[s, i] = jnp.broadcast_to(log_total, (BLOCK, LANES)).T[0:8, :]
            for k in range(sources):
                first = out[k * group : k * group + half]
                second = out[k * group + half : (k + 1) * group]
                source = i * sources + k
                o_st[s, source] = jnp.where(low_half, first, turn(second)).astype(BF16)
                spread(o_st.at[s, source], mix_r, s, source, o_ss.at[s], o_rs.at[s])
            return carry

        lax.fori_loop(0, q_blocks, q_step, 0)

    def forward_out(s):
        arrived(mix_r.at[s], o_rs.at[s])
        arrived(o_st.at[s, pl.ds(0, wide - 1)], o_ss.at[s])
        pl.when((s == 0) & (sect == 0))(loads[3].wait)
        pl.when(s > 0)(lambda: arrived(mixed_st, store_sem.at[3]))
        for pair in range(pairs):
            top, bottom = pair_up(
                mix_r[s, 2 * pair].astype(F32), mix_r[s, 2 * pair + 1].astype(F32), low_half
            )
            mixed_st[0:half, pair * LANES : (pair + 1) * LANES] = top.astype(BF16)
            mixed_st[half:group, pair * LANES : (pair + 1) * LANES] = bottom.astype(BF16)
        pltpu.make_async_copy(mixed_st, mixed_hbm.at[tokens_of(s)], store_sem.at[3]).start()
        part[...] += dot(mixed_st[...], wdense[...])
        rsf_st[...] = part[his_rows, :].astype(BF16)
        remote(rsf_st, rsf_r.at[s], rsf_ss.at[0], rsf_rs.at[s], y_dev).start()

    def forward_end(s):
        arrived(rsf_r.at[s], rsf_rs.at[s])
        arrived(rsf_st, rsf_ss.at[0])

        @pl.when(s > 0)
        def _():
            arrived(out_st, store_sem.at[4])
            pl.when(sect == 0)(lambda: arrived(out_st, xs_ss.at[0]))

        def out_step(i, carry):
            at = pl.ds(pl.multiple_of(i * 32, 32), 32)
            there = pl.ds(pl.multiple_of(tens * rows + i * 32, 32), 32)
            branch = part[there, :] + rsf_r[s, at, :].astype(F32) + out_b[...]
            out_st[at, :] = (xfull[s, there, :].astype(F32) + branch).astype(BF16)
            return carry

        lax.fori_loop(0, rows // 32, out_step, 0)

        @pl.when(sect == 0)
        def _():
            remote(out_st, xfull.at[s, my_rows], xs_ss.at[0], ownx_sem.at[s], x_dev).start()

        pltpu.make_async_copy(out_st, out_hbm.at[s], store_sem.at[4]).start()

    def backward(s):
        @pl.when(sect == 0)
        def _():
            arrived(gfull.at[s, my_rows], owng_sem.at[s])
            y_send_g(s).start()

        arrived(gfull.at[s, his_rows], yg_r.at[s])
        pl.when((s == 0) & (sect == 1))(loads[3].wait)
        pltpu.make_async_copy(gfull.at[s], g_hbm.at[tokens_of(s)], g_store.at[s]).start()

        def mixed_step(k, carry):
            pair = lax.rem(me // 2 + 1 + k, pairs)
            at = pl.ds(pl.multiple_of(pair * LANES, LANES), LANES)
            both = dot_t(gfull[s], wdense[at, :])
            first = jnp.where(low_half, both[:half], turn(both[half:]))
            second = jnp.where(low_half, turn(both[:half]), both[half:])
            do_st[s, 2 * pair] = first.astype(BF16)
            do_st[s, 2 * pair + 1] = second.astype(BF16)
            for i in range(2):
                dest = 2 * pair + i
                spread(do_st.at[s, dest], do_r, s, dest, do_ss.at[s], do_rs.at[s])
            return carry

        lax.fori_loop(0, pairs, mixed_step, 0)

    def backward_ff(s):
        pl.when(s > 0)(lambda: arrived(dpre_st, store_sem.at[6]))

        def ff_step(j, carry):
            cols = pl.ds(pl.multiple_of(j * COLS, COLS), COLS)
            grad = dot_t(gfull[s], wdown[cols, :])
            grad = (grad * slope[s, :, cols].astype(F32)).astype(BF16)
            dpre_st[:, cols] = grad
            sums_at = pl.ds(pl.multiple_of(3 * heads * HEAD_DIM + j * COLS, COLS), COLS)
            bias_sums[:, sums_at] += fold(grad.astype(F32))
            term = dot_t(grad, wup[:, cols])

            @pl.when(j == 0)
            def _():
                dn1[...] = term

            @pl.when(j > 0)
            def _():
                dn1[...] += term

            return carry

        lax.fori_loop(0, ff // COLS, ff_step, 0)
        pltpu.make_async_copy(dpre_st, dpre_hbm.at[tokens_of(s)], store_sem.at[6]).start()

    def backward_attention(s):
        arrived(do_r.at[s], do_rs.at[s])
        arrived(do_st.at[s, pl.ds(0, wide - 1)], do_ss.at[s])
        pl.when(sect == 0)(lambda: unpack_heads(s))

        def unpack_step(src, carry):
            at = pl.multiple_of(src * group, group)
            grad = do_r[s, src].astype(F32)
            dox[pl.ds(at, half), :] = jnp.where(low_half, grad, 0.0).astype(BF16)
            dox[pl.ds(pl.multiple_of(at + half, half), half), :] = jnp.where(
                low_half, turn(grad), 0.0
            ).astype(BF16)
            product = grad * o_st[s, src].astype(F32)
            left = jnp.sum(jnp.where(low_half, product, 0.0), axis=1, keepdims=True)
            right = jnp.sum(jnp.where(low_half, 0.0, product), axis=1, keepdims=True)
            delta[src, :, 0:half] = jnp.broadcast_to(left, (half, LANES)).T[0:8, :]
            delta[src, :, half:group] = jnp.broadcast_to(right, (half, LANES)).T[0:8, :]
            return carry

        lax.fori_loop(0, wide, unpack_step, 0)
        dq[...] = jnp.zeros_like(dq)
        slot = lax.rem(s, 2)

        def k_step(j, carry):
            k_at = pl.ds(pl.multiple_of(j * BLOCK, BLOCK), BLOCK)
            acc[...] = jnp.zeros_like(acc)
            peak[...] = jnp.zeros_like(peak)

            def q_step(i, inner):
                q_at = pl.ds(pl.multiple_of(i * BLOCK, BLOCK), BLOCK)
                tokens = i * BLOCK + lax.broadcasted_iota(jnp.int32, (8, BLOCK), 1)
                begin = starts_of(s, tokens)[0:1, :]
                token = tokens[0:1, :]
                raw = dot_t(kr[k_at, :], qm[q_at, :])
                u = j * BLOCK + lax.broadcasted_iota(jnp.int32, (BLOCK, BLOCK), 0)
                probs = jnp.exp2(raw * SCORE_SCALE - lse[s, i, 0:1, :])
                probs = jnp.where((u >= begin) & (u <= token), probs, 0.0)
                probs_grad = dot_t(vx[k_at, :], dox[q_at, :])
                inner_sum = jnp.concatenate(
                    [delta[i * sources + k, 0:1, :] for k in range(sources)], axis=1
                )
                score_grad = (
                    probs * (probs_grad - inner_sum) * (1.0 / math.sqrt(HEAD_DIM))
                ).astype(BF16)
                acc[...] += dot(probs.astype(BF16), dox[q_at, :])
                peak[...] += dot(score_grad, qm_turned[q_at, :])
                dq[q_at, :] += t_dot(score_grad, kr[k_at, :])
                return inner

            qm_turned = kr
            lax.fori_loop(j, q_blocks, q_step, 0)
            for k in range(sources):
                source = j * sources + k
                mine = slice(k * group, (k + 1) * group)
                at = pl.ds(pl.multiple_of(source * group, group), group)
                both = jnp.where(low_group, dq[at, :], peak[mine, :])
                value = acc[mine, :]
                value = jnp.where(low_half, value[:half], turn(value[half:]))
                dqkv_st[slot, source, 0:group, :] = both.astype(BF16)
                dqkv_st[slot, source, group:per_source, :] = value.astype(BF16)
                spread(
                    dqkv_st.at[slot, source], dqkv_r, s, source, dqkv_ss.at[slot], dqkv_rs.at[s]
                )
            return carry

        lax.fori_loop(0, q_blocks, k_step, 0)

    def backward_norm(s):
        arrived(dqkv_r.at[s], dqkv_rs.at[s])
        slot = lax.rem(s, 2)
        arrived(dqkv_st.at[slot, pl.ds(0, wide - 1)], dqkv_ss.at[slot])
        pl.when(s > 0)(lambda: arrived(dpk_st, store_sem.at[7]))

        def pair_step(pair, carry):
            qk0 = rotary(
                dqkv_r[s, 2 * pair, 0:group, :].astype(F32), cos, front, back, s, -1.0
            )
            qk1 = turn(
                rotary(
                    dqkv_r[s, 2 * pair + 1, 0:group, :].astype(F32), cos, front, back, s, -1.0
                )
            )
            top, bottom = pair_up(
                dqkv_r[s, 2 * pair, group:per_source, :].astype(F32),
                dqkv_r[s, 2 * pair + 1, group:per_source, :].astype(F32),
                low_half,
            )
            vv = jnp.concatenate([top, bottom], axis=0)
            columns = (qk0, jnp.where(low_group, vv, qk1), jnp.where(low_group, qk1, vv))
            for k, column in enumerate(columns):
                at = pl.ds(pl.multiple_of((pair * 3 + k) * LANES, LANES), LANES)
                column = column.astype(BF16)
                dpk_st[:, at] = column
                bias_sums[:, at] += fold(column.astype(F32))
            return carry

        lax.fori_loop(0, pairs, pair_step, 0)
        pltpu.make_async_copy(dpk_st, dpk_hbm.at[tokens_of(s)], store_sem.at[7]).start()
        part_b[...] = dot_t(dpk_st[...], wqkv[...])

        def e_step(i, carry):
            at = pl.ds(pl.multiple_of(i * 32, 32), 32)
            a, _ = normed_rows(xfull[s, at, :].astype(F32))
            first = part_b[at, :]
            second = dn1[at, :]
            small[0] += fold(first * a)
            small[1] += fold(second * a)
            small[2] += fold(first)
            small[3] += fold(second)
            part_b[at, :] = first * gain[0:1, :] + second * gain[1:2, :]
            return carry

        lax.fori_loop(0, group // 32, e_step, 0)
        rsb_st[...] = part_b[his_rows, :].astype(BF16)
        remote(rsb_st, rsb_r.at[s], rsb_ss.at[0], rsb_rs.at[s], y_dev).start()

    def backward_end(s):
        arrived(rsb_r.at[s], rsb_rs.at[s])
        arrived(rsb_st, rsb_ss.at[0])

        @pl.when(s > 0)
        def _():
            arrived(ig_st, store_sem.at[8])
            pl.when(sect == 1)(lambda: arrived(gx_st, gs_ss.at[0]))

        def in_step(i, carry):
            at = pl.ds(pl.multiple_of(i * 32, 32), 32)
            there = pl.ds(pl.multiple_of(tens * rows + i * 32, 32), 32)
            a, inv = normed_rows(xfull[s, there, :].astype(F32))
            e = part_b[there, :] + rsb_r[s, at, :].astype(F32)
            mean_e = jnp.mean(e, axis=-1, keepdims=True)
            cross = jnp.mean(e * a, axis=-1, keepdims=True)
            g_low = gfull[s, there, :].astype(F32)
            small[4] += fold(g_low)
            g = jnp.where(sect == 1, cot[s, at, :], g_low)
            grad = g + inv * (e - mean_e - a * cross)
            ig_st[at, :] = grad
            gx_st[at, :] = grad.astype(BF16)
            return carry

        lax.fori_loop(0, rows // 32, in_step, 0)

        @pl.when(sect == 1)
        def _():
            remote(gx_st, gfull.at[s, my_rows], gs_ss.at[0], owng_sem.at[s], x_dev).start()

        pltpu.make_async_copy(ig_st, ig_hbm.at[s], store_sem.at[8]).start()

    def at(seq, allowed, body):
        pl.when(allowed & (seq >= 0) & (seq < micro))(lambda: body(seq))

    @pl.when(sect == 1)
    def _():
        lax.fori_loop(0, micro, lambda s, carry: (backward(s), carry)[1], 0)

    first = jnp.int32(0)
    forward(first)
    forward_ff(first)
    always = sect >= 0

    def step(i, carry):
        f = i
        b = jnp.where(sect == 1, i, i - micro)
        at(b, sect == 0, backward)
        at(f, always, forward_attention)
        at(f + 1, always, forward)
        at(b, always, backward_attention)
        at(f, always, forward_out)
        at(b - 1, always, backward_norm)
        at(b, always, backward_ff)
        at(f, always, forward_end)
        at(b - 1, always, backward_end)
        at(f + 1, always, forward_ff)
        return carry

    lax.fori_loop(0, jnp.where(sect == 1, micro + 1, 2 * micro + 1), step, 0)

    for s in range(micro):
        arrived(xfull.at[s, my_rows], yx_s.at[s])
        arrived(gfull.at[s, my_rows], yg_s.at[s])
        arrived(gfull.at[s], g_store.at[s])
    arrived(norm_st.at[0], store_sem.at[0])
    arrived(norm_st.at[1], store_sem.at[1])
    arrived(hid_st, store_sem.at[2])
    arrived(mixed_st, store_sem.at[3])
    arrived(out_st, store_sem.at[4])
    arrived(dpre_st, store_sem.at[6])
    arrived(dpk_st, store_sem.at[7])
    arrived(ig_st, store_sem.at[8])
    pl.when(sect == 0)(lambda: arrived(out_st, xs_ss.at[0]))
    pl.when(sect == 1)(lambda: arrived(gx_st, gs_ss.at[0]))


def rotary_tables(doc_lengths, tokens):
    ends = jnp.cumsum(doc_lengths, axis=1)
    starts = ends - doc_lengths
    inside = (tokens[None, :, None] >= starts[:, None, :]) & (
        tokens[None, :, None] < ends[:, None, :]
    )
    begins = jnp.sum(jnp.where(inside, starts[:, None, :], 0), axis=2)
    offsets = (tokens[None, :] - begins).astype(F32)
    part_of = ROT // 2
    freqs = ROPE_BASE ** (-2.0 * jnp.arange(part_of, dtype=F32) / ROT)
    angle = offsets[:, :, None] * freqs
    cos, sin = jnp.cos(angle), jnp.sin(angle)
    ones = jnp.ones(offsets.shape + (HEAD_DIM - ROT,), F32)
    zeros = jnp.zeros_like(sin)

    def lanes(parts):
        return jnp.concatenate(parts + parts, axis=2)

    return (
        ends.astype(jnp.int32),
        lanes([cos, cos, ones]),
        lanes([-sin, zeros, 0.0 * ones]),
        lanes([zeros, sin, 0.0 * ones]),
    )


def relay(dims, doc_lengths, block_input, cotangent, weights, collective_id):
    micro, rows, group, wide, heads, d_model, ff = dims
    (
        norm_gain,
        norm_bias,
        qkv_weight,
        qkv_bias,
        dense_weight,
        dense_bias,
        up_weight,
        up_bias,
        down_weight,
        down_bias,
    ) = weights
    tokens = lax.axis_index("wide") * group + jnp.arange(group, dtype=jnp.int32)
    ends, cos, front, back = rotary_tables(doc_lengths, tokens)
    inner = heads * HEAD_DIM
    per_source = group + group // 2
    anywhere = pl.BlockSpec(memory_space=pl.ANY)
    local = pl.BlockSpec(memory_space=pltpu.VMEM)
    scalars = pl.BlockSpec(memory_space=pltpu.SMEM)
    dma = pltpu.SemaphoreType.DMA
    vmem = pltpu.VMEM
    outs = [
        jax.ShapeDtypeStruct((micro, rows, d_model), BF16),
        jax.ShapeDtypeStruct((micro, rows, d_model), F32),
        jax.ShapeDtypeStruct((2, micro * group, d_model), BF16),
        jax.ShapeDtypeStruct((micro * group, d_model), BF16),
        jax.ShapeDtypeStruct((micro * group, inner), BF16),
        jax.ShapeDtypeStruct((micro * group, ff), BF16),
        jax.ShapeDtypeStruct((micro * group, ff), BF16),
        jax.ShapeDtypeStruct((micro * group, 3 * inner), BF16),
        jax.ShapeDtypeStruct((5, 8, d_model), F32),
        jax.ShapeDtypeStruct((8, 3 * inner + ff), F32),
    ]
    scratch = [
        vmem(qkv_weight.shape, BF16),
        vmem(dense_weight.shape, BF16),
        vmem(up_weight.shape, BF16),
        vmem(down_weight.shape, BF16),
        vmem((micro, group, d_model), BF16),
        vmem((micro, group, d_model), BF16),
        vmem((micro, rows, d_model), F32),
        vmem((micro, wide, per_source, LANES), BF16),
        vmem((micro, wide, group // 2, LANES), BF16),
        vmem((micro, wide, group // 2, LANES), BF16),
        vmem((micro, wide, per_source, LANES), BF16),
        vmem((micro, rows, d_model), BF16),
        vmem((micro, rows, d_model), BF16),
        vmem((wide, per_source, LANES), BF16),
        vmem((micro, wide, group // 2, LANES), BF16),
        vmem((micro, wide, group // 2, LANES), BF16),
        vmem((2, wide, per_source, LANES), BF16),
        vmem((rows, d_model), BF16),
        vmem((rows, d_model), BF16),
        vmem((rows, d_model), BF16),
        vmem((rows, d_model), BF16),
        vmem((rows, d_model), F32),
        vmem((2, group, d_model), BF16),
        vmem((group, inner), BF16),
        vmem((group, ff), BF16),
        vmem((group, ff), BF16),
        vmem((group, 3 * inner), BF16),
        vmem((micro, group, ff), BF16),
        vmem((group, d_model), F32),
        vmem((group, d_model), F32),
        vmem((group, d_model), F32),
        vmem((SEQ, LANES), BF16),
        vmem((SEQ, LANES), BF16),
        vmem((SEQ, LANES), BF16),
        vmem((SEQ, LANES), BF16),
        vmem((SEQ, LANES), F32),
        vmem((micro, SEQ // BLOCK, 8, BLOCK), F32),
        vmem((wide, 8, group), F32),
        vmem((BLOCK, SEQ), F32),
        vmem((BLOCK, LANES), F32),
        vmem((BLOCK, LANES), F32),
        dma((4,)),
        dma((micro,)),
        dma((micro,)),
        dma((micro,)),
        dma((micro,)),
        dma((micro,)),
        dma((micro,)),
        dma((1,)),
        dma((micro,)),
        dma((micro,)),
        dma((micro,)),
        dma((micro,)),
        dma((micro,)),
        dma((2,)),
        dma((micro,)),
        dma((1,)),
        dma((micro,)),
        dma((1,)),
        dma((micro,)),
        dma((1,)),
        dma((1,)),
        dma((9,)),
        dma((micro,)),
    ]
    return pl.pallas_call(
        functools.partial(relay_kernel, dims),
        out_shape=outs,
        in_specs=[scalars, anywhere, anywhere]
        + [local] * 5
        + [anywhere] * 4
        + [local] * 3,
        out_specs=[anywhere] * 8 + [local] * 2,
        scratch_shapes=scratch,
        compiler_params=pltpu.CompilerParams(
            collective_id=collective_id, has_side_effects=True, vmem_limit_bytes=63 << 20
        ),
        name="relay",
    )(
        ends,
        block_input,
        cotangent,
        norm_gain,
        norm_bias,
        qkv_bias[None],
        up_bias[None],
        (dense_bias + down_bias)[None],
        qkv_weight,
        dense_weight,
        up_weight,
        down_weight,
        cos,
        front,
        back,
    )


TILE = 256
RING = 8
TOTALS = 4


def gradient_kinds(d_model, inner, ff):
    return ((d_model, ff), (ff, d_model), (inner, d_model), (d_model, 3 * inner))


def gradient_kernel(
    dims,
    norm_hbm,
    g_hbm,
    mixed_hbm,
    hid_hbm,
    dpre_hbm,
    dpk_hbm,
    small,
    biases,
    up_out,
    down_out,
    dense_out,
    qkv_out,
    sums,
    left_op,
    right_op,
    own,
    core_r,
    outer_r,
    inner_r,
    core_st,
    red_st,
    tot,
    sums_r,
    op_sem,
    core_ss,
    core_rs,
    outer_rs,
    inner_rs,
    red_ss,
    bc_rs,
    tot_ss,
    fwd_ss,
    share_ss,
    fin_rs,
    sum_ss,
    sum_rs,
    core_free,
    outer_free,
    inner_free,
):
    micro, rows, group, wide, heads, d_model, ff = dims
    tens = lax.axis_index("tensor")
    me = lax.axis_index("wide")
    chip, core = me // 2, lax.rem(me, 2)
    partner = {"wide": me + 1 - 2 * core}
    up_dev = {"wide": lax.rem(me + 2, wide)}
    down_dev = {"wide": lax.rem(me + wide - 2, wide)}
    at_bottom, at_top = chip == 0, chip == wide // 2 - 1
    at_end = at_bottom | at_top
    middle = jnp.logical_not(at_end)
    lower = chip == 1
    outer_of = {"wide": jnp.where(lower, me - 2, lax.rem(me + 2, wide))}
    inner_of = {"wide": jnp.where(lower, me + 2, lax.rem(me + wide - 2, wide))}
    end_of = {"wide": jnp.where(at_bottom, me + 2, lax.rem(me + wide - 2, wide))}
    inner = heads * HEAD_DIM
    kinds = gradient_kinds(d_model, inner, ff)
    targets = (up_out, down_out, dense_out, qkv_out)
    operands = (
        (norm_hbm.at[1], dpre_hbm),
        (hid_hbm, g_hbm),
        (mixed_hbm, g_hbm),
        (norm_hbm.at[0], dpk_hbm),
    )
    ranges, first = [], 0
    for height, width in kinds:
        count = (height // TILE) * (width // (2 * TILE))
        ranges.append((first, first + count, width // (2 * TILE)))
        first += count
    steps = first

    def remote(src, dst, ss, rs, dev):
        return pltpu.make_async_remote_copy(
            src_ref=src, dst_ref=dst, send_sem=ss, recv_sem=rs, device_id=dev, device_id_type=MESH
        )

    def arrived(ref, sem):
        pltpu.make_async_copy(ref, ref, sem).wait()

    tile_ref = tot.at[0]

    def by_kind(m, body):
        for kind, (low, high, across) in enumerate(ranges):

            @pl.when((m >= low) & (m < high))
            def _(kind=kind, low=low, across=across):
                at = m - low
                body(kind, at // across, lax.rem(at, across))

    def tile_of(kind, row, col, which):
        return targets[kind].at[
            pl.ds(pl.multiple_of(row * TILE, TILE), TILE),
            pl.ds(pl.multiple_of((2 * col + which) * TILE, TILE), TILE),
        ]

    def fetch(m):
        def body(kind, row, col):
            left, right = operands[kind]
            slot = lax.rem(m, 2)
            pltpu.make_async_copy(
                left.at[:, pl.ds(pl.multiple_of(row * TILE, TILE), TILE)],
                left_op.at[slot],
                op_sem.at[0, slot],
            ).start()
            pltpu.make_async_copy(
                right.at[:, pl.ds(pl.multiple_of(col * 2 * TILE, 2 * TILE), 2 * TILE)],
                right_op.at[slot],
                op_sem.at[1, slot],
            ).start()

        by_kind(m, body)

    def is_root(m):
        return middle & (chip == 1 + lax.rem(m, 2))

    def products(m):
        slot, ring = lax.rem(m, 2), lax.rem(m, RING)
        arrived(left_op.at[slot], op_sem.at[0, slot])
        arrived(right_op.at[slot], op_sem.at[1, slot])
        left = left_op[slot]
        mine = pl.ds(pl.multiple_of(core * TILE, TILE), TILE)
        other = pl.ds(pl.multiple_of((1 - core) * TILE, TILE), TILE)

        @pl.when(m >= RING)
        def _():
            arrived(tile_ref, core_ss.at[ring])
            pl.semaphore_wait(core_free, 1)

        core_st[ring] = t_dot(left, right_op[slot, :, other]).astype(BF16)
        remote(
            core_st.at[ring], core_r.at[ring], core_ss.at[ring], core_rs.at[ring], partner
        ).start()
        own[ring] = t_dot(left, right_op[slot, :, mine])

    def send_red(m, value, target, sem, dev, free):
        ring = lax.rem(m, RING)

        @pl.when(m >= RING)
        def _():
            pl.semaphore_wait(free, 1)

        red_st[ring] = value.astype(BF16)
        remote(red_st.at[ring], target.at[ring], red_ss.at[ring], sem.at[ring], dev).start()

    def chip_sum(m):
        ring = lax.rem(m, RING)
        arrived(tile_ref, core_rs.at[ring])
        total = own[ring] + core_r[ring].astype(F32)

        @pl.when(m + RING < steps)
        def _():
            pl.semaphore_signal(core_free, inc=1, device_id=partner, device_id_type=MESH)

        @pl.when(at_end)
        def _():
            @pl.when(m >= RING)
            def _():
                arrived(tile_ref, red_ss.at[ring])

            send_red(m, total, outer_r, outer_rs, end_of, outer_free.at[lax.rem(m, 2)])

        @pl.when(middle)
        def _():
            own[ring] = total

    def take_outer(m):
        ring = lax.rem(m, RING)
        arrived(tile_ref, outer_rs.at[ring])
        total = own[ring] + outer_r[ring].astype(F32)

        @pl.when(m + RING < steps)
        def _():
            pl.semaphore_signal(
                outer_free.at[lax.rem(m, 2)], inc=1, device_id=outer_of, device_id_type=MESH
            )

        return total

    def pass_in(m):
        ring = lax.rem(m, RING)
        total = take_outer(m)

        @pl.when(m >= RING)
        def _():
            arrived(tile_ref, red_ss.at[ring])

        send_red(m, total, inner_r, inner_rs, inner_of, inner_free)

    def finish(m):
        ring = lax.rem(m, RING)
        slot = lax.rem(m // 2, TOTALS)
        total = take_outer(m)
        arrived(tile_ref, inner_rs.at[ring])
        total = total + inner_r[ring].astype(F32)

        @pl.when(m + RING < steps)
        def _():
            pl.semaphore_signal(inner_free, inc=1, device_id=inner_of, device_id_type=MESH)

        @pl.when(m >= 2 * TOTALS)
        def _():
            for k in range(4):
                arrived(tile_ref, tot_ss.at[k, slot])

        tot[slot] = total.astype(BF16)

        def body(kind, row, col):
            here = tile_of(kind, row, col, core)
            remote(tot.at[slot], here, tot_ss.at[0, slot], bc_rs.at[m], outer_of).start()
            remote(tot.at[slot], here, tot_ss.at[1, slot], bc_rs.at[m], inner_of).start()
            remote(tot.at[slot], here, tot_ss.at[2, slot], fin_rs.at[kind], partner).start()
            pltpu.make_async_copy(tot.at[slot], here, tot_ss.at[3, slot]).start()

        by_kind(m, body)

    def hand_on(m):
        arrived(tile_ref, bc_rs.at[m])

        def body(kind, row, col):
            here = tile_of(kind, row, col, core)

            @pl.when(middle)
            def _():
                remote(here, here, fwd_ss.at[m], bc_rs.at[m], outer_of).start()

            remote(here, here, share_ss.at[m], fin_rs.at[kind], partner).start()

        by_kind(m, body)

    exchanges = (
        {"tensor": 1 - tens},
        partner,
        {"wide": me + 2 - 4 * lax.rem(chip, 2)},
        {"wide": me + 4 - 8 * (chip // 2)},
    )

    barrier = pltpu.get_barrier_semaphore()
    for dev in exchanges:
        pl.semaphore_signal(barrier, inc=1, device_id=dev, device_id_type=MESH)

    @pl.when(middle)
    def _():
        pl.semaphore_signal(barrier, inc=1, device_id=inner_of, device_id_type=MESH)

    fetch(jnp.int32(0))
    sums[:, 0:d_model] = jnp.concatenate(
        [jnp.sum(small[k], axis=0, keepdims=True) for k in range(5)]
        + [jnp.zeros((3, d_model), F32)],
        axis=0,
    )
    total = jnp.sum(biases[...], axis=0, keepdims=True)
    lines = [total[:, k * COLS : (k + 1) * COLS] for k in range(total.shape[1] // COLS)]
    lines.append(jnp.zeros((8 - len(lines), COLS), F32))
    sums[:, d_model:] = jnp.concatenate(lines, axis=0)
    pl.when(middle)(lambda: pl.semaphore_wait(barrier, len(exchanges) + 1))
    pl.when(at_end)(lambda: pl.semaphore_wait(barrier, len(exchanges)))

    def exchange_start(k):
        if k > 0:
            arrived(sums, sum_ss.at[0])
        sums_r[0] = sums[...]
        remote(sums_r.at[0], sums_r.at[k + 1], sum_ss.at[0], sum_rs.at[k], exchanges[k]).start()

    def exchange_end(k):
        arrived(sums, sum_rs.at[k])
        if k == 0:
            sums[:, 0:d_model] += sums_r[1, :, 0:d_model]
        else:
            sums[...] += sums_r[k + 1]

    def step(i, carry):
        pl.when(i + 1 < steps)(lambda: fetch(i + 1))
        pl.when(i < steps)(lambda: products(i))
        for k in range(4):
            pl.when(i == 4 * k + 2)(lambda k=k: exchange_start(k))
            pl.when(i == 4 * k + 5)(lambda k=k: exchange_end(k))

        def at(lag, allowed, body):
            m = i - lag
            pl.when((m >= 0) & (m < steps) & allowed(m))(lambda: body(m))

        at(1, lambda m: m >= 0, chip_sum)
        at(3, lambda m: middle & jnp.logical_not(is_root(m)), pass_in)
        at(5, is_root, finish)
        at(8, lambda m: middle & jnp.logical_not(is_root(m)), hand_on)
        at(10, lambda m: at_end, hand_on)
        return carry

    lax.fori_loop(0, steps + 10, step, 0)

    arrived(sums, sum_ss.at[0])
    for ring in range(RING):
        arrived(tile_ref, core_ss.at[ring])

    def drain(m, carry):
        ring = lax.rem(m, RING)
        root = is_root(m)
        last = m + RING >= steps
        pl.when(at_end & last)(lambda: arrived(tile_ref, red_ss.at[ring]))
        pl.when(middle & jnp.logical_not(root) & last)(
            lambda: arrived(tile_ref, red_ss.at[ring])
        )

        @pl.when(root & (m + 2 * TOTALS >= steps))
        def _():
            for k in range(4):
                arrived(tile_ref, tot_ss.at[k, lax.rem(m // 2, TOTALS)])

        @pl.when(middle & jnp.logical_not(root))
        def _():
            arrived(tile_ref, fwd_ss.at[m])

        pl.when(jnp.logical_not(root))(lambda: arrived(tile_ref, share_ss.at[m]))
        return carry

    lax.fori_loop(0, steps, drain, 0)
    for kind, (height, width) in enumerate(kinds):
        arrived(targets[kind].at[pl.ds(0, height // 2)], fin_rs.at[kind])


def gradient_sums(dims, operands, small, biases, collective_id):
    micro, rows, group, wide, heads, d_model, ff = dims
    inner = heads * HEAD_DIM
    kinds = gradient_kinds(d_model, inner, ff)
    steps = sum((height // TILE) * (width // (2 * TILE)) for height, width in kinds)
    count = micro * group
    anywhere = pl.BlockSpec(memory_space=pl.ANY)
    local = pl.BlockSpec(memory_space=pltpu.VMEM)
    dma = pltpu.SemaphoreType.DMA
    regular = pltpu.SemaphoreType.REGULAR
    vmem = pltpu.VMEM
    width = d_model + COLS
    return pl.pallas_call(
        functools.partial(gradient_kernel, dims),
        out_shape=[jax.ShapeDtypeStruct(kind, BF16) for kind in kinds]
        + [jax.ShapeDtypeStruct((8, width), F32)],
        in_specs=[anywhere] * 6 + [local] * 2,
        out_specs=[anywhere] * 4 + [local],
        scratch_shapes=[
            vmem((2, count, TILE), BF16),
            vmem((2, count, 2 * TILE), BF16),
            vmem((RING, TILE, TILE), F32),
            vmem((RING, TILE, TILE), BF16),
            vmem((RING, TILE, TILE), BF16),
            vmem((RING, TILE, TILE), BF16),
            vmem((RING, TILE, TILE), BF16),
            vmem((RING, TILE, TILE), BF16),
            vmem((TOTALS, TILE, TILE), BF16),
            vmem((5, 8, width), F32),
            dma((2, 2)),
            dma((RING,)),
            dma((RING,)),
            dma((RING,)),
            dma((RING,)),
            dma((RING,)),
            dma((steps,)),
            dma((4, TOTALS)),
            dma((steps,)),
            dma((steps,)),
            dma((4,)),
            dma((1,)),
            dma((4,)),
            regular,
            regular((2,)),
            regular,
        ],
        compiler_params=pltpu.CompilerParams(
            collective_id=collective_id, has_side_effects=True, vmem_limit_bytes=40 << 20
        ),
        name="gradient_sums",
    )(*operands, small, biases)


def relay_shards(
    block_input,
    doc_lengths,
    norm_gain,
    norm_bias,
    qkv_weight,
    qkv_bias,
    dense_weight,
    dense_bias,
    up_weight,
    up_bias,
    down_weight,
    down_bias,
    cotangent,
):
    weights = tuple(
        array[0]
        for array in (
            norm_gain,
            norm_bias,
            qkv_weight,
            qkv_bias,
            dense_weight,
            dense_bias,
            up_weight,
            up_bias,
            down_weight,
            down_bias,
        )
    )
    micro, rows, d_model = block_input.shape
    group = rows * lax.axis_size("tensor")
    wide = lax.axis_size("wide")
    heads = qkv_weight.shape[2] // (3 * HEAD_DIM)
    ff = up_weight.shape[2]
    dims = (micro, rows, group, wide, heads, d_model, ff)
    out, input_grad, *operands, small, bias_sums = relay(
        dims, doc_lengths, block_input, cotangent, weights, 1
    )
    up_grad, down_grad, dense_grad, qkv_grad, sums = gradient_sums(
        dims, operands, small, bias_sums, 2
    )
    up_grad, down_grad, dense_grad, qkv_grad = (
        grad.astype(F32)[None] for grad in (up_grad, down_grad, dense_grad, qkv_grad)
    )
    biases = sums[:, d_model:].reshape(1, -1)
    qkv_width = qkv_weight.shape[2]
    out_bias_grad = sums[4:5, :d_model]
    return (
        out[None],
        input_grad[None],
        sums[None, 0:2, :d_model],
        sums[None, 2:4, :d_model],
        qkv_grad,
        biases[:, :qkv_width],
        dense_grad,
        out_bias_grad,
        up_grad,
        biases[:, qkv_width : qkv_width + ff],
        down_grad,
        out_bias_grad,
    )


def shortened(shard):

    def short(part):
        return part.astype(jnp.bfloat16) if part.dtype == jnp.float32 else part

    return jax.tree.map(short, shard)


def from_behind(block, axis, distance):
    devices = range(lax.axis_size(axis))
    route = [(i - distance, i) for i in devices if i - distance in devices]
    return lax.ppermute(block, axis, route)


def norm_parts(values, gain, shift):
    center = jnp.mean(values, axis=-1, keepdims=True)
    centred = values - center
    spread = jnp.mean(centred * centred, axis=-1, keepdims=True)
    inv_scale = lax.rsqrt(spread + EPSILON)
    normed = centred * inv_scale
    return (normed * gain + shift, normed, inv_scale)


def norm_back(grad, normed, inv_scale, gain):
    scaled = grad * gain
    inner_mean = jnp.mean(scaled, axis=-1, keepdims=True)
    cross_mean = jnp.mean(scaled * normed, axis=-1, keepdims=True)
    return inv_scale * (scaled - inner_mean - normed * cross_mean)


def doc_layout(lengths, tok_index):
    ends = jnp.cumsum(lengths)
    starts = ends - lengths
    doc_ids = jnp.sum((tok_index[:, None] >= ends[None, :]).astype(jnp.int32), axis=1)
    numbers = jnp.arange(lengths.shape[0], dtype=jnp.int32)
    picked = doc_ids[:, None] == numbers[None, :]
    begins = jnp.sum(jnp.where(picked, starts[None, :], 0), axis=1)
    return (doc_ids, tok_index - begins)


def rope_tables(offsets):
    half = ROT // 2
    freqs = ROPE_BASE ** (-2.0 * jnp.arange(half, dtype=jnp.float32) / ROT)
    angle = offsets.astype(jnp.float32)[:, None] * freqs[None, :]
    return (jnp.cos(angle)[:, None, :], jnp.sin(angle)[:, None, :])


def rotate(values, cos_table, sin_table):
    half = ROT // 2
    front = values[..., :half]
    back = values[..., half:ROT]
    turned = [
        front * cos_table - back * sin_table,
        back * cos_table + front * sin_table,
        values[..., ROT:],
    ]
    return jnp.concatenate(turned, axis=-1)


def unrotate(values, cos_table, sin_table):
    half = ROT // 2
    front = values[..., :half]
    back = values[..., half:ROT]
    turned = [
        front * cos_table + back * sin_table,
        back * cos_table - front * sin_table,
        values[..., ROT:],
    ]
    return jnp.concatenate(turned, axis=-1)


def gelu_parts(pre_act):
    cumul = 0.5 * (1.0 + lax.erf(pre_act * (1.0 / math.sqrt(2.0))))
    density = jnp.exp(-0.5 * pre_act * pre_act) * (1.0 / math.sqrt(2.0 * math.pi))
    return (pre_act * cumul, cumul + pre_act * density)


def store_slot(buffer, update, slot_here, is_valid):
    previous = lax.dynamic_index_in_dim(buffer, slot_here, 0, keepdims=False)
    return lax.dynamic_update_index_in_dim(
        buffer, jnp.where(is_valid, update, previous), slot_here, 0
    )


def gather_keys(key_rows, value_rows):
    return (
        lax.all_gather(key_rows, "wide", axis=0, tiled=True),
        lax.all_gather(value_rows, "wide", axis=0, tiled=True),
    )


def forward_parts(inputs, lengths, weights, with_output):
    (
        norm_gain,
        norm_bias,
        qkv_weight,
        qkv_bias,
        dense_weight,
        dense_bias,
        up_weight,
        up_bias,
        down_weight,
        down_bias,
    ) = weights
    seq_len = SEQ
    group = inputs.shape[0] * lax.axis_size("tensor")
    head_count = qkv_weight.shape[1] // (3 * HEAD_DIM)
    factor = 1.0 / math.sqrt(HEAD_DIM)
    values = inputs.astype(jnp.float32)
    norm_first, normed_first, scale_first = norm_parts(values, norm_gain[0], norm_bias[0])
    norm_second, normed_second, scale_second = norm_parts(values, norm_gain[1], norm_bias[1])
    full_first, full_second = (
        lax.all_gather(norm_first.astype(jnp.bfloat16), "tensor", axis=0, tiled=True),
        lax.all_gather(norm_second.astype(jnp.bfloat16), "tensor", axis=0, tiled=True),
    )
    tok_index = lax.axis_index("wide") * group + jnp.arange(group, dtype=jnp.int32)
    doc_ids, offsets = doc_layout(lengths, tok_index)
    all_index = jnp.arange(seq_len, dtype=jnp.int32)
    all_docs = doc_layout(lengths, all_index)[0]
    cos_table, sin_table = rope_tables(offsets)
    packed = jnp.dot(full_first, qkv_weight, preferred_element_type=jnp.float32) + qkv_bias
    packed = packed.reshape(group, head_count, 3, HEAD_DIM)
    queries = rotate(packed[:, :, 0], cos_table, sin_table).astype(jnp.bfloat16)
    key_here = rotate(packed[:, :, 1], cos_table, sin_table).astype(jnp.bfloat16)
    value_here = packed[:, :, 2].astype(jnp.bfloat16)
    key_all, value_all = gather_keys(key_here.reshape(group, -1), value_here.reshape(group, -1))
    key_heads = key_all.reshape(seq_len, head_count, HEAD_DIM)
    value_heads = value_all.reshape(seq_len, head_count, HEAD_DIM)
    allowed = (doc_ids[:, None] == all_docs[None, :]) & (all_index[None, :] <= tok_index[:, None])
    raw_scores = jnp.einsum("qhd,khd->qhk", queries, key_heads, preferred_element_type=jnp.float32)
    scores = jnp.where(allowed[:, None, :], raw_scores * factor, -jnp.inf)
    row_max = jnp.max(scores, axis=-1, keepdims=True)
    log_total = row_max + jnp.log(jnp.sum(jnp.exp(scores - row_max), axis=-1, keepdims=True))
    attn_probs = jnp.exp(scores - log_total)
    probs_low = attn_probs.astype(jnp.bfloat16)
    mixed_out = jnp.einsum(
        "qhk,khd->qhd", probs_low, value_heads, preferred_element_type=jnp.float32
    )
    mixed_out = mixed_out.reshape(group, -1).astype(jnp.bfloat16)
    up_pre = jnp.dot(full_second, up_weight, preferred_element_type=jnp.float32) + up_bias
    up_act, gelu_slope = gelu_parts(up_pre)
    hidden = up_act.astype(jnp.bfloat16)
    output = None
    if with_output:
        partial_value = jnp.dot(mixed_out, dense_weight, preferred_element_type=jnp.float32)
        partial_value = partial_value + jnp.dot(
            hidden, down_weight, preferred_element_type=jnp.float32
        )
        branch = (
            lax.psum_scatter(
                partial_value.astype(jnp.bfloat16), "tensor", scatter_dimension=0, tiled=True
            ).astype(jnp.float32)
            + dense_bias
            + down_bias
        )
        output = (values + branch).astype(jnp.bfloat16)
    return dict(
        output=output,
        normed_first=normed_first,
        scale_first=scale_first,
        normed_second=normed_second,
        scale_second=scale_second,
        full_first=full_first,
        full_second=full_second,
        tok_index=tok_index,
        doc_ids=doc_ids,
        all_index=all_index,
        all_docs=all_docs,
        cos_table=cos_table,
        sin_table=sin_table,
        queries=queries,
        key_here=key_here,
        value_here=value_here,
        key_all=key_all,
        value_all=value_all,
        key_heads=key_heads,
        value_heads=value_heads,
        attn_probs=attn_probs,
        probs_low=probs_low,
        log_total=log_total,
        mixed_out=mixed_out,
        gelu_slope=gelu_slope,
        hidden=hidden,
    )


def backward_parts(inputs, grad_out, lengths, weights):
    (
        norm_gain,
        norm_bias,
        qkv_weight,
        qkv_bias,
        dense_weight,
        dense_bias,
        up_weight,
        up_bias,
        down_weight,
        down_bias,
    ) = weights
    parts = forward_parts(inputs, lengths, weights, False)
    seq_len = SEQ
    group = inputs.shape[0] * lax.axis_size("tensor")
    head_count = qkv_weight.shape[1] // (3 * HEAD_DIM)
    factor = 1.0 / math.sqrt(HEAD_DIM)
    cos_table = parts["cos_table"]
    sin_table = parts["sin_table"]
    grad_low = grad_out.astype(jnp.bfloat16)
    grad_rows = grad_low.astype(jnp.float32)
    grad_full = lax.all_gather(grad_low, "tensor", axis=0, tiled=True)
    dense_grad = jnp.einsum(
        "cf,cd->fd", parts["mixed_out"], grad_full, preferred_element_type=jnp.float32
    )
    down_grad = jnp.einsum(
        "cf,cd->fd", parts["hidden"], grad_full, preferred_element_type=jnp.float32
    )
    hidden_grad = jnp.einsum(
        "cd,fd->cf", grad_full, down_weight, preferred_element_type=jnp.float32
    )
    pre_grad = (hidden_grad * parts["gelu_slope"]).astype(jnp.bfloat16)
    up_grad = jnp.einsum(
        "cd,cf->df", parts["full_second"], pre_grad, preferred_element_type=jnp.float32
    )
    up_bias_grad = jnp.sum(pre_grad.astype(jnp.float32), axis=0)
    second_grad = jnp.einsum("cf,df->cd", pre_grad, up_weight, preferred_element_type=jnp.float32)
    mixed_grad = jnp.einsum(
        "cd,fd->cf", grad_full, dense_weight, preferred_element_type=jnp.float32
    )
    mixed_grad = mixed_grad.astype(jnp.bfloat16).reshape(group, head_count, HEAD_DIM)
    attn_probs = parts["attn_probs"]
    probs_grad = jnp.einsum(
        "qhd,khd->qhk", mixed_grad, parts["value_heads"], preferred_element_type=jnp.float32
    )
    inner = jnp.sum(attn_probs * probs_grad, axis=-1, keepdims=True)
    score_grad = (attn_probs * (probs_grad - inner) * factor).astype(jnp.bfloat16)
    query_grad = jnp.einsum(
        "qhk,khd->qhd", score_grad, parts["key_heads"], preferred_element_type=jnp.float32
    )
    key_sums = jnp.einsum(
        "qhk,qhd->khd", score_grad, parts["queries"], preferred_element_type=jnp.float32
    )
    value_sums = jnp.einsum(
        "qhk,qhd->khd", parts["probs_low"], mixed_grad, preferred_element_type=jnp.float32
    )
    key_flat, value_flat = (
        lax.psum_scatter(
            key_sums.reshape(seq_len, -1).astype(jnp.bfloat16),
            "wide",
            scatter_dimension=0,
            tiled=True,
        ).astype(jnp.float32),
        lax.psum_scatter(
            value_sums.reshape(seq_len, -1).astype(jnp.bfloat16),
            "wide",
            scatter_dimension=0,
            tiled=True,
        ).astype(jnp.float32),
    )
    key_grad = key_flat.reshape(group, head_count, HEAD_DIM)
    value_grad = value_flat.reshape(group, head_count, HEAD_DIM)
    query_back = unrotate(query_grad, cos_table, sin_table)
    key_back = unrotate(key_grad, cos_table, sin_table)
    packed_grad = (
        jnp.stack([query_back, key_back, value_grad], axis=2)
        .reshape(group, -1)
        .astype(jnp.bfloat16)
    )
    qkv_grad = jnp.einsum(
        "cd,cf->df", parts["full_first"], packed_grad, preferred_element_type=jnp.float32
    )
    qkv_bias_grad = jnp.sum(packed_grad.astype(jnp.float32), axis=0)
    first_grad = jnp.einsum(
        "cf,df->cd", packed_grad, qkv_weight, preferred_element_type=jnp.float32
    )
    norm_first_grad, norm_second_grad = (
        lax.psum_scatter(
            first_grad.astype(jnp.bfloat16), "tensor", scatter_dimension=0, tiled=True
        ).astype(jnp.float32),
        lax.psum_scatter(
            second_grad.astype(jnp.bfloat16), "tensor", scatter_dimension=0, tiled=True
        ).astype(jnp.float32),
    )
    gain_grad = jnp.stack(
        [
            jnp.sum(norm_first_grad * parts["normed_first"], axis=0),
            jnp.sum(norm_second_grad * parts["normed_second"], axis=0),
        ]
    )
    shift_grad = jnp.stack([jnp.sum(norm_first_grad, axis=0), jnp.sum(norm_second_grad, axis=0)])
    input_grad = grad_out + norm_back(
        norm_first_grad, parts["normed_first"], parts["scale_first"], norm_gain[0]
    )
    input_grad = input_grad + norm_back(
        norm_second_grad, parts["normed_second"], parts["scale_second"], norm_gain[1]
    )
    bias_rows = jnp.sum(grad_rows, axis=0)
    terms = (
        gain_grad,
        shift_grad,
        qkv_grad,
        qkv_bias_grad,
        dense_grad,
        bias_rows,
        up_grad,
        up_bias_grad,
        down_grad,
        bias_rows,
    )
    return (input_grad, terms)


def general_shards(
    block_input,
    doc_lengths,
    norm_gain,
    norm_bias,
    qkv_weight,
    qkv_bias,
    dense_weight,
    dense_bias,
    up_weight,
    up_bias,
    down_weight,
    down_bias,
    cotangent,
):
    weights = (
        norm_gain[0],
        norm_bias[0],
        qkv_weight[0],
        qkv_bias[0],
        dense_weight[0],
        dense_bias[0],
        up_weight[0],
        up_bias[0],
        down_weight[0],
        down_bias[0],
    )
    section_index = lax.axis_index("section")
    last_section = lax.axis_size("section") - 1
    micro_count = block_input.shape[0]
    row_count = block_input.shape[1]
    tick_count = micro_count + last_section

    def forward_tick(carry, tick_index):
        incoming, kept_inputs, outputs, kept_pairs = carry
        slot_raw = tick_index - section_index
        is_valid = (slot_raw >= 0) & (slot_raw < micro_count)
        slot_here = jnp.clip(slot_raw, 0, micro_count - 1)
        fresh = lax.dynamic_index_in_dim(
            block_input, jnp.clip(tick_index, 0, micro_count - 1), 0, keepdims=False
        )
        inputs = jnp.where(section_index == 0, fresh, incoming)
        lengths = lax.dynamic_index_in_dim(doc_lengths, slot_here, 0, keepdims=False)
        parts = forward_parts(inputs, lengths, weights, True)
        output = parts["output"]
        kept_inputs = store_slot(kept_inputs, inputs, slot_here, is_valid)
        outputs = store_slot(outputs, output, slot_here, is_valid)
        incoming = jax.tree.map(
            lambda part, own: part.astype(own.dtype),
            from_behind(shortened(output), "section", 1),
            output,
        )
        return ((incoming, kept_inputs, outputs, kept_pairs), None)

    pair_init = (jnp.zeros((1,), jnp.bfloat16), jnp.zeros((1,), jnp.bfloat16))
    zero_rows = jnp.zeros((row_count, block_input.shape[2]), jnp.bfloat16)
    zero_stack = jnp.zeros(block_input.shape, jnp.bfloat16)
    forward_init = (zero_rows, zero_stack, zero_stack, pair_init)
    forward_done = lax.scan(forward_tick, forward_init, jnp.arange(tick_count, dtype=jnp.int32))[0]
    kept_inputs = forward_done[1]
    outputs = forward_done[2]
    kept_pairs = forward_done[3]

    def add_masked(total, term, scale_mask):
        return total + scale_mask * term

    def backward_tick(carry, tick_index):
        incoming, grads, input_grads = carry
        slot_raw = tick_index - (last_section - section_index)
        is_valid = (slot_raw >= 0) & (slot_raw < micro_count)
        slot_here = jnp.clip(slot_raw, 0, micro_count - 1)
        top_grad = lax.dynamic_index_in_dim(cotangent, slot_here, 0, keepdims=False)
        grad_out = jnp.where(section_index == last_section, top_grad, incoming)
        inputs = lax.dynamic_index_in_dim(kept_inputs, slot_here, 0, keepdims=False)
        lengths = lax.dynamic_index_in_dim(doc_lengths, slot_here, 0, keepdims=False)
        input_grad, terms = backward_parts(inputs, grad_out, lengths, weights)
        scale_mask = is_valid.astype(jnp.float32)
        grads = tuple((add_masked(total, term, scale_mask) for total, term in zip(grads, terms)))
        input_grads = store_slot(input_grads, input_grad, slot_here, is_valid)
        incoming = from_behind(shortened(input_grad), "section", -1).astype(input_grad.dtype)
        return ((incoming, grads, input_grads), None)

    grad_init = tuple((jnp.zeros(weight.shape, jnp.float32) for weight in weights))
    backward_init = (
        jnp.zeros((row_count, block_input.shape[2]), jnp.float32),
        grad_init,
        jnp.zeros(block_input.shape, jnp.float32),
    )
    backward_done = lax.scan(backward_tick, backward_init, jnp.arange(tick_count, dtype=jnp.int32))[
        0
    ]
    grads = backward_done[1]
    input_grads = backward_done[2]
    wide_sums = (
        lax.psum(grads[2].astype(jnp.bfloat16), "wide").astype(jnp.float32),
        lax.psum(grads[3].astype(jnp.bfloat16), "wide").astype(jnp.float32),
        lax.psum(grads[4].astype(jnp.bfloat16), "wide").astype(jnp.float32),
        lax.psum(grads[6].astype(jnp.bfloat16), "wide").astype(jnp.float32),
        lax.psum(grads[7].astype(jnp.bfloat16), "wide").astype(jnp.float32),
        lax.psum(grads[8].astype(jnp.bfloat16), "wide").astype(jnp.float32),
    )
    shared = lax.psum((grads[0], grads[1], grads[5], grads[9]), ("tensor", "wide"))
    return (
        outputs[None],
        input_grads[None],
        shared[0][None],
        shared[1][None],
        wide_sums[0][None],
        wide_sums[1][None],
        wide_sums[2][None],
        shared[2][None],
        wide_sums[3][None],
        wide_sums[4][None],
        wide_sums[5][None],
        shared[3][None],
    )


def solution(mesh):
    placed = (
        P(None, ("wide", "tensor"), None),
        P(),
        P("section", None, None),
        P("section", None, None),
        P("section", None, "tensor"),
        P("section", "tensor"),
        P("section", "tensor", None),
        P("section", None),
        P("section", None, "tensor"),
        P("section", "tensor"),
        P("section", "tensor", None),
        P("section", None),
        P(None, ("wide", "tensor"), None),
    )
    results = (
        P("section", None, ("wide", "tensor"), None),
        P("section", None, ("wide", "tensor"), None),
        P("section", None, None),
        P("section", None, None),
        P("section", None, "tensor"),
        P("section", "tensor"),
        P("section", "tensor", None),
        P("section", None),
        P("section", None, "tensor"),
        P("section", "tensor"),
        P("section", "tensor", None),
        P("section", None),
    )

    def program(*args):
        heads = args[4].shape[2] // (3 * HEAD_DIM * mesh.shape["tensor"])
        one_head_each = heads == mesh.shape["wide"] and heads % 2 == 0
        two_by_two = mesh.shape["section"] == 2 and mesh.shape["tensor"] == 2
        body = relay_shards if one_head_each and two_by_two else general_shards
        return jax.shard_map(
            body, mesh=mesh, in_specs=placed, out_specs=results, check_vma=False
        )(*args)

    return program
```

```python
import functools
import math

import jax
import jax.numpy as jnp
from jax import lax
from jax.experimental import pallas as pl
from jax.experimental.pallas import tpu as pltpu
from jax.sharding import PartitionSpec as P

HEAD_DIM = 64
ROT = 16
SEQ = 2048


EPSILON = 1e-05
ROPE_BASE = 10000.0

MESH = pl.DeviceIdType.MESH
F32 = jnp.float32
BF16 = jnp.bfloat16
LANES = 128
BLOCK = 512
COLS = 512
NEG = -1e30
SCORE_SCALE = math.log2(math.e) / math.sqrt(HEAD_DIM)


def dot(a, b):
    return jnp.dot(a, b, preferred_element_type=F32)


def dot_t(a, b):
    return lax.dot_general(a, b, (((1,), (1,)), ((), ())), preferred_element_type=F32)


def t_dot(a, b):
    return lax.dot_general(a, b, (((0,), (0,)), ((), ())), preferred_element_type=F32)


def lane_low(rows):
    return lax.broadcasted_iota(jnp.int32, (rows, LANES), 1) < HEAD_DIM


def turn(values):
    return pltpu.roll(values, HEAD_DIM, 1)


def rotary(values, cos_ref, front_ref, back_ref, seq, sign):
    cos, front, back = cos_ref[seq], front_ref[seq], back_ref[seq]
    ahead = pltpu.roll(values, LANES - ROT // 2, 1)
    behind = pltpu.roll(values, ROT // 2, 1)
    return values * cos + sign * (ahead * front + behind * back)


def pair_up(first, second, low):
    return jnp.where(low, first, turn(second)), jnp.where(low, turn(first), second)


def relay_kernel(
    dims,
    ends,
    x_hbm,
    cot_hbm,
    gain,
    shift,
    qkv_b,
    up_b,
    out_b,
    wqkv_hbm,
    wdense_hbm,
    wup_hbm,
    wdown_hbm,
    cos,
    front,
    back,
    out_hbm,
    ig_hbm,
    norm_hbm,
    g_hbm,
    mixed_hbm,
    hid_hbm,
    dpre_hbm,
    dpk_hbm,
    small,
    bias_sums,
    wqkv,
    wdense,
    wup,
    wdown,
    xfull,
    gfull,
    cot,
    qkv_r,
    mix_r,
    do_r,
    dqkv_r,
    rsf_r,
    rsb_r,
    qkv_st,
    o_st,
    do_st,
    dqkv_st,
    rsf_st,
    rsb_st,
    out_st,
    gx_st,
    ig_st,
    norm_st,
    mixed_st,
    hid_st,
    dpre_st,
    dpk_st,
    slope,
    part,
    part_b,
    dn1,
    qm,
    kr,
    vx,
    dox,
    dq,
    lse,
    delta,
    scores,
    peak,
    acc,
    wsem,
    ownx_sem,
    yx_s,
    yx_r,
    owng_sem,
    yg_s,
    yg_r,
    qkv_ss,
    qkv_rs,
    o_ss,
    o_rs,
    do_ss,
    do_rs,
    dqkv_ss,
    dqkv_rs,
    rsf_ss,
    rsf_rs,
    rsb_ss,
    rsb_rs,
    xs_ss,
    gs_ss,
    store_sem,
    g_store,
):
    micro, rows, group, wide, heads, d_model, ff = dims
    sect = lax.axis_index("section")
    tens = lax.axis_index("tensor")
    me = lax.axis_index("wide")
    pairs = heads // 2
    per_source = group + group // 2
    half = group // 2
    q_blocks = SEQ // BLOCK
    sources = BLOCK // group
    my_rows = pl.ds(pl.multiple_of(tens * rows, rows), rows)
    his_rows = pl.ds(pl.multiple_of((1 - tens) * rows, rows), rows)
    x_dev = {"section": 1 - sect}
    y_dev = {"tensor": 1 - tens}
    low_half = lane_low(half)
    low_group = lane_low(group)

    def remote(src, dst, ss, rs, dev):
        return pltpu.make_async_remote_copy(
            src_ref=src, dst_ref=dst, send_sem=ss, recv_sem=rs, device_id=dev, device_id_type=MESH
        )

    def arrived(ref, sem):
        pltpu.make_async_copy(ref, ref, sem).wait()

    def tokens_of(s):
        return pl.ds(pl.multiple_of(s * group, group), group)

    def y_send_x(s):
        own = xfull.at[s, my_rows]
        return remote(own, own, yx_s.at[s], yx_r.at[s], y_dev)

    def y_send_g(s):
        own = gfull.at[s, my_rows]
        return remote(own, own, yg_s.at[s], yg_r.at[s], y_dev)

    def spread(stage, target, seq, dest, ss, rs):
        @pl.when(dest == me)
        def _():
            pltpu.make_async_copy(stage, target.at[seq, me], rs).start()

        @pl.when(dest != me)
        def _():
            remote(stage, target.at[seq, me], ss, rs, {"wide": dest}).start()

    loads = [
        pltpu.make_async_copy(source, target, wsem.at[i])
        for i, (source, target) in enumerate(
            ((wqkv_hbm, wqkv), (wup_hbm, wup), (wdown_hbm, wdown), (wdense_hbm, wdense))
        )
    ]

    barrier = pltpu.get_barrier_semaphore()
    for dev in [x_dev, y_dev] + [{"wide": lax.rem(me + k, wide)} for k in range(1, wide)]:
        pl.semaphore_signal(barrier, inc=1, device_id=dev, device_id_type=MESH)

    @pl.when(sect == 0)
    def _():
        for s in range(micro):
            pltpu.make_async_copy(x_hbm.at[s], xfull.at[s, my_rows], ownx_sem.at[s]).start()

    for load in loads:
        load.start()

    @pl.when(sect == 1)
    def _():
        for s in range(micro):
            pltpu.make_async_copy(cot_hbm.at[s], cot.at[s], owng_sem.at[s]).start()

    small[...] = jnp.zeros_like(small)
    bias_sums[...] = jnp.zeros_like(bias_sums)
    pl.semaphore_wait(barrier, wide + 1)

    @pl.when(sect == 0)
    def _():
        for s in range(micro):
            arrived(xfull.at[s, my_rows], ownx_sem.at[s])
            y_send_x(s).start()

    @pl.when(sect == 1)
    def _():
        for s in range(micro):
            arrived(cot.at[s], owng_sem.at[s])

            def chunk(i, carry, s=s):
                at = pl.ds(pl.multiple_of(i * 32, 32), 32)
                there = pl.ds(pl.multiple_of(tens * rows + i * 32, 32), 32)
                gfull[s, there, :] = cot[s, at, :].astype(BF16)
                return carry

            lax.fori_loop(0, rows // 32, chunk, 0)
            y_send_g(s).start()

    def fold(values):
        total = values[0:8]
        for k in range(1, values.shape[0] // 8):
            total = total + values[k * 8 : (k + 1) * 8]
        return total

    def normed_rows(values):
        center = jnp.mean(values, axis=-1, keepdims=True)
        centred = values - center
        spread_of = jnp.mean(centred * centred, axis=-1, keepdims=True)
        inv = lax.rsqrt(spread_of + EPSILON)
        return centred * inv, inv

    def starts_of(s, tokens):
        found = jnp.zeros_like(tokens)
        for j in range(ends.shape[1]):
            end = ends[s, j]
            found = jnp.where(tokens >= end, end, found)
        return found

    def unpack_heads(s):
        def step(src, carry):
            qk = qkv_r[s, src, 0:group, :].astype(F32)
            at = pl.multiple_of(src * group, group)
            qm[pl.ds(at, group), :] = jnp.where(low_group, qk, 0.0).astype(BF16)
            kr[pl.ds(at, group), :] = turn(qk).astype(BF16)
            packed_v = qkv_r[s, src, group:per_source, :].astype(F32)
            ones = jnp.where(
                lax.broadcasted_iota(jnp.int32, (half, LANES), 1) == HEAD_DIM, 1.0, 0.0
            )
            vx[pl.ds(at, half), :] = jnp.where(low_half, packed_v, ones).astype(BF16)
            vx[pl.ds(pl.multiple_of(at + half, half), half), :] = jnp.where(
                low_half, turn(packed_v), ones
            ).astype(BF16)
            return carry

        lax.fori_loop(0, wide, step, 0, unroll=True)

    def forward(s):
        @pl.when(sect == 1)
        def _():
            arrived(xfull.at[s, my_rows], ownx_sem.at[s])
            y_send_x(s).start()

        arrived(xfull.at[s, his_rows], yx_r.at[s])

        def norm_step(i, carry):
            at = pl.ds(pl.multiple_of(i * 32, 32), 32)
            a, _ = normed_rows(xfull[s, at, :].astype(F32))
            norm_st[0, at, :] = (a * gain[0:1, :] + shift[0:1, :]).astype(BF16)
            norm_st[1, at, :] = (a * gain[1:2, :] + shift[1:2, :]).astype(BF16)
            return carry

        @pl.when(s > 0)
        def _():
            arrived(norm_st.at[0], store_sem.at[0])
            arrived(norm_st.at[1], store_sem.at[1])

        lax.fori_loop(0, group // 32, norm_step, 0, unroll=True)
        pltpu.make_async_copy(norm_st.at[0], norm_hbm.at[0, tokens_of(s)], store_sem.at[0]).start()
        pltpu.make_async_copy(norm_st.at[1], norm_hbm.at[1, tokens_of(s)], store_sem.at[1]).start()

        def qkv_step(k, carry):
            pair = lax.rem(me // 2 + 1 + k, pairs)
            cols = pl.ds(pl.multiple_of(pair * 3 * LANES, LANES), 3 * LANES)
            packed = dot(norm_st[0], wqkv[:, cols]) + qkv_b[:, cols]
            first, middle, last = (packed[:, i * LANES : (i + 1) * LANES] for i in range(3))
            qk0 = rotary(first, cos, front, back, s, 1.0)
            qk1 = rotary(
                turn(jnp.where(low_group, last, middle)), cos, front, back, s, 1.0
            )
            vv = jnp.where(low_group, middle, last)
            v0 = jnp.where(low_half, vv[:half], turn(vv[half:]))
            v1 = jnp.where(low_half, turn(vv[:half]), vv[half:])
            for i, (qk, v) in enumerate(((qk0, v0), (qk1, v1))):
                qkv_st[2 * pair + i, 0:group, :] = qk.astype(BF16)
                qkv_st[2 * pair + i, group:per_source, :] = v.astype(BF16)
            for i in range(2):
                dest = 2 * pair + i
                spread(qkv_st.at[dest], qkv_r, s, dest, qkv_ss.at[0], qkv_rs.at[s])
            return carry

        pl.when(s == 0)(loads[0].wait)
        lax.fori_loop(0, pairs, qkv_step, 0, unroll=True)

    def forward_ff(s):
        @pl.when(s == 0)
        def _():
            loads[1].wait()
            loads[2].wait()

        @pl.when(s > 0)
        def _():
            arrived(hid_st, store_sem.at[2])

        def ff_step(j, carry):
            cols = pl.ds(pl.multiple_of(j * COLS, COLS), COLS)
            pre = dot(norm_st[1], wup[:, cols]) + up_b[:, cols]
            cumul = 0.5 * (1.0 + lax.erf(pre * (1.0 / math.sqrt(2.0))))
            density = jnp.exp(-0.5 * pre * pre) * (1.0 / math.sqrt(2.0 * math.pi))
            hid = (pre * cumul).astype(BF16)
            hid_st[:, cols] = hid
            slope[s, :, cols] = (cumul + pre * density).astype(BF16)
            term = dot(hid, wdown[cols, :])

            @pl.when(j == 0)
            def _():
                part[...] = term

            @pl.when(j > 0)
            def _():
                part[...] += term

            return carry

        lax.fori_loop(0, ff // COLS, ff_step, 0, unroll=True)
        pltpu.make_async_copy(hid_st, hid_hbm.at[tokens_of(s)], store_sem.at[2]).start()

    def forward_attention(s):
        arrived(qkv_r.at[s], qkv_rs.at[s])
        arrived(qkv_st.at[pl.ds(0, wide - 1)], qkv_ss.at[0])
        unpack_heads(s)

        for i in range(q_blocks):
            q_at = slice(i * BLOCK, (i + 1) * BLOCK)
            tokens = i * BLOCK + lax.broadcasted_iota(jnp.int32, (BLOCK, LANES), 0)
            begin = starts_of(s, tokens)[:, 0:1]
            best = jnp.full((BLOCK, LANES), NEG, F32)
            for j in range(i + 1):
                k_at = slice(j * BLOCK, (j + 1) * BLOCK)
                raw = dot_t(qm[q_at, :], kr[k_at, :])
                u = j * BLOCK + lax.broadcasted_iota(jnp.int32, (BLOCK, BLOCK), 1)
                seen = u >= begin
                if i == j:
                    seen = seen & (u <= tokens[:, 0:1])
                raw = jnp.where(seen, raw, NEG)
                scores[:, k_at] = raw
                for k in range(BLOCK // LANES):
                    best = jnp.maximum(best, raw[:, k * LANES : (k + 1) * LANES])
            top = jnp.max(best, axis=1, keepdims=True) * SCORE_SCALE
            out = jnp.zeros((BLOCK, LANES), F32)
            for j in range(i + 1):
                k_at = slice(j * BLOCK, (j + 1) * BLOCK)
                probs = jnp.exp2(scores[:, k_at] * SCORE_SCALE - top)
                out = out + dot(probs.astype(BF16), vx[k_at, :])
            total = out[:, HEAD_DIM : HEAD_DIM + 1]
            out = out / total
            log_total = top + jnp.log2(total)
            lse[s, i] = jnp.broadcast_to(log_total, (BLOCK, LANES)).T[0:8, :]
            for k in range(sources):
                first = out[k * group : k * group + half]
                second = out[k * group + half : (k + 1) * group]
                source = i * sources + k
                o_st[s, source] = jnp.where(low_half, first, turn(second)).astype(BF16)
                spread(o_st.at[s, source], mix_r, s, source, o_ss.at[s], o_rs.at[s])

    def forward_out(s):
        arrived(mix_r.at[s], o_rs.at[s])
        arrived(o_st.at[s, pl.ds(0, wide - 1)], o_ss.at[s])
        pl.when((s == 0) & (sect == 0))(loads[3].wait)
        pl.when(s > 0)(lambda: arrived(mixed_st, store_sem.at[3]))
        for pair in range(pairs):
            top, bottom = pair_up(
                mix_r[s, 2 * pair].astype(F32), mix_r[s, 2 * pair + 1].astype(F32), low_half
            )
            mixed_st[0:half, pair * LANES : (pair + 1) * LANES] = top.astype(BF16)
            mixed_st[half:group, pair * LANES : (pair + 1) * LANES] = bottom.astype(BF16)
        pltpu.make_async_copy(mixed_st, mixed_hbm.at[tokens_of(s)], store_sem.at[3]).start()
        part[...] += dot(mixed_st[...], wdense[...])
        rsf_st[...] = part[his_rows, :].astype(BF16)
        remote(rsf_st, rsf_r.at[s], rsf_ss.at[0], rsf_rs.at[s], y_dev).start()

    def forward_end(s):
        arrived(rsf_r.at[s], rsf_rs.at[s])
        arrived(rsf_st, rsf_ss.at[0])

        @pl.when(s > 0)
        def _():
            arrived(out_st, store_sem.at[4])
            pl.when(sect == 0)(lambda: arrived(out_st, xs_ss.at[0]))

        def out_step(i, carry):
            at = pl.ds(pl.multiple_of(i * 32, 32), 32)
            there = pl.ds(pl.multiple_of(tens * rows + i * 32, 32), 32)
            branch = part[there, :] + rsf_r[s, at, :].astype(F32) + out_b[...]
            out_st[at, :] = (xfull[s, there, :].astype(F32) + branch).astype(BF16)
            return carry

        lax.fori_loop(0, rows // 32, out_step, 0, unroll=True)

        @pl.when(sect == 0)
        def _():
            remote(out_st, xfull.at[s, my_rows], xs_ss.at[0], ownx_sem.at[s], x_dev).start()

        pltpu.make_async_copy(out_st, out_hbm.at[s], store_sem.at[4]).start()

    def backward(s):
        @pl.when(sect == 0)
        def _():
            arrived(gfull.at[s, my_rows], owng_sem.at[s])
            y_send_g(s).start()

        arrived(gfull.at[s, his_rows], yg_r.at[s])
        pl.when((s == 0) & (sect == 1))(loads[3].wait)
        pltpu.make_async_copy(gfull.at[s], g_hbm.at[tokens_of(s)], g_store.at[s]).start()

        def mixed_step(k, carry):
            pair = lax.rem(me // 2 + 1 + k, pairs)
            at = pl.ds(pl.multiple_of(pair * LANES, LANES), LANES)
            both = dot_t(gfull[s], wdense[at, :])
            first = jnp.where(low_half, both[:half], turn(both[half:]))
            second = jnp.where(low_half, turn(both[:half]), both[half:])
            do_st[s, 2 * pair] = first.astype(BF16)
            do_st[s, 2 * pair + 1] = second.astype(BF16)
            for i in range(2):
                dest = 2 * pair + i
                spread(do_st.at[s, dest], do_r, s, dest, do_ss.at[s], do_rs.at[s])
            return carry

        lax.fori_loop(0, pairs, mixed_step, 0, unroll=True)

    def backward_ff(s):
        pl.when(s > 0)(lambda: arrived(dpre_st, store_sem.at[6]))

        def ff_step(j, carry):
            cols = pl.ds(pl.multiple_of(j * COLS, COLS), COLS)
            grad = dot_t(gfull[s], wdown[cols, :])
            grad = (grad * slope[s, :, cols].astype(F32)).astype(BF16)
            dpre_st[:, cols] = grad
            sums_at = pl.ds(pl.multiple_of(3 * heads * HEAD_DIM + j * COLS, COLS), COLS)
            bias_sums[:, sums_at] += fold(grad.astype(F32))
            term = dot_t(grad, wup[:, cols])

            @pl.when(j == 0)
            def _():
                dn1[...] = term

            @pl.when(j > 0)
            def _():
                dn1[...] += term

            return carry

        lax.fori_loop(0, ff // COLS, ff_step, 0, unroll=True)
        pltpu.make_async_copy(dpre_st, dpre_hbm.at[tokens_of(s)], store_sem.at[6]).start()

    def backward_attention(s):
        arrived(do_r.at[s], do_rs.at[s])
        arrived(do_st.at[s, pl.ds(0, wide - 1)], do_ss.at[s])
        pl.when(sect == 0)(lambda: unpack_heads(s))

        def unpack_step(src, carry):
            at = pl.multiple_of(src * group, group)
            grad = do_r[s, src].astype(F32)
            dox[pl.ds(at, half), :] = jnp.where(low_half, grad, 0.0).astype(BF16)
            dox[pl.ds(pl.multiple_of(at + half, half), half), :] = jnp.where(
                low_half, turn(grad), 0.0
            ).astype(BF16)
            product = grad * o_st[s, src].astype(F32)
            left = jnp.sum(jnp.where(low_half, product, 0.0), axis=1, keepdims=True)
            right = jnp.sum(jnp.where(low_half, 0.0, product), axis=1, keepdims=True)
            delta[src, :, 0:half] = jnp.broadcast_to(left, (half, LANES)).T[0:8, :]
            delta[src, :, half:group] = jnp.broadcast_to(right, (half, LANES)).T[0:8, :]
            return carry

        lax.fori_loop(0, wide, unpack_step, 0, unroll=True)
        slot = lax.rem(s, 2)
        rows_of = []
        for i in range(q_blocks):
            tokens = i * BLOCK + lax.broadcasted_iota(jnp.int32, (8, BLOCK), 1)
            inner_sum = jnp.concatenate(
                [delta[i * sources + k, 0:1, :] for k in range(sources)], axis=1
            )
            rows_of.append((starts_of(s, tokens)[0:1, :], tokens[0:1, :], inner_sum))
        for j in range(q_blocks):
            k_at = slice(j * BLOCK, (j + 1) * BLOCK)
            for i in range(j, q_blocks):
                q_at = slice(i * BLOCK, (i + 1) * BLOCK)
                begin, token, inner_sum = rows_of[i]
                raw = dot_t(kr[k_at, :], qm[q_at, :])
                u = j * BLOCK + lax.broadcasted_iota(jnp.int32, (BLOCK, BLOCK), 0)
                probs = jnp.exp2(raw * SCORE_SCALE - lse[s, i, 0:1, :])
                seen = u >= begin
                if i == j:
                    seen = seen & (u <= token)
                probs = jnp.where(seen, probs, 0.0)
                probs_grad = dot_t(vx[k_at, :], dox[q_at, :])
                score_grad = (probs * (probs_grad - inner_sum)).astype(BF16)
                value_term = dot(probs.astype(BF16), dox[q_at, :])
                key_term = dot(score_grad, kr[q_at, :])
                query_term = t_dot(score_grad, kr[k_at, :])
                if i == j:
                    acc[...] = value_term
                    peak[...] = key_term
                else:
                    acc[...] += value_term
                    peak[...] += key_term
                if j == 0:
                    dq[q_at, :] = query_term
                else:
                    dq[q_at, :] += query_term
            for k in range(sources):
                source = j * sources + k
                mine = slice(k * group, (k + 1) * group)
                at = slice(source * group, (source + 1) * group)
                both = jnp.where(low_group, dq[at, :], peak[mine, :])
                both = both * (1.0 / math.sqrt(HEAD_DIM))
                value = acc[mine, :]
                value = jnp.where(low_half, value[:half], turn(value[half:]))
                dqkv_st[slot, source, 0:group, :] = both.astype(BF16)
                dqkv_st[slot, source, group:per_source, :] = value.astype(BF16)
                spread(
                    dqkv_st.at[slot, source], dqkv_r, s, source, dqkv_ss.at[slot], dqkv_rs.at[s]
                )

    def backward_norm(s):
        arrived(dqkv_r.at[s], dqkv_rs.at[s])
        slot = lax.rem(s, 2)
        arrived(dqkv_st.at[slot, pl.ds(0, wide - 1)], dqkv_ss.at[slot])
        pl.when(s > 0)(lambda: arrived(dpk_st, store_sem.at[7]))

        def pair_step(pair, carry):
            qk0 = rotary(
                dqkv_r[s, 2 * pair, 0:group, :].astype(F32), cos, front, back, s, -1.0
            )
            qk1 = turn(
                rotary(
                    dqkv_r[s, 2 * pair + 1, 0:group, :].astype(F32), cos, front, back, s, -1.0
                )
            )
            top, bottom = pair_up(
                dqkv_r[s, 2 * pair, group:per_source, :].astype(F32),
                dqkv_r[s, 2 * pair + 1, group:per_source, :].astype(F32),
                low_half,
            )
            vv = jnp.concatenate([top, bottom], axis=0)
            columns = (qk0, jnp.where(low_group, vv, qk1), jnp.where(low_group, qk1, vv))
            for k, column in enumerate(columns):
                at = pl.ds(pl.multiple_of((pair * 3 + k) * LANES, LANES), LANES)
                column = column.astype(BF16)
                dpk_st[:, at] = column
                bias_sums[:, at] += fold(column.astype(F32))
            return carry

        lax.fori_loop(0, pairs, pair_step, 0, unroll=True)
        pltpu.make_async_copy(dpk_st, dpk_hbm.at[tokens_of(s)], store_sem.at[7]).start()
        part_b[...] = dot_t(dpk_st[...], wqkv[...])

        def e_step(i, carry):
            at = pl.ds(pl.multiple_of(i * 32, 32), 32)
            a, _ = normed_rows(xfull[s, at, :].astype(F32))
            first = part_b[at, :]
            second = dn1[at, :]
            small[0] += fold(first * a)
            small[1] += fold(second * a)
            small[2] += fold(first)
            small[3] += fold(second)
            part_b[at, :] = first * gain[0:1, :] + second * gain[1:2, :]
            return carry

        lax.fori_loop(0, group // 32, e_step, 0, unroll=True)
        rsb_st[...] = part_b[his_rows, :].astype(BF16)
        remote(rsb_st, rsb_r.at[s], rsb_ss.at[0], rsb_rs.at[s], y_dev).start()

    def backward_end(s):
        arrived(rsb_r.at[s], rsb_rs.at[s])
        arrived(rsb_st, rsb_ss.at[0])

        @pl.when(s > 0)
        def _():
            arrived(ig_st, store_sem.at[8])
            pl.when(sect == 1)(lambda: arrived(gx_st, gs_ss.at[0]))

        def in_step(i, carry):
            at = pl.ds(pl.multiple_of(i * 32, 32), 32)
            there = pl.ds(pl.multiple_of(tens * rows + i * 32, 32), 32)
            a, inv = normed_rows(xfull[s, there, :].astype(F32))
            e = part_b[there, :] + rsb_r[s, at, :].astype(F32)
            mean_e = jnp.mean(e, axis=-1, keepdims=True)
            cross = jnp.mean(e * a, axis=-1, keepdims=True)
            g_low = gfull[s, there, :].astype(F32)
            small[4] += fold(g_low)
            g = jnp.where(sect == 1, cot[s, at, :], g_low)
            grad = g + inv * (e - mean_e - a * cross)
            ig_st[at, :] = grad
            gx_st[at, :] = grad.astype(BF16)
            return carry

        lax.fori_loop(0, rows // 32, in_step, 0, unroll=True)

        @pl.when(sect == 1)
        def _():
            remote(gx_st, gfull.at[s, my_rows], gs_ss.at[0], owng_sem.at[s], x_dev).start()

        pltpu.make_async_copy(ig_st, ig_hbm.at[s], store_sem.at[8]).start()

    def at(seq, allowed, body):
        pl.when(allowed & (seq >= 0) & (seq < micro))(lambda: body(seq))

    @pl.when(sect == 1)
    def _():
        lax.fori_loop(0, micro, lambda s, carry: (backward(s), carry)[1], 0)

    first = jnp.int32(0)
    forward(first)
    forward_ff(first)
    always = sect >= 0

    def step(i, carry):
        f = i
        b = jnp.where(sect == 1, i, i - micro)
        at(b, sect == 0, backward)
        at(f, always, forward_attention)
        at(f + 1, always, forward)
        at(b, always, backward_attention)
        at(f, always, forward_out)
        at(b - 1, always, backward_norm)
        at(b, always, backward_ff)
        at(f, always, forward_end)
        at(b - 1, always, backward_end)
        at(f + 1, always, forward_ff)
        return carry

    lax.fori_loop(0, jnp.where(sect == 1, micro + 1, 2 * micro + 1), step, 0)

    for s in range(micro):
        arrived(xfull.at[s, my_rows], yx_s.at[s])
        arrived(gfull.at[s, my_rows], yg_s.at[s])
        arrived(gfull.at[s], g_store.at[s])
    arrived(norm_st.at[0], store_sem.at[0])
    arrived(norm_st.at[1], store_sem.at[1])
    arrived(hid_st, store_sem.at[2])
    arrived(mixed_st, store_sem.at[3])
    arrived(out_st, store_sem.at[4])
    arrived(dpre_st, store_sem.at[6])
    arrived(dpk_st, store_sem.at[7])
    arrived(ig_st, store_sem.at[8])
    pl.when(sect == 0)(lambda: arrived(out_st, xs_ss.at[0]))
    pl.when(sect == 1)(lambda: arrived(gx_st, gs_ss.at[0]))


def rotary_tables(doc_lengths, tokens):
    ends = jnp.cumsum(doc_lengths, axis=1)
    starts = ends - doc_lengths
    inside = (tokens[None, :, None] >= starts[:, None, :]) & (
        tokens[None, :, None] < ends[:, None, :]
    )
    begins = jnp.sum(jnp.where(inside, starts[:, None, :], 0), axis=2)
    offsets = (tokens[None, :] - begins).astype(F32)
    part_of = ROT // 2
    freqs = ROPE_BASE ** (-2.0 * jnp.arange(part_of, dtype=F32) / ROT)
    angle = offsets[:, :, None] * freqs
    cos, sin = jnp.cos(angle), jnp.sin(angle)
    ones = jnp.ones(offsets.shape + (HEAD_DIM - ROT,), F32)
    zeros = jnp.zeros_like(sin)

    def lanes(parts):
        return jnp.concatenate(parts + parts, axis=2)

    return (
        ends.astype(jnp.int32),
        lanes([cos, cos, ones]),
        lanes([-sin, zeros, 0.0 * ones]),
        lanes([zeros, sin, 0.0 * ones]),
    )


def relay(dims, doc_lengths, block_input, cotangent, weights, collective_id):
    micro, rows, group, wide, heads, d_model, ff = dims
    (
        norm_gain,
        norm_bias,
        qkv_weight,
        qkv_bias,
        dense_weight,
        dense_bias,
        up_weight,
        up_bias,
        down_weight,
        down_bias,
    ) = weights
    tokens = lax.axis_index("wide") * group + jnp.arange(group, dtype=jnp.int32)
    ends, cos, front, back = rotary_tables(doc_lengths, tokens)
    inner = heads * HEAD_DIM
    per_source = group + group // 2
    anywhere = pl.BlockSpec(memory_space=pl.ANY)
    local = pl.BlockSpec(memory_space=pltpu.VMEM)
    scalars = pl.BlockSpec(memory_space=pltpu.SMEM)
    dma = pltpu.SemaphoreType.DMA
    vmem = pltpu.VMEM
    outs = [
        jax.ShapeDtypeStruct((micro, rows, d_model), BF16),
        jax.ShapeDtypeStruct((micro, rows, d_model), F32),
        jax.ShapeDtypeStruct((2, micro * group, d_model), BF16),
        jax.ShapeDtypeStruct((micro * group, d_model), BF16),
        jax.ShapeDtypeStruct((micro * group, inner), BF16),
        jax.ShapeDtypeStruct((micro * group, ff), BF16),
        jax.ShapeDtypeStruct((micro * group, ff), BF16),
        jax.ShapeDtypeStruct((micro * group, 3 * inner), BF16),
        jax.ShapeDtypeStruct((5, 8, d_model), F32),
        jax.ShapeDtypeStruct((8, 3 * inner + ff), F32),
    ]
    scratch = [
        vmem(qkv_weight.shape, BF16),
        vmem(dense_weight.shape, BF16),
        vmem(up_weight.shape, BF16),
        vmem(down_weight.shape, BF16),
        vmem((micro, group, d_model), BF16),
        vmem((micro, group, d_model), BF16),
        vmem((micro, rows, d_model), F32),
        vmem((micro, wide, per_source, LANES), BF16),
        vmem((micro, wide, group // 2, LANES), BF16),
        vmem((micro, wide, group // 2, LANES), BF16),
        vmem((micro, wide, per_source, LANES), BF16),
        vmem((micro, rows, d_model), BF16),
        vmem((micro, rows, d_model), BF16),
        vmem((wide, per_source, LANES), BF16),
        vmem((micro, wide, group // 2, LANES), BF16),
        vmem((micro, wide, group // 2, LANES), BF16),
        vmem((2, wide, per_source, LANES), BF16),
        vmem((rows, d_model), BF16),
        vmem((rows, d_model), BF16),
        vmem((rows, d_model), BF16),
        vmem((rows, d_model), BF16),
        vmem((rows, d_model), F32),
        vmem((2, group, d_model), BF16),
        vmem((group, inner), BF16),
        vmem((group, ff), BF16),
        vmem((group, ff), BF16),
        vmem((group, 3 * inner), BF16),
        vmem((micro, group, ff), BF16),
        vmem((group, d_model), F32),
        vmem((group, d_model), F32),
        vmem((group, d_model), F32),
        vmem((SEQ, LANES), BF16),
        vmem((SEQ, LANES), BF16),
        vmem((SEQ, LANES), BF16),
        vmem((SEQ, LANES), BF16),
        vmem((SEQ, LANES), F32),
        vmem((micro, SEQ // BLOCK, 8, BLOCK), F32),
        vmem((wide, 8, group), F32),
        vmem((BLOCK, SEQ), F32),
        vmem((BLOCK, LANES), F32),
        vmem((BLOCK, LANES), F32),
        dma((4,)),
        dma((micro,)),
        dma((micro,)),
        dma((micro,)),
        dma((micro,)),
        dma((micro,)),
        dma((micro,)),
        dma((1,)),
        dma((micro,)),
        dma((micro,)),
        dma((micro,)),
        dma((micro,)),
        dma((micro,)),
        dma((2,)),
        dma((micro,)),
        dma((1,)),
        dma((micro,)),
        dma((1,)),
        dma((micro,)),
        dma((1,)),
        dma((1,)),
        dma((9,)),
        dma((micro,)),
    ]
    return pl.pallas_call(
        functools.partial(relay_kernel, dims),
        out_shape=outs,
        in_specs=[scalars, anywhere, anywhere]
        + [local] * 5
        + [anywhere] * 4
        + [local] * 3,
        out_specs=[anywhere] * 8 + [local] * 2,
        scratch_shapes=scratch,
        compiler_params=pltpu.CompilerParams(
            collective_id=collective_id, has_side_effects=True, vmem_limit_bytes=63 << 20
        ),
        name="relay",
    )(
        ends,
        block_input,
        cotangent,
        norm_gain,
        norm_bias,
        qkv_bias[None],
        up_bias[None],
        (dense_bias + down_bias)[None],
        qkv_weight,
        dense_weight,
        up_weight,
        down_weight,
        cos,
        front,
        back,
    )


TILE = 256
RING = 8
TOTALS = 4


def gradient_kinds(d_model, inner, ff):
    return ((d_model, ff), (ff, d_model), (inner, d_model), (d_model, 3 * inner))


def gradient_kernel(
    dims,
    norm_hbm,
    g_hbm,
    mixed_hbm,
    hid_hbm,
    dpre_hbm,
    dpk_hbm,
    small,
    biases,
    up_out,
    down_out,
    dense_out,
    qkv_out,
    sums,
    left_op,
    right_op,
    own,
    core_r,
    outer_r,
    inner_r,
    core_st,
    red_st,
    tot,
    sums_r,
    op_sem,
    core_ss,
    core_rs,
    outer_rs,
    inner_rs,
    red_ss,
    bc_rs,
    tot_ss,
    fwd_ss,
    share_ss,
    fin_rs,
    sum_ss,
    sum_rs,
    core_free,
    outer_free,
    inner_free,
):
    micro, rows, group, wide, heads, d_model, ff = dims
    tens = lax.axis_index("tensor")
    me = lax.axis_index("wide")
    chip, core = me // 2, lax.rem(me, 2)
    partner = {"wide": me + 1 - 2 * core}
    up_dev = {"wide": lax.rem(me + 2, wide)}
    down_dev = {"wide": lax.rem(me + wide - 2, wide)}
    at_bottom, at_top = chip == 0, chip == wide // 2 - 1
    at_end = at_bottom | at_top
    middle = jnp.logical_not(at_end)
    lower = chip == 1
    outer_of = {"wide": jnp.where(lower, me - 2, lax.rem(me + 2, wide))}
    inner_of = {"wide": jnp.where(lower, me + 2, lax.rem(me + wide - 2, wide))}
    end_of = {"wide": jnp.where(at_bottom, me + 2, lax.rem(me + wide - 2, wide))}
    inner = heads * HEAD_DIM
    kinds = gradient_kinds(d_model, inner, ff)
    targets = (up_out, down_out, dense_out, qkv_out)
    operands = (
        (norm_hbm.at[1], dpre_hbm),
        (hid_hbm, g_hbm),
        (mixed_hbm, g_hbm),
        (norm_hbm.at[0], dpk_hbm),
    )
    ranges, first = [], 0
    for height, width in kinds:
        count = (height // TILE) * (width // (2 * TILE))
        ranges.append((first, first + count, width // (2 * TILE)))
        first += count
    steps = first

    def remote(src, dst, ss, rs, dev):
        return pltpu.make_async_remote_copy(
            src_ref=src, dst_ref=dst, send_sem=ss, recv_sem=rs, device_id=dev, device_id_type=MESH
        )

    def arrived(ref, sem):
        pltpu.make_async_copy(ref, ref, sem).wait()

    tile_ref = tot.at[0]

    def by_kind(m, body):
        for kind, (low, high, across) in enumerate(ranges):

            @pl.when((m >= low) & (m < high))
            def _(kind=kind, low=low, across=across):
                at = m - low
                body(kind, at // across, lax.rem(at, across))

    def tile_of(kind, row, col, which):
        return targets[kind].at[
            pl.ds(pl.multiple_of(row * TILE, TILE), TILE),
            pl.ds(pl.multiple_of((2 * col + which) * TILE, TILE), TILE),
        ]

    def fetch(m):
        def body(kind, row, col):
            left, right = operands[kind]
            slot = lax.rem(m, 2)
            pltpu.make_async_copy(
                left.at[:, pl.ds(pl.multiple_of(row * TILE, TILE), TILE)],
                left_op.at[slot],
                op_sem.at[0, slot],
            ).start()
            pltpu.make_async_copy(
                right.at[:, pl.ds(pl.multiple_of(col * 2 * TILE, 2 * TILE), 2 * TILE)],
                right_op.at[slot],
                op_sem.at[1, slot],
            ).start()

        by_kind(m, body)

    def is_root(m):
        return middle & (chip == 1 + lax.rem(m, 2))

    def products(m):
        slot, ring = lax.rem(m, 2), lax.rem(m, RING)
        arrived(left_op.at[slot], op_sem.at[0, slot])
        arrived(right_op.at[slot], op_sem.at[1, slot])
        left = left_op[slot]
        mine = pl.ds(pl.multiple_of(core * TILE, TILE), TILE)
        other = pl.ds(pl.multiple_of((1 - core) * TILE, TILE), TILE)

        @pl.when(m >= RING)
        def _():
            arrived(tile_ref, core_ss.at[ring])
            pl.semaphore_wait(core_free, 1)

        core_st[ring] = t_dot(left, right_op[slot, :, other]).astype(BF16)
        remote(
            core_st.at[ring], core_r.at[ring], core_ss.at[ring], core_rs.at[ring], partner
        ).start()
        own[ring] = t_dot(left, right_op[slot, :, mine])

    def send_red(m, value, target, sem, dev, free):
        ring = lax.rem(m, RING)

        @pl.when(m >= RING)
        def _():
            pl.semaphore_wait(free, 1)

        red_st[ring] = value.astype(BF16)
        remote(red_st.at[ring], target.at[ring], red_ss.at[ring], sem.at[ring], dev).start()

    def chip_sum(m):
        ring = lax.rem(m, RING)
        arrived(tile_ref, core_rs.at[ring])
        total = own[ring] + core_r[ring].astype(F32)

        @pl.when(m + RING < steps)
        def _():
            pl.semaphore_signal(core_free, inc=1, device_id=partner, device_id_type=MESH)

        @pl.when(at_end)
        def _():
            @pl.when(m >= RING)
            def _():
                arrived(tile_ref, red_ss.at[ring])

            send_red(m, total, outer_r, outer_rs, end_of, outer_free.at[lax.rem(m, 2)])

        @pl.when(middle)
        def _():
            own[ring] = total

    def take_outer(m):
        ring = lax.rem(m, RING)
        arrived(tile_ref, outer_rs.at[ring])
        total = own[ring] + outer_r[ring].astype(F32)

        @pl.when(m + RING < steps)
        def _():
            pl.semaphore_signal(
                outer_free.at[lax.rem(m, 2)], inc=1, device_id=outer_of, device_id_type=MESH
            )

        return total

    def pass_in(m):
        ring = lax.rem(m, RING)
        total = take_outer(m)

        @pl.when(m >= RING)
        def _():
            arrived(tile_ref, red_ss.at[ring])

        send_red(m, total, inner_r, inner_rs, inner_of, inner_free)

    def finish(m):
        ring = lax.rem(m, RING)
        slot = lax.rem(m // 2, TOTALS)
        total = take_outer(m)
        arrived(tile_ref, inner_rs.at[ring])
        total = total + inner_r[ring].astype(F32)

        @pl.when(m + RING < steps)
        def _():
            pl.semaphore_signal(inner_free, inc=1, device_id=inner_of, device_id_type=MESH)

        @pl.when(m >= 2 * TOTALS)
        def _():
            for k in range(4):
                arrived(tile_ref, tot_ss.at[k, slot])

        tot[slot] = total.astype(BF16)

        def body(kind, row, col):
            here = tile_of(kind, row, col, core)
            remote(tot.at[slot], here, tot_ss.at[0, slot], bc_rs.at[m], outer_of).start()
            remote(tot.at[slot], here, tot_ss.at[1, slot], bc_rs.at[m], inner_of).start()
            remote(tot.at[slot], here, tot_ss.at[2, slot], fin_rs.at[kind], partner).start()
            pltpu.make_async_copy(tot.at[slot], here, tot_ss.at[3, slot]).start()

        by_kind(m, body)

    def hand_on(m):
        arrived(tile_ref, bc_rs.at[m])

        def body(kind, row, col):
            here = tile_of(kind, row, col, core)

            @pl.when(middle)
            def _():
                remote(here, here, fwd_ss.at[m], bc_rs.at[m], outer_of).start()

            remote(here, here, share_ss.at[m], fin_rs.at[kind], partner).start()

        by_kind(m, body)

    exchanges = (
        {"tensor": 1 - tens},
        partner,
        {"wide": me + 2 - 4 * lax.rem(chip, 2)},
        {"wide": me + 4 - 8 * (chip // 2)},
    )

    barrier = pltpu.get_barrier_semaphore()
    for dev in exchanges:
        pl.semaphore_signal(barrier, inc=1, device_id=dev, device_id_type=MESH)

    @pl.when(middle)
    def _():
        pl.semaphore_signal(barrier, inc=1, device_id=inner_of, device_id_type=MESH)

    fetch(jnp.int32(0))
    sums[:, 0:d_model] = jnp.concatenate(
        [jnp.sum(small[k], axis=0, keepdims=True) for k in range(5)]
        + [jnp.zeros((3, d_model), F32)],
        axis=0,
    )
    total = jnp.sum(biases[...], axis=0, keepdims=True)
    lines = [total[:, k * COLS : (k + 1) * COLS] for k in range(total.shape[1] // COLS)]
    lines.append(jnp.zeros((8 - len(lines), COLS), F32))
    sums[:, d_model:] = jnp.concatenate(lines, axis=0)
    pl.when(middle)(lambda: pl.semaphore_wait(barrier, len(exchanges) + 1))
    pl.when(at_end)(lambda: pl.semaphore_wait(barrier, len(exchanges)))

    def exchange_start(k):
        if k > 0:
            arrived(sums, sum_ss.at[0])
        sums_r[0] = sums[...]
        remote(sums_r.at[0], sums_r.at[k + 1], sum_ss.at[0], sum_rs.at[k], exchanges[k]).start()

    def exchange_end(k):
        arrived(sums, sum_rs.at[k])
        if k == 0:
            sums[:, 0:d_model] += sums_r[1, :, 0:d_model]
        else:
            sums[...] += sums_r[k + 1]

    def step(i, carry):
        pl.when(i + 1 < steps)(lambda: fetch(i + 1))
        pl.when(i < steps)(lambda: products(i))
        for k in range(4):
            pl.when(i == 4 * k + 2)(lambda k=k: exchange_start(k))
            pl.when(i == 4 * k + 5)(lambda k=k: exchange_end(k))

        def at(lag, allowed, body):
            m = i - lag
            pl.when((m >= 0) & (m < steps) & allowed(m))(lambda: body(m))

        at(1, lambda m: m >= 0, chip_sum)
        at(3, lambda m: middle & jnp.logical_not(is_root(m)), pass_in)
        at(5, is_root, finish)
        at(8, lambda m: middle & jnp.logical_not(is_root(m)), hand_on)
        at(10, lambda m: at_end, hand_on)
        return carry

    lax.fori_loop(0, steps + 10, step, 0)

    arrived(sums, sum_ss.at[0])
    for ring in range(RING):
        arrived(tile_ref, core_ss.at[ring])

    def drain(m, carry):
        ring = lax.rem(m, RING)
        root = is_root(m)
        last = m + RING >= steps
        pl.when(at_end & last)(lambda: arrived(tile_ref, red_ss.at[ring]))
        pl.when(middle & jnp.logical_not(root) & last)(
            lambda: arrived(tile_ref, red_ss.at[ring])
        )

        @pl.when(root & (m + 2 * TOTALS >= steps))
        def _():
            for k in range(4):
                arrived(tile_ref, tot_ss.at[k, lax.rem(m // 2, TOTALS)])

        @pl.when(middle & jnp.logical_not(root))
        def _():
            arrived(tile_ref, fwd_ss.at[m])

        pl.when(jnp.logical_not(root))(lambda: arrived(tile_ref, share_ss.at[m]))
        return carry

    lax.fori_loop(0, steps, drain, 0)
    for kind, (height, width) in enumerate(kinds):
        arrived(targets[kind].at[pl.ds(0, height // 2)], fin_rs.at[kind])


def gradient_sums(dims, operands, small, biases, collective_id):
    micro, rows, group, wide, heads, d_model, ff = dims
    inner = heads * HEAD_DIM
    kinds = gradient_kinds(d_model, inner, ff)
    steps = sum((height // TILE) * (width // (2 * TILE)) for height, width in kinds)
    count = micro * group
    anywhere = pl.BlockSpec(memory_space=pl.ANY)
    local = pl.BlockSpec(memory_space=pltpu.VMEM)
    dma = pltpu.SemaphoreType.DMA
    regular = pltpu.SemaphoreType.REGULAR
    vmem = pltpu.VMEM
    width = d_model + COLS
    return pl.pallas_call(
        functools.partial(gradient_kernel, dims),
        out_shape=[jax.ShapeDtypeStruct(kind, BF16) for kind in kinds]
        + [jax.ShapeDtypeStruct((8, width), F32)],
        in_specs=[anywhere] * 6 + [local] * 2,
        out_specs=[anywhere] * 4 + [local],
        scratch_shapes=[
            vmem((2, count, TILE), BF16),
            vmem((2, count, 2 * TILE), BF16),
            vmem((RING, TILE, TILE), F32),
            vmem((RING, TILE, TILE), BF16),
            vmem((RING, TILE, TILE), BF16),
            vmem((RING, TILE, TILE), BF16),
            vmem((RING, TILE, TILE), BF16),
            vmem((RING, TILE, TILE), BF16),
            vmem((TOTALS, TILE, TILE), BF16),
            vmem((5, 8, width), F32),
            dma((2, 2)),
            dma((RING,)),
            dma((RING,)),
            dma((RING,)),
            dma((RING,)),
            dma((RING,)),
            dma((steps,)),
            dma((4, TOTALS)),
            dma((steps,)),
            dma((steps,)),
            dma((4,)),
            dma((1,)),
            dma((4,)),
            regular,
            regular((2,)),
            regular,
        ],
        compiler_params=pltpu.CompilerParams(
            collective_id=collective_id, has_side_effects=True, vmem_limit_bytes=40 << 20
        ),
        name="gradient_sums",
    )(*operands, small, biases)


def relay_shards(
    block_input,
    doc_lengths,
    norm_gain,
    norm_bias,
    qkv_weight,
    qkv_bias,
    dense_weight,
    dense_bias,
    up_weight,
    up_bias,
    down_weight,
    down_bias,
    cotangent,
):
    weights = tuple(
        array[0]
        for array in (
            norm_gain,
            norm_bias,
            qkv_weight,
            qkv_bias,
            dense_weight,
            dense_bias,
            up_weight,
            up_bias,
            down_weight,
            down_bias,
        )
    )
    micro, rows, d_model = block_input.shape
    group = rows * lax.axis_size("tensor")
    wide = lax.axis_size("wide")
    heads = qkv_weight.shape[2] // (3 * HEAD_DIM)
    ff = up_weight.shape[2]
    dims = (micro, rows, group, wide, heads, d_model, ff)
    out, input_grad, *operands, small, bias_sums = relay(
        dims, doc_lengths, block_input, cotangent, weights, 1
    )
    up_grad, down_grad, dense_grad, qkv_grad, sums = gradient_sums(
        dims, operands, small, bias_sums, 2
    )
    up_grad, down_grad, dense_grad, qkv_grad = (
        grad.astype(F32)[None] for grad in (up_grad, down_grad, dense_grad, qkv_grad)
    )
    biases = sums[:, d_model:].reshape(1, -1)
    qkv_width = qkv_weight.shape[2]
    out_bias_grad = sums[4:5, :d_model]
    return (
        out[None],
        input_grad[None],
        sums[None, 0:2, :d_model],
        sums[None, 2:4, :d_model],
        qkv_grad,
        biases[:, :qkv_width],
        dense_grad,
        out_bias_grad,
        up_grad,
        biases[:, qkv_width : qkv_width + ff],
        down_grad,
        out_bias_grad,
    )


def shortened(shard):

    def short(part):
        return part.astype(jnp.bfloat16) if part.dtype == jnp.float32 else part

    return jax.tree.map(short, shard)


def from_behind(block, axis, distance):
    devices = range(lax.axis_size(axis))
    route = [(i - distance, i) for i in devices if i - distance in devices]
    return lax.ppermute(block, axis, route)


def norm_parts(values, gain, shift):
    center = jnp.mean(values, axis=-1, keepdims=True)
    centred = values - center
    spread = jnp.mean(centred * centred, axis=-1, keepdims=True)
    inv_scale = lax.rsqrt(spread + EPSILON)
    normed = centred * inv_scale
    return (normed * gain + shift, normed, inv_scale)


def norm_back(grad, normed, inv_scale, gain):
    scaled = grad * gain
    inner_mean = jnp.mean(scaled, axis=-1, keepdims=True)
    cross_mean = jnp.mean(scaled * normed, axis=-1, keepdims=True)
    return inv_scale * (scaled - inner_mean - normed * cross_mean)


def doc_layout(lengths, tok_index):
    ends = jnp.cumsum(lengths)
    starts = ends - lengths
    doc_ids = jnp.sum((tok_index[:, None] >= ends[None, :]).astype(jnp.int32), axis=1)
    numbers = jnp.arange(lengths.shape[0], dtype=jnp.int32)
    picked = doc_ids[:, None] == numbers[None, :]
    begins = jnp.sum(jnp.where(picked, starts[None, :], 0), axis=1)
    return (doc_ids, tok_index - begins)


def rope_tables(offsets):
    half = ROT // 2
    freqs = ROPE_BASE ** (-2.0 * jnp.arange(half, dtype=jnp.float32) / ROT)
    angle = offsets.astype(jnp.float32)[:, None] * freqs[None, :]
    return (jnp.cos(angle)[:, None, :], jnp.sin(angle)[:, None, :])


def rotate(values, cos_table, sin_table):
    half = ROT // 2
    front = values[..., :half]
    back = values[..., half:ROT]
    turned = [
        front * cos_table - back * sin_table,
        back * cos_table + front * sin_table,
        values[..., ROT:],
    ]
    return jnp.concatenate(turned, axis=-1)


def unrotate(values, cos_table, sin_table):
    half = ROT // 2
    front = values[..., :half]
    back = values[..., half:ROT]
    turned = [
        front * cos_table + back * sin_table,
        back * cos_table - front * sin_table,
        values[..., ROT:],
    ]
    return jnp.concatenate(turned, axis=-1)


def gelu_parts(pre_act):
    cumul = 0.5 * (1.0 + lax.erf(pre_act * (1.0 / math.sqrt(2.0))))
    density = jnp.exp(-0.5 * pre_act * pre_act) * (1.0 / math.sqrt(2.0 * math.pi))
    return (pre_act * cumul, cumul + pre_act * density)


def store_slot(buffer, update, slot_here, is_valid):
    previous = lax.dynamic_index_in_dim(buffer, slot_here, 0, keepdims=False)
    return lax.dynamic_update_index_in_dim(
        buffer, jnp.where(is_valid, update, previous), slot_here, 0
    )


def gather_keys(key_rows, value_rows):
    return (
        lax.all_gather(key_rows, "wide", axis=0, tiled=True),
        lax.all_gather(value_rows, "wide", axis=0, tiled=True),
    )


def forward_parts(inputs, lengths, weights, with_output):
    (
        norm_gain,
        norm_bias,
        qkv_weight,
        qkv_bias,
        dense_weight,
        dense_bias,
        up_weight,
        up_bias,
        down_weight,
        down_bias,
    ) = weights
    seq_len = SEQ
    group = inputs.shape[0] * lax.axis_size("tensor")
    head_count = qkv_weight.shape[1] // (3 * HEAD_DIM)
    factor = 1.0 / math.sqrt(HEAD_DIM)
    values = inputs.astype(jnp.float32)
    norm_first, normed_first, scale_first = norm_parts(values, norm_gain[0], norm_bias[0])
    norm_second, normed_second, scale_second = norm_parts(values, norm_gain[1], norm_bias[1])
    full_first, full_second = (
        lax.all_gather(norm_first.astype(jnp.bfloat16), "tensor", axis=0, tiled=True),
        lax.all_gather(norm_second.astype(jnp.bfloat16), "tensor", axis=0, tiled=True),
    )
    tok_index = lax.axis_index("wide") * group + jnp.arange(group, dtype=jnp.int32)
    doc_ids, offsets = doc_layout(lengths, tok_index)
    all_index = jnp.arange(seq_len, dtype=jnp.int32)
    all_docs = doc_layout(lengths, all_index)[0]
    cos_table, sin_table = rope_tables(offsets)
    packed = jnp.dot(full_first, qkv_weight, preferred_element_type=jnp.float32) + qkv_bias
    packed = packed.reshape(group, head_count, 3, HEAD_DIM)
    queries = rotate(packed[:, :, 0], cos_table, sin_table).astype(jnp.bfloat16)
    key_here = rotate(packed[:, :, 1], cos_table, sin_table).astype(jnp.bfloat16)
    value_here = packed[:, :, 2].astype(jnp.bfloat16)
    key_all, value_all = gather_keys(key_here.reshape(group, -1), value_here.reshape(group, -1))
    key_heads = key_all.reshape(seq_len, head_count, HEAD_DIM)
    value_heads = value_all.reshape(seq_len, head_count, HEAD_DIM)
    allowed = (doc_ids[:, None] == all_docs[None, :]) & (all_index[None, :] <= tok_index[:, None])
    raw_scores = jnp.einsum("qhd,khd->qhk", queries, key_heads, preferred_element_type=jnp.float32)
    scores = jnp.where(allowed[:, None, :], raw_scores * factor, -jnp.inf)
    row_max = jnp.max(scores, axis=-1, keepdims=True)
    log_total = row_max + jnp.log(jnp.sum(jnp.exp(scores - row_max), axis=-1, keepdims=True))
    attn_probs = jnp.exp(scores - log_total)
    probs_low = attn_probs.astype(jnp.bfloat16)
    mixed_out = jnp.einsum(
        "qhk,khd->qhd", probs_low, value_heads, preferred_element_type=jnp.float32
    )
    mixed_out = mixed_out.reshape(group, -1).astype(jnp.bfloat16)
    up_pre = jnp.dot(full_second, up_weight, preferred_element_type=jnp.float32) + up_bias
    up_act, gelu_slope = gelu_parts(up_pre)
    hidden = up_act.astype(jnp.bfloat16)
    output = None
    if with_output:
        partial_value = jnp.dot(mixed_out, dense_weight, preferred_element_type=jnp.float32)
        partial_value = partial_value + jnp.dot(
            hidden, down_weight, preferred_element_type=jnp.float32
        )
        branch = (
            lax.psum_scatter(
                partial_value.astype(jnp.bfloat16), "tensor", scatter_dimension=0, tiled=True
            ).astype(jnp.float32)
            + dense_bias
            + down_bias
        )
        output = (values + branch).astype(jnp.bfloat16)
    return dict(
        output=output,
        normed_first=normed_first,
        scale_first=scale_first,
        normed_second=normed_second,
        scale_second=scale_second,
        full_first=full_first,
        full_second=full_second,
        tok_index=tok_index,
        doc_ids=doc_ids,
        all_index=all_index,
        all_docs=all_docs,
        cos_table=cos_table,
        sin_table=sin_table,
        queries=queries,
        key_here=key_here,
        value_here=value_here,
        key_all=key_all,
        value_all=value_all,
        key_heads=key_heads,
        value_heads=value_heads,
        attn_probs=attn_probs,
        probs_low=probs_low,
        log_total=log_total,
        mixed_out=mixed_out,
        gelu_slope=gelu_slope,
        hidden=hidden,
    )


def backward_parts(inputs, grad_out, lengths, weights):
    (
        norm_gain,
        norm_bias,
        qkv_weight,
        qkv_bias,
        dense_weight,
        dense_bias,
        up_weight,
        up_bias,
        down_weight,
        down_bias,
    ) = weights
    parts = forward_parts(inputs, lengths, weights, False)
    seq_len = SEQ
    group = inputs.shape[0] * lax.axis_size("tensor")
    head_count = qkv_weight.shape[1] // (3 * HEAD_DIM)
    factor = 1.0 / math.sqrt(HEAD_DIM)
    cos_table = parts["cos_table"]
    sin_table = parts["sin_table"]
    grad_low = grad_out.astype(jnp.bfloat16)
    grad_rows = grad_low.astype(jnp.float32)
    grad_full = lax.all_gather(grad_low, "tensor", axis=0, tiled=True)
    dense_grad = jnp.einsum(
        "cf,cd->fd", parts["mixed_out"], grad_full, preferred_element_type=jnp.float32
    )
    down_grad = jnp.einsum(
        "cf,cd->fd", parts["hidden"], grad_full, preferred_element_type=jnp.float32
    )
    hidden_grad = jnp.einsum(
        "cd,fd->cf", grad_full, down_weight, preferred_element_type=jnp.float32
    )
    pre_grad = (hidden_grad * parts["gelu_slope"]).astype(jnp.bfloat16)
    up_grad = jnp.einsum(
        "cd,cf->df", parts["full_second"], pre_grad, preferred_element_type=jnp.float32
    )
    up_bias_grad = jnp.sum(pre_grad.astype(jnp.float32), axis=0)
    second_grad = jnp.einsum("cf,df->cd", pre_grad, up_weight, preferred_element_type=jnp.float32)
    mixed_grad = jnp.einsum(
        "cd,fd->cf", grad_full, dense_weight, preferred_element_type=jnp.float32
    )
    mixed_grad = mixed_grad.astype(jnp.bfloat16).reshape(group, head_count, HEAD_DIM)
    attn_probs = parts["attn_probs"]
    probs_grad = jnp.einsum(
        "qhd,khd->qhk", mixed_grad, parts["value_heads"], preferred_element_type=jnp.float32
    )
    inner = jnp.sum(attn_probs * probs_grad, axis=-1, keepdims=True)
    score_grad = (attn_probs * (probs_grad - inner) * factor).astype(jnp.bfloat16)
    query_grad = jnp.einsum(
        "qhk,khd->qhd", score_grad, parts["key_heads"], preferred_element_type=jnp.float32
    )
    key_sums = jnp.einsum(
        "qhk,qhd->khd", score_grad, parts["queries"], preferred_element_type=jnp.float32
    )
    value_sums = jnp.einsum(
        "qhk,qhd->khd", parts["probs_low"], mixed_grad, preferred_element_type=jnp.float32
    )
    key_flat, value_flat = (
        lax.psum_scatter(
            key_sums.reshape(seq_len, -1).astype(jnp.bfloat16),
            "wide",
            scatter_dimension=0,
            tiled=True,
        ).astype(jnp.float32),
        lax.psum_scatter(
            value_sums.reshape(seq_len, -1).astype(jnp.bfloat16),
            "wide",
            scatter_dimension=0,
            tiled=True,
        ).astype(jnp.float32),
    )
    key_grad = key_flat.reshape(group, head_count, HEAD_DIM)
    value_grad = value_flat.reshape(group, head_count, HEAD_DIM)
    query_back = unrotate(query_grad, cos_table, sin_table)
    key_back = unrotate(key_grad, cos_table, sin_table)
    packed_grad = (
        jnp.stack([query_back, key_back, value_grad], axis=2)
        .reshape(group, -1)
        .astype(jnp.bfloat16)
    )
    qkv_grad = jnp.einsum(
        "cd,cf->df", parts["full_first"], packed_grad, preferred_element_type=jnp.float32
    )
    qkv_bias_grad = jnp.sum(packed_grad.astype(jnp.float32), axis=0)
    first_grad = jnp.einsum(
        "cf,df->cd", packed_grad, qkv_weight, preferred_element_type=jnp.float32
    )
    norm_first_grad, norm_second_grad = (
        lax.psum_scatter(
            first_grad.astype(jnp.bfloat16), "tensor", scatter_dimension=0, tiled=True
        ).astype(jnp.float32),
        lax.psum_scatter(
            second_grad.astype(jnp.bfloat16), "tensor", scatter_dimension=0, tiled=True
        ).astype(jnp.float32),
    )
    gain_grad = jnp.stack(
        [
            jnp.sum(norm_first_grad * parts["normed_first"], axis=0),
            jnp.sum(norm_second_grad * parts["normed_second"], axis=0),
        ]
    )
    shift_grad = jnp.stack([jnp.sum(norm_first_grad, axis=0), jnp.sum(norm_second_grad, axis=0)])
    input_grad = grad_out + norm_back(
        norm_first_grad, parts["normed_first"], parts["scale_first"], norm_gain[0]
    )
    input_grad = input_grad + norm_back(
        norm_second_grad, parts["normed_second"], parts["scale_second"], norm_gain[1]
    )
    bias_rows = jnp.sum(grad_rows, axis=0)
    terms = (
        gain_grad,
        shift_grad,
        qkv_grad,
        qkv_bias_grad,
        dense_grad,
        bias_rows,
        up_grad,
        up_bias_grad,
        down_grad,
        bias_rows,
    )
    return (input_grad, terms)


def general_shards(
    block_input,
    doc_lengths,
    norm_gain,
    norm_bias,
    qkv_weight,
    qkv_bias,
    dense_weight,
    dense_bias,
    up_weight,
    up_bias,
    down_weight,
    down_bias,
    cotangent,
):
    weights = (
        norm_gain[0],
        norm_bias[0],
        qkv_weight[0],
        qkv_bias[0],
        dense_weight[0],
        dense_bias[0],
        up_weight[0],
        up_bias[0],
        down_weight[0],
        down_bias[0],
    )
    section_index = lax.axis_index("section")
    last_section = lax.axis_size("section") - 1
    micro_count = block_input.shape[0]
    row_count = block_input.shape[1]
    tick_count = micro_count + last_section

    def forward_tick(carry, tick_index):
        incoming, kept_inputs, outputs, kept_pairs = carry
        slot_raw = tick_index - section_index
        is_valid = (slot_raw >= 0) & (slot_raw < micro_count)
        slot_here = jnp.clip(slot_raw, 0, micro_count - 1)
        fresh = lax.dynamic_index_in_dim(
            block_input, jnp.clip(tick_index, 0, micro_count - 1), 0, keepdims=False
        )
        inputs = jnp.where(section_index == 0, fresh, incoming)
        lengths = lax.dynamic_index_in_dim(doc_lengths, slot_here, 0, keepdims=False)
        parts = forward_parts(inputs, lengths, weights, True)
        output = parts["output"]
        kept_inputs = store_slot(kept_inputs, inputs, slot_here, is_valid)
        outputs = store_slot(outputs, output, slot_here, is_valid)
        incoming = jax.tree.map(
            lambda part, own: part.astype(own.dtype),
            from_behind(shortened(output), "section", 1),
            output,
        )
        return ((incoming, kept_inputs, outputs, kept_pairs), None)

    pair_init = (jnp.zeros((1,), jnp.bfloat16), jnp.zeros((1,), jnp.bfloat16))
    zero_rows = jnp.zeros((row_count, block_input.shape[2]), jnp.bfloat16)
    zero_stack = jnp.zeros(block_input.shape, jnp.bfloat16)
    forward_init = (zero_rows, zero_stack, zero_stack, pair_init)
    forward_done = lax.scan(forward_tick, forward_init, jnp.arange(tick_count, dtype=jnp.int32))[0]
    kept_inputs = forward_done[1]
    outputs = forward_done[2]
    kept_pairs = forward_done[3]

    def add_masked(total, term, scale_mask):
        return total + scale_mask * term

    def backward_tick(carry, tick_index):
        incoming, grads, input_grads = carry
        slot_raw = tick_index - (last_section - section_index)
        is_valid = (slot_raw >= 0) & (slot_raw < micro_count)
        slot_here = jnp.clip(slot_raw, 0, micro_count - 1)
        top_grad = lax.dynamic_index_in_dim(cotangent, slot_here, 0, keepdims=False)
        grad_out = jnp.where(section_index == last_section, top_grad, incoming)
        inputs = lax.dynamic_index_in_dim(kept_inputs, slot_here, 0, keepdims=False)
        lengths = lax.dynamic_index_in_dim(doc_lengths, slot_here, 0, keepdims=False)
        input_grad, terms = backward_parts(inputs, grad_out, lengths, weights)
        scale_mask = is_valid.astype(jnp.float32)
        grads = tuple((add_masked(total, term, scale_mask) for total, term in zip(grads, terms)))
        input_grads = store_slot(input_grads, input_grad, slot_here, is_valid)
        incoming = from_behind(shortened(input_grad), "section", -1).astype(input_grad.dtype)
        return ((incoming, grads, input_grads), None)

    grad_init = tuple((jnp.zeros(weight.shape, jnp.float32) for weight in weights))
    backward_init = (
        jnp.zeros((row_count, block_input.shape[2]), jnp.float32),
        grad_init,
        jnp.zeros(block_input.shape, jnp.float32),
    )
    backward_done = lax.scan(backward_tick, backward_init, jnp.arange(tick_count, dtype=jnp.int32))[
        0
    ]
    grads = backward_done[1]
    input_grads = backward_done[2]
    wide_sums = (
        lax.psum(grads[2].astype(jnp.bfloat16), "wide").astype(jnp.float32),
        lax.psum(grads[3].astype(jnp.bfloat16), "wide").astype(jnp.float32),
        lax.psum(grads[4].astype(jnp.bfloat16), "wide").astype(jnp.float32),
        lax.psum(grads[6].astype(jnp.bfloat16), "wide").astype(jnp.float32),
        lax.psum(grads[7].astype(jnp.bfloat16), "wide").astype(jnp.float32),
        lax.psum(grads[8].astype(jnp.bfloat16), "wide").astype(jnp.float32),
    )
    shared = lax.psum((grads[0], grads[1], grads[5], grads[9]), ("tensor", "wide"))
    return (
        outputs[None],
        input_grads[None],
        shared[0][None],
        shared[1][None],
        wide_sums[0][None],
        wide_sums[1][None],
        wide_sums[2][None],
        shared[2][None],
        wide_sums[3][None],
        wide_sums[4][None],
        wide_sums[5][None],
        shared[3][None],
    )


def solution(mesh):
    placed = (
        P(None, ("wide", "tensor"), None),
        P(),
        P("section", None, None),
        P("section", None, None),
        P("section", None, "tensor"),
        P("section", "tensor"),
        P("section", "tensor", None),
        P("section", None),
        P("section", None, "tensor"),
        P("section", "tensor"),
        P("section", "tensor", None),
        P("section", None),
        P(None, ("wide", "tensor"), None),
    )
    results = (
        P("section", None, ("wide", "tensor"), None),
        P("section", None, ("wide", "tensor"), None),
        P("section", None, None),
        P("section", None, None),
        P("section", None, "tensor"),
        P("section", "tensor"),
        P("section", "tensor", None),
        P("section", None),
        P("section", None, "tensor"),
        P("section", "tensor"),
        P("section", "tensor", None),
        P("section", None),
    )

    def program(*args):
        heads = args[4].shape[2] // (3 * HEAD_DIM * mesh.shape["tensor"])
        one_head_each = heads == mesh.shape["wide"] and heads % 2 == 0
        two_by_two = mesh.shape["section"] == 2 and mesh.shape["tensor"] == 2
        body = relay_shards if one_head_each and two_by_two else general_shards
        return jax.shard_map(
            body, mesh=mesh, in_specs=placed, out_specs=results, check_vma=False
        )(*args)

    return program
```

```python
import functools
import math

import jax
import jax.numpy as jnp
from jax import lax
from jax.experimental import pallas as pl
from jax.experimental.pallas import tpu as pltpu
from jax.sharding import PartitionSpec as P

HEAD_DIM = 64
ROT = 16
SEQ = 2048


EPSILON = 1e-05
ROPE_BASE = 10000.0

MESH = pl.DeviceIdType.MESH
F32 = jnp.float32
BF16 = jnp.bfloat16
LANES = 128
BLOCK = 512
COLS = 512
NEG = -1e30
SCORE_SCALE = math.log2(math.e) / math.sqrt(HEAD_DIM)


TILE = 256
ACROSS = 256
AHEAD = 3
RING = 8
TOTALS = 8
LAGS = (1, 3, 5, 8, 10)
EARLY = 16


def gradient_kinds(d_model, inner, ff):
    return ((d_model, ff), (ff, d_model), (inner, d_model), (d_model, 3 * inner))


def dot(a, b):
    return jnp.dot(a, b, preferred_element_type=F32)


def dot_t(a, b):
    return lax.dot_general(a, b, (((1,), (1,)), ((), ())), preferred_element_type=F32)


def t_dot(a, b):
    return lax.dot_general(a, b, (((0,), (0,)), ((), ())), preferred_element_type=F32)


def lane_low(rows):
    return lax.broadcasted_iota(jnp.int32, (rows, LANES), 1) < HEAD_DIM


def turn(values):
    return pltpu.roll(values, HEAD_DIM, 1)


def rotary(values, cos_ref, front_ref, back_ref, seq, sign):
    cos, front, back = cos_ref[seq], front_ref[seq], back_ref[seq]
    ahead = pltpu.roll(values, LANES - ROT // 2, 1)
    behind = pltpu.roll(values, ROT // 2, 1)
    return values * cos + sign * (ahead * front + behind * back)


def pair_up(first, second, low):
    return jnp.where(low, first, turn(second)), jnp.where(low, turn(first), second)


def relay_kernel(
    dims,
    lengths,
    x_hbm,
    cot_hbm,
    gain,
    shift,
    qkv_b,
    up_b,
    dense_b,
    down_b,
    wqkv_hbm,
    wdense_hbm,
    wup_hbm,
    wdown_hbm,
    out_hbm,
    ig_hbm,
    norm_hbm,
    g_hbm,
    mixed_hbm,
    hid_hbm,
    dpre_hbm,
    dpk_hbm,
    up_out,
    down_out,
    dense_out,
    qkv_out,
    sums,
    small,
    bias_sums,
    cos,
    front,
    back,
    wqkv,
    wdense,
    wup,
    wdown,
    xfull,
    gfull,
    cot,
    qkv_r,
    mix_r,
    do_r,
    dqkv_r,
    rsf_r,
    rsb_r,
    qkv_st,
    o_st,
    do_st,
    dqkv_st,
    rsf_st,
    rsb_st,
    out_st,
    gx_st,
    ig_st,
    norm_st,
    mixed_st,
    hid_st,
    dpre_st,
    dpk_st,
    slope,
    part,
    part_b,
    dn1,
    qm,
    kr,
    vx,
    dox,
    dq,
    lse,
    delta,
    scores,
    peak,
    acc,
    wsem,
    ownx_sem,
    yx_s,
    yx_r,
    owng_sem,
    yg_s,
    yg_r,
    qkv_ss,
    qkv_rs,
    o_ss,
    o_rs,
    do_ss,
    do_rs,
    dqkv_ss,
    dqkv_rs,
    rsf_ss,
    rsf_rs,
    rsb_ss,
    rsb_rs,
    xs_ss,
    gs_ss,
    store_sem,
    g_store,
    core_r,
    outer_r,
    inner_r,
    sums_r,
    op_sem,
    core_ss,
    core_rs,
    outer_rs,
    inner_rs,
    red_ss,
    bc_rs,
    tot_ss,
    fwd_ss,
    share_ss,
    fin_rs,
    sum_ss,
    sum_rs,
    core_free,
    outer_free,
    inner_free,
):
    micro, rows, group, wide, heads, d_model, ff = dims
    sect = lax.axis_index("section")
    tens = lax.axis_index("tensor")
    me = lax.axis_index("wide")
    pairs = heads // 2
    per_source = group + group // 2
    half = group // 2
    q_blocks = SEQ // BLOCK
    sources = BLOCK // group
    my_rows = pl.ds(pl.multiple_of(tens * rows, rows), rows)
    his_rows = pl.ds(pl.multiple_of((1 - tens) * rows, rows), rows)
    x_dev = {"section": 1 - sect}
    y_dev = {"tensor": 1 - tens}
    low_half = lane_low(half)
    low_group = lane_low(group)

    def remote(src, dst, ss, rs, dev):
        return pltpu.make_async_remote_copy(
            src_ref=src, dst_ref=dst, send_sem=ss, recv_sem=rs, device_id=dev, device_id_type=MESH
        )

    def arrived(ref, sem):
        pltpu.make_async_copy(ref, ref, sem).wait()

    def tokens_of(s):
        return pl.ds(pl.multiple_of(s * group, group), group)

    def y_send_x(s):
        own = xfull.at[s, my_rows]
        return remote(own, own, yx_s.at[s], yx_r.at[s], y_dev)

    def y_send_g(s):
        own = gfull.at[s, my_rows]
        return remote(own, own, yg_s.at[s], yg_r.at[s], y_dev)

    def spread(stage, target, seq, dest, ss, rs):
        @pl.when(dest == me)
        def _():
            pltpu.make_async_copy(stage, target.at[seq, me], rs).start()

        @pl.when(dest != me)
        def _():
            remote(stage, target.at[seq, me], ss, rs, {"wide": dest}).start()

    loads = [
        pltpu.make_async_copy(source, target, wsem.at[i])
        for i, (source, target) in enumerate(
            ((wqkv_hbm, wqkv), (wup_hbm, wup), (wdown_hbm, wdown), (wdense_hbm, wdense))
        )
    ]

    barrier = pltpu.get_barrier_semaphore()
    for dev in [x_dev, y_dev] + [{"wide": lax.rem(me + k, wide)} for k in range(1, wide)]:
        pl.semaphore_signal(barrier, inc=1, device_id=dev, device_id_type=MESH)

    @pl.when(sect == 0)
    def _():
        for s in range(micro):
            pltpu.make_async_copy(x_hbm.at[s], xfull.at[s, my_rows], ownx_sem.at[s]).start()

    for load in loads:
        load.start()

    @pl.when(sect == 1)
    def _():
        for s in range(micro):
            pltpu.make_async_copy(cot_hbm.at[s], cot.at[s], owng_sem.at[s]).start()

    def starts_of(s, tokens):
        found = jnp.zeros_like(tokens)
        end = jnp.int32(0)
        for j in range(lengths.shape[1]):
            end = end + lengths[s, j]
            found = jnp.where(tokens >= end, end, found)
        return found

    lane = lax.rem(lax.broadcasted_iota(jnp.int32, (8, LANES), 1), HEAD_DIM)
    number = lax.rem(lane, ROT // 2)
    freq = jnp.zeros((8, LANES), F32)
    for k in range(ROT // 2):
        freq = jnp.where(number == k, ROPE_BASE ** (-2.0 * k / ROT), freq)
    lane, freq = lane[0:1, :], freq[0:1, :]

    def table_step(s, carry):
        tokens = me * group + lax.broadcasted_iota(jnp.int32, (group, LANES), 0)
        angle = (tokens - starts_of(s, tokens)).astype(F32) * freq
        sine = jnp.sin(angle)
        cos[s] = jnp.where(lane < ROT, jnp.cos(angle), 1.0)
        front[s] = jnp.where(lane < ROT // 2, -sine, 0.0)
        back[s] = jnp.where((lane >= ROT // 2) & (lane < ROT), sine, 0.0)
        return carry

    lax.fori_loop(0, micro, table_step, 0)
    small[...] = jnp.zeros_like(small)
    bias_sums[...] = jnp.zeros_like(bias_sums)
    pl.semaphore_wait(barrier, wide + 1)

    @pl.when(sect == 0)
    def _():
        for s in range(micro):
            arrived(xfull.at[s, my_rows], ownx_sem.at[s])
            y_send_x(s).start()

    @pl.when(sect == 1)
    def _():
        for s in range(micro):
            arrived(cot.at[s], owng_sem.at[s])

            def chunk(i, carry, s=s):
                at = pl.ds(pl.multiple_of(i * 32, 32), 32)
                there = pl.ds(pl.multiple_of(tens * rows + i * 32, 32), 32)
                gfull[s, there, :] = cot[s, at, :].astype(BF16)
                return carry

            lax.fori_loop(0, rows // 32, chunk, 0)
            y_send_g(s).start()

    def fold(values):
        total = values[0:8]
        for k in range(1, values.shape[0] // 8):
            total = total + values[k * 8 : (k + 1) * 8]
        return total

    def normed_rows(values):
        center = jnp.mean(values, axis=-1, keepdims=True)
        centred = values - center
        spread_of = jnp.mean(centred * centred, axis=-1, keepdims=True)
        inv = lax.rsqrt(spread_of + EPSILON)
        return centred * inv, inv

    def unpack_heads(s):
        def step(src, carry):
            qk = qkv_r[s, src, 0:group, :].astype(F32)
            at = pl.multiple_of(src * group, group)
            qm[pl.ds(at, group), :] = jnp.where(low_group, qk, 0.0).astype(BF16)
            kr[pl.ds(at, group), :] = turn(qk).astype(BF16)
            packed_v = qkv_r[s, src, group:per_source, :].astype(F32)
            ones = jnp.where(
                lax.broadcasted_iota(jnp.int32, (half, LANES), 1) == HEAD_DIM, 1.0, 0.0
            )
            vx[pl.ds(at, half), :] = jnp.where(low_half, packed_v, ones).astype(BF16)
            vx[pl.ds(pl.multiple_of(at + half, half), half), :] = jnp.where(
                low_half, turn(packed_v), ones
            ).astype(BF16)
            return carry

        lax.fori_loop(0, wide, step, 0, unroll=True)

    def forward_meet(s):
        arrived(xfull.at[s, my_rows], ownx_sem.at[s])
        y_send_x(s).start()

    def backward_meet(s):
        arrived(gfull.at[s, my_rows], owng_sem.at[s])
        y_send_g(s).start()

    def forward(s):
        arrived(xfull.at[s, his_rows], yx_r.at[s])

        def norm_step(i, carry):
            at = pl.ds(pl.multiple_of(i * 32, 32), 32)
            a, _ = normed_rows(xfull[s, at, :].astype(F32))
            norm_st[0, at, :] = (a * gain[0:1, :] + shift[0:1, :]).astype(BF16)
            norm_st[1, at, :] = (a * gain[1:2, :] + shift[1:2, :]).astype(BF16)
            return carry

        @pl.when(s > 0)
        def _():
            arrived(norm_st.at[0], store_sem.at[0])
            arrived(norm_st.at[1], store_sem.at[1])

        lax.fori_loop(0, group // 32, norm_step, 0, unroll=True)
        pltpu.make_async_copy(norm_st.at[0], norm_hbm.at[0, tokens_of(s)], store_sem.at[0]).start()
        pltpu.make_async_copy(norm_st.at[1], norm_hbm.at[1, tokens_of(s)], store_sem.at[1]).start()

        def qkv_step(k, carry):
            pair = lax.rem(me // 2 + 1 + k, pairs)
            cols = pl.ds(pl.multiple_of(pair * 3 * LANES, LANES), 3 * LANES)
            packed = dot(norm_st[0], wqkv[:, cols]) + qkv_b[:, cols]
            first, middle, last = (packed[:, i * LANES : (i + 1) * LANES] for i in range(3))
            qk0 = rotary(first, cos, front, back, s, 1.0)
            qk1 = rotary(
                turn(jnp.where(low_group, last, middle)), cos, front, back, s, 1.0
            )
            vv = jnp.where(low_group, middle, last)
            v0 = jnp.where(low_half, vv[:half], turn(vv[half:]))
            v1 = jnp.where(low_half, turn(vv[:half]), vv[half:])
            for i, (qk, v) in enumerate(((qk0, v0), (qk1, v1))):
                qkv_st[2 * pair + i, 0:group, :] = qk.astype(BF16)
                qkv_st[2 * pair + i, group:per_source, :] = v.astype(BF16)
            for i in range(2):
                dest = 2 * pair + i
                spread(qkv_st.at[dest], qkv_r, s, dest, qkv_ss.at[0], qkv_rs.at[s])
            return carry

        pl.when(s == 0)(loads[0].wait)
        lax.fori_loop(0, pairs, qkv_step, 0, unroll=True)

    def forward_ff(s):
        @pl.when(s == 0)
        def _():
            loads[1].wait()
            loads[2].wait()

        @pl.when(s > 0)
        def _():
            arrived(hid_st, store_sem.at[2])

        def ff_step(j, carry):
            cols = pl.ds(pl.multiple_of(j * COLS, COLS), COLS)
            pre = dot(norm_st[1], wup[:, cols]) + up_b[:, cols]
            cumul = 0.5 * (1.0 + lax.erf(pre * (1.0 / math.sqrt(2.0))))
            density = jnp.exp(-0.5 * pre * pre) * (1.0 / math.sqrt(2.0 * math.pi))
            hid = (pre * cumul).astype(BF16)
            hid_st[:, cols] = hid
            slope[s, :, cols] = (cumul + pre * density).astype(BF16)
            term = dot(hid, wdown[cols, :])

            @pl.when(j == 0)
            def _():
                part[...] = term

            @pl.when(j > 0)
            def _():
                part[...] += term

            return carry

        lax.fori_loop(0, ff // COLS, ff_step, 0, unroll=True)
        pltpu.make_async_copy(hid_st, hid_hbm.at[tokens_of(s)], store_sem.at[2]).start()

    def forward_attention(s):
        arrived(qkv_r.at[s], qkv_rs.at[s])
        arrived(qkv_st.at[pl.ds(0, wide - 1)], qkv_ss.at[0])
        unpack_heads(s)

        for i in range(q_blocks):
            q_at = slice(i * BLOCK, (i + 1) * BLOCK)
            tokens = i * BLOCK + lax.broadcasted_iota(jnp.int32, (BLOCK, LANES), 0)
            begin = starts_of(s, tokens)[:, 0:1]
            best = jnp.full((BLOCK, LANES), NEG, F32)
            for j in range(i + 1):
                k_at = slice(j * BLOCK, (j + 1) * BLOCK)
                raw = dot_t(qm[q_at, :], kr[k_at, :])
                u = j * BLOCK + lax.broadcasted_iota(jnp.int32, (BLOCK, BLOCK), 1)
                seen = u >= begin
                if i == j:
                    seen = seen & (u <= tokens[:, 0:1])
                raw = jnp.where(seen, raw, NEG)
                scores[:, k_at] = raw
                for k in range(BLOCK // LANES):
                    best = jnp.maximum(best, raw[:, k * LANES : (k + 1) * LANES])
            top = jnp.max(best, axis=1, keepdims=True) * SCORE_SCALE
            out = jnp.zeros((BLOCK, LANES), F32)
            for j in range(i + 1):
                k_at = slice(j * BLOCK, (j + 1) * BLOCK)
                probs = jnp.exp2(scores[:, k_at] * SCORE_SCALE - top)
                out = out + dot(probs.astype(BF16), vx[k_at, :])
            total = out[:, HEAD_DIM : HEAD_DIM + 1]
            out = out / total
            log_total = top + jnp.log2(total)
            lse[s, i] = jnp.broadcast_to(log_total, (BLOCK, LANES)).T[0:8, :]
            for k in range(sources):
                first = out[k * group : k * group + half]
                second = out[k * group + half : (k + 1) * group]
                source = i * sources + k
                o_st[s, source] = jnp.where(low_half, first, turn(second)).astype(BF16)
                spread(o_st.at[s, source], mix_r, s, source, o_ss.at[s], o_rs.at[s])

    def forward_out(s):
        arrived(mix_r.at[s], o_rs.at[s])
        arrived(o_st.at[s, pl.ds(0, wide - 1)], o_ss.at[s])
        pl.when((s == 0) & (sect == 0))(loads[3].wait)
        pl.when(s > 0)(lambda: arrived(mixed_st, store_sem.at[3]))
        for pair in range(pairs):
            top, bottom = pair_up(
                mix_r[s, 2 * pair].astype(F32), mix_r[s, 2 * pair + 1].astype(F32), low_half
            )
            mixed_st[0:half, pair * LANES : (pair + 1) * LANES] = top.astype(BF16)
            mixed_st[half:group, pair * LANES : (pair + 1) * LANES] = bottom.astype(BF16)
        pltpu.make_async_copy(mixed_st, mixed_hbm.at[tokens_of(s)], store_sem.at[3]).start()
        part[...] += dot(mixed_st[...], wdense[...])
        rsf_st[...] = part[his_rows, :].astype(BF16)
        remote(rsf_st, rsf_r.at[s], rsf_ss.at[0], rsf_rs.at[s], y_dev).start()

    def forward_end(s):
        arrived(rsf_r.at[s], rsf_rs.at[s])
        arrived(rsf_st, rsf_ss.at[0])

        @pl.when(s > 0)
        def _():
            arrived(out_st, store_sem.at[4])
            pl.when(sect == 0)(lambda: arrived(out_st, xs_ss.at[0]))

        def out_step(i, carry):
            at = pl.ds(pl.multiple_of(i * 32, 32), 32)
            there = pl.ds(pl.multiple_of(tens * rows + i * 32, 32), 32)
            branch = part[there, :] + rsf_r[s, at, :].astype(F32) + (dense_b[...] + down_b[...])
            out_st[at, :] = (xfull[s, there, :].astype(F32) + branch).astype(BF16)
            return carry

        lax.fori_loop(0, rows // 32, out_step, 0, unroll=True)

        @pl.when(sect == 0)
        def _():
            remote(out_st, xfull.at[s, my_rows], xs_ss.at[0], ownx_sem.at[s], x_dev).start()

        pltpu.make_async_copy(out_st, out_hbm.at[s], store_sem.at[4]).start()

    def backward(s):
        arrived(gfull.at[s, his_rows], yg_r.at[s])
        pl.when((s == 0) & (sect == 1))(loads[3].wait)
        pltpu.make_async_copy(gfull.at[s], g_hbm.at[tokens_of(s)], g_store.at[s]).start()

        def mixed_step(k, carry):
            pair = lax.rem(me // 2 + 1 + k, pairs)
            at = pl.ds(pl.multiple_of(pair * LANES, LANES), LANES)
            both = dot_t(gfull[s], wdense[at, :])
            first = jnp.where(low_half, both[:half], turn(both[half:]))
            second = jnp.where(low_half, turn(both[:half]), both[half:])
            do_st[s, 2 * pair] = first.astype(BF16)
            do_st[s, 2 * pair + 1] = second.astype(BF16)
            for i in range(2):
                dest = 2 * pair + i
                spread(do_st.at[s, dest], do_r, s, dest, do_ss.at[s], do_rs.at[s])
            return carry

        lax.fori_loop(0, pairs, mixed_step, 0, unroll=True)

    def backward_ff(s):
        pl.when(s > 0)(lambda: arrived(dpre_st, store_sem.at[6]))

        def ff_step(j, carry):
            cols = pl.ds(pl.multiple_of(j * COLS, COLS), COLS)
            grad = dot_t(gfull[s], wdown[cols, :])
            grad = (grad * slope[s, :, cols].astype(F32)).astype(BF16)
            dpre_st[:, cols] = grad
            sums_at = pl.ds(pl.multiple_of(3 * heads * HEAD_DIM + j * COLS, COLS), COLS)
            bias_sums[:, sums_at] += fold(grad.astype(F32))
            term = dot_t(grad, wup[:, cols])

            @pl.when(j == 0)
            def _():
                dn1[...] = term

            @pl.when(j > 0)
            def _():
                dn1[...] += term

            return carry

        lax.fori_loop(0, ff // COLS, ff_step, 0, unroll=True)
        pltpu.make_async_copy(dpre_st, dpre_hbm.at[tokens_of(s)], store_sem.at[6]).start()

    def backward_attention(s):
        arrived(do_r.at[s], do_rs.at[s])
        arrived(do_st.at[s, pl.ds(0, wide - 1)], do_ss.at[s])
        pl.when(sect == 0)(lambda: unpack_heads(s))

        def unpack_step(src, carry):
            at = pl.multiple_of(src * group, group)
            grad = do_r[s, src].astype(F32)
            dox[pl.ds(at, half), :] = jnp.where(low_half, grad, 0.0).astype(BF16)
            dox[pl.ds(pl.multiple_of(at + half, half), half), :] = jnp.where(
                low_half, turn(grad), 0.0
            ).astype(BF16)
            product = grad * o_st[s, src].astype(F32)
            left = jnp.sum(jnp.where(low_half, product, 0.0), axis=1, keepdims=True)
            right = jnp.sum(jnp.where(low_half, 0.0, product), axis=1, keepdims=True)
            delta[src, :, 0:half] = jnp.broadcast_to(left, (half, LANES)).T[0:8, :]
            delta[src, :, half:group] = jnp.broadcast_to(right, (half, LANES)).T[0:8, :]
            return carry

        lax.fori_loop(0, wide, unpack_step, 0, unroll=True)
        slot = lax.rem(s, 2)
        rows_of = []
        for i in range(q_blocks):
            tokens = i * BLOCK + lax.broadcasted_iota(jnp.int32, (8, BLOCK), 1)
            inner_sum = jnp.concatenate(
                [delta[i * sources + k, 0:1, :] for k in range(sources)], axis=1
            )
            rows_of.append((starts_of(s, tokens)[0:1, :], tokens[0:1, :], inner_sum))
        for j in range(q_blocks):
            k_at = slice(j * BLOCK, (j + 1) * BLOCK)
            for i in range(j, q_blocks):
                q_at = slice(i * BLOCK, (i + 1) * BLOCK)
                begin, token, inner_sum = rows_of[i]
                raw = dot_t(kr[k_at, :], qm[q_at, :])
                u = j * BLOCK + lax.broadcasted_iota(jnp.int32, (BLOCK, BLOCK), 0)
                probs = jnp.exp2(raw * SCORE_SCALE - lse[s, i, 0:1, :])
                seen = u >= begin
                if i == j:
                    seen = seen & (u <= token)
                probs = jnp.where(seen, probs, 0.0)
                probs_grad = dot_t(vx[k_at, :], dox[q_at, :])
                score_grad = (probs * (probs_grad - inner_sum)).astype(BF16)
                value_term = dot(probs.astype(BF16), dox[q_at, :])
                key_term = dot(score_grad, kr[q_at, :])
                query_term = t_dot(score_grad, kr[k_at, :])
                if i == j:
                    acc[...] = value_term
                    peak[...] = key_term
                else:
                    acc[...] += value_term
                    peak[...] += key_term
                if j == 0:
                    dq[q_at, :] = query_term
                else:
                    dq[q_at, :] += query_term
            for k in range(sources):
                source = j * sources + k
                mine = slice(k * group, (k + 1) * group)
                at = slice(source * group, (source + 1) * group)
                both = jnp.where(low_group, dq[at, :], peak[mine, :])
                both = both * (1.0 / math.sqrt(HEAD_DIM))
                value = acc[mine, :]
                value = jnp.where(low_half, value[:half], turn(value[half:]))
                dqkv_st[slot, source, 0:group, :] = both.astype(BF16)
                dqkv_st[slot, source, group:per_source, :] = value.astype(BF16)
                spread(
                    dqkv_st.at[slot, source], dqkv_r, s, source, dqkv_ss.at[slot], dqkv_rs.at[s]
                )

    def backward_norm(s):
        arrived(dqkv_r.at[s], dqkv_rs.at[s])
        slot = lax.rem(s, 2)
        arrived(dqkv_st.at[slot, pl.ds(0, wide - 1)], dqkv_ss.at[slot])
        pl.when(s > 0)(lambda: arrived(dpk_st, store_sem.at[7]))

        def pair_step(pair, carry):
            qk0 = rotary(
                dqkv_r[s, 2 * pair, 0:group, :].astype(F32), cos, front, back, s, -1.0
            )
            qk1 = turn(
                rotary(
                    dqkv_r[s, 2 * pair + 1, 0:group, :].astype(F32), cos, front, back, s, -1.0
                )
            )
            top, bottom = pair_up(
                dqkv_r[s, 2 * pair, group:per_source, :].astype(F32),
                dqkv_r[s, 2 * pair + 1, group:per_source, :].astype(F32),
                low_half,
            )
            vv = jnp.concatenate([top, bottom], axis=0)
            columns = (qk0, jnp.where(low_group, vv, qk1), jnp.where(low_group, qk1, vv))
            for k, column in enumerate(columns):
                at = pl.ds(pl.multiple_of((pair * 3 + k) * LANES, LANES), LANES)
                column = column.astype(BF16)
                dpk_st[:, at] = column
                bias_sums[:, at] += fold(column.astype(F32))
            return carry

        lax.fori_loop(0, pairs, pair_step, 0, unroll=True)
        pltpu.make_async_copy(dpk_st, dpk_hbm.at[tokens_of(s)], store_sem.at[7]).start()
        part_b[...] = dot_t(dpk_st[...], wqkv[...])

        def e_step(i, carry):
            at = pl.ds(pl.multiple_of(i * 32, 32), 32)
            a, _ = normed_rows(xfull[s, at, :].astype(F32))
            first = part_b[at, :]
            second = dn1[at, :]
            small[0] += fold(first * a)
            small[1] += fold(second * a)
            small[2] += fold(first)
            small[3] += fold(second)
            part_b[at, :] = first * gain[0:1, :] + second * gain[1:2, :]
            return carry

        lax.fori_loop(0, group // 32, e_step, 0, unroll=True)
        rsb_st[...] = part_b[his_rows, :].astype(BF16)
        remote(rsb_st, rsb_r.at[s], rsb_ss.at[0], rsb_rs.at[s], y_dev).start()

    def backward_end(s):
        arrived(rsb_r.at[s], rsb_rs.at[s])
        arrived(rsb_st, rsb_ss.at[0])

        @pl.when(s > 0)
        def _():
            arrived(ig_st, store_sem.at[8])
            pl.when(sect == 1)(lambda: arrived(gx_st, gs_ss.at[0]))

        def in_step(i, carry):
            at = pl.ds(pl.multiple_of(i * 32, 32), 32)
            there = pl.ds(pl.multiple_of(tens * rows + i * 32, 32), 32)
            a, inv = normed_rows(xfull[s, there, :].astype(F32))
            e = part_b[there, :] + rsb_r[s, at, :].astype(F32)
            mean_e = jnp.mean(e, axis=-1, keepdims=True)
            cross = jnp.mean(e * a, axis=-1, keepdims=True)
            g_low = gfull[s, there, :].astype(F32)
            small[4] += fold(g_low)
            g = jnp.where(sect == 1, cot[s, at, :], g_low)
            grad = g + inv * (e - mean_e - a * cross)
            ig_st[at, :] = grad
            gx_st[at, :] = grad.astype(BF16)
            return carry

        lax.fori_loop(0, rows // 32, in_step, 0, unroll=True)

        @pl.when(sect == 1)
        def _():
            remote(gx_st, gfull.at[s, my_rows], gs_ss.at[0], owng_sem.at[s], x_dev).start()

        pltpu.make_async_copy(ig_st, ig_hbm.at[s], store_sem.at[8]).start()

    chip, core = me // 2, lax.rem(me, 2)
    partner = {"wide": me + 1 - 2 * core}
    up_dev = {"wide": lax.rem(me + 2, wide)}
    down_dev = {"wide": lax.rem(me + wide - 2, wide)}
    at_bottom, at_top = chip == 0, chip == wide // 2 - 1
    at_end = at_bottom | at_top
    middle = jnp.logical_not(at_end)
    lower = chip == 1
    outer_of = {"wide": jnp.where(lower, me - 2, lax.rem(me + 2, wide))}
    inner_of = {"wide": jnp.where(lower, me + 2, lax.rem(me + wide - 2, wide))}
    end_of = {"wide": jnp.where(at_bottom, me + 2, lax.rem(me + wide - 2, wide))}
    kinds = gradient_kinds(d_model, heads * HEAD_DIM, ff)
    targets = (up_out, down_out, dense_out, qkv_out)
    operands = (
        (norm_hbm.at[1], dpre_hbm),
        (hid_hbm, g_hbm),
        (mixed_hbm, g_hbm),
        (norm_hbm.at[0], dpk_hbm),
    )
    ranges, first = [], 0
    for height, width in kinds:
        count = (height // TILE) * (width // (2 * ACROSS))
        ranges.append((first, first + count, width // (2 * ACROSS)))
        first += count
    steps = first

    def own_at(ring):
        return scores.at[0:TILE, pl.ds(pl.multiple_of(ring * ACROSS, ACROSS), ACROSS)]

    def core_st_at(ring):
        return hid_st.at[:, pl.ds(pl.multiple_of(ring * ACROSS, ACROSS), ACROSS)]

    def red_st_at(ring):
        return dpre_st.at[:, pl.ds(pl.multiple_of(ring * ACROSS, ACROSS), ACROSS)]

    def tot_at(slot):
        cols = pl.ds(pl.multiple_of(lax.rem(slot, 4) * ACROSS, ACROSS), ACROSS)
        return norm_st.at[slot // 4, :, cols]

    def left_at(slot):
        return wup.at[:, pl.ds(pl.multiple_of(slot * TILE, TILE), TILE)]

    def right_at(slot):
        return wdown.at[
            pl.ds(pl.multiple_of((slot // 2) * d_model, d_model), d_model),
            pl.ds(pl.multiple_of(lax.rem(slot, 2) * 2 * ACROSS, 2 * ACROSS), 2 * ACROSS),
        ]

    tile_ref = core_r.at[0]

    def by_kind(m, body):
        for kind, (low, high, across) in enumerate(ranges):

            @pl.when((m >= low) & (m < high))
            def _(kind=kind, low=low, across=across):
                at = m - low
                body(kind, at // across, lax.rem(at, across))

    def tile_of(kind, row, col, which):
        return targets[kind].at[
            pl.ds(pl.multiple_of(row * TILE, TILE), TILE),
            pl.ds(pl.multiple_of((2 * col + which) * ACROSS, ACROSS), ACROSS),
        ]

    def fetch(m):
        pl.when(m == ranges[3][0])(lambda: arrived(dpk_st, store_sem.at[7]))

        def body(kind, row, col):
            left, right = operands[kind]
            slot = lax.rem(m, AHEAD + 1)
            pltpu.make_async_copy(
                left.at[:, pl.ds(pl.multiple_of(row * TILE, TILE), TILE)],
                left_at(slot),
                op_sem.at[0, slot],
            ).start()
            pltpu.make_async_copy(
                right.at[:, pl.ds(pl.multiple_of(col * 2 * ACROSS, 2 * ACROSS), 2 * ACROSS)],
                right_at(slot),
                op_sem.at[1, slot],
            ).start()

        by_kind(m, body)

    def is_root(m):
        return middle & (chip == 1 + lax.rem(m, 2))

    def products(m):
        slot, ring = lax.rem(m, AHEAD + 1), lax.rem(m, RING)
        arrived(left_at(slot), op_sem.at[0, slot])
        arrived(right_at(slot), op_sem.at[1, slot])
        left, right = left_at(slot), right_at(slot)
        mine = pl.ds(pl.multiple_of(core * ACROSS, ACROSS), ACROSS)
        other = pl.ds(pl.multiple_of((1 - core) * ACROSS, ACROSS), ACROSS)

        @pl.when(m >= RING)
        def _():
            arrived(tile_ref, core_ss.at[ring])
            pl.semaphore_wait(core_free, 1)

        core_st_at(ring)[...] = t_dot(left[...], right[:, other]).astype(BF16)
        remote(
            core_st_at(ring), core_r.at[ring], core_ss.at[ring], core_rs.at[ring], partner
        ).start()
        own_at(ring)[...] = t_dot(left[...], right[:, mine])

    def send_red(m, value, target, sem, dev, free):
        ring = lax.rem(m, RING)

        @pl.when(m >= RING)
        def _():
            pl.semaphore_wait(free, 1)

        red_st_at(ring)[...] = value.astype(BF16)
        remote(red_st_at(ring), target.at[ring], red_ss.at[ring], sem.at[ring], dev).start()

    def chip_sum(m):
        ring = lax.rem(m, RING)
        arrived(tile_ref, core_rs.at[ring])
        total = own_at(ring)[...] + core_r[ring].astype(F32)

        @pl.when(m + RING < steps)
        def _():
            pl.semaphore_signal(core_free, inc=1, device_id=partner, device_id_type=MESH)

        @pl.when(at_end)
        def _():
            @pl.when(m >= RING)
            def _():
                arrived(tile_ref, red_ss.at[ring])

            send_red(m, total, outer_r, outer_rs, end_of, outer_free.at[lax.rem(m, 2)])

        @pl.when(middle)
        def _():
            own_at(ring)[...] = total

    def take_outer(m):
        ring = lax.rem(m, RING)
        arrived(tile_ref, outer_rs.at[ring])
        total = own_at(ring)[...] + outer_r[ring].astype(F32)

        @pl.when(m + RING < steps)
        def _():
            pl.semaphore_signal(
                outer_free.at[lax.rem(m, 2)], inc=1, device_id=outer_of, device_id_type=MESH
            )

        return total

    def pass_in(m):
        ring = lax.rem(m, RING)
        total = take_outer(m)

        @pl.when(m >= RING)
        def _():
            arrived(tile_ref, red_ss.at[ring])

        send_red(m, total, inner_r, inner_rs, inner_of, inner_free)

    def finish(m):
        ring = lax.rem(m, RING)
        slot = lax.rem(m // 2, TOTALS)
        total = take_outer(m)
        arrived(tile_ref, inner_rs.at[ring])
        total = total + inner_r[ring].astype(F32)

        @pl.when(m + RING < steps)
        def _():
            pl.semaphore_signal(inner_free, inc=1, device_id=inner_of, device_id_type=MESH)

        @pl.when(m >= 2 * TOTALS)
        def _():
            for k in range(4):
                arrived(tile_ref, tot_ss.at[k, slot])

        tot_at(slot)[...] = total.astype(BF16)

        def body(kind, row, col):
            here = tile_of(kind, row, col, core)
            remote(tot_at(slot), here, tot_ss.at[0, slot], bc_rs.at[m], outer_of).start()
            remote(tot_at(slot), here, tot_ss.at[1, slot], bc_rs.at[m], inner_of).start()
            remote(tot_at(slot), here, tot_ss.at[2, slot], fin_rs.at[kind], partner).start()
            pltpu.make_async_copy(tot_at(slot), here, tot_ss.at[3, slot]).start()

        by_kind(m, body)

    def hand_on(m):
        arrived(tile_ref, bc_rs.at[m])

        def body(kind, row, col):
            here = tile_of(kind, row, col, core)

            @pl.when(middle)
            def _():
                remote(here, here, fwd_ss.at[m], bc_rs.at[m], outer_of).start()

            remote(here, here, share_ss.at[m], fin_rs.at[kind], partner).start()

        by_kind(m, body)

    exchanges = (
        {"tensor": 1 - tens},
        partner,
        {"wide": me + 2 - 4 * lax.rem(chip, 2)},
        {"wide": me + 4 - 8 * (chip // 2)},
    )

    def sums_begin():
        sums[:, 0:d_model] = jnp.concatenate(
            [jnp.sum(small[k], axis=0, keepdims=True) for k in range(5)]
            + [jnp.zeros((3, d_model), F32)],
            axis=0,
        )
        total = jnp.sum(bias_sums[...], axis=0, keepdims=True)
        lines = [total[:, k * COLS : (k + 1) * COLS] for k in range(total.shape[1] // COLS)]
        lines.append(jnp.zeros((8 - len(lines), COLS), F32))
        sums[:, d_model:] = jnp.concatenate(lines, axis=0)

    def exchange_start(k):
        if k == 0:
            sums_begin()
        else:
            arrived(sums, sum_ss.at[0])
        sums_r[0] = sums[...]
        remote(sums_r.at[0], sums_r.at[k + 1], sum_ss.at[0], sum_rs.at[k], exchanges[k]).start()

    def exchange_end(k):
        arrived(sums, sum_rs.at[k])
        if k == 0:
            sums[:, 0:d_model] += sums_r[1, :, 0:d_model]
        else:
            sums[...] += sums_r[k + 1]

    def gradient_step(i, carry):
        pl.when(i + AHEAD < steps)(lambda: fetch(i + AHEAD))
        pl.when(i < steps)(lambda: products(i))
        for k in range(4):
            pl.when(i == EARLY + 4 * k + 2)(lambda k=k: exchange_start(k))
            pl.when(i == EARLY + 4 * k + 5)(lambda k=k: exchange_end(k))

        def late(lag, allowed, body):
            m = i - lag
            pl.when((m >= 0) & (m < steps) & allowed(m))(lambda: body(m))

        late(LAGS[0], lambda m: m >= 0, chip_sum)
        late(LAGS[1], lambda m: middle & jnp.logical_not(is_root(m)), pass_in)
        late(LAGS[2], is_root, finish)
        late(LAGS[3], lambda m: middle & jnp.logical_not(is_root(m)), hand_on)
        late(LAGS[4], lambda m: at_end, hand_on)
        return carry

    def gradient_begin():
        arrived(norm_st.at[0], store_sem.at[0])
        arrived(norm_st.at[1], store_sem.at[1])
        arrived(hid_st, store_sem.at[2])
        arrived(mixed_st, store_sem.at[3])
        arrived(dpre_st, store_sem.at[6])
        for s in range(micro):
            arrived(gfull.at[s], g_store.at[s])
        for m in range(AHEAD):
            fetch(jnp.int32(m))

    def at(seq, allowed, body):
        pl.when(allowed & (seq >= 0) & (seq < micro))(lambda: body(seq))

    @pl.when(sect == 1)
    def _():
        lax.fori_loop(0, micro, lambda s, carry: (backward(s), carry)[1], 0)

    first = jnp.int32(0)
    pl.when(sect == 1)(lambda: forward_meet(first))
    forward(first)
    forward_ff(first)
    always = sect >= 0

    def step(i, carry):
        f = i
        b = jnp.where(sect == 1, i, i - micro)
        at(b, (sect == 0) & (b == 0), backward_meet)
        at(b, sect == 0, backward)
        at(f + 1, sect == 1, forward_meet)
        at(f, always, forward_attention)
        at(f + 1, always, forward)
        at(b, always, backward_attention)
        at(b - 1, always, backward_norm)
        at(f, always, forward_out)
        at(b, always, backward_ff)
        at(b + 1, (sect == 0) & (b >= 0), backward_meet)
        at(b - 1, always, backward_end)
        at(f, always, forward_end)
        at(f + 1, always, forward_ff)

        starts = jnp.where(sect == 1, i == micro, i == 2 * micro - 1)
        goes_on = (sect == 0) & (i == 2 * micro)
        pl.when(starts)(gradient_begin)
        low = jnp.where(goes_on, EARLY, 0)
        high = jnp.where(
            goes_on | (starts & (sect == 1)), steps + LAGS[4], jnp.where(starts, EARLY, 0)
        )
        lax.fori_loop(low, high, gradient_step, 0)
        return carry

    lax.fori_loop(0, jnp.where(sect == 1, micro + 1, 2 * micro + 1), step, 0)

    for s in range(micro):
        arrived(xfull.at[s, my_rows], yx_s.at[s])
        arrived(gfull.at[s, my_rows], yg_s.at[s])
    arrived(out_st, store_sem.at[4])
    arrived(ig_st, store_sem.at[8])
    pl.when(sect == 0)(lambda: arrived(out_st, xs_ss.at[0]))
    pl.when(sect == 1)(lambda: arrived(gx_st, gs_ss.at[0]))

    arrived(sums, sum_ss.at[0])
    for ring in range(RING):
        arrived(tile_ref, core_ss.at[ring])

    def drain(m, carry):
        ring = lax.rem(m, RING)
        root = is_root(m)
        last = m + RING >= steps
        pl.when(at_end & last)(lambda: arrived(tile_ref, red_ss.at[ring]))
        pl.when(middle & jnp.logical_not(root) & last)(
            lambda: arrived(tile_ref, red_ss.at[ring])
        )

        @pl.when(root & (m + 2 * TOTALS >= steps))
        def _():
            for k in range(4):
                arrived(tile_ref, tot_ss.at[k, lax.rem(m // 2, TOTALS)])

        @pl.when(middle & jnp.logical_not(root))
        def _():
            arrived(tile_ref, fwd_ss.at[m])

        pl.when(jnp.logical_not(root))(lambda: arrived(tile_ref, share_ss.at[m]))
        return carry

    lax.fori_loop(0, steps, drain, 0)
    for kind, (height, width) in enumerate(kinds):
        arrived(targets[kind].at[pl.ds(0, height // 2)], fin_rs.at[kind])


def relay(dims, doc_lengths, block_input, cotangent, weights, collective_id):
    micro, rows, group, wide, heads, d_model, ff = dims
    (
        norm_gain,
        norm_bias,
        qkv_weight,
        qkv_bias,
        dense_weight,
        dense_bias,
        up_weight,
        up_bias,
        down_weight,
        down_bias,
    ) = weights
    inner = heads * HEAD_DIM
    per_source = group + group // 2
    anywhere = pl.BlockSpec(memory_space=pl.ANY)
    local = pl.BlockSpec(memory_space=pltpu.VMEM)
    scalars = pl.BlockSpec(memory_space=pltpu.SMEM)
    dma = pltpu.SemaphoreType.DMA
    vmem = pltpu.VMEM
    outs = [
        jax.ShapeDtypeStruct((micro, rows, d_model), BF16),
        jax.ShapeDtypeStruct((micro, rows, d_model), F32),
        jax.ShapeDtypeStruct((2, micro * group, d_model), BF16),
        jax.ShapeDtypeStruct((micro * group, d_model), BF16),
        jax.ShapeDtypeStruct((micro * group, inner), BF16),
        jax.ShapeDtypeStruct((micro * group, ff), BF16),
        jax.ShapeDtypeStruct((micro * group, ff), BF16),
        jax.ShapeDtypeStruct((micro * group, 3 * inner), BF16),
    ]
    kinds = gradient_kinds(d_model, inner, ff)
    steps = sum((height // TILE) * (width // (2 * ACROSS)) for height, width in kinds)
    outs += [jax.ShapeDtypeStruct(kind, BF16) for kind in kinds]
    outs += [jax.ShapeDtypeStruct((8, d_model + COLS), F32)]
    regular = pltpu.SemaphoreType.REGULAR
    scratch = [
        vmem((5, 8, d_model), F32),
        vmem((8, 3 * inner + ff), F32),
        vmem((micro, group, LANES), F32),
        vmem((micro, group, LANES), F32),
        vmem((micro, group, LANES), F32),
        vmem(qkv_weight.shape, BF16),
        vmem(dense_weight.shape, BF16),
        vmem(up_weight.shape, BF16),
        vmem(down_weight.shape, BF16),
        vmem((micro, group, d_model), BF16),
        vmem((micro, group, d_model), BF16),
        vmem((micro, rows, d_model), F32),
        vmem((micro, wide, per_source, LANES), BF16),
        vmem((micro, wide, group // 2, LANES), BF16),
        vmem((micro, wide, group // 2, LANES), BF16),
        vmem((micro, wide, per_source, LANES), BF16),
        vmem((micro, rows, d_model), BF16),
        vmem((micro, rows, d_model), BF16),
        vmem((wide, per_source, LANES), BF16),
        vmem((micro, wide, group // 2, LANES), BF16),
        vmem((micro, wide, group // 2, LANES), BF16),
        vmem((2, wide, per_source, LANES), BF16),
        vmem((rows, d_model), BF16),
        vmem((rows, d_model), BF16),
        vmem((rows, d_model), BF16),
        vmem((rows, d_model), BF16),
        vmem((rows, d_model), F32),
        vmem((2, group, d_model), BF16),
        vmem((group, inner), BF16),
        vmem((group, ff), BF16),
        vmem((group, ff), BF16),
        vmem((group, 3 * inner), BF16),
        vmem((micro, group, ff), BF16),
        vmem((group, d_model), F32),
        vmem((group, d_model), F32),
        vmem((group, d_model), F32),
        vmem((SEQ, LANES), BF16),
        vmem((SEQ, LANES), BF16),
        vmem((SEQ, LANES), BF16),
        vmem((SEQ, LANES), BF16),
        vmem((SEQ, LANES), F32),
        vmem((micro, SEQ // BLOCK, 8, BLOCK), F32),
        vmem((wide, 8, group), F32),
        vmem((BLOCK, SEQ), F32),
        vmem((BLOCK, LANES), F32),
        vmem((BLOCK, LANES), F32),
        dma((4,)),
        dma((micro,)),
        dma((micro,)),
        dma((micro,)),
        dma((micro,)),
        dma((micro,)),
        dma((micro,)),
        dma((1,)),
        dma((micro,)),
        dma((micro,)),
        dma((micro,)),
        dma((micro,)),
        dma((micro,)),
        dma((2,)),
        dma((micro,)),
        dma((1,)),
        dma((micro,)),
        dma((1,)),
        dma((micro,)),
        dma((1,)),
        dma((1,)),
        dma((9,)),
        dma((micro,)),
        vmem((RING, TILE, ACROSS), BF16),
        vmem((RING, TILE, ACROSS), BF16),
        vmem((RING, TILE, ACROSS), BF16),
        vmem((5, 8, d_model + COLS), F32),
        dma((2, AHEAD + 1)),
        dma((RING,)),
        dma((RING,)),
        dma((RING,)),
        dma((RING,)),
        dma((RING,)),
        dma((steps,)),
        dma((4, TOTALS)),
        dma((steps,)),
        dma((steps,)),
        dma((4,)),
        dma((1,)),
        dma((4,)),
        regular,
        regular((2,)),
        regular,
    ]
    return pl.pallas_call(
        functools.partial(relay_kernel, dims),
        out_shape=outs,
        in_specs=[scalars, anywhere, anywhere] + [local] * 6 + [anywhere] * 4,
        out_specs=[anywhere] * 12 + [local],
        scratch_shapes=scratch,
        compiler_params=pltpu.CompilerParams(
            collective_id=collective_id, has_side_effects=True, vmem_limit_bytes=63 << 20
        ),
        name="relay",
    )(
        doc_lengths,
        block_input,
        cotangent,
        norm_gain,
        norm_bias,
        qkv_bias[None],
        up_bias[None],
        dense_bias[None],
        down_bias[None],
        qkv_weight,
        dense_weight,
        up_weight,
        down_weight,
    )


def relay_shards(
    block_input,
    doc_lengths,
    norm_gain,
    norm_bias,
    qkv_weight,
    qkv_bias,
    dense_weight,
    dense_bias,
    up_weight,
    up_bias,
    down_weight,
    down_bias,
    cotangent,
):
    weights = tuple(
        array[0]
        for array in (
            norm_gain,
            norm_bias,
            qkv_weight,
            qkv_bias,
            dense_weight,
            dense_bias,
            up_weight,
            up_bias,
            down_weight,
            down_bias,
        )
    )
    micro, rows, d_model = block_input.shape
    group = rows * lax.axis_size("tensor")
    wide = lax.axis_size("wide")
    heads = qkv_weight.shape[2] // (3 * HEAD_DIM)
    ff = up_weight.shape[2]
    dims = (micro, rows, group, wide, heads, d_model, ff)
    out, input_grad, *_, up_grad, down_grad, dense_grad, qkv_grad, sums = relay(
        dims, doc_lengths, block_input, cotangent, weights, 1
    )
    up_grad, down_grad, dense_grad, qkv_grad = (
        grad.astype(F32)[None] for grad in (up_grad, down_grad, dense_grad, qkv_grad)
    )
    biases = sums[:, d_model:].reshape(1, -1)
    qkv_width = qkv_weight.shape[2]
    out_bias_grad = sums[4:5, :d_model]
    return (
        out[None],
        input_grad[None],
        sums[None, 0:2, :d_model],
        sums[None, 2:4, :d_model],
        qkv_grad,
        biases[:, :qkv_width],
        dense_grad,
        out_bias_grad,
        up_grad,
        biases[:, qkv_width : qkv_width + ff],
        down_grad,
        out_bias_grad,
    )


def shortened(shard):

    def short(part):
        return part.astype(jnp.bfloat16) if part.dtype == jnp.float32 else part

    return jax.tree.map(short, shard)


def from_behind(block, axis, distance):
    devices = range(lax.axis_size(axis))
    route = [(i - distance, i) for i in devices if i - distance in devices]
    return lax.ppermute(block, axis, route)


def norm_parts(values, gain, shift):
    center = jnp.mean(values, axis=-1, keepdims=True)
    centred = values - center
    spread = jnp.mean(centred * centred, axis=-1, keepdims=True)
    inv_scale = lax.rsqrt(spread + EPSILON)
    normed = centred * inv_scale
    return (normed * gain + shift, normed, inv_scale)


def norm_back(grad, normed, inv_scale, gain):
    scaled = grad * gain
    inner_mean = jnp.mean(scaled, axis=-1, keepdims=True)
    cross_mean = jnp.mean(scaled * normed, axis=-1, keepdims=True)
    return inv_scale * (scaled - inner_mean - normed * cross_mean)


def doc_layout(lengths, tok_index):
    ends = jnp.cumsum(lengths)
    starts = ends - lengths
    doc_ids = jnp.sum((tok_index[:, None] >= ends[None, :]).astype(jnp.int32), axis=1)
    numbers = jnp.arange(lengths.shape[0], dtype=jnp.int32)
    picked = doc_ids[:, None] == numbers[None, :]
    begins = jnp.sum(jnp.where(picked, starts[None, :], 0), axis=1)
    return (doc_ids, tok_index - begins)


def rope_tables(offsets):
    half = ROT // 2
    freqs = ROPE_BASE ** (-2.0 * jnp.arange(half, dtype=jnp.float32) / ROT)
    angle = offsets.astype(jnp.float32)[:, None] * freqs[None, :]
    return (jnp.cos(angle)[:, None, :], jnp.sin(angle)[:, None, :])


def rotate(values, cos_table, sin_table):
    half = ROT // 2
    front = values[..., :half]
    back = values[..., half:ROT]
    turned = [
        front * cos_table - back * sin_table,
        back * cos_table + front * sin_table,
        values[..., ROT:],
    ]
    return jnp.concatenate(turned, axis=-1)


def unrotate(values, cos_table, sin_table):
    half = ROT // 2
    front = values[..., :half]
    back = values[..., half:ROT]
    turned = [
        front * cos_table + back * sin_table,
        back * cos_table - front * sin_table,
        values[..., ROT:],
    ]
    return jnp.concatenate(turned, axis=-1)


def gelu_parts(pre_act):
    cumul = 0.5 * (1.0 + lax.erf(pre_act * (1.0 / math.sqrt(2.0))))
    density = jnp.exp(-0.5 * pre_act * pre_act) * (1.0 / math.sqrt(2.0 * math.pi))
    return (pre_act * cumul, cumul + pre_act * density)


def store_slot(buffer, update, slot_here, is_valid):
    previous = lax.dynamic_index_in_dim(buffer, slot_here, 0, keepdims=False)
    return lax.dynamic_update_index_in_dim(
        buffer, jnp.where(is_valid, update, previous), slot_here, 0
    )


def gather_keys(key_rows, value_rows):
    return (
        lax.all_gather(key_rows, "wide", axis=0, tiled=True),
        lax.all_gather(value_rows, "wide", axis=0, tiled=True),
    )


def forward_parts(inputs, lengths, weights, with_output):
    (
        norm_gain,
        norm_bias,
        qkv_weight,
        qkv_bias,
        dense_weight,
        dense_bias,
        up_weight,
        up_bias,
        down_weight,
        down_bias,
    ) = weights
    seq_len = SEQ
    group = inputs.shape[0] * lax.axis_size("tensor")
    head_count = qkv_weight.shape[1] // (3 * HEAD_DIM)
    factor = 1.0 / math.sqrt(HEAD_DIM)
    values = inputs.astype(jnp.float32)
    norm_first, normed_first, scale_first = norm_parts(values, norm_gain[0], norm_bias[0])
    norm_second, normed_second, scale_second = norm_parts(values, norm_gain[1], norm_bias[1])
    full_first, full_second = (
        lax.all_gather(norm_first.astype(jnp.bfloat16), "tensor", axis=0, tiled=True),
        lax.all_gather(norm_second.astype(jnp.bfloat16), "tensor", axis=0, tiled=True),
    )
    tok_index = lax.axis_index("wide") * group + jnp.arange(group, dtype=jnp.int32)
    doc_ids, offsets = doc_layout(lengths, tok_index)
    all_index = jnp.arange(seq_len, dtype=jnp.int32)
    all_docs = doc_layout(lengths, all_index)[0]
    cos_table, sin_table = rope_tables(offsets)
    packed = jnp.dot(full_first, qkv_weight, preferred_element_type=jnp.float32) + qkv_bias
    packed = packed.reshape(group, head_count, 3, HEAD_DIM)
    queries = rotate(packed[:, :, 0], cos_table, sin_table).astype(jnp.bfloat16)
    key_here = rotate(packed[:, :, 1], cos_table, sin_table).astype(jnp.bfloat16)
    value_here = packed[:, :, 2].astype(jnp.bfloat16)
    key_all, value_all = gather_keys(key_here.reshape(group, -1), value_here.reshape(group, -1))
    key_heads = key_all.reshape(seq_len, head_count, HEAD_DIM)
    value_heads = value_all.reshape(seq_len, head_count, HEAD_DIM)
    allowed = (doc_ids[:, None] == all_docs[None, :]) & (all_index[None, :] <= tok_index[:, None])
    raw_scores = jnp.einsum("qhd,khd->qhk", queries, key_heads, preferred_element_type=jnp.float32)
    scores = jnp.where(allowed[:, None, :], raw_scores * factor, -jnp.inf)
    row_max = jnp.max(scores, axis=-1, keepdims=True)
    log_total = row_max + jnp.log(jnp.sum(jnp.exp(scores - row_max), axis=-1, keepdims=True))
    attn_probs = jnp.exp(scores - log_total)
    probs_low = attn_probs.astype(jnp.bfloat16)
    mixed_out = jnp.einsum(
        "qhk,khd->qhd", probs_low, value_heads, preferred_element_type=jnp.float32
    )
    mixed_out = mixed_out.reshape(group, -1).astype(jnp.bfloat16)
    up_pre = jnp.dot(full_second, up_weight, preferred_element_type=jnp.float32) + up_bias
    up_act, gelu_slope = gelu_parts(up_pre)
    hidden = up_act.astype(jnp.bfloat16)
    output = None
    if with_output:
        partial_value = jnp.dot(mixed_out, dense_weight, preferred_element_type=jnp.float32)
        partial_value = partial_value + jnp.dot(
            hidden, down_weight, preferred_element_type=jnp.float32
        )
        branch = (
            lax.psum_scatter(
                partial_value.astype(jnp.bfloat16), "tensor", scatter_dimension=0, tiled=True
            ).astype(jnp.float32)
            + dense_bias
            + down_bias
        )
        output = (values + branch).astype(jnp.bfloat16)
    return dict(
        output=output,
        normed_first=normed_first,
        scale_first=scale_first,
        normed_second=normed_second,
        scale_second=scale_second,
        full_first=full_first,
        full_second=full_second,
        tok_index=tok_index,
        doc_ids=doc_ids,
        all_index=all_index,
        all_docs=all_docs,
        cos_table=cos_table,
        sin_table=sin_table,
        queries=queries,
        key_here=key_here,
        value_here=value_here,
        key_all=key_all,
        value_all=value_all,
        key_heads=key_heads,
        value_heads=value_heads,
        attn_probs=attn_probs,
        probs_low=probs_low,
        log_total=log_total,
        mixed_out=mixed_out,
        gelu_slope=gelu_slope,
        hidden=hidden,
    )


def backward_parts(inputs, grad_out, lengths, weights):
    (
        norm_gain,
        norm_bias,
        qkv_weight,
        qkv_bias,
        dense_weight,
        dense_bias,
        up_weight,
        up_bias,
        down_weight,
        down_bias,
    ) = weights
    parts = forward_parts(inputs, lengths, weights, False)
    seq_len = SEQ
    group = inputs.shape[0] * lax.axis_size("tensor")
    head_count = qkv_weight.shape[1] // (3 * HEAD_DIM)
    factor = 1.0 / math.sqrt(HEAD_DIM)
    cos_table = parts["cos_table"]
    sin_table = parts["sin_table"]
    grad_low = grad_out.astype(jnp.bfloat16)
    grad_rows = grad_low.astype(jnp.float32)
    grad_full = lax.all_gather(grad_low, "tensor", axis=0, tiled=True)
    dense_grad = jnp.einsum(
        "cf,cd->fd", parts["mixed_out"], grad_full, preferred_element_type=jnp.float32
    )
    down_grad = jnp.einsum(
        "cf,cd->fd", parts["hidden"], grad_full, preferred_element_type=jnp.float32
    )
    hidden_grad = jnp.einsum(
        "cd,fd->cf", grad_full, down_weight, preferred_element_type=jnp.float32
    )
    pre_grad = (hidden_grad * parts["gelu_slope"]).astype(jnp.bfloat16)
    up_grad = jnp.einsum(
        "cd,cf->df", parts["full_second"], pre_grad, preferred_element_type=jnp.float32
    )
    up_bias_grad = jnp.sum(pre_grad.astype(jnp.float32), axis=0)
    second_grad = jnp.einsum("cf,df->cd", pre_grad, up_weight, preferred_element_type=jnp.float32)
    mixed_grad = jnp.einsum(
        "cd,fd->cf", grad_full, dense_weight, preferred_element_type=jnp.float32
    )
    mixed_grad = mixed_grad.astype(jnp.bfloat16).reshape(group, head_count, HEAD_DIM)
    attn_probs = parts["attn_probs"]
    probs_grad = jnp.einsum(
        "qhd,khd->qhk", mixed_grad, parts["value_heads"], preferred_element_type=jnp.float32
    )
    inner = jnp.sum(attn_probs * probs_grad, axis=-1, keepdims=True)
    score_grad = (attn_probs * (probs_grad - inner) * factor).astype(jnp.bfloat16)
    query_grad = jnp.einsum(
        "qhk,khd->qhd", score_grad, parts["key_heads"], preferred_element_type=jnp.float32
    )
    key_sums = jnp.einsum(
        "qhk,qhd->khd", score_grad, parts["queries"], preferred_element_type=jnp.float32
    )
    value_sums = jnp.einsum(
        "qhk,qhd->khd", parts["probs_low"], mixed_grad, preferred_element_type=jnp.float32
    )
    key_flat, value_flat = (
        lax.psum_scatter(
            key_sums.reshape(seq_len, -1).astype(jnp.bfloat16),
            "wide",
            scatter_dimension=0,
            tiled=True,
        ).astype(jnp.float32),
        lax.psum_scatter(
            value_sums.reshape(seq_len, -1).astype(jnp.bfloat16),
            "wide",
            scatter_dimension=0,
            tiled=True,
        ).astype(jnp.float32),
    )
    key_grad = key_flat.reshape(group, head_count, HEAD_DIM)
    value_grad = value_flat.reshape(group, head_count, HEAD_DIM)
    query_back = unrotate(query_grad, cos_table, sin_table)
    key_back = unrotate(key_grad, cos_table, sin_table)
    packed_grad = (
        jnp.stack([query_back, key_back, value_grad], axis=2)
        .reshape(group, -1)
        .astype(jnp.bfloat16)
    )
    qkv_grad = jnp.einsum(
        "cd,cf->df", parts["full_first"], packed_grad, preferred_element_type=jnp.float32
    )
    qkv_bias_grad = jnp.sum(packed_grad.astype(jnp.float32), axis=0)
    first_grad = jnp.einsum(
        "cf,df->cd", packed_grad, qkv_weight, preferred_element_type=jnp.float32
    )
    norm_first_grad, norm_second_grad = (
        lax.psum_scatter(
            first_grad.astype(jnp.bfloat16), "tensor", scatter_dimension=0, tiled=True
        ).astype(jnp.float32),
        lax.psum_scatter(
            second_grad.astype(jnp.bfloat16), "tensor", scatter_dimension=0, tiled=True
        ).astype(jnp.float32),
    )
    gain_grad = jnp.stack(
        [
            jnp.sum(norm_first_grad * parts["normed_first"], axis=0),
            jnp.sum(norm_second_grad * parts["normed_second"], axis=0),
        ]
    )
    shift_grad = jnp.stack([jnp.sum(norm_first_grad, axis=0), jnp.sum(norm_second_grad, axis=0)])
    input_grad = grad_out + norm_back(
        norm_first_grad, parts["normed_first"], parts["scale_first"], norm_gain[0]
    )
    input_grad = input_grad + norm_back(
        norm_second_grad, parts["normed_second"], parts["scale_second"], norm_gain[1]
    )
    bias_rows = jnp.sum(grad_rows, axis=0)
    terms = (
        gain_grad,
        shift_grad,
        qkv_grad,
        qkv_bias_grad,
        dense_grad,
        bias_rows,
        up_grad,
        up_bias_grad,
        down_grad,
        bias_rows,
    )
    return (input_grad, terms)


def general_shards(
    block_input,
    doc_lengths,
    norm_gain,
    norm_bias,
    qkv_weight,
    qkv_bias,
    dense_weight,
    dense_bias,
    up_weight,
    up_bias,
    down_weight,
    down_bias,
    cotangent,
):
    weights = (
        norm_gain[0],
        norm_bias[0],
        qkv_weight[0],
        qkv_bias[0],
        dense_weight[0],
        dense_bias[0],
        up_weight[0],
        up_bias[0],
        down_weight[0],
        down_bias[0],
    )
    section_index = lax.axis_index("section")
    last_section = lax.axis_size("section") - 1
    micro_count = block_input.shape[0]
    row_count = block_input.shape[1]
    tick_count = micro_count + last_section

    def forward_tick(carry, tick_index):
        incoming, kept_inputs, outputs, kept_pairs = carry
        slot_raw = tick_index - section_index
        is_valid = (slot_raw >= 0) & (slot_raw < micro_count)
        slot_here = jnp.clip(slot_raw, 0, micro_count - 1)
        fresh = lax.dynamic_index_in_dim(
            block_input, jnp.clip(tick_index, 0, micro_count - 1), 0, keepdims=False
        )
        inputs = jnp.where(section_index == 0, fresh, incoming)
        lengths = lax.dynamic_index_in_dim(doc_lengths, slot_here, 0, keepdims=False)
        parts = forward_parts(inputs, lengths, weights, True)
        output = parts["output"]
        kept_inputs = store_slot(kept_inputs, inputs, slot_here, is_valid)
        outputs = store_slot(outputs, output, slot_here, is_valid)
        incoming = jax.tree.map(
            lambda part, own: part.astype(own.dtype),
            from_behind(shortened(output), "section", 1),
            output,
        )
        return ((incoming, kept_inputs, outputs, kept_pairs), None)

    pair_init = (jnp.zeros((1,), jnp.bfloat16), jnp.zeros((1,), jnp.bfloat16))
    zero_rows = jnp.zeros((row_count, block_input.shape[2]), jnp.bfloat16)
    zero_stack = jnp.zeros(block_input.shape, jnp.bfloat16)
    forward_init = (zero_rows, zero_stack, zero_stack, pair_init)
    forward_done = lax.scan(forward_tick, forward_init, jnp.arange(tick_count, dtype=jnp.int32))[0]
    kept_inputs = forward_done[1]
    outputs = forward_done[2]
    kept_pairs = forward_done[3]

    def add_masked(total, term, scale_mask):
        return total + scale_mask * term

    def backward_tick(carry, tick_index):
        incoming, grads, input_grads = carry
        slot_raw = tick_index - (last_section - section_index)
        is_valid = (slot_raw >= 0) & (slot_raw < micro_count)
        slot_here = jnp.clip(slot_raw, 0, micro_count - 1)
        top_grad = lax.dynamic_index_in_dim(cotangent, slot_here, 0, keepdims=False)
        grad_out = jnp.where(section_index == last_section, top_grad, incoming)
        inputs = lax.dynamic_index_in_dim(kept_inputs, slot_here, 0, keepdims=False)
        lengths = lax.dynamic_index_in_dim(doc_lengths, slot_here, 0, keepdims=False)
        input_grad, terms = backward_parts(inputs, grad_out, lengths, weights)
        scale_mask = is_valid.astype(jnp.float32)
        grads = tuple((add_masked(total, term, scale_mask) for total, term in zip(grads, terms)))
        input_grads = store_slot(input_grads, input_grad, slot_here, is_valid)
        incoming = from_behind(shortened(input_grad), "section", -1).astype(input_grad.dtype)
        return ((incoming, grads, input_grads), None)

    grad_init = tuple((jnp.zeros(weight.shape, jnp.float32) for weight in weights))
    backward_init = (
        jnp.zeros((row_count, block_input.shape[2]), jnp.float32),
        grad_init,
        jnp.zeros(block_input.shape, jnp.float32),
    )
    backward_done = lax.scan(backward_tick, backward_init, jnp.arange(tick_count, dtype=jnp.int32))[
        0
    ]
    grads = backward_done[1]
    input_grads = backward_done[2]
    wide_sums = (
        lax.psum(grads[2].astype(jnp.bfloat16), "wide").astype(jnp.float32),
        lax.psum(grads[3].astype(jnp.bfloat16), "wide").astype(jnp.float32),
        lax.psum(grads[4].astype(jnp.bfloat16), "wide").astype(jnp.float32),
        lax.psum(grads[6].astype(jnp.bfloat16), "wide").astype(jnp.float32),
        lax.psum(grads[7].astype(jnp.bfloat16), "wide").astype(jnp.float32),
        lax.psum(grads[8].astype(jnp.bfloat16), "wide").astype(jnp.float32),
    )
    shared = lax.psum((grads[0], grads[1], grads[5], grads[9]), ("tensor", "wide"))
    return (
        outputs[None],
        input_grads[None],
        shared[0][None],
        shared[1][None],
        wide_sums[0][None],
        wide_sums[1][None],
        wide_sums[2][None],
        shared[2][None],
        wide_sums[3][None],
        wide_sums[4][None],
        wide_sums[5][None],
        shared[3][None],
    )


def solution(mesh):
    placed = (
        P(None, ("wide", "tensor"), None),
        P(),
        P("section", None, None),
        P("section", None, None),
        P("section", None, "tensor"),
        P("section", "tensor"),
        P("section", "tensor", None),
        P("section", None),
        P("section", None, "tensor"),
        P("section", "tensor"),
        P("section", "tensor", None),
        P("section", None),
        P(None, ("wide", "tensor"), None),
    )
    results = (
        P("section", None, ("wide", "tensor"), None),
        P("section", None, ("wide", "tensor"), None),
        P("section", None, None),
        P("section", None, None),
        P("section", None, "tensor"),
        P("section", "tensor"),
        P("section", "tensor", None),
        P("section", None),
        P("section", None, "tensor"),
        P("section", "tensor"),
        P("section", "tensor", None),
        P("section", None),
    )

    def program(*args):
        heads = args[4].shape[2] // (3 * HEAD_DIM * mesh.shape["tensor"])
        micro, seq_len, d_model = args[0].shape
        group = seq_len // mesh.shape["wide"]
        fits = heads == mesh.shape["wide"] == 8
        fits = fits and mesh.shape["section"] == 2 and mesh.shape["tensor"] == 2
        fits = fits and micro * group == d_model and args[8].shape[2] == 4 * d_model
        body = relay_shards if fits and group == TILE else general_shards
        return jax.shard_map(
            body, mesh=mesh, in_specs=placed, out_specs=results, check_vma=False
        )(*args)

    return program
```

```python
import functools
import math

import jax
import jax.numpy as jnp
from jax import lax
from jax.experimental import pallas as pl
from jax.experimental.pallas import tpu as pltpu
from jax.sharding import PartitionSpec as P

HEAD_DIM = 64
ROT = 16
SEQ = 2048


EPSILON = 1e-05
ROPE_BASE = 10000.0

MESH = pl.DeviceIdType.MESH
F32 = jnp.float32
BF16 = jnp.bfloat16
LANES = 128
BLOCK = 512
COLS = 512
NEG = -1e30
SCORE_SCALE = math.log2(math.e) / math.sqrt(HEAD_DIM)


TILE = 256
ACROSS = 256
AHEAD = 3
RING = 8
TOTALS = 8
LAGS = (2, 5, 8, 12, 15)
OWN = 16
GUESTS = 10
EARLY = 24


def gradient_kinds(d_model, inner, ff):
    return ((d_model, ff), (ff, d_model), (inner, d_model), (d_model, 3 * inner))


def dot(a, b):
    return jnp.dot(a, b, preferred_element_type=F32)


def dot_t(a, b):
    return lax.dot_general(a, b, (((1,), (1,)), ((), ())), preferred_element_type=F32)


def t_dot(a, b):
    return lax.dot_general(a, b, (((0,), (0,)), ((), ())), preferred_element_type=F32)


def lane_low(rows):
    return lax.broadcasted_iota(jnp.int32, (rows, LANES), 1) < HEAD_DIM


def turn(values):
    return pltpu.roll(values, HEAD_DIM, 1)


def rotary(values, cos_ref, front_ref, back_ref, seq, sign):
    cos, front, back = cos_ref[seq], front_ref[seq], back_ref[seq]
    ahead = pltpu.roll(values, LANES - ROT // 2, 1)
    behind = pltpu.roll(values, ROT // 2, 1)
    return values * cos + sign * (ahead * front + behind * back)


def pair_up(first, second, low):
    return jnp.where(low, first, turn(second)), jnp.where(low, turn(first), second)


def relay_kernel(
    dims,
    lengths,
    x_hbm,
    cot_hbm,
    gain,
    shift,
    qkv_b,
    up_b,
    dense_b,
    down_b,
    wqkv_hbm,
    wdense_hbm,
    wup_hbm,
    wdown_hbm,
    out_hbm,
    ig_hbm,
    norm_hbm,
    g_hbm,
    mixed_hbm,
    hid_hbm,
    dpre_hbm,
    dpk_hbm,
    up_out,
    down_out,
    dense_out,
    qkv_out,
    guest_hbm,
    sums,
    small,
    bias_sums,
    cos,
    front,
    back,
    wqkv,
    wdense,
    wup,
    wdown,
    xfull,
    gfull,
    cot,
    qkv_r,
    mix_r,
    do_r,
    dqkv_r,
    rsf_r,
    rsb_r,
    qkv_st,
    o_st,
    do_st,
    dqkv_st,
    rsf_st,
    rsb_st,
    out_st,
    gx_st,
    ig_st,
    norm_st,
    mixed_st,
    hid_st,
    dpre_st,
    dpk_st,
    slope,
    part,
    part_b,
    dn1,
    qm,
    kr,
    vx,
    dox,
    dq,
    lse,
    delta,
    scores,
    peak,
    acc,
    wsem,
    ownx_sem,
    yx_s,
    yx_r,
    owng_sem,
    yg_s,
    yg_r,
    qkv_ss,
    qkv_rs,
    o_ss,
    o_rs,
    do_ss,
    do_rs,
    dqkv_ss,
    dqkv_rs,
    rsf_ss,
    rsf_rs,
    rsb_ss,
    rsb_rs,
    xs_ss,
    gs_ss,
    store_sem,
    g_store,
    core_r,
    outer_r,
    inner_r,
    turned,
    sums_r,
    op_sem,
    core_ss,
    core_rs,
    outer_rs,
    inner_rs,
    red_ss,
    bc_rs,
    tot_ss,
    fwd_ss,
    share_ss,
    fin_rs,
    sum_ss,
    sum_rs,
    guest_ss,
    guest_rs,
    core_free,
    outer_free,
    inner_free,
):
    micro, rows, group, wide, heads, d_model, ff = dims
    sect = lax.axis_index("section")
    tens = lax.axis_index("tensor")
    me = lax.axis_index("wide")
    pairs = heads // 2
    per_source = group + group // 2
    half = group // 2
    q_blocks = SEQ // BLOCK
    sources = BLOCK // group
    my_rows = pl.ds(pl.multiple_of(tens * rows, rows), rows)
    his_rows = pl.ds(pl.multiple_of((1 - tens) * rows, rows), rows)
    x_dev = {"section": 1 - sect}
    y_dev = {"tensor": 1 - tens}
    low_half = lane_low(half)
    low_group = lane_low(group)

    def remote(src, dst, ss, rs, dev):
        return pltpu.make_async_remote_copy(
            src_ref=src, dst_ref=dst, send_sem=ss, recv_sem=rs, device_id=dev, device_id_type=MESH
        )

    def arrived(ref, sem):
        pltpu.make_async_copy(ref, ref, sem).wait()

    def tokens_of(s):
        return pl.ds(pl.multiple_of(s * group, group), group)

    def y_send_x(s):
        own = xfull.at[s, my_rows]
        return remote(own, own, yx_s.at[s], yx_r.at[s], y_dev)

    def y_send_g(s):
        own = gfull.at[s, my_rows]
        return remote(own, own, yg_s.at[s], yg_r.at[s], y_dev)

    def spread(stage, target, seq, dest, ss, rs):
        @pl.when(dest == me)
        def _():
            pltpu.make_async_copy(stage, target.at[seq, me], rs).start()

        @pl.when(dest != me)
        def _():
            remote(stage, target.at[seq, me], ss, rs, {"wide": dest}).start()

    loads = [
        pltpu.make_async_copy(source, target, wsem.at[i])
        for i, (source, target) in enumerate(
            ((wqkv_hbm, wqkv), (wup_hbm, wup), (wdown_hbm, wdown), (wdense_hbm, wdense))
        )
    ]

    barrier = pltpu.get_barrier_semaphore()
    for dev in [x_dev, y_dev] + [{"wide": lax.rem(me + k, wide)} for k in range(1, wide)]:
        pl.semaphore_signal(barrier, inc=1, device_id=dev, device_id_type=MESH)

    @pl.when(sect == 0)
    def _():
        for s in range(micro):
            pltpu.make_async_copy(x_hbm.at[s], xfull.at[s, my_rows], ownx_sem.at[s]).start()

    for load in loads:
        load.start()

    @pl.when(sect == 1)
    def _():
        for s in range(micro):
            pltpu.make_async_copy(cot_hbm.at[s], cot.at[s], owng_sem.at[s]).start()

    def starts_of(s, tokens):
        found = jnp.zeros_like(tokens)
        end = jnp.int32(0)
        for j in range(lengths.shape[1]):
            end = end + lengths[s, j]
            found = jnp.where(tokens >= end, end, found)
        return found

    lane = lax.rem(lax.broadcasted_iota(jnp.int32, (8, LANES), 1), HEAD_DIM)
    number = lax.rem(lane, ROT // 2)
    freq = jnp.zeros((8, LANES), F32)
    for k in range(ROT // 2):
        freq = jnp.where(number == k, ROPE_BASE ** (-2.0 * k / ROT), freq)
    lane, freq = lane[0:1, :], freq[0:1, :]

    def table_step(s, carry):
        tokens = me * group + lax.broadcasted_iota(jnp.int32, (group, LANES), 0)
        angle = (tokens - starts_of(s, tokens)).astype(F32) * freq
        sine = jnp.sin(angle)
        cos[s] = jnp.where(lane < ROT, jnp.cos(angle), 1.0)
        front[s] = jnp.where(lane < ROT // 2, -sine, 0.0)
        back[s] = jnp.where((lane >= ROT // 2) & (lane < ROT), sine, 0.0)
        return carry

    lax.fori_loop(0, micro, table_step, 0)
    small[...] = jnp.zeros_like(small)
    bias_sums[...] = jnp.zeros_like(bias_sums)
    pl.semaphore_wait(barrier, wide + 1)

    @pl.when(sect == 0)
    def _():
        for s in range(micro):
            arrived(xfull.at[s, my_rows], ownx_sem.at[s])
            y_send_x(s).start()

    @pl.when(sect == 1)
    def _():
        for s in range(micro):
            arrived(cot.at[s], owng_sem.at[s])

            def chunk(i, carry, s=s):
                at = pl.ds(pl.multiple_of(i * 32, 32), 32)
                there = pl.ds(pl.multiple_of(tens * rows + i * 32, 32), 32)
                gfull[s, there, :] = cot[s, at, :].astype(BF16)
                return carry

            lax.fori_loop(0, rows // 32, chunk, 0)
            y_send_g(s).start()

    def fold(values):
        total = values[0:8]
        for k in range(1, values.shape[0] // 8):
            total = total + values[k * 8 : (k + 1) * 8]
        return total

    def normed_rows(values):
        center = jnp.mean(values, axis=-1, keepdims=True)
        centred = values - center
        spread_of = jnp.mean(centred * centred, axis=-1, keepdims=True)
        inv = lax.rsqrt(spread_of + EPSILON)
        return centred * inv, inv

    def unpack_heads(s):
        def step(src, carry):
            qk = qkv_r[s, src, 0:group, :].astype(F32)
            at = pl.multiple_of(src * group, group)
            qm[pl.ds(at, group), :] = jnp.where(low_group, qk, 0.0).astype(BF16)
            kr[pl.ds(at, group), :] = turn(qk).astype(BF16)
            packed_v = qkv_r[s, src, group:per_source, :].astype(F32)
            ones = jnp.where(
                lax.broadcasted_iota(jnp.int32, (half, LANES), 1) == HEAD_DIM, 1.0, 0.0
            )
            vx[pl.ds(at, half), :] = jnp.where(low_half, packed_v, ones).astype(BF16)
            vx[pl.ds(pl.multiple_of(at + half, half), half), :] = jnp.where(
                low_half, turn(packed_v), ones
            ).astype(BF16)
            return carry

        lax.fori_loop(0, wide, step, 0, unroll=True)

    def forward_meet(s):
        arrived(xfull.at[s, my_rows], ownx_sem.at[s])
        y_send_x(s).start()

    def backward_meet(s):
        arrived(gfull.at[s, my_rows], owng_sem.at[s])
        y_send_g(s).start()

    def forward(s):
        arrived(xfull.at[s, his_rows], yx_r.at[s])

        def norm_step(i, carry):
            at = pl.ds(pl.multiple_of(i * 32, 32), 32)
            a, _ = normed_rows(xfull[s, at, :].astype(F32))
            norm_st[0, at, :] = (a * gain[0:1, :] + shift[0:1, :]).astype(BF16)
            norm_st[1, at, :] = (a * gain[1:2, :] + shift[1:2, :]).astype(BF16)
            return carry

        @pl.when(s > 0)
        def _():
            arrived(norm_st.at[0], store_sem.at[0])
            arrived(norm_st.at[1], store_sem.at[1])

        lax.fori_loop(0, group // 32, norm_step, 0, unroll=True)
        pltpu.make_async_copy(norm_st.at[0], norm_hbm.at[0, tokens_of(s)], store_sem.at[0]).start()
        pltpu.make_async_copy(norm_st.at[1], norm_hbm.at[1, tokens_of(s)], store_sem.at[1]).start()

        def qkv_step(k, carry):
            pair = lax.rem(me // 2 + 1 + k, pairs)
            cols = pl.ds(pl.multiple_of(pair * 3 * LANES, LANES), 3 * LANES)
            packed = dot(norm_st[0], wqkv[:, cols]) + qkv_b[:, cols]
            first, middle, last = (packed[:, i * LANES : (i + 1) * LANES] for i in range(3))
            qk0 = rotary(first, cos, front, back, s, 1.0)
            qk1 = rotary(
                turn(jnp.where(low_group, last, middle)), cos, front, back, s, 1.0
            )
            vv = jnp.where(low_group, middle, last)
            v0 = jnp.where(low_half, vv[:half], turn(vv[half:]))
            v1 = jnp.where(low_half, turn(vv[:half]), vv[half:])
            for i, (qk, v) in enumerate(((qk0, v0), (qk1, v1))):
                qkv_st[2 * pair + i, 0:group, :] = qk.astype(BF16)
                qkv_st[2 * pair + i, group:per_source, :] = v.astype(BF16)
            for i in range(2):
                dest = 2 * pair + i
                spread(qkv_st.at[dest], qkv_r, s, dest, qkv_ss.at[0], qkv_rs.at[s])
            return carry

        pl.when(s == 0)(loads[0].wait)
        lax.fori_loop(0, pairs, qkv_step, 0, unroll=True)

    def forward_ff(s):
        @pl.when(s == 0)
        def _():
            loads[1].wait()
            loads[2].wait()

        @pl.when(s > 0)
        def _():
            arrived(hid_st, store_sem.at[2])

        def ff_step(j, carry):
            cols = pl.ds(pl.multiple_of(j * COLS, COLS), COLS)
            pre = dot(norm_st[1], wup[:, cols]) + up_b[:, cols]
            cumul = 0.5 * (1.0 + lax.erf(pre * (1.0 / math.sqrt(2.0))))
            density = jnp.exp(-0.5 * pre * pre) * (1.0 / math.sqrt(2.0 * math.pi))
            hid = (pre * cumul).astype(BF16)
            hid_st[:, cols] = hid
            slope[s, :, cols] = (cumul + pre * density).astype(BF16)
            term = dot(hid, wdown[cols, :])

            @pl.when(j == 0)
            def _():
                part[...] = term

            @pl.when(j > 0)
            def _():
                part[...] += term

            return carry

        lax.fori_loop(0, ff // COLS, ff_step, 0, unroll=True)
        pltpu.make_async_copy(hid_st, hid_hbm.at[tokens_of(s)], store_sem.at[2]).start()

    def forward_attention(s):
        arrived(qkv_r.at[s], qkv_rs.at[s])
        arrived(qkv_st.at[pl.ds(0, wide - 1)], qkv_ss.at[0])
        unpack_heads(s)

        for i in range(q_blocks):
            q_at = slice(i * BLOCK, (i + 1) * BLOCK)
            tokens = i * BLOCK + lax.broadcasted_iota(jnp.int32, (BLOCK, LANES), 0)
            begin = starts_of(s, tokens)[:, 0:1]
            best = jnp.full((BLOCK, LANES), NEG, F32)
            for j in range(i + 1):
                k_at = slice(j * BLOCK, (j + 1) * BLOCK)
                raw = dot_t(qm[q_at, :], kr[k_at, :])
                u = j * BLOCK + lax.broadcasted_iota(jnp.int32, (BLOCK, BLOCK), 1)
                seen = u >= begin
                if i == j:
                    seen = seen & (u <= tokens[:, 0:1])
                raw = jnp.where(seen, raw, NEG)
                scores[:, k_at] = raw
                for k in range(BLOCK // LANES):
                    best = jnp.maximum(best, raw[:, k * LANES : (k + 1) * LANES])
            top = jnp.max(best, axis=1, keepdims=True) * SCORE_SCALE
            out = jnp.zeros((BLOCK, LANES), F32)
            for j in range(i + 1):
                k_at = slice(j * BLOCK, (j + 1) * BLOCK)
                probs = jnp.exp2(scores[:, k_at] * SCORE_SCALE - top)
                out = out + dot(probs.astype(BF16), vx[k_at, :])
            total = out[:, HEAD_DIM : HEAD_DIM + 1]
            out = out / total
            log_total = top + jnp.log2(total)
            lse[s, i] = jnp.broadcast_to(log_total, (BLOCK, LANES)).T[0:8, :]
            for k in range(sources):
                first = out[k * group : k * group + half]
                second = out[k * group + half : (k + 1) * group]
                source = i * sources + k
                o_st[s, source] = jnp.where(low_half, first, turn(second)).astype(BF16)
                spread(o_st.at[s, source], mix_r, s, source, o_ss.at[s], o_rs.at[s])

    def forward_out(s):
        arrived(mix_r.at[s], o_rs.at[s])
        arrived(o_st.at[s, pl.ds(0, wide - 1)], o_ss.at[s])
        pl.when((s == 0) & (sect == 0))(loads[3].wait)
        pl.when(s > 0)(lambda: arrived(mixed_st, store_sem.at[3]))
        for pair in range(pairs):
            top, bottom = pair_up(
                mix_r[s, 2 * pair].astype(F32), mix_r[s, 2 * pair + 1].astype(F32), low_half
            )
            mixed_st[0:half, pair * LANES : (pair + 1) * LANES] = top.astype(BF16)
            mixed_st[half:group, pair * LANES : (pair + 1) * LANES] = bottom.astype(BF16)
        pltpu.make_async_copy(mixed_st, mixed_hbm.at[tokens_of(s)], store_sem.at[3]).start()
        part[...] += dot(mixed_st[...], wdense[...])
        rsf_st[...] = part[his_rows, :].astype(BF16)
        remote(rsf_st, rsf_r.at[s], rsf_ss.at[0], rsf_rs.at[s], y_dev).start()

    def forward_end(s):
        arrived(rsf_r.at[s], rsf_rs.at[s])
        arrived(rsf_st, rsf_ss.at[0])

        @pl.when(s > 0)
        def _():
            arrived(out_st, store_sem.at[4])
            pl.when(sect == 0)(lambda: arrived(out_st, xs_ss.at[0]))

        def out_step(i, carry):
            at = pl.ds(pl.multiple_of(i * 32, 32), 32)
            there = pl.ds(pl.multiple_of(tens * rows + i * 32, 32), 32)
            branch = part[there, :] + rsf_r[s, at, :].astype(F32) + (dense_b[...] + down_b[...])
            out_st[at, :] = (xfull[s, there, :].astype(F32) + branch).astype(BF16)
            return carry

        lax.fori_loop(0, rows // 32, out_step, 0, unroll=True)

        @pl.when(sect == 0)
        def _():
            remote(out_st, xfull.at[s, my_rows], xs_ss.at[0], ownx_sem.at[s], x_dev).start()

        pltpu.make_async_copy(out_st, out_hbm.at[s], store_sem.at[4]).start()

    def backward(s):
        arrived(gfull.at[s, his_rows], yg_r.at[s])
        pl.when((s == 0) & (sect == 1))(loads[3].wait)
        pltpu.make_async_copy(gfull.at[s], g_hbm.at[tokens_of(s)], g_store.at[s]).start()

        def mixed_step(k, carry):
            pair = lax.rem(me // 2 + 1 + k, pairs)
            at = pl.ds(pl.multiple_of(pair * LANES, LANES), LANES)
            both = dot_t(gfull[s], wdense[at, :])
            first = jnp.where(low_half, both[:half], turn(both[half:]))
            second = jnp.where(low_half, turn(both[:half]), both[half:])
            do_st[s, 2 * pair] = first.astype(BF16)
            do_st[s, 2 * pair + 1] = second.astype(BF16)
            for i in range(2):
                dest = 2 * pair + i
                spread(do_st.at[s, dest], do_r, s, dest, do_ss.at[s], do_rs.at[s])
            return carry

        lax.fori_loop(0, pairs, mixed_step, 0, unroll=True)

    def backward_ff(s):
        pl.when(s > 0)(lambda: arrived(dpre_st, store_sem.at[6]))

        def ff_step(j, carry):
            cols = pl.ds(pl.multiple_of(j * COLS, COLS), COLS)
            grad = dot_t(gfull[s], wdown[cols, :])
            grad = (grad * slope[s, :, cols].astype(F32)).astype(BF16)
            dpre_st[:, cols] = grad
            sums_at = pl.ds(pl.multiple_of(3 * heads * HEAD_DIM + j * COLS, COLS), COLS)
            bias_sums[:, sums_at] += fold(grad.astype(F32))
            term = dot_t(grad, wup[:, cols])

            @pl.when(j == 0)
            def _():
                dn1[...] = term

            @pl.when(j > 0)
            def _():
                dn1[...] += term

            return carry

        lax.fori_loop(0, ff // COLS, ff_step, 0, unroll=True)
        pltpu.make_async_copy(dpre_st, dpre_hbm.at[tokens_of(s)], store_sem.at[6]).start()

    def backward_attention(s):
        arrived(do_r.at[s], do_rs.at[s])
        arrived(do_st.at[s, pl.ds(0, wide - 1)], do_ss.at[s])
        pl.when(sect == 0)(lambda: unpack_heads(s))

        def unpack_step(src, carry):
            at = pl.multiple_of(src * group, group)
            grad = do_r[s, src].astype(F32)
            dox[pl.ds(at, half), :] = jnp.where(low_half, grad, 0.0).astype(BF16)
            dox[pl.ds(pl.multiple_of(at + half, half), half), :] = jnp.where(
                low_half, turn(grad), 0.0
            ).astype(BF16)
            product = grad * o_st[s, src].astype(F32)
            left = jnp.sum(jnp.where(low_half, product, 0.0), axis=1, keepdims=True)
            right = jnp.sum(jnp.where(low_half, 0.0, product), axis=1, keepdims=True)
            delta[src, :, 0:half] = jnp.broadcast_to(left, (half, LANES)).T[0:8, :]
            delta[src, :, half:group] = jnp.broadcast_to(right, (half, LANES)).T[0:8, :]
            return carry

        lax.fori_loop(0, wide, unpack_step, 0, unroll=True)
        slot = lax.rem(s, 2)
        rows_of = []
        for i in range(q_blocks):
            tokens = i * BLOCK + lax.broadcasted_iota(jnp.int32, (8, BLOCK), 1)
            inner_sum = jnp.concatenate(
                [delta[i * sources + k, 0:1, :] for k in range(sources)], axis=1
            )
            rows_of.append((starts_of(s, tokens)[0:1, :], tokens[0:1, :], inner_sum))
        for j in range(q_blocks):
            k_at = slice(j * BLOCK, (j + 1) * BLOCK)
            for i in range(j, q_blocks):
                q_at = slice(i * BLOCK, (i + 1) * BLOCK)
                begin, token, inner_sum = rows_of[i]
                raw = dot_t(kr[k_at, :], qm[q_at, :])
                u = j * BLOCK + lax.broadcasted_iota(jnp.int32, (BLOCK, BLOCK), 0)
                probs = jnp.exp2(raw * SCORE_SCALE - lse[s, i, 0:1, :])
                seen = u >= begin
                if i == j:
                    seen = seen & (u <= token)
                probs = jnp.where(seen, probs, 0.0)
                probs_grad = dot_t(vx[k_at, :], dox[q_at, :])
                score_grad = (probs * (probs_grad - inner_sum)).astype(BF16)
                value_term = dot(probs.astype(BF16), dox[q_at, :])
                key_term = dot(score_grad, kr[q_at, :])
                query_term = t_dot(score_grad, kr[k_at, :])
                if i == j:
                    acc[...] = value_term
                    peak[...] = key_term
                else:
                    acc[...] += value_term
                    peak[...] += key_term
                if j == 0:
                    dq[q_at, :] = query_term
                else:
                    dq[q_at, :] += query_term
            for k in range(sources):
                source = j * sources + k
                mine = slice(k * group, (k + 1) * group)
                at = slice(source * group, (source + 1) * group)
                both = jnp.where(low_group, dq[at, :], peak[mine, :])
                both = both * (1.0 / math.sqrt(HEAD_DIM))
                value = acc[mine, :]
                value = jnp.where(low_half, value[:half], turn(value[half:]))
                dqkv_st[slot, source, 0:group, :] = both.astype(BF16)
                dqkv_st[slot, source, group:per_source, :] = value.astype(BF16)
                spread(
                    dqkv_st.at[slot, source], dqkv_r, s, source, dqkv_ss.at[slot], dqkv_rs.at[s]
                )

    def backward_norm(s):
        arrived(dqkv_r.at[s], dqkv_rs.at[s])
        slot = lax.rem(s, 2)
        arrived(dqkv_st.at[slot, pl.ds(0, wide - 1)], dqkv_ss.at[slot])
        pl.when(s > 0)(lambda: arrived(dpk_st, store_sem.at[7]))

        def pair_step(pair, carry):
            qk0 = rotary(
                dqkv_r[s, 2 * pair, 0:group, :].astype(F32), cos, front, back, s, -1.0
            )
            qk1 = turn(
                rotary(
                    dqkv_r[s, 2 * pair + 1, 0:group, :].astype(F32), cos, front, back, s, -1.0
                )
            )
            top, bottom = pair_up(
                dqkv_r[s, 2 * pair, group:per_source, :].astype(F32),
                dqkv_r[s, 2 * pair + 1, group:per_source, :].astype(F32),
                low_half,
            )
            vv = jnp.concatenate([top, bottom], axis=0)
            columns = (qk0, jnp.where(low_group, vv, qk1), jnp.where(low_group, qk1, vv))
            for k, column in enumerate(columns):
                at = pl.ds(pl.multiple_of((pair * 3 + k) * LANES, LANES), LANES)
                column = column.astype(BF16)
                dpk_st[:, at] = column
                bias_sums[:, at] += fold(column.astype(F32))
            return carry

        lax.fori_loop(0, pairs, pair_step, 0, unroll=True)
        pltpu.make_async_copy(dpk_st, dpk_hbm.at[tokens_of(s)], store_sem.at[7]).start()
        part_b[...] = dot_t(dpk_st[...], wqkv[...])

        def e_step(i, carry):
            at = pl.ds(pl.multiple_of(i * 32, 32), 32)
            a, _ = normed_rows(xfull[s, at, :].astype(F32))
            first = part_b[at, :]
            second = dn1[at, :]
            small[0] += fold(first * a)
            small[1] += fold(second * a)
            small[2] += fold(first)
            small[3] += fold(second)
            part_b[at, :] = first * gain[0:1, :] + second * gain[1:2, :]
            return carry

        lax.fori_loop(0, group // 32, e_step, 0, unroll=True)
        rsb_st[...] = part_b[his_rows, :].astype(BF16)
        remote(rsb_st, rsb_r.at[s], rsb_ss.at[0], rsb_rs.at[s], y_dev).start()

    def backward_end(s):
        arrived(rsb_r.at[s], rsb_rs.at[s])
        arrived(rsb_st, rsb_ss.at[0])

        @pl.when(s > 0)
        def _():
            arrived(ig_st, store_sem.at[8])
            pl.when(sect == 1)(lambda: arrived(gx_st, gs_ss.at[0]))

        def in_step(i, carry):
            at = pl.ds(pl.multiple_of(i * 32, 32), 32)
            there = pl.ds(pl.multiple_of(tens * rows + i * 32, 32), 32)
            a, inv = normed_rows(xfull[s, there, :].astype(F32))
            e = part_b[there, :] + rsb_r[s, at, :].astype(F32)
            mean_e = jnp.mean(e, axis=-1, keepdims=True)
            cross = jnp.mean(e * a, axis=-1, keepdims=True)
            g_low = gfull[s, there, :].astype(F32)
            small[4] += fold(g_low)
            g = jnp.where(sect == 1, cot[s, at, :], g_low)
            grad = g + inv * (e - mean_e - a * cross)
            ig_st[at, :] = grad
            gx_st[at, :] = grad.astype(BF16)
            return carry

        lax.fori_loop(0, rows // 32, in_step, 0, unroll=True)

        @pl.when(s == micro - 1)
        def _():
            for k in range(micro):
                arrived(xfull.at[k, my_rows], yx_s.at[k])

        @pl.when(sect == 1)
        def _():
            remote(gx_st, gfull.at[s, my_rows], gs_ss.at[0], owng_sem.at[s], x_dev).start()

        pltpu.make_async_copy(ig_st, ig_hbm.at[s], store_sem.at[8]).start()

    chip, core = me // 2, lax.rem(me, 2)
    partner = {"wide": me + 1 - 2 * core}
    up_dev = {"wide": lax.rem(me + 2, wide)}
    down_dev = {"wide": lax.rem(me + wide - 2, wide)}
    at_bottom, at_top = chip == 0, chip == wide // 2 - 1
    at_end = at_bottom | at_top
    middle = jnp.logical_not(at_end)
    lower = chip == 1
    outer_of = {"wide": jnp.where(lower, me - 2, lax.rem(me + 2, wide))}
    inner_of = {"wide": jnp.where(lower, me + 2, lax.rem(me + wide - 2, wide))}
    end_of = {"wide": jnp.where(at_bottom, me + 2, lax.rem(me + wide - 2, wide))}
    kinds = gradient_kinds(d_model, heads * HEAD_DIM, ff)
    targets = (up_out, down_out, dense_out, qkv_out)
    operands = (
        (norm_hbm.at[1], dpre_hbm),
        (hid_hbm, g_hbm),
        (mixed_hbm, g_hbm),
        (norm_hbm.at[0], dpk_hbm),
    )
    ranges, first = [], 0
    for height, width in kinds:
        count = (height // TILE) * (width // (2 * ACROSS))
        ranges.append((first, first + count, width // (2 * ACROSS)))
        first += count
    steps = first

    def own_at(ring):
        rows_at = pl.ds(pl.multiple_of((ring // RING) * TILE, TILE), TILE)
        return scores.at[
            rows_at, pl.ds(pl.multiple_of(lax.rem(ring, RING) * ACROSS, ACROSS), ACROSS)
        ]

    def guest_at(number):
        cols = pl.ds(pl.multiple_of(lax.rem(number, 4) * ACROSS, ACROSS), ACROSS)
        return xfull.at[number // 4, :, cols]

    def guest_st_at(slot):
        return mixed_st.at[:, pl.ds(pl.multiple_of(slot * ACROSS, ACROSS), ACROSS)]

    def core_st_at(ring):
        return hid_st.at[:, pl.ds(pl.multiple_of(ring * ACROSS, ACROSS), ACROSS)]

    def red_st_at(ring):
        return dpre_st.at[:, pl.ds(pl.multiple_of(ring * ACROSS, ACROSS), ACROSS)]

    def tot_at(slot):
        cols = pl.ds(pl.multiple_of(lax.rem(slot, 4) * ACROSS, ACROSS), ACROSS)
        return norm_st.at[slot // 4, :, cols]

    def left_at(slot):
        return wup.at[:, pl.ds(pl.multiple_of(slot * TILE, TILE), TILE)]

    def right_at(slot):
        return wdown.at[
            pl.ds(pl.multiple_of((slot // 2) * d_model, d_model), d_model),
            pl.ds(pl.multiple_of(lax.rem(slot, 2) * 2 * ACROSS, 2 * ACROSS), 2 * ACROSS),
        ]

    tile_ref = core_r.at[0]

    def by_kind(m, body):
        for kind, (low, high, across) in enumerate(ranges):

            @pl.when((m >= low) & (m < high))
            def _(kind=kind, low=low, across=across):
                at = m - low
                body(kind, at // across, lax.rem(at, across))

    def tile_of(kind, row, col, which):
        return targets[kind].at[
            pl.ds(pl.multiple_of(row * TILE, TILE), TILE),
            pl.ds(pl.multiple_of((2 * col + which) * ACROSS, ACROSS), ACROSS),
        ]

    def fetch(m):
        pl.when(m == ranges[3][0])(lambda: arrived(dpk_st, store_sem.at[7]))

        def body(kind, row, col):
            left, right = operands[kind]
            slot = lax.rem(m, AHEAD + 1)

            @pl.when(col == 0)
            def _():
                pltpu.make_async_copy(
                    left.at[:, pl.ds(pl.multiple_of(row * TILE, TILE), TILE)],
                    left_at(slot),
                    op_sem.at[0, slot],
                ).start()

            pltpu.make_async_copy(
                right.at[:, pl.ds(pl.multiple_of(col * 2 * ACROSS, 2 * ACROSS), 2 * ACROSS)],
                right_at(slot),
                op_sem.at[1, slot],
            ).start()

        by_kind(m, body)

    chain = jnp.where(sect == 1, steps + GUESTS, steps - GUESTS)

    def place(m):
        shared = (sect == 0) & (m < 2 * GUESTS)
        away = shared & (lax.rem(m, 2) == 1)
        visitor = (sect == 1) & (m >= steps)
        n = jnp.where(shared, m // 2, jnp.where(sect == 0, m - GUESTS, m))
        number = jnp.where(visitor, m - steps, m // 2)
        tile = jnp.where(visitor, 2 * (m - steps) + 1, m)
        return away, visitor, n, number, tile

    def is_root(n):
        return middle & (chip == 1 + lax.rem(n, 2))

    def products(m):
        slot, ring = lax.rem(m, AHEAD + 1), lax.rem(m, RING)

        def body(kind, row, col):
            @pl.when(col == 0)
            def _():
                arrived(left_at(slot), op_sem.at[0, slot])
                turned[...] = left_at(slot)[...].T

        by_kind(m, body)
        arrived(right_at(slot), op_sem.at[1, slot])
        both = dot(turned[...], right_at(slot)[...])
        first, second = both[:, :ACROSS], both[:, ACROSS:]
        own_at(lax.rem(m, OWN))[...] = jnp.where(core == 0, first, second)

        @pl.when(m >= RING)
        def _():
            arrived(tile_ref, core_ss.at[ring])
            pl.semaphore_wait(core_free, 1)

        core_st_at(ring)[...] = jnp.where(core == 0, second, first).astype(BF16)
        remote(
            core_st_at(ring), core_r.at[ring], core_ss.at[ring], core_rs.at[ring], partner
        ).start()

    def send_red(m, value, target, sem, dev, free):
        ring = lax.rem(m, RING)

        @pl.when(m >= RING)
        def _():
            pl.semaphore_wait(free, 1)

        red_st_at(ring)[...] = value.astype(BF16)
        remote(red_st_at(ring), target.at[ring], red_ss.at[ring], sem.at[ring], dev).start()

    def chip_sum(m):
        away, visitor, n, number, _ = place(m)
        ring = lax.rem(m, RING)
        own = own_at(lax.rem(m, OWN))

        @pl.when(visitor)
        def _():
            arrived(tile_ref, guest_rs.at[number])
            own[...] = guest_at(number)[...].astype(F32)

        @pl.when(jnp.logical_not(visitor))
        def _():
            arrived(tile_ref, core_rs.at[ring])
            own[...] = own[...] + core_r[ring].astype(F32)

            @pl.when(m + RING < steps)
            def _():
                pl.semaphore_signal(core_free, inc=1, device_id=partner, device_id_type=MESH)

        @pl.when(away)
        def _():
            slot = lax.rem(number, 2)
            pl.when(number >= 2)(lambda: arrived(tile_ref, guest_ss.at[slot]))
            guest_st_at(slot)[...] = own[...].astype(BF16)
            remote(
                guest_st_at(slot),
                guest_at(number),
                guest_ss.at[slot],
                guest_rs.at[number],
                x_dev,
            ).start()

        @pl.when(at_end & jnp.logical_not(away))
        def _():
            pl.when(n >= RING)(lambda: arrived(tile_ref, red_ss.at[lax.rem(n, RING)]))
            send_red(n, own[...], outer_r, outer_rs, end_of, outer_free.at[lax.rem(n, 2)])

    def take_outer(m, n):
        ring = lax.rem(n, RING)
        arrived(tile_ref, outer_rs.at[ring])
        total = own_at(lax.rem(m, OWN))[...] + outer_r[ring].astype(F32)

        @pl.when(n + RING < chain)
        def _():
            pl.semaphore_signal(
                outer_free.at[lax.rem(n, 2)], inc=1, device_id=outer_of, device_id_type=MESH
            )

        return total

    def pass_in(m):
        _, _, n, _, _ = place(m)
        total = take_outer(m, n)
        pl.when(n >= RING)(lambda: arrived(tile_ref, red_ss.at[lax.rem(n, RING)]))
        send_red(n, total, inner_r, inner_rs, inner_of, inner_free)

    def finish(m):
        _, visitor, n, number, tile = place(m)
        ring = lax.rem(n, RING)
        slot = lax.rem(n // 2, TOTALS)
        total = take_outer(m, n)
        arrived(tile_ref, inner_rs.at[ring])
        total = total + inner_r[ring].astype(F32)

        @pl.when(n + RING < chain)
        def _():
            pl.semaphore_signal(inner_free, inc=1, device_id=inner_of, device_id_type=MESH)

        @pl.when(n >= 2 * TOTALS)
        def _():
            for k in range(4):
                arrived(tile_ref, tot_ss.at[k, slot])

        tot_at(slot)[...] = total.astype(BF16)

        def send(here):
            remote(tot_at(slot), here, tot_ss.at[0, slot], bc_rs.at[m], outer_of).start()
            remote(tot_at(slot), here, tot_ss.at[1, slot], bc_rs.at[m], inner_of).start()
            pltpu.make_async_copy(tot_at(slot), here, tot_ss.at[3, slot]).start()

        def body(kind, row, col):
            here = tile_of(kind, row, col, core)

            @pl.when(visitor)
            def _():
                send(guest_hbm.at[number])
                remote(tot_at(slot), here, tot_ss.at[2, slot], bc_rs.at[tile], x_dev).start()

            @pl.when(jnp.logical_not(visitor))
            def _():
                send(here)
                remote(
                    tot_at(slot), here, tot_ss.at[2, slot], fin_rs.at[kind], partner
                ).start()

        by_kind(tile, body)

    def hand_on(m):
        _, visitor, _, number, tile = place(m)
        arrived(tile_ref, bc_rs.at[m])

        def body(kind, row, col):
            here = tile_of(kind, row, col, core)

            @pl.when(visitor)
            def _():
                held = guest_hbm.at[number]

                @pl.when(middle)
                def _():
                    remote(held, held, fwd_ss.at[m], bc_rs.at[m], outer_of).start()

                remote(held, here, share_ss.at[m], bc_rs.at[tile], x_dev).start()

            @pl.when(jnp.logical_not(visitor))
            def _():
                @pl.when(middle)
                def _():
                    remote(here, here, fwd_ss.at[m], bc_rs.at[m], outer_of).start()

                remote(here, here, share_ss.at[m], fin_rs.at[kind], partner).start()

        by_kind(tile, body)

    def guest_home(number, carry):
        m = 2 * number + 1
        arrived(tile_ref, bc_rs.at[m])

        def body(kind, row, col):
            here = tile_of(kind, row, col, core)
            remote(here, here, share_ss.at[m], fin_rs.at[kind], partner).start()

        by_kind(m, body)
        return carry

    exchanges = (
        {"tensor": 1 - tens},
        partner,
        {"wide": me + 2 - 4 * lax.rem(chip, 2)},
        {"wide": me + 4 - 8 * (chip // 2)},
    )

    def sums_begin():
        sums[:, 0:d_model] = jnp.concatenate(
            [jnp.sum(small[k], axis=0, keepdims=True) for k in range(5)]
            + [jnp.zeros((3, d_model), F32)],
            axis=0,
        )
        total = jnp.sum(bias_sums[...], axis=0, keepdims=True)
        lines = [total[:, k * COLS : (k + 1) * COLS] for k in range(total.shape[1] // COLS)]
        lines.append(jnp.zeros((8 - len(lines), COLS), F32))
        sums[:, d_model:] = jnp.concatenate(lines, axis=0)

    def exchange_start(k):
        if k == 0:
            sums_begin()
        else:
            arrived(sums, sum_ss.at[0])
        sums_r[0] = sums[...]
        remote(sums_r.at[0], sums_r.at[k + 1], sum_ss.at[0], sum_rs.at[k], exchanges[k]).start()

    def exchange_end(k):
        arrived(sums, sum_rs.at[k])
        if k == 0:
            sums[:, 0:d_model] += sums_r[1, :, 0:d_model]
        else:
            sums[...] += sums_r[k + 1]

    def gradient_step(i, carry):
        pl.when(i + AHEAD < steps)(lambda: fetch(i + AHEAD))
        pl.when(i < steps)(lambda: products(i))
        for k in range(4):
            pl.when(i == EARLY + 4 * k + 2)(lambda k=k: exchange_start(k))
            pl.when(i == EARLY + 4 * k + 5)(lambda k=k: exchange_end(k))

        def late(lag, allowed, body):
            m = i - lag
            away, _, n, _, _ = place(m)
            inside = (m >= 0) & (m < jnp.where(sect == 1, steps + GUESTS, steps))
            pl.when(inside & allowed(away, n))(lambda: body(m))

        def outside(away, n):
            return middle & jnp.logical_not(away | is_root(n))

        late(LAGS[0], lambda away, n: n >= 0, chip_sum)
        late(LAGS[1], outside, pass_in)
        late(LAGS[2], lambda away, n: is_root(n) & jnp.logical_not(away), finish)
        late(LAGS[3], outside, hand_on)
        late(LAGS[4], lambda away, n: at_end & jnp.logical_not(away), hand_on)
        return carry

    def gradient_begin():
        arrived(norm_st.at[0], store_sem.at[0])
        arrived(norm_st.at[1], store_sem.at[1])
        arrived(hid_st, store_sem.at[2])
        arrived(mixed_st, store_sem.at[3])
        arrived(dpre_st, store_sem.at[6])
        for s in range(micro):
            arrived(gfull.at[s], g_store.at[s])
        for m in range(AHEAD):
            fetch(jnp.int32(m))

    def at(seq, allowed, body):
        pl.when(allowed & (seq >= 0) & (seq < micro))(lambda: body(seq))

    @pl.when(sect == 1)
    def _():
        lax.fori_loop(0, micro, lambda s, carry: (backward(s), carry)[1], 0)

    first = jnp.int32(0)
    pl.when(sect == 1)(lambda: forward_meet(first))
    forward(first)
    forward_ff(first)
    always = sect >= 0

    def step(i, carry):
        f = i
        b = jnp.where(sect == 1, i, i - micro)
        at(b, (sect == 0) & (b == 0), backward_meet)
        at(b, sect == 0, backward)
        at(f + 1, sect == 1, forward_meet)
        at(f, always, forward_attention)
        at(f + 1, always, forward)
        at(b, always, backward_attention)
        at(b - 1, always, backward_norm)
        at(f, always, forward_out)
        at(b, always, backward_ff)
        at(b + 1, (sect == 0) & (b >= 0), backward_meet)
        at(b - 1, always, backward_end)
        at(f, always, forward_end)
        at(f + 1, always, forward_ff)

        starts = jnp.where(sect == 1, i == micro, i == 2 * micro - 1)
        goes_on = (sect == 0) & (i == 2 * micro)
        pl.when(starts)(gradient_begin)
        low = jnp.where(goes_on, EARLY, 0)
        high = jnp.where(
            goes_on | (starts & (sect == 1)),
            steps + LAGS[4] + jnp.where(sect == 1, GUESTS, 0),
            jnp.where(starts, EARLY, 0),
        )
        lax.fori_loop(low, high, gradient_step, 0)
        return carry

    lax.fori_loop(0, jnp.where(sect == 1, micro + 1, 2 * micro + 1), step, 0)

    for s in range(micro):
        arrived(gfull.at[s, my_rows], yg_s.at[s])
    arrived(out_st, store_sem.at[4])
    arrived(ig_st, store_sem.at[8])
    pl.when(sect == 0)(lambda: arrived(out_st, xs_ss.at[0]))
    pl.when(sect == 1)(lambda: arrived(gx_st, gs_ss.at[0]))

    arrived(sums, sum_ss.at[0])
    for ring in range(RING):
        arrived(tile_ref, core_ss.at[ring])

    @pl.when(sect == 0)
    def _():
        lax.fori_loop(0, GUESTS, guest_home, 0)
        for slot in range(2):
            arrived(tile_ref, guest_ss.at[slot])

    def drain(m, carry):
        away, _, n, _, _ = place(m)
        root = is_root(n)
        stays = jnp.logical_not(away)
        ring = lax.rem(n, RING)
        sends = at_end | (middle & jnp.logical_not(root))
        pl.when(stays & sends & (n + RING >= chain))(lambda: arrived(tile_ref, red_ss.at[ring]))

        @pl.when(stays & root & (n + 2 * TOTALS >= chain))
        def _():
            for k in range(4):
                arrived(tile_ref, tot_ss.at[k, lax.rem(n // 2, TOTALS)])

        @pl.when(stays & middle & jnp.logical_not(root))
        def _():
            arrived(tile_ref, fwd_ss.at[m])

        pl.when(away | jnp.logical_not(root))(lambda: arrived(tile_ref, share_ss.at[m]))
        return carry

    lax.fori_loop(0, jnp.where(sect == 1, steps + GUESTS, steps), drain, 0)
    for kind, (height, width) in enumerate(kinds):
        arrived(targets[kind].at[pl.ds(0, height // 2)], fin_rs.at[kind])


def relay(dims, doc_lengths, block_input, cotangent, weights, collective_id):
    micro, rows, group, wide, heads, d_model, ff = dims
    (
        norm_gain,
        norm_bias,
        qkv_weight,
        qkv_bias,
        dense_weight,
        dense_bias,
        up_weight,
        up_bias,
        down_weight,
        down_bias,
    ) = weights
    inner = heads * HEAD_DIM
    per_source = group + group // 2
    anywhere = pl.BlockSpec(memory_space=pl.ANY)
    local = pl.BlockSpec(memory_space=pltpu.VMEM)
    scalars = pl.BlockSpec(memory_space=pltpu.SMEM)
    dma = pltpu.SemaphoreType.DMA
    vmem = pltpu.VMEM
    outs = [
        jax.ShapeDtypeStruct((micro, rows, d_model), BF16),
        jax.ShapeDtypeStruct((micro, rows, d_model), F32),
        jax.ShapeDtypeStruct((2, micro * group, d_model), BF16),
        jax.ShapeDtypeStruct((micro * group, d_model), BF16),
        jax.ShapeDtypeStruct((micro * group, inner), BF16),
        jax.ShapeDtypeStruct((micro * group, ff), BF16),
        jax.ShapeDtypeStruct((micro * group, ff), BF16),
        jax.ShapeDtypeStruct((micro * group, 3 * inner), BF16),
    ]
    kinds = gradient_kinds(d_model, inner, ff)
    steps = sum((height // TILE) * (width // (2 * ACROSS)) for height, width in kinds)
    outs += [jax.ShapeDtypeStruct(kind, BF16) for kind in kinds]
    outs += [jax.ShapeDtypeStruct((GUESTS, TILE, ACROSS), BF16)]
    outs += [jax.ShapeDtypeStruct((8, d_model + COLS), F32)]
    regular = pltpu.SemaphoreType.REGULAR
    scratch = [
        vmem((5, 8, d_model), F32),
        vmem((8, 3 * inner + ff), F32),
        vmem((micro, group, LANES), F32),
        vmem((micro, group, LANES), F32),
        vmem((micro, group, LANES), F32),
        vmem(qkv_weight.shape, BF16),
        vmem(dense_weight.shape, BF16),
        vmem(up_weight.shape, BF16),
        vmem(down_weight.shape, BF16),
        vmem((micro, group, d_model), BF16),
        vmem((micro, group, d_model), BF16),
        vmem((micro, rows, d_model), F32),
        vmem((micro, wide, per_source, LANES), BF16),
        vmem((micro, wide, group // 2, LANES), BF16),
        vmem((micro, wide, group // 2, LANES), BF16),
        vmem((micro, wide, per_source, LANES), BF16),
        vmem((micro, rows, d_model), BF16),
        vmem((micro, rows, d_model), BF16),
        vmem((wide, per_source, LANES), BF16),
        vmem((micro, wide, group // 2, LANES), BF16),
        vmem((micro, wide, group // 2, LANES), BF16),
        vmem((2, wide, per_source, LANES), BF16),
        vmem((rows, d_model), BF16),
        vmem((rows, d_model), BF16),
        vmem((rows, d_model), BF16),
        vmem((rows, d_model), BF16),
        vmem((rows, d_model), F32),
        vmem((2, group, d_model), BF16),
        vmem((group, inner), BF16),
        vmem((group, ff), BF16),
        vmem((group, ff), BF16),
        vmem((group, 3 * inner), BF16),
        vmem((micro, group, ff), BF16),
        vmem((group, d_model), F32),
        vmem((group, d_model), F32),
        vmem((group, d_model), F32),
        vmem((SEQ, LANES), BF16),
        vmem((SEQ, LANES), BF16),
        vmem((SEQ, LANES), BF16),
        vmem((SEQ, LANES), BF16),
        vmem((SEQ, LANES), F32),
        vmem((micro, SEQ // BLOCK, 8, BLOCK), F32),
        vmem((wide, 8, group), F32),
        vmem((BLOCK, SEQ), F32),
        vmem((BLOCK, LANES), F32),
        vmem((BLOCK, LANES), F32),
        dma((4,)),
        dma((micro,)),
        dma((micro,)),
        dma((micro,)),
        dma((micro,)),
        dma((micro,)),
        dma((micro,)),
        dma((1,)),
        dma((micro,)),
        dma((micro,)),
        dma((micro,)),
        dma((micro,)),
        dma((micro,)),
        dma((2,)),
        dma((micro,)),
        dma((1,)),
        dma((micro,)),
        dma((1,)),
        dma((micro,)),
        dma((1,)),
        dma((1,)),
        dma((9,)),
        dma((micro,)),
        vmem((RING, TILE, ACROSS), BF16),
        vmem((RING, TILE, ACROSS), BF16),
        vmem((RING, TILE, ACROSS), BF16),
        vmem((TILE, micro * group), BF16),
        vmem((5, 8, d_model + COLS), F32),
        dma((2, AHEAD + 1)),
        dma((RING,)),
        dma((RING,)),
        dma((RING,)),
        dma((RING,)),
        dma((RING,)),
        dma((steps + GUESTS,)),
        dma((4, TOTALS)),
        dma((steps + GUESTS,)),
        dma((steps + GUESTS,)),
        dma((4,)),
        dma((1,)),
        dma((4,)),
        dma((2,)),
        dma((GUESTS,)),
        regular,
        regular((2,)),
        regular,
    ]
    return pl.pallas_call(
        functools.partial(relay_kernel, dims),
        out_shape=outs,
        in_specs=[scalars, anywhere, anywhere] + [local] * 6 + [anywhere] * 4,
        out_specs=[anywhere] * 13 + [local],
        scratch_shapes=scratch,
        compiler_params=pltpu.CompilerParams(
            collective_id=collective_id, has_side_effects=True, vmem_limit_bytes=63 << 20
        ),
        name="relay",
    )(
        doc_lengths,
        block_input,
        cotangent,
        norm_gain,
        norm_bias,
        qkv_bias[None],
        up_bias[None],
        dense_bias[None],
        down_bias[None],
        qkv_weight,
        dense_weight,
        up_weight,
        down_weight,
    )


def relay_shards(
    block_input,
    doc_lengths,
    norm_gain,
    norm_bias,
    qkv_weight,
    qkv_bias,
    dense_weight,
    dense_bias,
    up_weight,
    up_bias,
    down_weight,
    down_bias,
    cotangent,
):
    weights = tuple(
        array[0]
        for array in (
            norm_gain,
            norm_bias,
            qkv_weight,
            qkv_bias,
            dense_weight,
            dense_bias,
            up_weight,
            up_bias,
            down_weight,
            down_bias,
        )
    )
    micro, rows, d_model = block_input.shape
    group = rows * lax.axis_size("tensor")
    wide = lax.axis_size("wide")
    heads = qkv_weight.shape[2] // (3 * HEAD_DIM)
    ff = up_weight.shape[2]
    dims = (micro, rows, group, wide, heads, d_model, ff)
    out, input_grad, *_, up_grad, down_grad, dense_grad, qkv_grad, _, sums = relay(
        dims, doc_lengths, block_input, cotangent, weights, 1
    )
    up_grad, down_grad, dense_grad, qkv_grad = (
        grad.astype(F32)[None] for grad in (up_grad, down_grad, dense_grad, qkv_grad)
    )
    biases = sums[:, d_model:].reshape(1, -1)
    qkv_width = qkv_weight.shape[2]
    out_bias_grad = sums[4:5, :d_model]
    return (
        out[None],
        input_grad[None],
        sums[None, 0:2, :d_model],
        sums[None, 2:4, :d_model],
        qkv_grad,
        biases[:, :qkv_width],
        dense_grad,
        out_bias_grad,
        up_grad,
        biases[:, qkv_width : qkv_width + ff],
        down_grad,
        out_bias_grad,
    )


def shortened(shard):

    def short(part):
        return part.astype(jnp.bfloat16) if part.dtype == jnp.float32 else part

    return jax.tree.map(short, shard)


def from_behind(block, axis, distance):
    devices = range(lax.axis_size(axis))
    route = [(i - distance, i) for i in devices if i - distance in devices]
    return lax.ppermute(block, axis, route)


def norm_parts(values, gain, shift):
    center = jnp.mean(values, axis=-1, keepdims=True)
    centred = values - center
    spread = jnp.mean(centred * centred, axis=-1, keepdims=True)
    inv_scale = lax.rsqrt(spread + EPSILON)
    normed = centred * inv_scale
    return (normed * gain + shift, normed, inv_scale)


def norm_back(grad, normed, inv_scale, gain):
    scaled = grad * gain
    inner_mean = jnp.mean(scaled, axis=-1, keepdims=True)
    cross_mean = jnp.mean(scaled * normed, axis=-1, keepdims=True)
    return inv_scale * (scaled - inner_mean - normed * cross_mean)


def doc_layout(lengths, tok_index):
    ends = jnp.cumsum(lengths)
    starts = ends - lengths
    doc_ids = jnp.sum((tok_index[:, None] >= ends[None, :]).astype(jnp.int32), axis=1)
    numbers = jnp.arange(lengths.shape[0], dtype=jnp.int32)
    picked = doc_ids[:, None] == numbers[None, :]
    begins = jnp.sum(jnp.where(picked, starts[None, :], 0), axis=1)
    return (doc_ids, tok_index - begins)


def rope_tables(offsets):
    half = ROT // 2
    freqs = ROPE_BASE ** (-2.0 * jnp.arange(half, dtype=jnp.float32) / ROT)
    angle = offsets.astype(jnp.float32)[:, None] * freqs[None, :]
    return (jnp.cos(angle)[:, None, :], jnp.sin(angle)[:, None, :])


def rotate(values, cos_table, sin_table):
    half = ROT // 2
    front = values[..., :half]
    back = values[..., half:ROT]
    turned = [
        front * cos_table - back * sin_table,
        back * cos_table + front * sin_table,
        values[..., ROT:],
    ]
    return jnp.concatenate(turned, axis=-1)


def unrotate(values, cos_table, sin_table):
    half = ROT // 2
    front = values[..., :half]
    back = values[..., half:ROT]
    turned = [
        front * cos_table + back * sin_table,
        back * cos_table - front * sin_table,
        values[..., ROT:],
    ]
    return jnp.concatenate(turned, axis=-1)


def gelu_parts(pre_act):
    cumul = 0.5 * (1.0 + lax.erf(pre_act * (1.0 / math.sqrt(2.0))))
    density = jnp.exp(-0.5 * pre_act * pre_act) * (1.0 / math.sqrt(2.0 * math.pi))
    return (pre_act * cumul, cumul + pre_act * density)


def store_slot(buffer, update, slot_here, is_valid):
    previous = lax.dynamic_index_in_dim(buffer, slot_here, 0, keepdims=False)
    return lax.dynamic_update_index_in_dim(
        buffer, jnp.where(is_valid, update, previous), slot_here, 0
    )


def gather_keys(key_rows, value_rows):
    return (
        lax.all_gather(key_rows, "wide", axis=0, tiled=True),
        lax.all_gather(value_rows, "wide", axis=0, tiled=True),
    )


def forward_parts(inputs, lengths, weights, with_output):
    (
        norm_gain,
        norm_bias,
        qkv_weight,
        qkv_bias,
        dense_weight,
        dense_bias,
        up_weight,
        up_bias,
        down_weight,
        down_bias,
    ) = weights
    seq_len = SEQ
    group = inputs.shape[0] * lax.axis_size("tensor")
    head_count = qkv_weight.shape[1] // (3 * HEAD_DIM)
    factor = 1.0 / math.sqrt(HEAD_DIM)
    values = inputs.astype(jnp.float32)
    norm_first, normed_first, scale_first = norm_parts(values, norm_gain[0], norm_bias[0])
    norm_second, normed_second, scale_second = norm_parts(values, norm_gain[1], norm_bias[1])
    full_first, full_second = (
        lax.all_gather(norm_first.astype(jnp.bfloat16), "tensor", axis=0, tiled=True),
        lax.all_gather(norm_second.astype(jnp.bfloat16), "tensor", axis=0, tiled=True),
    )
    tok_index = lax.axis_index("wide") * group + jnp.arange(group, dtype=jnp.int32)
    doc_ids, offsets = doc_layout(lengths, tok_index)
    all_index = jnp.arange(seq_len, dtype=jnp.int32)
    all_docs = doc_layout(lengths, all_index)[0]
    cos_table, sin_table = rope_tables(offsets)
    packed = jnp.dot(full_first, qkv_weight, preferred_element_type=jnp.float32) + qkv_bias
    packed = packed.reshape(group, head_count, 3, HEAD_DIM)
    queries = rotate(packed[:, :, 0], cos_table, sin_table).astype(jnp.bfloat16)
    key_here = rotate(packed[:, :, 1], cos_table, sin_table).astype(jnp.bfloat16)
    value_here = packed[:, :, 2].astype(jnp.bfloat16)
    key_all, value_all = gather_keys(key_here.reshape(group, -1), value_here.reshape(group, -1))
    key_heads = key_all.reshape(seq_len, head_count, HEAD_DIM)
    value_heads = value_all.reshape(seq_len, head_count, HEAD_DIM)
    allowed = (doc_ids[:, None] == all_docs[None, :]) & (all_index[None, :] <= tok_index[:, None])
    raw_scores = jnp.einsum("qhd,khd->qhk", queries, key_heads, preferred_element_type=jnp.float32)
    scores = jnp.where(allowed[:, None, :], raw_scores * factor, -jnp.inf)
    row_max = jnp.max(scores, axis=-1, keepdims=True)
    log_total = row_max + jnp.log(jnp.sum(jnp.exp(scores - row_max), axis=-1, keepdims=True))
    attn_probs = jnp.exp(scores - log_total)
    probs_low = attn_probs.astype(jnp.bfloat16)
    mixed_out = jnp.einsum(
        "qhk,khd->qhd", probs_low, value_heads, preferred_element_type=jnp.float32
    )
    mixed_out = mixed_out.reshape(group, -1).astype(jnp.bfloat16)
    up_pre = jnp.dot(full_second, up_weight, preferred_element_type=jnp.float32) + up_bias
    up_act, gelu_slope = gelu_parts(up_pre)
    hidden = up_act.astype(jnp.bfloat16)
    output = None
    if with_output:
        partial_value = jnp.dot(mixed_out, dense_weight, preferred_element_type=jnp.float32)
        partial_value = partial_value + jnp.dot(
            hidden, down_weight, preferred_element_type=jnp.float32
        )
        branch = (
            lax.psum_scatter(
                partial_value.astype(jnp.bfloat16), "tensor", scatter_dimension=0, tiled=True
            ).astype(jnp.float32)
            + dense_bias
            + down_bias
        )
        output = (values + branch).astype(jnp.bfloat16)
    return dict(
        output=output,
        normed_first=normed_first,
        scale_first=scale_first,
        normed_second=normed_second,
        scale_second=scale_second,
        full_first=full_first,
        full_second=full_second,
        tok_index=tok_index,
        doc_ids=doc_ids,
        all_index=all_index,
        all_docs=all_docs,
        cos_table=cos_table,
        sin_table=sin_table,
        queries=queries,
        key_here=key_here,
        value_here=value_here,
        key_all=key_all,
        value_all=value_all,
        key_heads=key_heads,
        value_heads=value_heads,
        attn_probs=attn_probs,
        probs_low=probs_low,
        log_total=log_total,
        mixed_out=mixed_out,
        gelu_slope=gelu_slope,
        hidden=hidden,
    )


def backward_parts(inputs, grad_out, lengths, weights):
    (
        norm_gain,
        norm_bias,
        qkv_weight,
        qkv_bias,
        dense_weight,
        dense_bias,
        up_weight,
        up_bias,
        down_weight,
        down_bias,
    ) = weights
    parts = forward_parts(inputs, lengths, weights, False)
    seq_len = SEQ
    group = inputs.shape[0] * lax.axis_size("tensor")
    head_count = qkv_weight.shape[1] // (3 * HEAD_DIM)
    factor = 1.0 / math.sqrt(HEAD_DIM)
    cos_table = parts["cos_table"]
    sin_table = parts["sin_table"]
    grad_low = grad_out.astype(jnp.bfloat16)
    grad_rows = grad_low.astype(jnp.float32)
    grad_full = lax.all_gather(grad_low, "tensor", axis=0, tiled=True)
    dense_grad = jnp.einsum(
        "cf,cd->fd", parts["mixed_out"], grad_full, preferred_element_type=jnp.float32
    )
    down_grad = jnp.einsum(
        "cf,cd->fd", parts["hidden"], grad_full, preferred_element_type=jnp.float32
    )
    hidden_grad = jnp.einsum(
        "cd,fd->cf", grad_full, down_weight, preferred_element_type=jnp.float32
    )
    pre_grad = (hidden_grad * parts["gelu_slope"]).astype(jnp.bfloat16)
    up_grad = jnp.einsum(
        "cd,cf->df", parts["full_second"], pre_grad, preferred_element_type=jnp.float32
    )
    up_bias_grad = jnp.sum(pre_grad.astype(jnp.float32), axis=0)
    second_grad = jnp.einsum("cf,df->cd", pre_grad, up_weight, preferred_element_type=jnp.float32)
    mixed_grad = jnp.einsum(
        "cd,fd->cf", grad_full, dense_weight, preferred_element_type=jnp.float32
    )
    mixed_grad = mixed_grad.astype(jnp.bfloat16).reshape(group, head_count, HEAD_DIM)
    attn_probs = parts["attn_probs"]
    probs_grad = jnp.einsum(
        "qhd,khd->qhk", mixed_grad, parts["value_heads"], preferred_element_type=jnp.float32
    )
    inner = jnp.sum(attn_probs * probs_grad, axis=-1, keepdims=True)
    score_grad = (attn_probs * (probs_grad - inner) * factor).astype(jnp.bfloat16)
    query_grad = jnp.einsum(
        "qhk,khd->qhd", score_grad, parts["key_heads"], preferred_element_type=jnp.float32
    )
    key_sums = jnp.einsum(
        "qhk,qhd->khd", score_grad, parts["queries"], preferred_element_type=jnp.float32
    )
    value_sums = jnp.einsum(
        "qhk,qhd->khd", parts["probs_low"], mixed_grad, preferred_element_type=jnp.float32
    )
    key_flat, value_flat = (
        lax.psum_scatter(
            key_sums.reshape(seq_len, -1).astype(jnp.bfloat16),
            "wide",
            scatter_dimension=0,
            tiled=True,
        ).astype(jnp.float32),
        lax.psum_scatter(
            value_sums.reshape(seq_len, -1).astype(jnp.bfloat16),
            "wide",
            scatter_dimension=0,
            tiled=True,
        ).astype(jnp.float32),
    )
    key_grad = key_flat.reshape(group, head_count, HEAD_DIM)
    value_grad = value_flat.reshape(group, head_count, HEAD_DIM)
    query_back = unrotate(query_grad, cos_table, sin_table)
    key_back = unrotate(key_grad, cos_table, sin_table)
    packed_grad = (
        jnp.stack([query_back, key_back, value_grad], axis=2)
        .reshape(group, -1)
        .astype(jnp.bfloat16)
    )
    qkv_grad = jnp.einsum(
        "cd,cf->df", parts["full_first"], packed_grad, preferred_element_type=jnp.float32
    )
    qkv_bias_grad = jnp.sum(packed_grad.astype(jnp.float32), axis=0)
    first_grad = jnp.einsum(
        "cf,df->cd", packed_grad, qkv_weight, preferred_element_type=jnp.float32
    )
    norm_first_grad, norm_second_grad = (
        lax.psum_scatter(
            first_grad.astype(jnp.bfloat16), "tensor", scatter_dimension=0, tiled=True
        ).astype(jnp.float32),
        lax.psum_scatter(
            second_grad.astype(jnp.bfloat16), "tensor", scatter_dimension=0, tiled=True
        ).astype(jnp.float32),
    )
    gain_grad = jnp.stack(
        [
            jnp.sum(norm_first_grad * parts["normed_first"], axis=0),
            jnp.sum(norm_second_grad * parts["normed_second"], axis=0),
        ]
    )
    shift_grad = jnp.stack([jnp.sum(norm_first_grad, axis=0), jnp.sum(norm_second_grad, axis=0)])
    input_grad = grad_out + norm_back(
        norm_first_grad, parts["normed_first"], parts["scale_first"], norm_gain[0]
    )
    input_grad = input_grad + norm_back(
        norm_second_grad, parts["normed_second"], parts["scale_second"], norm_gain[1]
    )
    bias_rows = jnp.sum(grad_rows, axis=0)
    terms = (
        gain_grad,
        shift_grad,
        qkv_grad,
        qkv_bias_grad,
        dense_grad,
        bias_rows,
        up_grad,
        up_bias_grad,
        down_grad,
        bias_rows,
    )
    return (input_grad, terms)


def general_shards(
    block_input,
    doc_lengths,
    norm_gain,
    norm_bias,
    qkv_weight,
    qkv_bias,
    dense_weight,
    dense_bias,
    up_weight,
    up_bias,
    down_weight,
    down_bias,
    cotangent,
):
    weights = (
        norm_gain[0],
        norm_bias[0],
        qkv_weight[0],
        qkv_bias[0],
        dense_weight[0],
        dense_bias[0],
        up_weight[0],
        up_bias[0],
        down_weight[0],
        down_bias[0],
    )
    section_index = lax.axis_index("section")
    last_section = lax.axis_size("section") - 1
    micro_count = block_input.shape[0]
    row_count = block_input.shape[1]
    tick_count = micro_count + last_section

    def forward_tick(carry, tick_index):
        incoming, kept_inputs, outputs, kept_pairs = carry
        slot_raw = tick_index - section_index
        is_valid = (slot_raw >= 0) & (slot_raw < micro_count)
        slot_here = jnp.clip(slot_raw, 0, micro_count - 1)
        fresh = lax.dynamic_index_in_dim(
            block_input, jnp.clip(tick_index, 0, micro_count - 1), 0, keepdims=False
        )
        inputs = jnp.where(section_index == 0, fresh, incoming)
        lengths = lax.dynamic_index_in_dim(doc_lengths, slot_here, 0, keepdims=False)
        parts = forward_parts(inputs, lengths, weights, True)
        output = parts["output"]
        kept_inputs = store_slot(kept_inputs, inputs, slot_here, is_valid)
        outputs = store_slot(outputs, output, slot_here, is_valid)
        incoming = jax.tree.map(
            lambda part, own: part.astype(own.dtype),
            from_behind(shortened(output), "section", 1),
            output,
        )
        return ((incoming, kept_inputs, outputs, kept_pairs), None)

    pair_init = (jnp.zeros((1,), jnp.bfloat16), jnp.zeros((1,), jnp.bfloat16))
    zero_rows = jnp.zeros((row_count, block_input.shape[2]), jnp.bfloat16)
    zero_stack = jnp.zeros(block_input.shape, jnp.bfloat16)
    forward_init = (zero_rows, zero_stack, zero_stack, pair_init)
    forward_done = lax.scan(forward_tick, forward_init, jnp.arange(tick_count, dtype=jnp.int32))[0]
    kept_inputs = forward_done[1]
    outputs = forward_done[2]
    kept_pairs = forward_done[3]

    def add_masked(total, term, scale_mask):
        return total + scale_mask * term

    def backward_tick(carry, tick_index):
        incoming, grads, input_grads = carry
        slot_raw = tick_index - (last_section - section_index)
        is_valid = (slot_raw >= 0) & (slot_raw < micro_count)
        slot_here = jnp.clip(slot_raw, 0, micro_count - 1)
        top_grad = lax.dynamic_index_in_dim(cotangent, slot_here, 0, keepdims=False)
        grad_out = jnp.where(section_index == last_section, top_grad, incoming)
        inputs = lax.dynamic_index_in_dim(kept_inputs, slot_here, 0, keepdims=False)
        lengths = lax.dynamic_index_in_dim(doc_lengths, slot_here, 0, keepdims=False)
        input_grad, terms = backward_parts(inputs, grad_out, lengths, weights)
        scale_mask = is_valid.astype(jnp.float32)
        grads = tuple((add_masked(total, term, scale_mask) for total, term in zip(grads, terms)))
        input_grads = store_slot(input_grads, input_grad, slot_here, is_valid)
        incoming = from_behind(shortened(input_grad), "section", -1).astype(input_grad.dtype)
        return ((incoming, grads, input_grads), None)

    grad_init = tuple((jnp.zeros(weight.shape, jnp.float32) for weight in weights))
    backward_init = (
        jnp.zeros((row_count, block_input.shape[2]), jnp.float32),
        grad_init,
        jnp.zeros(block_input.shape, jnp.float32),
    )
    backward_done = lax.scan(backward_tick, backward_init, jnp.arange(tick_count, dtype=jnp.int32))[
        0
    ]
    grads = backward_done[1]
    input_grads = backward_done[2]
    wide_sums = (
        lax.psum(grads[2].astype(jnp.bfloat16), "wide").astype(jnp.float32),
        lax.psum(grads[3].astype(jnp.bfloat16), "wide").astype(jnp.float32),
        lax.psum(grads[4].astype(jnp.bfloat16), "wide").astype(jnp.float32),
        lax.psum(grads[6].astype(jnp.bfloat16), "wide").astype(jnp.float32),
        lax.psum(grads[7].astype(jnp.bfloat16), "wide").astype(jnp.float32),
        lax.psum(grads[8].astype(jnp.bfloat16), "wide").astype(jnp.float32),
    )
    shared = lax.psum((grads[0], grads[1], grads[5], grads[9]), ("tensor", "wide"))
    return (
        outputs[None],
        input_grads[None],
        shared[0][None],
        shared[1][None],
        wide_sums[0][None],
        wide_sums[1][None],
        wide_sums[2][None],
        shared[2][None],
        wide_sums[3][None],
        wide_sums[4][None],
        wide_sums[5][None],
        shared[3][None],
    )


def solution(mesh):
    placed = (
        P(None, ("wide", "tensor"), None),
        P(),
        P("section", None, None),
        P("section", None, None),
        P("section", None, "tensor"),
        P("section", "tensor"),
        P("section", "tensor", None),
        P("section", None),
        P("section", None, "tensor"),
        P("section", "tensor"),
        P("section", "tensor", None),
        P("section", None),
        P(None, ("wide", "tensor"), None),
    )
    results = (
        P("section", None, ("wide", "tensor"), None),
        P("section", None, ("wide", "tensor"), None),
        P("section", None, None),
        P("section", None, None),
        P("section", None, "tensor"),
        P("section", "tensor"),
        P("section", "tensor", None),
        P("section", None),
        P("section", None, "tensor"),
        P("section", "tensor"),
        P("section", "tensor", None),
        P("section", None),
    )

    def program(*args):
        heads = args[4].shape[2] // (3 * HEAD_DIM * mesh.shape["tensor"])
        micro, seq_len, d_model = args[0].shape
        group = seq_len // mesh.shape["wide"]
        fits = heads == mesh.shape["wide"] == 8
        fits = fits and mesh.shape["section"] == 2 and mesh.shape["tensor"] == 2
        fits = fits and micro * group == d_model and args[8].shape[2] == 4 * d_model
        body = relay_shards if fits and group == TILE else general_shards
        return jax.shard_map(
            body, mesh=mesh, in_specs=placed, out_specs=results, check_vma=False
        )(*args)

    return program
```

```python
import functools
import math

import jax
import jax.numpy as jnp
from jax import lax
from jax.experimental import pallas as pl
from jax.experimental.pallas import tpu as pltpu
from jax.sharding import PartitionSpec as P

HEAD_DIM = 64
ROT = 16
SEQ = 2048


EPSILON = 1e-05
ROPE_BASE = 10000.0

MESH = pl.DeviceIdType.MESH
F32 = jnp.float32
BF16 = jnp.bfloat16
LANES = 128
BLOCK = 512
COLS = 512
NEG = -1e30
SCORE_SCALE = math.log2(math.e) / math.sqrt(HEAD_DIM)


TILE = 256
ACROSS = 256
AHEAD = 3
RING = 8
TOTALS = 8
LAGS = (2, 5, 8, 12, 15)
OWN = 16
GUESTS = 10
EARLY = 24


def gradient_kinds(d_model, inner, ff):
    return ((d_model, ff), (ff, d_model), (inner, d_model), (d_model, 3 * inner))


def dot(a, b):
    return jnp.dot(a, b, preferred_element_type=F32)


def dot_t(a, b):
    return lax.dot_general(a, b, (((1,), (1,)), ((), ())), preferred_element_type=F32)


def t_dot(a, b):
    return lax.dot_general(a, b, (((0,), (0,)), ((), ())), preferred_element_type=F32)


def lane_low(rows):
    return lax.broadcasted_iota(jnp.int32, (rows, LANES), 1) < HEAD_DIM


def turn(values):
    return pltpu.roll(values, HEAD_DIM, 1)


def rotary(values, cos_ref, front_ref, back_ref, seq, sign):
    cos, front, back = cos_ref[seq], front_ref[seq], back_ref[seq]
    ahead = pltpu.roll(values, LANES - ROT // 2, 1)
    behind = pltpu.roll(values, ROT // 2, 1)
    return values * cos + sign * (ahead * front + behind * back)


def pair_up(first, second, low):
    return jnp.where(low, first, turn(second)), jnp.where(low, turn(first), second)


def relay_kernel(
    dims,
    lengths,
    x_hbm,
    cot_hbm,
    gain,
    shift,
    qkv_b,
    up_b,
    dense_b,
    down_b,
    wqkv_hbm,
    wdense_hbm,
    wup_hbm,
    wdown_hbm,
    out_hbm,
    ig_hbm,
    norm_hbm,
    g_hbm,
    mixed_hbm,
    hid_hbm,
    dpre_hbm,
    dpk_hbm,
    up_out,
    down_out,
    dense_out,
    qkv_out,
    guest_hbm,
    sums,
    small,
    bias_sums,
    cos,
    front,
    back,
    wqkv,
    wdense,
    wup,
    wdown,
    xfull,
    gfull,
    cot,
    qkv_r,
    mix_r,
    do_r,
    dqkv_r,
    rsf_r,
    rsb_r,
    qkv_st,
    o_st,
    do_st,
    dqkv_st,
    rsf_st,
    rsb_st,
    out_st,
    gx_st,
    ig_st,
    norm_st,
    mixed_st,
    hid_st,
    dpre_st,
    dpk_st,
    slope,
    part,
    part_b,
    dn1,
    qm,
    kr,
    vx,
    dox,
    dq,
    lse,
    delta,
    scores,
    peak,
    acc,
    wsem,
    ownx_sem,
    yx_s,
    yx_r,
    owng_sem,
    yg_s,
    yg_r,
    qkv_ss,
    qkv_rs,
    o_ss,
    o_rs,
    do_ss,
    do_rs,
    dqkv_ss,
    dqkv_rs,
    rsf_ss,
    rsf_rs,
    rsb_ss,
    rsb_rs,
    xs_ss,
    gs_ss,
    store_sem,
    g_store,
    core_r,
    outer_r,
    inner_r,
    turned,
    sums_r,
    op_sem,
    core_ss,
    core_rs,
    outer_rs,
    inner_rs,
    red_ss,
    bc_rs,
    tot_ss,
    fwd_ss,
    share_ss,
    fin_rs,
    sum_ss,
    sum_rs,
    guest_ss,
    guest_rs,
    core_free,
    outer_free,
    inner_free,
):
    micro, rows, group, wide, heads, d_model, ff = dims
    sect = lax.axis_index("section")
    tens = lax.axis_index("tensor")
    me = lax.axis_index("wide")
    pairs = heads // 2
    per_source = group + group // 2
    half = group // 2
    q_blocks = SEQ // BLOCK
    sources = BLOCK // group
    my_rows = pl.ds(pl.multiple_of(tens * rows, rows), rows)
    his_rows = pl.ds(pl.multiple_of((1 - tens) * rows, rows), rows)
    x_dev = {"section": 1 - sect}
    y_dev = {"tensor": 1 - tens}
    low_half = lane_low(half)
    low_group = lane_low(group)

    def remote(src, dst, ss, rs, dev):
        return pltpu.make_async_remote_copy(
            src_ref=src, dst_ref=dst, send_sem=ss, recv_sem=rs, device_id=dev, device_id_type=MESH
        )

    def arrived(ref, sem):
        pltpu.make_async_copy(ref, ref, sem).wait()

    def tokens_of(s):
        return pl.ds(pl.multiple_of(s * group, group), group)

    def y_send_x(s):
        own = xfull.at[s, my_rows]
        return remote(own, own, yx_s.at[s], yx_r.at[s], y_dev)

    def y_send_g(s):
        own = gfull.at[s, my_rows]
        return remote(own, own, yg_s.at[s], yg_r.at[s], y_dev)

    def spread(stage, target, seq, dest, ss, rs):
        @pl.when(dest == me)
        def _():
            pltpu.make_async_copy(stage, target.at[seq, me], rs).start()

        @pl.when(dest != me)
        def _():
            remote(stage, target.at[seq, me], ss, rs, {"wide": dest}).start()

    loads = [
        pltpu.make_async_copy(source, target, wsem.at[i])
        for i, (source, target) in enumerate(
            ((wqkv_hbm, wqkv), (wup_hbm, wup), (wdown_hbm, wdown), (wdense_hbm, wdense))
        )
    ]

    barrier = pltpu.get_barrier_semaphore()
    for dev in [x_dev, y_dev] + [{"wide": lax.rem(me + k, wide)} for k in range(1, wide)]:
        pl.semaphore_signal(barrier, inc=1, device_id=dev, device_id_type=MESH)

    @pl.when(sect == 0)
    def _():
        for s in range(micro):
            pltpu.make_async_copy(x_hbm.at[s], xfull.at[s, my_rows], ownx_sem.at[s]).start()

    for load in loads:
        load.start()

    @pl.when(sect == 1)
    def _():
        for s in range(micro):
            pltpu.make_async_copy(cot_hbm.at[s], cot.at[s], owng_sem.at[s]).start()

    def starts_of(s, tokens):
        found = jnp.zeros_like(tokens)
        end = jnp.int32(0)
        for j in range(lengths.shape[1]):
            end = end + lengths[s, j]
            found = jnp.where(tokens >= end, end, found)
        return found

    lane = lax.rem(lax.broadcasted_iota(jnp.int32, (8, LANES), 1), HEAD_DIM)
    number = lax.rem(lane, ROT // 2)
    freq = jnp.zeros((8, LANES), F32)
    for k in range(ROT // 2):
        freq = jnp.where(number == k, ROPE_BASE ** (-2.0 * k / ROT), freq)
    lane, freq = lane[0:1, :], freq[0:1, :]

    def table_step(s, carry):
        tokens = me * group + lax.broadcasted_iota(jnp.int32, (group, LANES), 0)
        angle = (tokens - starts_of(s, tokens)).astype(F32) * freq
        sine = jnp.sin(angle)
        cos[s] = jnp.where(lane < ROT, jnp.cos(angle), 1.0)
        front[s] = jnp.where(lane < ROT // 2, -sine, 0.0)
        back[s] = jnp.where((lane >= ROT // 2) & (lane < ROT), sine, 0.0)
        return carry

    lax.fori_loop(0, micro, table_step, 0)
    small[...] = jnp.zeros_like(small)
    bias_sums[...] = jnp.zeros_like(bias_sums)
    pl.semaphore_wait(barrier, wide + 1)

    @pl.when(sect == 0)
    def _():
        for s in range(micro):
            arrived(xfull.at[s, my_rows], ownx_sem.at[s])
            y_send_x(s).start()

    @pl.when(sect == 1)
    def _():
        for s in range(micro):
            arrived(cot.at[s], owng_sem.at[s])

            def chunk(i, carry, s=s):
                at = pl.ds(pl.multiple_of(i * 32, 32), 32)
                there = pl.ds(pl.multiple_of(tens * rows + i * 32, 32), 32)
                gfull[s, there, :] = cot[s, at, :].astype(BF16)
                return carry

            lax.fori_loop(0, rows // 32, chunk, 0)
            y_send_g(s).start()

    def fold(values):
        total = values[0:8]
        for k in range(1, values.shape[0] // 8):
            total = total + values[k * 8 : (k + 1) * 8]
        return total

    def normed_rows(values):
        center = jnp.mean(values, axis=-1, keepdims=True)
        centred = values - center
        spread_of = jnp.mean(centred * centred, axis=-1, keepdims=True)
        inv = lax.rsqrt(spread_of + EPSILON)
        return centred * inv, inv

    def unpack_heads(s):
        def step(src, carry):
            qk = qkv_r[s, src, 0:group, :].astype(F32)
            at = pl.multiple_of(src * group, group)
            qm[pl.ds(at, group), :] = jnp.where(low_group, qk, 0.0).astype(BF16)
            kr[pl.ds(at, group), :] = turn(qk).astype(BF16)
            packed_v = qkv_r[s, src, group:per_source, :].astype(F32)
            ones = jnp.where(
                lax.broadcasted_iota(jnp.int32, (half, LANES), 1) == HEAD_DIM, 1.0, 0.0
            )
            vx[pl.ds(at, half), :] = jnp.where(low_half, packed_v, ones).astype(BF16)
            vx[pl.ds(pl.multiple_of(at + half, half), half), :] = jnp.where(
                low_half, turn(packed_v), ones
            ).astype(BF16)
            return carry

        lax.fori_loop(0, wide, step, 0, unroll=True)

    def forward_meet(s):
        arrived(xfull.at[s, my_rows], ownx_sem.at[s])
        y_send_x(s).start()

    def backward_meet(s):
        arrived(gfull.at[s, my_rows], owng_sem.at[s])
        y_send_g(s).start()

    def forward(s):
        arrived(xfull.at[s, his_rows], yx_r.at[s])

        def norm_step(i, carry):
            at = pl.ds(pl.multiple_of(i * 32, 32), 32)
            a, _ = normed_rows(xfull[s, at, :].astype(F32))
            norm_st[0, at, :] = (a * gain[0:1, :] + shift[0:1, :]).astype(BF16)
            norm_st[1, at, :] = (a * gain[1:2, :] + shift[1:2, :]).astype(BF16)
            return carry

        @pl.when(s > 0)
        def _():
            arrived(norm_st.at[0], store_sem.at[0])
            arrived(norm_st.at[1], store_sem.at[1])

        lax.fori_loop(0, group // 32, norm_step, 0, unroll=True)
        pltpu.make_async_copy(norm_st.at[0], norm_hbm.at[0, tokens_of(s)], store_sem.at[0]).start()
        pltpu.make_async_copy(norm_st.at[1], norm_hbm.at[1, tokens_of(s)], store_sem.at[1]).start()

        def qkv_step(k, carry):
            pair = lax.rem(me // 2 + 1 + k, pairs)
            cols = pl.ds(pl.multiple_of(pair * 3 * LANES, LANES), 3 * LANES)
            packed = dot(norm_st[0], wqkv[:, cols]) + qkv_b[:, cols]
            first, middle, last = (packed[:, i * LANES : (i + 1) * LANES] for i in range(3))
            qk0 = rotary(first, cos, front, back, s, 1.0)
            qk1 = rotary(
                turn(jnp.where(low_group, last, middle)), cos, front, back, s, 1.0
            )
            vv = jnp.where(low_group, middle, last)
            v0 = jnp.where(low_half, vv[:half], turn(vv[half:]))
            v1 = jnp.where(low_half, turn(vv[:half]), vv[half:])
            for i, (qk, v) in enumerate(((qk0, v0), (qk1, v1))):
                qkv_st[2 * pair + i, 0:group, :] = qk.astype(BF16)
                qkv_st[2 * pair + i, group:per_source, :] = v.astype(BF16)
            for i in range(2):
                dest = 2 * pair + i
                spread(qkv_st.at[dest], qkv_r, s, dest, qkv_ss.at[0], qkv_rs.at[s])
            return carry

        pl.when(s == 0)(loads[0].wait)
        lax.fori_loop(0, pairs, qkv_step, 0, unroll=True)

    def forward_ff(s):
        @pl.when(s == 0)
        def _():
            loads[1].wait()
            loads[2].wait()

        @pl.when(s > 0)
        def _():
            arrived(hid_st, store_sem.at[2])

        def ff_step(j, carry):
            cols = pl.ds(pl.multiple_of(j * COLS, COLS), COLS)
            pre = dot(norm_st[1], wup[:, cols]) + up_b[:, cols]
            cumul = 0.5 * (1.0 + lax.erf(pre * (1.0 / math.sqrt(2.0))))
            density = jnp.exp(-0.5 * pre * pre) * (1.0 / math.sqrt(2.0 * math.pi))
            hid = (pre * cumul).astype(BF16)
            hid_st[:, cols] = hid
            slope[s, :, cols] = (cumul + pre * density).astype(BF16)
            term = dot(hid, wdown[cols, :])

            @pl.when(j == 0)
            def _():
                part[...] = term

            @pl.when(j > 0)
            def _():
                part[...] += term

            return carry

        lax.fori_loop(0, ff // COLS, ff_step, 0, unroll=True)
        pltpu.make_async_copy(hid_st, hid_hbm.at[tokens_of(s)], store_sem.at[2]).start()

    def forward_attention(s):
        arrived(qkv_r.at[s], qkv_rs.at[s])
        arrived(qkv_st.at[pl.ds(0, wide - 1)], qkv_ss.at[0])
        unpack_heads(s)

        for i in range(q_blocks):
            q_at = slice(i * BLOCK, (i + 1) * BLOCK)
            tokens = i * BLOCK + lax.broadcasted_iota(jnp.int32, (BLOCK, LANES), 0)
            begin = starts_of(s, tokens)[:, 0:1]
            best = jnp.full((BLOCK, LANES), NEG, F32)
            for j in range(i + 1):
                k_at = slice(j * BLOCK, (j + 1) * BLOCK)
                raw = dot_t(qm[q_at, :], kr[k_at, :])
                u = j * BLOCK + lax.broadcasted_iota(jnp.int32, (BLOCK, BLOCK), 1)
                seen = u >= begin
                if i == j:
                    seen = seen & (u <= tokens[:, 0:1])
                raw = jnp.where(seen, raw, NEG)
                scores[:, k_at] = raw
                for k in range(BLOCK // LANES):
                    best = jnp.maximum(best, raw[:, k * LANES : (k + 1) * LANES])
            top = jnp.max(best, axis=1, keepdims=True) * SCORE_SCALE
            out = jnp.zeros((BLOCK, LANES), F32)
            for j in range(i + 1):
                k_at = slice(j * BLOCK, (j + 1) * BLOCK)
                probs = jnp.exp2(scores[:, k_at] * SCORE_SCALE - top)
                out = out + dot(probs.astype(BF16), vx[k_at, :])
            total = out[:, HEAD_DIM : HEAD_DIM + 1]
            out = out / total
            log_total = top + jnp.log2(total)
            lse[s, i] = jnp.broadcast_to(log_total, (BLOCK, LANES)).T[0:8, :]
            for k in range(sources):
                first = out[k * group : k * group + half]
                second = out[k * group + half : (k + 1) * group]
                source = i * sources + k
                o_st[s, source] = jnp.where(low_half, first, turn(second)).astype(BF16)
                spread(o_st.at[s, source], mix_r, s, source, o_ss.at[s], o_rs.at[s])

    def forward_out(s):
        arrived(mix_r.at[s], o_rs.at[s])
        arrived(o_st.at[s, pl.ds(0, wide - 1)], o_ss.at[s])
        pl.when((s == 0) & (sect == 0))(loads[3].wait)
        pl.when(s > 0)(lambda: arrived(mixed_st, store_sem.at[3]))
        for pair in range(pairs):
            top, bottom = pair_up(
                mix_r[s, 2 * pair].astype(F32), mix_r[s, 2 * pair + 1].astype(F32), low_half
            )
            mixed_st[0:half, pair * LANES : (pair + 1) * LANES] = top.astype(BF16)
            mixed_st[half:group, pair * LANES : (pair + 1) * LANES] = bottom.astype(BF16)
        pltpu.make_async_copy(mixed_st, mixed_hbm.at[tokens_of(s)], store_sem.at[3]).start()
        part[...] += dot(mixed_st[...], wdense[...])
        rsf_st[...] = part[his_rows, :].astype(BF16)
        remote(rsf_st, rsf_r.at[s], rsf_ss.at[0], rsf_rs.at[s], y_dev).start()

    def forward_end(s):
        arrived(rsf_r.at[s], rsf_rs.at[s])
        arrived(rsf_st, rsf_ss.at[0])

        @pl.when(s > 0)
        def _():
            arrived(out_st, store_sem.at[4])
            pl.when(sect == 0)(lambda: arrived(out_st, xs_ss.at[0]))

        def out_step(i, carry):
            at = pl.ds(pl.multiple_of(i * 32, 32), 32)
            there = pl.ds(pl.multiple_of(tens * rows + i * 32, 32), 32)
            branch = part[there, :] + rsf_r[s, at, :].astype(F32) + (dense_b[...] + down_b[...])
            out_st[at, :] = (xfull[s, there, :].astype(F32) + branch).astype(BF16)
            return carry

        lax.fori_loop(0, rows // 32, out_step, 0, unroll=True)

        @pl.when(sect == 0)
        def _():
            remote(out_st, xfull.at[s, my_rows], xs_ss.at[0], ownx_sem.at[s], x_dev).start()

        pltpu.make_async_copy(out_st, out_hbm.at[s], store_sem.at[4]).start()

    def backward(s):
        arrived(gfull.at[s, his_rows], yg_r.at[s])
        pl.when((s == 0) & (sect == 1))(loads[3].wait)
        pltpu.make_async_copy(gfull.at[s], g_hbm.at[tokens_of(s)], g_store.at[s]).start()

        def mixed_step(k, carry):
            pair = lax.rem(me // 2 + 1 + k, pairs)
            at = pl.ds(pl.multiple_of(pair * LANES, LANES), LANES)
            both = dot_t(gfull[s], wdense[at, :])
            first = jnp.where(low_half, both[:half], turn(both[half:]))
            second = jnp.where(low_half, turn(both[:half]), both[half:])
            do_st[s, 2 * pair] = first.astype(BF16)
            do_st[s, 2 * pair + 1] = second.astype(BF16)
            for i in range(2):
                dest = 2 * pair + i
                spread(do_st.at[s, dest], do_r, s, dest, do_ss.at[s], do_rs.at[s])
            return carry

        lax.fori_loop(0, pairs, mixed_step, 0, unroll=True)

    def backward_ff(s):
        pl.when(s > 0)(lambda: arrived(dpre_st, store_sem.at[6]))

        def ff_step(j, carry):
            cols = pl.ds(pl.multiple_of(j * COLS, COLS), COLS)
            grad = dot_t(gfull[s], wdown[cols, :])
            grad = (grad * slope[s, :, cols].astype(F32)).astype(BF16)
            dpre_st[:, cols] = grad
            sums_at = pl.ds(pl.multiple_of(3 * heads * HEAD_DIM + j * COLS, COLS), COLS)
            bias_sums[:, sums_at] += fold(grad.astype(F32))
            term = dot_t(grad, wup[:, cols])

            @pl.when(j == 0)
            def _():
                dn1[...] = term

            @pl.when(j > 0)
            def _():
                dn1[...] += term

            return carry

        lax.fori_loop(0, ff // COLS, ff_step, 0, unroll=True)
        pltpu.make_async_copy(dpre_st, dpre_hbm.at[tokens_of(s)], store_sem.at[6]).start()

    def backward_attention(s):
        arrived(do_r.at[s], do_rs.at[s])
        arrived(do_st.at[s, pl.ds(0, wide - 1)], do_ss.at[s])
        pl.when(sect == 0)(lambda: unpack_heads(s))

        def unpack_step(src, carry):
            at = pl.multiple_of(src * group, group)
            grad = do_r[s, src].astype(F32)
            dox[pl.ds(at, half), :] = jnp.where(low_half, grad, 0.0).astype(BF16)
            dox[pl.ds(pl.multiple_of(at + half, half), half), :] = jnp.where(
                low_half, turn(grad), 0.0
            ).astype(BF16)
            product = grad * o_st[s, src].astype(F32)
            left = jnp.sum(jnp.where(low_half, product, 0.0), axis=1, keepdims=True)
            right = jnp.sum(jnp.where(low_half, 0.0, product), axis=1, keepdims=True)
            delta[src, :, 0:half] = jnp.broadcast_to(left, (half, LANES)).T[0:8, :]
            delta[src, :, half:group] = jnp.broadcast_to(right, (half, LANES)).T[0:8, :]
            return carry

        lax.fori_loop(0, wide, unpack_step, 0, unroll=True)
        slot = lax.rem(s, 2)
        rows_of = []
        for i in range(q_blocks):
            tokens = i * BLOCK + lax.broadcasted_iota(jnp.int32, (8, BLOCK), 1)
            inner_sum = jnp.concatenate(
                [delta[i * sources + k, 0:1, :] for k in range(sources)], axis=1
            )
            rows_of.append((starts_of(s, tokens)[0:1, :], tokens[0:1, :], inner_sum))
        for j in range(q_blocks):
            k_at = slice(j * BLOCK, (j + 1) * BLOCK)
            for i in range(j, q_blocks):
                q_at = slice(i * BLOCK, (i + 1) * BLOCK)
                begin, token, inner_sum = rows_of[i]
                raw = dot_t(kr[k_at, :], qm[q_at, :])
                u = j * BLOCK + lax.broadcasted_iota(jnp.int32, (BLOCK, BLOCK), 0)
                probs = jnp.exp2(raw * SCORE_SCALE - lse[s, i, 0:1, :])
                seen = u >= begin
                if i == j:
                    seen = seen & (u <= token)
                probs = jnp.where(seen, probs, 0.0)
                probs_grad = dot_t(vx[k_at, :], dox[q_at, :])
                score_grad = (probs * (probs_grad - inner_sum)).astype(BF16)
                value_term = dot(probs.astype(BF16), dox[q_at, :])
                key_term = dot(score_grad, kr[q_at, :])
                query_term = t_dot(score_grad, kr[k_at, :])
                if i == j:
                    acc[...] = value_term
                    peak[...] = key_term
                else:
                    acc[...] += value_term
                    peak[...] += key_term
                if j == 0:
                    dq[q_at, :] = query_term
                else:
                    dq[q_at, :] += query_term
            for k in range(sources):
                source = j * sources + k
                mine = slice(k * group, (k + 1) * group)
                at = slice(source * group, (source + 1) * group)
                both = jnp.where(low_group, dq[at, :], peak[mine, :])
                both = both * (1.0 / math.sqrt(HEAD_DIM))
                value = acc[mine, :]
                value = jnp.where(low_half, value[:half], turn(value[half:]))
                dqkv_st[slot, source, 0:group, :] = both.astype(BF16)
                dqkv_st[slot, source, group:per_source, :] = value.astype(BF16)
                spread(
                    dqkv_st.at[slot, source], dqkv_r, s, source, dqkv_ss.at[slot], dqkv_rs.at[s]
                )

    def backward_norm(s):
        arrived(dqkv_r.at[s], dqkv_rs.at[s])
        slot = lax.rem(s, 2)
        arrived(dqkv_st.at[slot, pl.ds(0, wide - 1)], dqkv_ss.at[slot])
        pl.when(s > 0)(lambda: arrived(dpk_st, store_sem.at[7]))

        def pair_step(pair, carry):
            qk0 = rotary(
                dqkv_r[s, 2 * pair, 0:group, :].astype(F32), cos, front, back, s, -1.0
            )
            qk1 = turn(
                rotary(
                    dqkv_r[s, 2 * pair + 1, 0:group, :].astype(F32), cos, front, back, s, -1.0
                )
            )
            top, bottom = pair_up(
                dqkv_r[s, 2 * pair, group:per_source, :].astype(F32),
                dqkv_r[s, 2 * pair + 1, group:per_source, :].astype(F32),
                low_half,
            )
            vv = jnp.concatenate([top, bottom], axis=0)
            columns = (qk0, jnp.where(low_group, vv, qk1), jnp.where(low_group, qk1, vv))
            for k, column in enumerate(columns):
                at = pl.ds(pl.multiple_of((pair * 3 + k) * LANES, LANES), LANES)
                column = column.astype(BF16)
                dpk_st[:, at] = column
                bias_sums[:, at] += fold(column.astype(F32))
            return carry

        lax.fori_loop(0, pairs, pair_step, 0, unroll=True)
        pltpu.make_async_copy(dpk_st, dpk_hbm.at[tokens_of(s)], store_sem.at[7]).start()
        part_b[...] = dot_t(dpk_st[...], wqkv[...])

        def e_step(i, carry):
            at = pl.ds(pl.multiple_of(i * 32, 32), 32)
            a, _ = normed_rows(xfull[s, at, :].astype(F32))
            first = part_b[at, :]
            second = dn1[at, :]
            small[0] += fold(first * a)
            small[1] += fold(second * a)
            small[2] += fold(first)
            small[3] += fold(second)
            part_b[at, :] = first * gain[0:1, :] + second * gain[1:2, :]
            return carry

        lax.fori_loop(0, group // 32, e_step, 0, unroll=True)
        rsb_st[...] = part_b[his_rows, :].astype(BF16)
        remote(rsb_st, rsb_r.at[s], rsb_ss.at[0], rsb_rs.at[s], y_dev).start()

    def backward_end(s):
        arrived(rsb_r.at[s], rsb_rs.at[s])
        arrived(rsb_st, rsb_ss.at[0])

        @pl.when(s > 0)
        def _():
            arrived(ig_st, store_sem.at[8])
            pl.when(sect == 1)(lambda: arrived(gx_st, gs_ss.at[0]))

        def in_step(i, carry):
            at = pl.ds(pl.multiple_of(i * 32, 32), 32)
            there = pl.ds(pl.multiple_of(tens * rows + i * 32, 32), 32)
            a, inv = normed_rows(xfull[s, there, :].astype(F32))
            e = part_b[there, :] + rsb_r[s, at, :].astype(F32)
            mean_e = jnp.mean(e, axis=-1, keepdims=True)
            cross = jnp.mean(e * a, axis=-1, keepdims=True)
            g_low = gfull[s, there, :].astype(F32)
            small[4] += fold(g_low)
            g = jnp.where(sect == 1, cot[s, at, :], g_low)
            grad = g + inv * (e - mean_e - a * cross)
            ig_st[at, :] = grad
            gx_st[at, :] = grad.astype(BF16)
            return carry

        lax.fori_loop(0, rows // 32, in_step, 0, unroll=True)

        @pl.when(s == micro - 1)
        def _():
            for k in range(micro):
                arrived(xfull.at[k, my_rows], yx_s.at[k])

        @pl.when(sect == 1)
        def _():
            remote(gx_st, gfull.at[s, my_rows], gs_ss.at[0], owng_sem.at[s], x_dev).start()

        pltpu.make_async_copy(ig_st, ig_hbm.at[s], store_sem.at[8]).start()

    chip, core = me // 2, lax.rem(me, 2)
    partner = {"wide": me + 1 - 2 * core}
    up_dev = {"wide": lax.rem(me + 2, wide)}
    down_dev = {"wide": lax.rem(me + wide - 2, wide)}
    at_bottom, at_top = chip == 0, chip == wide // 2 - 1
    at_end = at_bottom | at_top
    middle = jnp.logical_not(at_end)
    lower = chip == 1
    outer_of = {"wide": jnp.where(lower, me - 2, lax.rem(me + 2, wide))}
    inner_of = {"wide": jnp.where(lower, me + 2, lax.rem(me + wide - 2, wide))}
    end_of = {"wide": jnp.where(at_bottom, me + 2, lax.rem(me + wide - 2, wide))}
    kinds = gradient_kinds(d_model, heads * HEAD_DIM, ff)
    targets = (up_out, down_out, dense_out, qkv_out)
    operands = (
        (norm_hbm.at[1], dpre_hbm),
        (hid_hbm, g_hbm),
        (mixed_hbm, g_hbm),
        (norm_hbm.at[0], dpk_hbm),
    )
    ranges, first = [], 0
    for height, width in kinds:
        count = (height // TILE) * (width // (2 * ACROSS))
        ranges.append((first, first + count, width // (2 * ACROSS)))
        first += count
    steps = first

    def own_at(ring):
        rows_at = pl.ds(pl.multiple_of((ring // RING) * TILE, TILE), TILE)
        return scores.at[
            rows_at, pl.ds(pl.multiple_of(lax.rem(ring, RING) * ACROSS, ACROSS), ACROSS)
        ]

    def guest_at(number):
        cols = pl.ds(pl.multiple_of(lax.rem(number, 4) * ACROSS, ACROSS), ACROSS)
        return xfull.at[number // 4, :, cols]

    def guest_st_at(slot):
        return mixed_st.at[:, pl.ds(pl.multiple_of(slot * ACROSS, ACROSS), ACROSS)]

    def core_st_at(ring):
        return hid_st.at[:, pl.ds(pl.multiple_of(ring * ACROSS, ACROSS), ACROSS)]

    def red_st_at(ring):
        return dpre_st.at[:, pl.ds(pl.multiple_of(ring * ACROSS, ACROSS), ACROSS)]

    def tot_at(slot):
        cols = pl.ds(pl.multiple_of(lax.rem(slot, 4) * ACROSS, ACROSS), ACROSS)
        return norm_st.at[slot // 4, :, cols]

    def left_at(slot):
        return wup.at[:, pl.ds(pl.multiple_of(slot * TILE, TILE), TILE)]

    def right_at(slot):
        return wdown.at[
            pl.ds(pl.multiple_of((slot // 2) * d_model, d_model), d_model),
            pl.ds(pl.multiple_of(lax.rem(slot, 2) * 2 * ACROSS, 2 * ACROSS), 2 * ACROSS),
        ]

    tile_ref = core_r.at[0]

    def by_kind(m, body):
        for kind, (low, high, across) in enumerate(ranges):

            @pl.when((m >= low) & (m < high))
            def _(kind=kind, low=low, across=across):
                at = m - low
                body(kind, at // across, lax.rem(at, across))

    def tile_of(kind, row, col, which):
        return targets[kind].at[
            pl.ds(pl.multiple_of(row * TILE, TILE), TILE),
            pl.ds(pl.multiple_of((2 * col + which) * ACROSS, ACROSS), ACROSS),
        ]

    def fetch(m):
        pl.when(m == ranges[3][0])(lambda: arrived(dpk_st, store_sem.at[7]))

        def body(kind, row, col):
            left, right = operands[kind]
            slot = lax.rem(m, AHEAD + 1)

            @pl.when(col == 0)
            def _():
                pltpu.make_async_copy(
                    left.at[:, pl.ds(pl.multiple_of(row * TILE, TILE), TILE)],
                    left_at(slot),
                    op_sem.at[0, slot],
                ).start()

            pltpu.make_async_copy(
                right.at[:, pl.ds(pl.multiple_of(col * 2 * ACROSS, 2 * ACROSS), 2 * ACROSS)],
                right_at(slot),
                op_sem.at[1, slot],
            ).start()

        by_kind(m, body)

    total_steps = jnp.where(sect == 1, steps + GUESTS, steps)
    chain = jnp.where(sect == 1, steps + GUESTS, steps - GUESTS)
    visit = ranges[2][0]

    def place(m):
        shared = (sect == 0) & (m < 2 * GUESTS)
        away = shared & (lax.rem(m, 2) == 1)
        later = (sect == 1) & (m >= visit)
        visitor = later & (m < visit + GUESTS)
        n = jnp.where(shared, m // 2, jnp.where(sect == 0, m - GUESTS, m))
        number = jnp.where(visitor, m - visit, m // 2)
        tile = jnp.where(visitor, 2 * (m - visit) + 1, jnp.where(later, m - GUESTS, m))
        return away, visitor, n, number, tile

    def is_root(n):
        return middle & (chip == 1 + lax.rem(n, 2))

    def products(step_at, m):
        slot, ring = lax.rem(m, AHEAD + 1), lax.rem(m, RING)

        def body(kind, row, col):
            @pl.when(col == 0)
            def _():
                arrived(left_at(slot), op_sem.at[0, slot])
                turned[...] = left_at(slot)[...].T

        by_kind(m, body)
        arrived(right_at(slot), op_sem.at[1, slot])
        both = dot(turned[...], right_at(slot)[...])
        first, second = both[:, :ACROSS], both[:, ACROSS:]
        own_at(lax.rem(step_at, OWN))[...] = jnp.where(core == 0, first, second)

        @pl.when(m >= RING)
        def _():
            arrived(tile_ref, core_ss.at[ring])
            pl.semaphore_wait(core_free, 1)

        core_st_at(ring)[...] = jnp.where(core == 0, second, first).astype(BF16)
        remote(
            core_st_at(ring), core_r.at[ring], core_ss.at[ring], core_rs.at[ring], partner
        ).start()

    def send_red(m, value, target, sem, dev, free):
        ring = lax.rem(m, RING)

        @pl.when(m >= RING)
        def _():
            pl.semaphore_wait(free, 1)

        red_st_at(ring)[...] = value.astype(BF16)
        remote(red_st_at(ring), target.at[ring], red_ss.at[ring], sem.at[ring], dev).start()

    def chip_sum(m):
        away, visitor, n, number, tile = place(m)
        ring = lax.rem(tile, RING)
        own = own_at(lax.rem(m, OWN))

        @pl.when(visitor)
        def _():
            arrived(tile_ref, guest_rs.at[number])
            own[...] = guest_at(number)[...].astype(F32)

        @pl.when(jnp.logical_not(visitor))
        def _():
            arrived(tile_ref, core_rs.at[ring])
            own[...] = own[...] + core_r[ring].astype(F32)

            @pl.when(tile + RING < steps)
            def _():
                pl.semaphore_signal(core_free, inc=1, device_id=partner, device_id_type=MESH)

        @pl.when(away)
        def _():
            slot = lax.rem(number, 2)
            pl.when(number >= 2)(lambda: arrived(tile_ref, guest_ss.at[slot]))
            guest_st_at(slot)[...] = own[...].astype(BF16)
            remote(
                guest_st_at(slot),
                guest_at(number),
                guest_ss.at[slot],
                guest_rs.at[number],
                x_dev,
            ).start()

        @pl.when(at_end & jnp.logical_not(away))
        def _():
            pl.when(n >= RING)(lambda: arrived(tile_ref, red_ss.at[lax.rem(n, RING)]))
            send_red(n, own[...], outer_r, outer_rs, end_of, outer_free.at[lax.rem(n, 2)])

    def take_outer(m, n):
        ring = lax.rem(n, RING)
        arrived(tile_ref, outer_rs.at[ring])
        total = own_at(lax.rem(m, OWN))[...] + outer_r[ring].astype(F32)

        @pl.when(n + RING < chain)
        def _():
            pl.semaphore_signal(
                outer_free.at[lax.rem(n, 2)], inc=1, device_id=outer_of, device_id_type=MESH
            )

        return total

    def pass_in(m):
        _, _, n, _, _ = place(m)
        total = take_outer(m, n)
        pl.when(n >= RING)(lambda: arrived(tile_ref, red_ss.at[lax.rem(n, RING)]))
        send_red(n, total, inner_r, inner_rs, inner_of, inner_free)

    def finish(m):
        _, visitor, n, number, tile = place(m)
        ring = lax.rem(n, RING)
        slot = lax.rem(n // 2, TOTALS)
        total = take_outer(m, n)
        arrived(tile_ref, inner_rs.at[ring])
        total = total + inner_r[ring].astype(F32)

        @pl.when(n + RING < chain)
        def _():
            pl.semaphore_signal(inner_free, inc=1, device_id=inner_of, device_id_type=MESH)

        @pl.when(n >= 2 * TOTALS)
        def _():
            for k in range(4):
                arrived(tile_ref, tot_ss.at[k, slot])

        tot_at(slot)[...] = total.astype(BF16)

        def send(here):
            remote(tot_at(slot), here, tot_ss.at[0, slot], bc_rs.at[m], outer_of).start()
            remote(tot_at(slot), here, tot_ss.at[1, slot], bc_rs.at[m], inner_of).start()
            pltpu.make_async_copy(tot_at(slot), here, tot_ss.at[3, slot]).start()

        def body(kind, row, col):
            here = tile_of(kind, row, col, core)

            @pl.when(visitor)
            def _():
                send(guest_hbm.at[number])
                remote(tot_at(slot), here, tot_ss.at[2, slot], bc_rs.at[tile], x_dev).start()

            @pl.when(jnp.logical_not(visitor))
            def _():
                send(here)
                remote(
                    tot_at(slot), here, tot_ss.at[2, slot], fin_rs.at[kind], partner
                ).start()

        by_kind(tile, body)

    def hand_on(m):
        _, visitor, _, number, tile = place(m)
        arrived(tile_ref, bc_rs.at[m])

        def body(kind, row, col):
            here = tile_of(kind, row, col, core)

            @pl.when(visitor)
            def _():
                held = guest_hbm.at[number]

                @pl.when(middle)
                def _():
                    remote(held, held, fwd_ss.at[m], bc_rs.at[m], outer_of).start()

                remote(held, here, share_ss.at[m], bc_rs.at[tile], x_dev).start()

            @pl.when(jnp.logical_not(visitor))
            def _():
                @pl.when(middle)
                def _():
                    remote(here, here, fwd_ss.at[m], bc_rs.at[m], outer_of).start()

                remote(here, here, share_ss.at[m], fin_rs.at[kind], partner).start()

        by_kind(tile, body)

    def guest_home(number, carry):
        m = 2 * number + 1
        arrived(tile_ref, bc_rs.at[m])

        def body(kind, row, col):
            here = tile_of(kind, row, col, core)
            remote(here, here, share_ss.at[m], fin_rs.at[kind], partner).start()

        by_kind(m, body)
        return carry

    exchanges = (
        {"tensor": 1 - tens},
        partner,
        {"wide": me + 2 - 4 * lax.rem(chip, 2)},
        {"wide": me + 4 - 8 * (chip // 2)},
    )

    def sums_begin():
        sums[:, 0:d_model] = jnp.concatenate(
            [jnp.sum(small[k], axis=0, keepdims=True) for k in range(5)]
            + [jnp.zeros((3, d_model), F32)],
            axis=0,
        )
        total = jnp.sum(bias_sums[...], axis=0, keepdims=True)
        lines = [total[:, k * COLS : (k + 1) * COLS] for k in range(total.shape[1] // COLS)]
        lines.append(jnp.zeros((8 - len(lines), COLS), F32))
        sums[:, d_model:] = jnp.concatenate(lines, axis=0)

    def exchange_start(k):
        if k == 0:
            sums_begin()
        else:
            arrived(sums, sum_ss.at[0])
        sums_r[0] = sums[...]
        remote(sums_r.at[0], sums_r.at[k + 1], sum_ss.at[0], sum_rs.at[k], exchanges[k]).start()

    def exchange_end(k):
        arrived(sums, sum_rs.at[k])
        if k == 0:
            sums[:, 0:d_model] += sums_r[1, :, 0:d_model]
        else:
            sums[...] += sums_r[k + 1]

    def gradient_step(i, carry):
        _, visits, _, _, here_tile = place(i)
        works = (i < total_steps) & jnp.logical_not(visits)
        pl.when(works & (here_tile + AHEAD < steps))(lambda: fetch(here_tile + AHEAD))
        pl.when(works)(lambda: products(i, here_tile))
        for k in range(4):
            pl.when(i == EARLY + 4 * k + 2)(lambda k=k: exchange_start(k))
            pl.when(i == EARLY + 4 * k + 5)(lambda k=k: exchange_end(k))

        def late(lag, allowed, body):
            m = i - lag
            away, _, n, _, _ = place(m)
            inside = (m >= 0) & (m < total_steps)
            pl.when(inside & allowed(away, n))(lambda: body(m))

        def outside(away, n):
            return middle & jnp.logical_not(away | is_root(n))

        late(LAGS[0], lambda away, n: n >= 0, chip_sum)
        late(LAGS[1], outside, pass_in)
        late(LAGS[2], lambda away, n: is_root(n) & jnp.logical_not(away), finish)
        late(LAGS[3], outside, hand_on)
        late(LAGS[4], lambda away, n: at_end & jnp.logical_not(away), hand_on)
        return carry

    def gradient_begin():
        arrived(norm_st.at[0], store_sem.at[0])
        arrived(norm_st.at[1], store_sem.at[1])
        arrived(hid_st, store_sem.at[2])
        arrived(mixed_st, store_sem.at[3])
        arrived(dpre_st, store_sem.at[6])
        for s in range(micro):
            arrived(gfull.at[s], g_store.at[s])
        for m in range(AHEAD):
            fetch(jnp.int32(m))

    def at(seq, allowed, body):
        pl.when(allowed & (seq >= 0) & (seq < micro))(lambda: body(seq))

    @pl.when(sect == 1)
    def _():
        lax.fori_loop(0, micro, lambda s, carry: (backward(s), carry)[1], 0)

    first = jnp.int32(0)
    pl.when(sect == 1)(lambda: forward_meet(first))
    forward(first)
    forward_ff(first)
    always = sect >= 0

    def step(i, carry):
        f = i
        b = jnp.where(sect == 1, i, i - micro)
        at(b, (sect == 0) & (b == 0), backward_meet)
        at(b, sect == 0, backward)
        at(f + 1, sect == 1, forward_meet)
        at(f, always, forward_attention)
        at(f + 1, always, forward)
        at(b, always, backward_attention)
        at(b - 1, always, backward_norm)
        at(f, always, forward_out)
        at(b, always, backward_ff)
        at(b + 1, (sect == 0) & (b >= 0), backward_meet)
        at(b - 1, always, backward_end)
        at(f, always, forward_end)
        at(f + 1, always, forward_ff)

        starts = jnp.where(sect == 1, i == micro, i == 2 * micro - 1)
        goes_on = (sect == 0) & (i == 2 * micro)
        pl.when(starts)(gradient_begin)
        low = jnp.where(goes_on, EARLY, 0)
        high = jnp.where(
            goes_on | (starts & (sect == 1)),
            total_steps + LAGS[4],
            jnp.where(starts, EARLY, 0),
        )
        lax.fori_loop(low, high, gradient_step, 0)
        return carry

    lax.fori_loop(0, jnp.where(sect == 1, micro + 1, 2 * micro + 1), step, 0)

    for s in range(micro):
        arrived(gfull.at[s, my_rows], yg_s.at[s])
    arrived(out_st, store_sem.at[4])
    arrived(ig_st, store_sem.at[8])
    pl.when(sect == 0)(lambda: arrived(out_st, xs_ss.at[0]))
    pl.when(sect == 1)(lambda: arrived(gx_st, gs_ss.at[0]))

    arrived(sums, sum_ss.at[0])
    for ring in range(RING):
        arrived(tile_ref, core_ss.at[ring])

    @pl.when(sect == 0)
    def _():
        lax.fori_loop(0, GUESTS, guest_home, 0)
        for slot in range(2):
            arrived(tile_ref, guest_ss.at[slot])

    def drain(m, carry):
        away, _, n, _, _ = place(m)
        root = is_root(n)
        stays = jnp.logical_not(away)
        ring = lax.rem(n, RING)
        sends = at_end | (middle & jnp.logical_not(root))
        pl.when(stays & sends & (n + RING >= chain))(lambda: arrived(tile_ref, red_ss.at[ring]))

        @pl.when(stays & root & (n + 2 * TOTALS >= chain))
        def _():
            for k in range(4):
                arrived(tile_ref, tot_ss.at[k, lax.rem(n // 2, TOTALS)])

        @pl.when(stays & middle & jnp.logical_not(root))
        def _():
            arrived(tile_ref, fwd_ss.at[m])

        pl.when(away | jnp.logical_not(root))(lambda: arrived(tile_ref, share_ss.at[m]))
        return carry

    lax.fori_loop(0, total_steps, drain, 0)
    for kind, (height, width) in enumerate(kinds):
        arrived(targets[kind].at[pl.ds(0, height // 2)], fin_rs.at[kind])


def relay(dims, doc_lengths, block_input, cotangent, weights, collective_id):
    micro, rows, group, wide, heads, d_model, ff = dims
    (
        norm_gain,
        norm_bias,
        qkv_weight,
        qkv_bias,
        dense_weight,
        dense_bias,
        up_weight,
        up_bias,
        down_weight,
        down_bias,
    ) = weights
    inner = heads * HEAD_DIM
    per_source = group + group // 2
    anywhere = pl.BlockSpec(memory_space=pl.ANY)
    local = pl.BlockSpec(memory_space=pltpu.VMEM)
    scalars = pl.BlockSpec(memory_space=pltpu.SMEM)
    dma = pltpu.SemaphoreType.DMA
    vmem = pltpu.VMEM
    outs = [
        jax.ShapeDtypeStruct((micro, rows, d_model), BF16),
        jax.ShapeDtypeStruct((micro, rows, d_model), F32),
        jax.ShapeDtypeStruct((2, micro * group, d_model), BF16),
        jax.ShapeDtypeStruct((micro * group, d_model), BF16),
        jax.ShapeDtypeStruct((micro * group, inner), BF16),
        jax.ShapeDtypeStruct((micro * group, ff), BF16),
        jax.ShapeDtypeStruct((micro * group, ff), BF16),
        jax.ShapeDtypeStruct((micro * group, 3 * inner), BF16),
    ]
    kinds = gradient_kinds(d_model, inner, ff)
    steps = sum((height // TILE) * (width // (2 * ACROSS)) for height, width in kinds)
    outs += [jax.ShapeDtypeStruct(kind, BF16) for kind in kinds]
    outs += [jax.ShapeDtypeStruct((GUESTS, TILE, ACROSS), BF16)]
    outs += [jax.ShapeDtypeStruct((8, d_model + COLS), F32)]
    regular = pltpu.SemaphoreType.REGULAR
    scratch = [
        vmem((5, 8, d_model), F32),
        vmem((8, 3 * inner + ff), F32),
        vmem((micro, group, LANES), F32),
        vmem((micro, group, LANES), F32),
        vmem((micro, group, LANES), F32),
        vmem(qkv_weight.shape, BF16),
        vmem(dense_weight.shape, BF16),
        vmem(up_weight.shape, BF16),
        vmem(down_weight.shape, BF16),
        vmem((micro, group, d_model), BF16),
        vmem((micro, group, d_model), BF16),
        vmem((micro, rows, d_model), F32),
        vmem((micro, wide, per_source, LANES), BF16),
        vmem((micro, wide, group // 2, LANES), BF16),
        vmem((micro, wide, group // 2, LANES), BF16),
        vmem((micro, wide, per_source, LANES), BF16),
        vmem((micro, rows, d_model), BF16),
        vmem((micro, rows, d_model), BF16),
        vmem((wide, per_source, LANES), BF16),
        vmem((micro, wide, group // 2, LANES), BF16),
        vmem((micro, wide, group // 2, LANES), BF16),
        vmem((2, wide, per_source, LANES), BF16),
        vmem((rows, d_model), BF16),
        vmem((rows, d_model), BF16),
        vmem((rows, d_model), BF16),
        vmem((rows, d_model), BF16),
        vmem((rows, d_model), F32),
        vmem((2, group, d_model), BF16),
        vmem((group, inner), BF16),
        vmem((group, ff), BF16),
        vmem((group, ff), BF16),
        vmem((group, 3 * inner), BF16),
        vmem((micro, group, ff), BF16),
        vmem((group, d_model), F32),
        vmem((group, d_model), F32),
        vmem((group, d_model), F32),
        vmem((SEQ, LANES), BF16),
        vmem((SEQ, LANES), BF16),
        vmem((SEQ, LANES), BF16),
        vmem((SEQ, LANES), BF16),
        vmem((SEQ, LANES), F32),
        vmem((micro, SEQ // BLOCK, 8, BLOCK), F32),
        vmem((wide, 8, group), F32),
        vmem((BLOCK, SEQ), F32),
        vmem((BLOCK, LANES), F32),
        vmem((BLOCK, LANES), F32),
        dma((4,)),
        dma((micro,)),
        dma((micro,)),
        dma((micro,)),
        dma((micro,)),
        dma((micro,)),
        dma((micro,)),
        dma((1,)),
        dma((micro,)),
        dma((micro,)),
        dma((micro,)),
        dma((micro,)),
        dma((micro,)),
        dma((2,)),
        dma((micro,)),
        dma((1,)),
        dma((micro,)),
        dma((1,)),
        dma((micro,)),
        dma((1,)),
        dma((1,)),
        dma((9,)),
        dma((micro,)),
        vmem((RING, TILE, ACROSS), BF16),
        vmem((RING, TILE, ACROSS), BF16),
        vmem((RING, TILE, ACROSS), BF16),
        vmem((TILE, micro * group), BF16),
        vmem((5, 8, d_model + COLS), F32),
        dma((2, AHEAD + 1)),
        dma((RING,)),
        dma((RING,)),
        dma((RING,)),
        dma((RING,)),
        dma((RING,)),
        dma((steps + GUESTS,)),
        dma((4, TOTALS)),
        dma((steps + GUESTS,)),
        dma((steps + GUESTS,)),
        dma((4,)),
        dma((1,)),
        dma((4,)),
        dma((2,)),
        dma((GUESTS,)),
        regular,
        regular((2,)),
        regular,
    ]
    return pl.pallas_call(
        functools.partial(relay_kernel, dims),
        out_shape=outs,
        in_specs=[scalars, anywhere, anywhere] + [local] * 6 + [anywhere] * 4,
        out_specs=[anywhere] * 13 + [local],
        scratch_shapes=scratch,
        compiler_params=pltpu.CompilerParams(
            collective_id=collective_id, has_side_effects=True, vmem_limit_bytes=63 << 20
        ),
        name="relay",
    )(
        doc_lengths,
        block_input,
        cotangent,
        norm_gain,
        norm_bias,
        qkv_bias[None],
        up_bias[None],
        dense_bias[None],
        down_bias[None],
        qkv_weight,
        dense_weight,
        up_weight,
        down_weight,
    )


WIDEN_STEPS = 8


def widen_kernel(sums, *refs):
    count = (len(refs) - 5) // 2
    sources, targets = refs[:count], refs[count : 2 * count]
    gain, shift, out_bias, qkv_bias, up_bias = refs[2 * count :]
    for source, target in zip(sources, targets):
        target[0] = source[...].astype(F32)
    d_model = gain.shape[2]
    gain[0] = sums[0:2, :d_model]
    shift[0] = sums[2:4, :d_model]
    out_bias[...] = sums[4:5, :d_model]
    lines = qkv_bias.shape[1] // COLS
    for k in range(lines):
        qkv_bias[:, k * COLS : (k + 1) * COLS] = sums[k : k + 1, d_model:]
    for k in range(up_bias.shape[1] // COLS):
        up_bias[:, k * COLS : (k + 1) * COLS] = sums[lines + k : lines + k + 1, d_model:]


def widened(grads, sums, d_model, qkv_width, ff):
    def rows_of(grad):
        return grad.shape[0] // WIDEN_STEPS, grad.shape[1]

    small = [(1, 2, d_model), (1, 2, d_model), (1, d_model), (1, qkv_width), (1, ff)]
    return pl.pallas_call(
        widen_kernel,
        grid=(WIDEN_STEPS,),
        out_shape=[jax.ShapeDtypeStruct((1,) + grad.shape, F32) for grad in grads]
        + [jax.ShapeDtypeStruct(shape, F32) for shape in small],
        in_specs=[pl.BlockSpec(sums.shape, lambda i: (0, 0))]
        + [pl.BlockSpec(rows_of(grad), lambda i: (i, 0)) for grad in grads],
        out_specs=[pl.BlockSpec((1,) + rows_of(grad), lambda i: (0, i, 0)) for grad in grads]
        + [pl.BlockSpec(shape, lambda i, zeros=(0,) * len(shape): zeros) for shape in small],
        name="widened",
    )(sums, *grads)


def relay_shards(
    block_input,
    doc_lengths,
    norm_gain,
    norm_bias,
    qkv_weight,
    qkv_bias,
    dense_weight,
    dense_bias,
    up_weight,
    up_bias,
    down_weight,
    down_bias,
    cotangent,
):
    weights = tuple(
        array[0]
        for array in (
            norm_gain,
            norm_bias,
            qkv_weight,
            qkv_bias,
            dense_weight,
            dense_bias,
            up_weight,
            up_bias,
            down_weight,
            down_bias,
        )
    )
    micro, rows, d_model = block_input.shape
    group = rows * lax.axis_size("tensor")
    wide = lax.axis_size("wide")
    heads = qkv_weight.shape[2] // (3 * HEAD_DIM)
    ff = up_weight.shape[2]
    dims = (micro, rows, group, wide, heads, d_model, ff)
    out, input_grad, *_, up_grad, down_grad, dense_grad, qkv_grad, _, sums = relay(
        dims, doc_lengths, block_input, cotangent, weights, 1
    )
    up_grad, down_grad, dense_grad, qkv_grad, gain, shift, out_bias, qkv_b, up_b = widened(
        (up_grad, down_grad, dense_grad, qkv_grad), sums, d_model, qkv_weight.shape[2], ff
    )
    return (
        out[None],
        input_grad[None],
        gain,
        shift,
        qkv_grad,
        qkv_b,
        dense_grad,
        out_bias,
        up_grad,
        up_b,
        down_grad,
        out_bias,
    )


def shortened(shard):

    def short(part):
        return part.astype(jnp.bfloat16) if part.dtype == jnp.float32 else part

    return jax.tree.map(short, shard)


def from_behind(block, axis, distance):
    devices = range(lax.axis_size(axis))
    route = [(i - distance, i) for i in devices if i - distance in devices]
    return lax.ppermute(block, axis, route)


def norm_parts(values, gain, shift):
    center = jnp.mean(values, axis=-1, keepdims=True)
    centred = values - center
    spread = jnp.mean(centred * centred, axis=-1, keepdims=True)
    inv_scale = lax.rsqrt(spread + EPSILON)
    normed = centred * inv_scale
    return (normed * gain + shift, normed, inv_scale)


def norm_back(grad, normed, inv_scale, gain):
    scaled = grad * gain
    inner_mean = jnp.mean(scaled, axis=-1, keepdims=True)
    cross_mean = jnp.mean(scaled * normed, axis=-1, keepdims=True)
    return inv_scale * (scaled - inner_mean - normed * cross_mean)


def doc_layout(lengths, tok_index):
    ends = jnp.cumsum(lengths)
    starts = ends - lengths
    doc_ids = jnp.sum((tok_index[:, None] >= ends[None, :]).astype(jnp.int32), axis=1)
    numbers = jnp.arange(lengths.shape[0], dtype=jnp.int32)
    picked = doc_ids[:, None] == numbers[None, :]
    begins = jnp.sum(jnp.where(picked, starts[None, :], 0), axis=1)
    return (doc_ids, tok_index - begins)


def rope_tables(offsets):
    half = ROT // 2
    freqs = ROPE_BASE ** (-2.0 * jnp.arange(half, dtype=jnp.float32) / ROT)
    angle = offsets.astype(jnp.float32)[:, None] * freqs[None, :]
    return (jnp.cos(angle)[:, None, :], jnp.sin(angle)[:, None, :])


def rotate(values, cos_table, sin_table):
    half = ROT // 2
    front = values[..., :half]
    back = values[..., half:ROT]
    turned = [
        front * cos_table - back * sin_table,
        back * cos_table + front * sin_table,
        values[..., ROT:],
    ]
    return jnp.concatenate(turned, axis=-1)


def unrotate(values, cos_table, sin_table):
    half = ROT // 2
    front = values[..., :half]
    back = values[..., half:ROT]
    turned = [
        front * cos_table + back * sin_table,
        back * cos_table - front * sin_table,
        values[..., ROT:],
    ]
    return jnp.concatenate(turned, axis=-1)


def gelu_parts(pre_act):
    cumul = 0.5 * (1.0 + lax.erf(pre_act * (1.0 / math.sqrt(2.0))))
    density = jnp.exp(-0.5 * pre_act * pre_act) * (1.0 / math.sqrt(2.0 * math.pi))
    return (pre_act * cumul, cumul + pre_act * density)


def store_slot(buffer, update, slot_here, is_valid):
    previous = lax.dynamic_index_in_dim(buffer, slot_here, 0, keepdims=False)
    return lax.dynamic_update_index_in_dim(
        buffer, jnp.where(is_valid, update, previous), slot_here, 0
    )


def gather_keys(key_rows, value_rows):
    return (
        lax.all_gather(key_rows, "wide", axis=0, tiled=True),
        lax.all_gather(value_rows, "wide", axis=0, tiled=True),
    )


def forward_parts(inputs, lengths, weights, with_output):
    (
        norm_gain,
        norm_bias,
        qkv_weight,
        qkv_bias,
        dense_weight,
        dense_bias,
        up_weight,
        up_bias,
        down_weight,
        down_bias,
    ) = weights
    seq_len = SEQ
    group = inputs.shape[0] * lax.axis_size("tensor")
    head_count = qkv_weight.shape[1] // (3 * HEAD_DIM)
    factor = 1.0 / math.sqrt(HEAD_DIM)
    values = inputs.astype(jnp.float32)
    norm_first, normed_first, scale_first = norm_parts(values, norm_gain[0], norm_bias[0])
    norm_second, normed_second, scale_second = norm_parts(values, norm_gain[1], norm_bias[1])
    full_first, full_second = (
        lax.all_gather(norm_first.astype(jnp.bfloat16), "tensor", axis=0, tiled=True),
        lax.all_gather(norm_second.astype(jnp.bfloat16), "tensor", axis=0, tiled=True),
    )
    tok_index = lax.axis_index("wide") * group + jnp.arange(group, dtype=jnp.int32)
    doc_ids, offsets = doc_layout(lengths, tok_index)
    all_index = jnp.arange(seq_len, dtype=jnp.int32)
    all_docs = doc_layout(lengths, all_index)[0]
    cos_table, sin_table = rope_tables(offsets)
    packed = jnp.dot(full_first, qkv_weight, preferred_element_type=jnp.float32) + qkv_bias
    packed = packed.reshape(group, head_count, 3, HEAD_DIM)
    queries = rotate(packed[:, :, 0], cos_table, sin_table).astype(jnp.bfloat16)
    key_here = rotate(packed[:, :, 1], cos_table, sin_table).astype(jnp.bfloat16)
    value_here = packed[:, :, 2].astype(jnp.bfloat16)
    key_all, value_all = gather_keys(key_here.reshape(group, -1), value_here.reshape(group, -1))
    key_heads = key_all.reshape(seq_len, head_count, HEAD_DIM)
    value_heads = value_all.reshape(seq_len, head_count, HEAD_DIM)
    allowed = (doc_ids[:, None] == all_docs[None, :]) & (all_index[None, :] <= tok_index[:, None])
    raw_scores = jnp.einsum("qhd,khd->qhk", queries, key_heads, preferred_element_type=jnp.float32)
    scores = jnp.where(allowed[:, None, :], raw_scores * factor, -jnp.inf)
    row_max = jnp.max(scores, axis=-1, keepdims=True)
    log_total = row_max + jnp.log(jnp.sum(jnp.exp(scores - row_max), axis=-1, keepdims=True))
    attn_probs = jnp.exp(scores - log_total)
    probs_low = attn_probs.astype(jnp.bfloat16)
    mixed_out = jnp.einsum(
        "qhk,khd->qhd", probs_low, value_heads, preferred_element_type=jnp.float32
    )
    mixed_out = mixed_out.reshape(group, -1).astype(jnp.bfloat16)
    up_pre = jnp.dot(full_second, up_weight, preferred_element_type=jnp.float32) + up_bias
    up_act, gelu_slope = gelu_parts(up_pre)
    hidden = up_act.astype(jnp.bfloat16)
    output = None
    if with_output:
        partial_value = jnp.dot(mixed_out, dense_weight, preferred_element_type=jnp.float32)
        partial_value = partial_value + jnp.dot(
            hidden, down_weight, preferred_element_type=jnp.float32
        )
        branch = (
            lax.psum_scatter(
                partial_value.astype(jnp.bfloat16), "tensor", scatter_dimension=0, tiled=True
            ).astype(jnp.float32)
            + dense_bias
            + down_bias
        )
        output = (values + branch).astype(jnp.bfloat16)
    return dict(
        output=output,
        normed_first=normed_first,
        scale_first=scale_first,
        normed_second=normed_second,
        scale_second=scale_second,
        full_first=full_first,
        full_second=full_second,
        tok_index=tok_index,
        doc_ids=doc_ids,
        all_index=all_index,
        all_docs=all_docs,
        cos_table=cos_table,
        sin_table=sin_table,
        queries=queries,
        key_here=key_here,
        value_here=value_here,
        key_all=key_all,
        value_all=value_all,
        key_heads=key_heads,
        value_heads=value_heads,
        attn_probs=attn_probs,
        probs_low=probs_low,
        log_total=log_total,
        mixed_out=mixed_out,
        gelu_slope=gelu_slope,
        hidden=hidden,
    )


def backward_parts(inputs, grad_out, lengths, weights):
    (
        norm_gain,
        norm_bias,
        qkv_weight,
        qkv_bias,
        dense_weight,
        dense_bias,
        up_weight,
        up_bias,
        down_weight,
        down_bias,
    ) = weights
    parts = forward_parts(inputs, lengths, weights, False)
    seq_len = SEQ
    group = inputs.shape[0] * lax.axis_size("tensor")
    head_count = qkv_weight.shape[1] // (3 * HEAD_DIM)
    factor = 1.0 / math.sqrt(HEAD_DIM)
    cos_table = parts["cos_table"]
    sin_table = parts["sin_table"]
    grad_low = grad_out.astype(jnp.bfloat16)
    grad_rows = grad_low.astype(jnp.float32)
    grad_full = lax.all_gather(grad_low, "tensor", axis=0, tiled=True)
    dense_grad = jnp.einsum(
        "cf,cd->fd", parts["mixed_out"], grad_full, preferred_element_type=jnp.float32
    )
    down_grad = jnp.einsum(
        "cf,cd->fd", parts["hidden"], grad_full, preferred_element_type=jnp.float32
    )
    hidden_grad = jnp.einsum(
        "cd,fd->cf", grad_full, down_weight, preferred_element_type=jnp.float32
    )
    pre_grad = (hidden_grad * parts["gelu_slope"]).astype(jnp.bfloat16)
    up_grad = jnp.einsum(
        "cd,cf->df", parts["full_second"], pre_grad, preferred_element_type=jnp.float32
    )
    up_bias_grad = jnp.sum(pre_grad.astype(jnp.float32), axis=0)
    second_grad = jnp.einsum("cf,df->cd", pre_grad, up_weight, preferred_element_type=jnp.float32)
    mixed_grad = jnp.einsum(
        "cd,fd->cf", grad_full, dense_weight, preferred_element_type=jnp.float32
    )
    mixed_grad = mixed_grad.astype(jnp.bfloat16).reshape(group, head_count, HEAD_DIM)
    attn_probs = parts["attn_probs"]
    probs_grad = jnp.einsum(
        "qhd,khd->qhk", mixed_grad, parts["value_heads"], preferred_element_type=jnp.float32
    )
    inner = jnp.sum(attn_probs * probs_grad, axis=-1, keepdims=True)
    score_grad = (attn_probs * (probs_grad - inner) * factor).astype(jnp.bfloat16)
    query_grad = jnp.einsum(
        "qhk,khd->qhd", score_grad, parts["key_heads"], preferred_element_type=jnp.float32
    )
    key_sums = jnp.einsum(
        "qhk,qhd->khd", score_grad, parts["queries"], preferred_element_type=jnp.float32
    )
    value_sums = jnp.einsum(
        "qhk,qhd->khd", parts["probs_low"], mixed_grad, preferred_element_type=jnp.float32
    )
    key_flat, value_flat = (
        lax.psum_scatter(
            key_sums.reshape(seq_len, -1).astype(jnp.bfloat16),
            "wide",
            scatter_dimension=0,
            tiled=True,
        ).astype(jnp.float32),
        lax.psum_scatter(
            value_sums.reshape(seq_len, -1).astype(jnp.bfloat16),
            "wide",
            scatter_dimension=0,
            tiled=True,
        ).astype(jnp.float32),
    )
    key_grad = key_flat.reshape(group, head_count, HEAD_DIM)
    value_grad = value_flat.reshape(group, head_count, HEAD_DIM)
    query_back = unrotate(query_grad, cos_table, sin_table)
    key_back = unrotate(key_grad, cos_table, sin_table)
    packed_grad = (
        jnp.stack([query_back, key_back, value_grad], axis=2)
        .reshape(group, -1)
        .astype(jnp.bfloat16)
    )
    qkv_grad = jnp.einsum(
        "cd,cf->df", parts["full_first"], packed_grad, preferred_element_type=jnp.float32
    )
    qkv_bias_grad = jnp.sum(packed_grad.astype(jnp.float32), axis=0)
    first_grad = jnp.einsum(
        "cf,df->cd", packed_grad, qkv_weight, preferred_element_type=jnp.float32
    )
    norm_first_grad, norm_second_grad = (
        lax.psum_scatter(
            first_grad.astype(jnp.bfloat16), "tensor", scatter_dimension=0, tiled=True
        ).astype(jnp.float32),
        lax.psum_scatter(
            second_grad.astype(jnp.bfloat16), "tensor", scatter_dimension=0, tiled=True
        ).astype(jnp.float32),
    )
    gain_grad = jnp.stack(
        [
            jnp.sum(norm_first_grad * parts["normed_first"], axis=0),
            jnp.sum(norm_second_grad * parts["normed_second"], axis=0),
        ]
    )
    shift_grad = jnp.stack([jnp.sum(norm_first_grad, axis=0), jnp.sum(norm_second_grad, axis=0)])
    input_grad = grad_out + norm_back(
        norm_first_grad, parts["normed_first"], parts["scale_first"], norm_gain[0]
    )
    input_grad = input_grad + norm_back(
        norm_second_grad, parts["normed_second"], parts["scale_second"], norm_gain[1]
    )
    bias_rows = jnp.sum(grad_rows, axis=0)
    terms = (
        gain_grad,
        shift_grad,
        qkv_grad,
        qkv_bias_grad,
        dense_grad,
        bias_rows,
        up_grad,
        up_bias_grad,
        down_grad,
        bias_rows,
    )
    return (input_grad, terms)


def general_shards(
    block_input,
    doc_lengths,
    norm_gain,
    norm_bias,
    qkv_weight,
    qkv_bias,
    dense_weight,
    dense_bias,
    up_weight,
    up_bias,
    down_weight,
    down_bias,
    cotangent,
):
    weights = (
        norm_gain[0],
        norm_bias[0],
        qkv_weight[0],
        qkv_bias[0],
        dense_weight[0],
        dense_bias[0],
        up_weight[0],
        up_bias[0],
        down_weight[0],
        down_bias[0],
    )
    section_index = lax.axis_index("section")
    last_section = lax.axis_size("section") - 1
    micro_count = block_input.shape[0]
    row_count = block_input.shape[1]
    tick_count = micro_count + last_section

    def forward_tick(carry, tick_index):
        incoming, kept_inputs, outputs, kept_pairs = carry
        slot_raw = tick_index - section_index
        is_valid = (slot_raw >= 0) & (slot_raw < micro_count)
        slot_here = jnp.clip(slot_raw, 0, micro_count - 1)
        fresh = lax.dynamic_index_in_dim(
            block_input, jnp.clip(tick_index, 0, micro_count - 1), 0, keepdims=False
        )
        inputs = jnp.where(section_index == 0, fresh, incoming)
        lengths = lax.dynamic_index_in_dim(doc_lengths, slot_here, 0, keepdims=False)
        parts = forward_parts(inputs, lengths, weights, True)
        output = parts["output"]
        kept_inputs = store_slot(kept_inputs, inputs, slot_here, is_valid)
        outputs = store_slot(outputs, output, slot_here, is_valid)
        incoming = jax.tree.map(
            lambda part, own: part.astype(own.dtype),
            from_behind(shortened(output), "section", 1),
            output,
        )
        return ((incoming, kept_inputs, outputs, kept_pairs), None)

    pair_init = (jnp.zeros((1,), jnp.bfloat16), jnp.zeros((1,), jnp.bfloat16))
    zero_rows = jnp.zeros((row_count, block_input.shape[2]), jnp.bfloat16)
    zero_stack = jnp.zeros(block_input.shape, jnp.bfloat16)
    forward_init = (zero_rows, zero_stack, zero_stack, pair_init)
    forward_done = lax.scan(forward_tick, forward_init, jnp.arange(tick_count, dtype=jnp.int32))[0]
    kept_inputs = forward_done[1]
    outputs = forward_done[2]
    kept_pairs = forward_done[3]

    def add_masked(total, term, scale_mask):
        return total + scale_mask * term

    def backward_tick(carry, tick_index):
        incoming, grads, input_grads = carry
        slot_raw = tick_index - (last_section - section_index)
        is_valid = (slot_raw >= 0) & (slot_raw < micro_count)
        slot_here = jnp.clip(slot_raw, 0, micro_count - 1)
        top_grad = lax.dynamic_index_in_dim(cotangent, slot_here, 0, keepdims=False)
        grad_out = jnp.where(section_index == last_section, top_grad, incoming)
        inputs = lax.dynamic_index_in_dim(kept_inputs, slot_here, 0, keepdims=False)
        lengths = lax.dynamic_index_in_dim(doc_lengths, slot_here, 0, keepdims=False)
        input_grad, terms = backward_parts(inputs, grad_out, lengths, weights)
        scale_mask = is_valid.astype(jnp.float32)
        grads = tuple((add_masked(total, term, scale_mask) for total, term in zip(grads, terms)))
        input_grads = store_slot(input_grads, input_grad, slot_here, is_valid)
        incoming = from_behind(shortened(input_grad), "section", -1).astype(input_grad.dtype)
        return ((incoming, grads, input_grads), None)

    grad_init = tuple((jnp.zeros(weight.shape, jnp.float32) for weight in weights))
    backward_init = (
        jnp.zeros((row_count, block_input.shape[2]), jnp.float32),
        grad_init,
        jnp.zeros(block_input.shape, jnp.float32),
    )
    backward_done = lax.scan(backward_tick, backward_init, jnp.arange(tick_count, dtype=jnp.int32))[
        0
    ]
    grads = backward_done[1]
    input_grads = backward_done[2]
    wide_sums = (
        lax.psum(grads[2].astype(jnp.bfloat16), "wide").astype(jnp.float32),
        lax.psum(grads[3].astype(jnp.bfloat16), "wide").astype(jnp.float32),
        lax.psum(grads[4].astype(jnp.bfloat16), "wide").astype(jnp.float32),
        lax.psum(grads[6].astype(jnp.bfloat16), "wide").astype(jnp.float32),
        lax.psum(grads[7].astype(jnp.bfloat16), "wide").astype(jnp.float32),
        lax.psum(grads[8].astype(jnp.bfloat16), "wide").astype(jnp.float32),
    )
    shared = lax.psum((grads[0], grads[1], grads[5], grads[9]), ("tensor", "wide"))
    return (
        outputs[None],
        input_grads[None],
        shared[0][None],
        shared[1][None],
        wide_sums[0][None],
        wide_sums[1][None],
        wide_sums[2][None],
        shared[2][None],
        wide_sums[3][None],
        wide_sums[4][None],
        wide_sums[5][None],
        shared[3][None],
    )


def solution(mesh):
    placed = (
        P(None, ("wide", "tensor"), None),
        P(),
        P("section", None, None),
        P("section", None, None),
        P("section", None, "tensor"),
        P("section", "tensor"),
        P("section", "tensor", None),
        P("section", None),
        P("section", None, "tensor"),
        P("section", "tensor"),
        P("section", "tensor", None),
        P("section", None),
        P(None, ("wide", "tensor"), None),
    )
    results = (
        P("section", None, ("wide", "tensor"), None),
        P("section", None, ("wide", "tensor"), None),
        P("section", None, None),
        P("section", None, None),
        P("section", None, "tensor"),
        P("section", "tensor"),
        P("section", "tensor", None),
        P("section", None),
        P("section", None, "tensor"),
        P("section", "tensor"),
        P("section", "tensor", None),
        P("section", None),
    )

    def program(*args):
        heads = args[4].shape[2] // (3 * HEAD_DIM * mesh.shape["tensor"])
        micro, seq_len, d_model = args[0].shape
        group = seq_len // mesh.shape["wide"]
        fits = heads == mesh.shape["wide"] == 8
        fits = fits and mesh.shape["section"] == 2 and mesh.shape["tensor"] == 2
        fits = fits and micro * group == d_model and args[8].shape[2] == 4 * d_model
        body = relay_shards if fits and group == TILE else general_shards
        return jax.shard_map(
            body, mesh=mesh, in_specs=placed, out_specs=results, check_vma=False
        )(*args)

    return program
```

```python
import functools
import math

import jax
import jax.numpy as jnp
from jax import lax
from jax.experimental import pallas as pl
from jax.experimental.pallas import tpu as pltpu
from jax.sharding import PartitionSpec as P

HEAD_DIM = 64
ROT = 16
SEQ = 2048


EPSILON = 1e-05
ROPE_BASE = 10000.0

MESH = pl.DeviceIdType.MESH
F32 = jnp.float32
BF16 = jnp.bfloat16
LANES = 128
BLOCK = 512
COLS = 512
NEG = -1e30
SCORE_SCALE = math.log2(math.e) / math.sqrt(HEAD_DIM)


TILE = 256
ACROSS = 256
AHEAD = 3
RING = 8
TOTALS = 8
LAGS = (2, 5, 8, 12, 15)
OWN = 16
GUESTS = 10
EARLY = 24


def gradient_kinds(d_model, inner, ff):
    return ((d_model, ff), (ff, d_model), (inner, d_model), (d_model, 3 * inner))


def dot(a, b):
    return jnp.dot(a, b, preferred_element_type=F32)


def dot_t(a, b):
    return lax.dot_general(a, b, (((1,), (1,)), ((), ())), preferred_element_type=F32)


def t_dot(a, b):
    return lax.dot_general(a, b, (((0,), (0,)), ((), ())), preferred_element_type=F32)


def lane_low(rows):
    return lax.broadcasted_iota(jnp.int32, (rows, LANES), 1) < HEAD_DIM


def turn(values):
    return pltpu.roll(values, HEAD_DIM, 1)


def rotary(values, cos_ref, front_ref, back_ref, seq, sign):
    cos, front, back = cos_ref[seq], front_ref[seq], back_ref[seq]
    ahead = pltpu.roll(values, LANES - ROT // 2, 1)
    behind = pltpu.roll(values, ROT // 2, 1)
    return values * cos + sign * (ahead * front + behind * back)


def pair_up(first, second, low):
    return jnp.where(low, first, turn(second)), jnp.where(low, turn(first), second)


def relay_kernel(
    dims,
    lengths,
    x_hbm,
    cot_hbm,
    gain,
    shift,
    qkv_b,
    up_b,
    dense_b,
    down_b,
    wqkv_hbm,
    wdense_hbm,
    wup_hbm,
    wdown_hbm,
    out_hbm,
    ig_hbm,
    norm_hbm,
    g_hbm,
    mixed_hbm,
    hid_hbm,
    dpre_hbm,
    dpk_hbm,
    up_out,
    down_out,
    dense_out,
    qkv_out,
    guest_hbm,
    sums,
    small,
    bias_sums,
    cos,
    front,
    back,
    wqkv,
    wdense,
    wup,
    wdown,
    xfull,
    gfull,
    cot,
    qkv_r,
    mix_r,
    do_r,
    dqkv_r,
    rsf_r,
    rsb_r,
    qkv_st,
    o_st,
    do_st,
    dqkv_st,
    rsf_st,
    rsb_st,
    out_st,
    gx_st,
    ig_st,
    norm_st,
    mixed_st,
    hid_st,
    dpre_st,
    dpk_st,
    slope,
    part,
    part_b,
    dn1,
    qm,
    kr,
    vx,
    dox,
    dq,
    lse,
    delta,
    scores,
    peak,
    acc,
    wsem,
    ownx_sem,
    yx_s,
    yx_r,
    owng_sem,
    yg_s,
    yg_r,
    qkv_ss,
    qkv_rs,
    o_ss,
    o_rs,
    do_ss,
    do_rs,
    dqkv_ss,
    dqkv_rs,
    rsf_ss,
    rsf_rs,
    rsb_ss,
    rsb_rs,
    xs_ss,
    gs_ss,
    store_sem,
    g_store,
    core_r,
    outer_r,
    inner_r,
    turned,
    sums_r,
    op_sem,
    core_ss,
    core_rs,
    outer_rs,
    inner_rs,
    red_ss,
    bc_rs,
    tot_ss,
    fwd_ss,
    share_ss,
    fin_rs,
    sum_ss,
    sum_rs,
    guest_ss,
    guest_rs,
    core_free,
    outer_free,
    inner_free,
):
    micro, rows, group, wide, heads, d_model, ff = dims
    sect = lax.axis_index("section")
    tens = lax.axis_index("tensor")
    me = lax.axis_index("wide")
    pairs = heads // 2
    per_source = group + group // 2
    half = group // 2
    q_blocks = SEQ // BLOCK
    sources = BLOCK // group
    my_rows = pl.ds(pl.multiple_of(tens * rows, rows), rows)
    his_rows = pl.ds(pl.multiple_of((1 - tens) * rows, rows), rows)
    x_dev = {"section": 1 - sect}
    y_dev = {"tensor": 1 - tens}
    low_half = lane_low(half)
    low_group = lane_low(group)

    def remote(src, dst, ss, rs, dev):
        return pltpu.make_async_remote_copy(
            src_ref=src, dst_ref=dst, send_sem=ss, recv_sem=rs, device_id=dev, device_id_type=MESH
        )

    def arrived(ref, sem):
        pltpu.make_async_copy(ref, ref, sem).wait()

    def tokens_of(s):
        return pl.ds(pl.multiple_of(s * group, group), group)

    def y_send_x(s):
        own = xfull.at[s, my_rows]
        return remote(own, own, yx_s.at[s], yx_r.at[s], y_dev)

    def y_send_g(s):
        own = gfull.at[s, my_rows]
        return remote(own, own, yg_s.at[s], yg_r.at[s], y_dev)

    def spread(stage, target, seq, dest, ss, rs):
        @pl.when(dest == me)
        def _():
            pltpu.make_async_copy(stage, target.at[seq, me], rs).start()

        @pl.when(dest != me)
        def _():
            remote(stage, target.at[seq, me], ss, rs, {"wide": dest}).start()

    loads = [
        pltpu.make_async_copy(source, target, wsem.at[i])
        for i, (source, target) in enumerate(
            ((wqkv_hbm, wqkv), (wup_hbm, wup), (wdown_hbm, wdown), (wdense_hbm, wdense))
        )
    ]

    barrier = pltpu.get_barrier_semaphore()
    for dev in [x_dev, y_dev] + [{"wide": lax.rem(me + k, wide)} for k in range(1, wide)]:
        pl.semaphore_signal(barrier, inc=1, device_id=dev, device_id_type=MESH)

    @pl.when(sect == 0)
    def _():
        for s in range(micro):
            pltpu.make_async_copy(x_hbm.at[s], xfull.at[s, my_rows], ownx_sem.at[s]).start()

    for load in loads:
        load.start()

    @pl.when(sect == 1)
    def _():
        for s in range(micro):
            pltpu.make_async_copy(cot_hbm.at[s], cot.at[s], owng_sem.at[s]).start()

    def starts_of(s, tokens):
        found = jnp.zeros_like(tokens)
        end = jnp.int32(0)
        for j in range(lengths.shape[1]):
            end = end + lengths[s, j]
            found = jnp.where(tokens >= end, end, found)
        return found

    lane = lax.rem(lax.broadcasted_iota(jnp.int32, (8, LANES), 1), HEAD_DIM)
    number = lax.rem(lane, ROT // 2)
    freq = jnp.zeros((8, LANES), F32)
    for k in range(ROT // 2):
        freq = jnp.where(number == k, ROPE_BASE ** (-2.0 * k / ROT), freq)
    lane, freq = lane[0:1, :], freq[0:1, :]

    def table_step(s, carry):
        tokens = me * group + lax.broadcasted_iota(jnp.int32, (group, LANES), 0)
        angle = (tokens - starts_of(s, tokens)).astype(F32) * freq
        sine = jnp.sin(angle)
        cos[s] = jnp.where(lane < ROT, jnp.cos(angle), 1.0)
        front[s] = jnp.where(lane < ROT // 2, -sine, 0.0)
        back[s] = jnp.where((lane >= ROT // 2) & (lane < ROT), sine, 0.0)
        return carry

    lax.fori_loop(0, micro, table_step, 0)
    small[...] = jnp.zeros_like(small)
    bias_sums[...] = jnp.zeros_like(bias_sums)
    pl.semaphore_wait(barrier, wide + 1)

    @pl.when(sect == 0)
    def _():
        for s in range(micro):
            remote(x_hbm.at[s], xfull.at[s, my_rows], yx_s.at[s], yx_r.at[s], y_dev).start()
        for s in range(micro):
            arrived(xfull.at[s, my_rows], ownx_sem.at[s])

    @pl.when(sect == 1)
    def _():
        for s in range(micro):
            arrived(cot.at[s], owng_sem.at[s])

            def chunk(i, carry, s=s):
                at = pl.ds(pl.multiple_of(i * 32, 32), 32)
                there = pl.ds(pl.multiple_of(tens * rows + i * 32, 32), 32)
                gfull[s, there, :] = cot[s, at, :].astype(BF16)
                return carry

            lax.fori_loop(0, rows // 32, chunk, 0)
            y_send_g(s).start()

    def fold(values):
        total = values[0:8]
        for k in range(1, values.shape[0] // 8):
            total = total + values[k * 8 : (k + 1) * 8]
        return total

    def normed_rows(values):
        center = jnp.mean(values, axis=-1, keepdims=True)
        centred = values - center
        spread_of = jnp.mean(centred * centred, axis=-1, keepdims=True)
        inv = lax.rsqrt(spread_of + EPSILON)
        return centred * inv, inv

    def unpack_heads(s):
        def step(src, carry):
            qk = qkv_r[s, src, 0:group, :].astype(F32)
            at = pl.multiple_of(src * group, group)
            qm[pl.ds(at, group), :] = jnp.where(low_group, qk, 0.0).astype(BF16)
            kr[pl.ds(at, group), :] = turn(qk).astype(BF16)
            packed_v = qkv_r[s, src, group:per_source, :].astype(F32)
            ones = jnp.where(
                lax.broadcasted_iota(jnp.int32, (half, LANES), 1) == HEAD_DIM, 1.0, 0.0
            )
            vx[pl.ds(at, half), :] = jnp.where(low_half, packed_v, ones).astype(BF16)
            vx[pl.ds(pl.multiple_of(at + half, half), half), :] = jnp.where(
                low_half, turn(packed_v), ones
            ).astype(BF16)
            return carry

        lax.fori_loop(0, wide, step, 0, unroll=True)

    def forward_meet(s):
        arrived(xfull.at[s, my_rows], ownx_sem.at[s])
        y_send_x(s).start()

    def backward_meet(s):
        arrived(gfull.at[s, my_rows], owng_sem.at[s])
        y_send_g(s).start()

    def forward(s):
        arrived(xfull.at[s, his_rows], yx_r.at[s])

        def norm_step(i, carry):
            at = pl.ds(pl.multiple_of(i * 32, 32), 32)
            a, _ = normed_rows(xfull[s, at, :].astype(F32))
            norm_st[0, at, :] = (a * gain[0:1, :] + shift[0:1, :]).astype(BF16)
            norm_st[1, at, :] = (a * gain[1:2, :] + shift[1:2, :]).astype(BF16)
            return carry

        @pl.when(s > 0)
        def _():
            arrived(norm_st.at[0], store_sem.at[0])
            arrived(norm_st.at[1], store_sem.at[1])

        lax.fori_loop(0, group // 32, norm_step, 0, unroll=True)
        pltpu.make_async_copy(norm_st.at[0], norm_hbm.at[0, tokens_of(s)], store_sem.at[0]).start()
        pltpu.make_async_copy(norm_st.at[1], norm_hbm.at[1, tokens_of(s)], store_sem.at[1]).start()

        def qkv_step(k, carry):
            pair = lax.rem(me // 2 + 1 + k, pairs)
            cols = pl.ds(pl.multiple_of(pair * 3 * LANES, LANES), 3 * LANES)
            packed = dot(norm_st[0], wqkv[:, cols]) + qkv_b[:, cols]
            first, middle, last = (packed[:, i * LANES : (i + 1) * LANES] for i in range(3))
            qk0 = rotary(first, cos, front, back, s, 1.0)
            qk1 = rotary(
                turn(jnp.where(low_group, last, middle)), cos, front, back, s, 1.0
            )
            vv = jnp.where(low_group, middle, last)
            v0 = jnp.where(low_half, vv[:half], turn(vv[half:]))
            v1 = jnp.where(low_half, turn(vv[:half]), vv[half:])
            for i, (qk, v) in enumerate(((qk0, v0), (qk1, v1))):
                qkv_st[2 * pair + i, 0:group, :] = qk.astype(BF16)
                qkv_st[2 * pair + i, group:per_source, :] = v.astype(BF16)
            for i in range(2):
                dest = 2 * pair + i
                spread(qkv_st.at[dest], qkv_r, s, dest, qkv_ss.at[0], qkv_rs.at[s])
            return carry

        pl.when(s == 0)(loads[0].wait)
        lax.fori_loop(0, pairs, qkv_step, 0, unroll=True)

    def forward_ff(s):
        @pl.when(s == 0)
        def _():
            loads[1].wait()
            loads[2].wait()

        @pl.when(s > 0)
        def _():
            arrived(hid_st, store_sem.at[2])

        def ff_step(j, carry):
            cols = pl.ds(pl.multiple_of(j * COLS, COLS), COLS)
            pre = dot(norm_st[1], wup[:, cols]) + up_b[:, cols]
            cumul = 0.5 * (1.0 + lax.erf(pre * (1.0 / math.sqrt(2.0))))
            density = jnp.exp(-0.5 * pre * pre) * (1.0 / math.sqrt(2.0 * math.pi))
            hid = (pre * cumul).astype(BF16)
            hid_st[:, cols] = hid
            slope[s, :, cols] = (cumul + pre * density).astype(BF16)
            term = dot(hid, wdown[cols, :])

            @pl.when(j == 0)
            def _():
                part[...] = term

            @pl.when(j > 0)
            def _():
                part[...] += term

            return carry

        lax.fori_loop(0, ff // COLS, ff_step, 0, unroll=True)
        pltpu.make_async_copy(hid_st, hid_hbm.at[tokens_of(s)], store_sem.at[2]).start()

    def forward_attention(s):
        arrived(qkv_r.at[s], qkv_rs.at[s])
        arrived(qkv_st.at[pl.ds(0, wide - 1)], qkv_ss.at[0])
        unpack_heads(s)

        for i in range(q_blocks):
            q_at = slice(i * BLOCK, (i + 1) * BLOCK)
            tokens = i * BLOCK + lax.broadcasted_iota(jnp.int32, (BLOCK, LANES), 0)
            begin = starts_of(s, tokens)[:, 0:1]
            best = jnp.full((BLOCK, LANES), NEG, F32)
            for j in range(i + 1):
                k_at = slice(j * BLOCK, (j + 1) * BLOCK)
                raw = dot_t(qm[q_at, :], kr[k_at, :])
                u = j * BLOCK + lax.broadcasted_iota(jnp.int32, (BLOCK, BLOCK), 1)
                seen = u >= begin
                if i == j:
                    seen = seen & (u <= tokens[:, 0:1])
                raw = jnp.where(seen, raw, NEG)
                scores[:, k_at] = raw
                for k in range(BLOCK // LANES):
                    best = jnp.maximum(best, raw[:, k * LANES : (k + 1) * LANES])
            top = jnp.max(best, axis=1, keepdims=True) * SCORE_SCALE
            out = jnp.zeros((BLOCK, LANES), F32)
            for j in range(i + 1):
                k_at = slice(j * BLOCK, (j + 1) * BLOCK)
                probs = jnp.exp2(scores[:, k_at] * SCORE_SCALE - top)
                out = out + dot(probs.astype(BF16), vx[k_at, :])
            total = out[:, HEAD_DIM : HEAD_DIM + 1]
            out = out / total
            log_total = top + jnp.log2(total)
            lse[s, i] = jnp.broadcast_to(log_total, (BLOCK, LANES)).T[0:8, :]
            for k in range(sources):
                first = out[k * group : k * group + half]
                second = out[k * group + half : (k + 1) * group]
                source = i * sources + k
                o_st[s, source] = jnp.where(low_half, first, turn(second)).astype(BF16)
                spread(o_st.at[s, source], mix_r, s, source, o_ss.at[s], o_rs.at[s])

    def forward_out(s):
        arrived(mix_r.at[s], o_rs.at[s])
        arrived(o_st.at[s, pl.ds(0, wide - 1)], o_ss.at[s])
        pl.when((s == 0) & (sect == 0))(loads[3].wait)
        pl.when(s > 0)(lambda: arrived(mixed_st, store_sem.at[3]))
        for pair in range(pairs):
            top, bottom = pair_up(
                mix_r[s, 2 * pair].astype(F32), mix_r[s, 2 * pair + 1].astype(F32), low_half
            )
            mixed_st[0:half, pair * LANES : (pair + 1) * LANES] = top.astype(BF16)
            mixed_st[half:group, pair * LANES : (pair + 1) * LANES] = bottom.astype(BF16)
        pltpu.make_async_copy(mixed_st, mixed_hbm.at[tokens_of(s)], store_sem.at[3]).start()
        part[...] += dot(mixed_st[...], wdense[...])
        rsf_st[...] = part[his_rows, :].astype(BF16)
        remote(rsf_st, rsf_r.at[s], rsf_ss.at[0], rsf_rs.at[s], y_dev).start()

    def forward_end(s):
        arrived(rsf_r.at[s], rsf_rs.at[s])
        arrived(rsf_st, rsf_ss.at[0])

        @pl.when(s > 0)
        def _():
            arrived(out_st, store_sem.at[4])
            pl.when(sect == 0)(lambda: arrived(out_st, xs_ss.at[0]))

        def out_step(i, carry):
            at = pl.ds(pl.multiple_of(i * 32, 32), 32)
            there = pl.ds(pl.multiple_of(tens * rows + i * 32, 32), 32)
            branch = part[there, :] + rsf_r[s, at, :].astype(F32) + (dense_b[...] + down_b[...])
            out_st[at, :] = (xfull[s, there, :].astype(F32) + branch).astype(BF16)
            return carry

        lax.fori_loop(0, rows // 32, out_step, 0, unroll=True)

        @pl.when(sect == 0)
        def _():
            remote(out_st, xfull.at[s, my_rows], xs_ss.at[0], ownx_sem.at[s], x_dev).start()

        pltpu.make_async_copy(out_st, out_hbm.at[s], store_sem.at[4]).start()

    def backward(s):
        arrived(gfull.at[s, his_rows], yg_r.at[s])
        pl.when((s == 0) & (sect == 1))(loads[3].wait)
        pltpu.make_async_copy(gfull.at[s], g_hbm.at[tokens_of(s)], g_store.at[s]).start()

        def mixed_step(k, carry):
            pair = lax.rem(me // 2 + 1 + k, pairs)
            at = pl.ds(pl.multiple_of(pair * LANES, LANES), LANES)
            both = dot_t(gfull[s], wdense[at, :])
            first = jnp.where(low_half, both[:half], turn(both[half:]))
            second = jnp.where(low_half, turn(both[:half]), both[half:])
            do_st[s, 2 * pair] = first.astype(BF16)
            do_st[s, 2 * pair + 1] = second.astype(BF16)
            for i in range(2):
                dest = 2 * pair + i
                spread(do_st.at[s, dest], do_r, s, dest, do_ss.at[s], do_rs.at[s])
            return carry

        lax.fori_loop(0, pairs, mixed_step, 0, unroll=True)

    def backward_ff(s):
        pl.when(s > 0)(lambda: arrived(dpre_st, store_sem.at[6]))

        def ff_step(j, carry):
            cols = pl.ds(pl.multiple_of(j * COLS, COLS), COLS)
            grad = dot_t(gfull[s], wdown[cols, :])
            grad = (grad * slope[s, :, cols].astype(F32)).astype(BF16)
            dpre_st[:, cols] = grad
            sums_at = pl.ds(pl.multiple_of(3 * heads * HEAD_DIM + j * COLS, COLS), COLS)
            bias_sums[:, sums_at] += fold(grad.astype(F32))
            term = dot_t(grad, wup[:, cols])

            @pl.when(j == 0)
            def _():
                dn1[...] = term

            @pl.when(j > 0)
            def _():
                dn1[...] += term

            return carry

        lax.fori_loop(0, ff // COLS, ff_step, 0, unroll=True)
        pltpu.make_async_copy(dpre_st, dpre_hbm.at[tokens_of(s)], store_sem.at[6]).start()

    def backward_attention(s):
        arrived(do_r.at[s], do_rs.at[s])
        arrived(do_st.at[s, pl.ds(0, wide - 1)], do_ss.at[s])
        pl.when(sect == 0)(lambda: unpack_heads(s))

        def unpack_step(src, carry):
            at = pl.multiple_of(src * group, group)
            grad = do_r[s, src].astype(F32)
            dox[pl.ds(at, half), :] = jnp.where(low_half, grad, 0.0).astype(BF16)
            dox[pl.ds(pl.multiple_of(at + half, half), half), :] = jnp.where(
                low_half, turn(grad), 0.0
            ).astype(BF16)
            product = grad * o_st[s, src].astype(F32)
            left = jnp.sum(jnp.where(low_half, product, 0.0), axis=1, keepdims=True)
            right = jnp.sum(jnp.where(low_half, 0.0, product), axis=1, keepdims=True)
            delta[src, :, 0:half] = jnp.broadcast_to(left, (half, LANES)).T[0:8, :]
            delta[src, :, half:group] = jnp.broadcast_to(right, (half, LANES)).T[0:8, :]
            return carry

        lax.fori_loop(0, wide, unpack_step, 0, unroll=True)
        slot = lax.rem(s, 2)
        rows_of = []
        for i in range(q_blocks):
            tokens = i * BLOCK + lax.broadcasted_iota(jnp.int32, (8, BLOCK), 1)
            inner_sum = jnp.concatenate(
                [delta[i * sources + k, 0:1, :] for k in range(sources)], axis=1
            )
            rows_of.append((starts_of(s, tokens)[0:1, :], tokens[0:1, :], inner_sum))
        for j in range(q_blocks):
            k_at = slice(j * BLOCK, (j + 1) * BLOCK)
            for i in range(j, q_blocks):
                q_at = slice(i * BLOCK, (i + 1) * BLOCK)
                begin, token, inner_sum = rows_of[i]
                raw = dot_t(kr[k_at, :], qm[q_at, :])
                u = j * BLOCK + lax.broadcasted_iota(jnp.int32, (BLOCK, BLOCK), 0)
                probs = jnp.exp2(raw * SCORE_SCALE - lse[s, i, 0:1, :])
                seen = u >= begin
                if i == j:
                    seen = seen & (u <= token)
                probs = jnp.where(seen, probs, 0.0)
                probs_grad = dot_t(vx[k_at, :], dox[q_at, :])
                score_grad = (probs * (probs_grad - inner_sum)).astype(BF16)
                value_term = dot(probs.astype(BF16), dox[q_at, :])
                key_term = dot(score_grad, kr[q_at, :])
                query_term = t_dot(score_grad, kr[k_at, :])
                if i == j:
                    acc[...] = value_term
                    peak[...] = key_term
                else:
                    acc[...] += value_term
                    peak[...] += key_term
                if j == 0:
                    dq[q_at, :] = query_term
                else:
                    dq[q_at, :] += query_term
            for k in range(sources):
                source = j * sources + k
                mine = slice(k * group, (k + 1) * group)
                at = slice(source * group, (source + 1) * group)
                both = jnp.where(low_group, dq[at, :], peak[mine, :])
                both = both * (1.0 / math.sqrt(HEAD_DIM))
                value = acc[mine, :]
                value = jnp.where(low_half, value[:half], turn(value[half:]))
                dqkv_st[slot, source, 0:group, :] = both.astype(BF16)
                dqkv_st[slot, source, group:per_source, :] = value.astype(BF16)
                spread(
                    dqkv_st.at[slot, source], dqkv_r, s, source, dqkv_ss.at[slot], dqkv_rs.at[s]
                )

    def backward_norm(s):
        arrived(dqkv_r.at[s], dqkv_rs.at[s])
        slot = lax.rem(s, 2)
        arrived(dqkv_st.at[slot, pl.ds(0, wide - 1)], dqkv_ss.at[slot])
        pl.when(s > 0)(lambda: arrived(dpk_st, store_sem.at[7]))

        def pair_step(pair, carry):
            qk0 = rotary(
                dqkv_r[s, 2 * pair, 0:group, :].astype(F32), cos, front, back, s, -1.0
            )
            qk1 = turn(
                rotary(
                    dqkv_r[s, 2 * pair + 1, 0:group, :].astype(F32), cos, front, back, s, -1.0
                )
            )
            top, bottom = pair_up(
                dqkv_r[s, 2 * pair, group:per_source, :].astype(F32),
                dqkv_r[s, 2 * pair + 1, group:per_source, :].astype(F32),
                low_half,
            )
            vv = jnp.concatenate([top, bottom], axis=0)
            columns = (qk0, jnp.where(low_group, vv, qk1), jnp.where(low_group, qk1, vv))
            for k, column in enumerate(columns):
                at = pl.ds(pl.multiple_of((pair * 3 + k) * LANES, LANES), LANES)
                column = column.astype(BF16)
                dpk_st[:, at] = column
                bias_sums[:, at] += fold(column.astype(F32))
            return carry

        lax.fori_loop(0, pairs, pair_step, 0, unroll=True)
        pltpu.make_async_copy(dpk_st, dpk_hbm.at[tokens_of(s)], store_sem.at[7]).start()
        part_b[...] = dot_t(dpk_st[...], wqkv[...])

        def e_step(i, carry):
            at = pl.ds(pl.multiple_of(i * 32, 32), 32)
            a, _ = normed_rows(xfull[s, at, :].astype(F32))
            first = part_b[at, :]
            second = dn1[at, :]
            small[0] += fold(first * a)
            small[1] += fold(second * a)
            small[2] += fold(first)
            small[3] += fold(second)
            part_b[at, :] = first * gain[0:1, :] + second * gain[1:2, :]
            return carry

        lax.fori_loop(0, group // 32, e_step, 0, unroll=True)
        rsb_st[...] = part_b[his_rows, :].astype(BF16)
        remote(rsb_st, rsb_r.at[s], rsb_ss.at[0], rsb_rs.at[s], y_dev).start()

    def backward_end(s):
        arrived(rsb_r.at[s], rsb_rs.at[s])
        arrived(rsb_st, rsb_ss.at[0])

        @pl.when(s > 0)
        def _():
            arrived(ig_st, store_sem.at[8])
            pl.when(sect == 1)(lambda: arrived(gx_st, gs_ss.at[0]))

        def in_step(i, carry):
            at = pl.ds(pl.multiple_of(i * 32, 32), 32)
            there = pl.ds(pl.multiple_of(tens * rows + i * 32, 32), 32)
            a, inv = normed_rows(xfull[s, there, :].astype(F32))
            e = part_b[there, :] + rsb_r[s, at, :].astype(F32)
            mean_e = jnp.mean(e, axis=-1, keepdims=True)
            cross = jnp.mean(e * a, axis=-1, keepdims=True)
            g_low = gfull[s, there, :].astype(F32)
            small[4] += fold(g_low)
            g = jnp.where(sect == 1, cot[s, at, :], g_low)
            grad = g + inv * (e - mean_e - a * cross)
            ig_st[at, :] = grad
            gx_st[at, :] = grad.astype(BF16)
            return carry

        lax.fori_loop(0, rows // 32, in_step, 0, unroll=True)

        @pl.when(s == micro - 1)
        def _():
            for k in range(micro):
                arrived(xfull.at[k, my_rows], yx_s.at[k])

        @pl.when(sect == 1)
        def _():
            remote(gx_st, gfull.at[s, my_rows], gs_ss.at[0], owng_sem.at[s], x_dev).start()

        pltpu.make_async_copy(ig_st, ig_hbm.at[s], store_sem.at[8]).start()

    chip, core = me // 2, lax.rem(me, 2)
    partner = {"wide": me + 1 - 2 * core}
    up_dev = {"wide": lax.rem(me + 2, wide)}
    down_dev = {"wide": lax.rem(me + wide - 2, wide)}
    at_bottom, at_top = chip == 0, chip == wide // 2 - 1
    at_end = at_bottom | at_top
    middle = jnp.logical_not(at_end)
    lower = chip == 1
    outer_of = {"wide": jnp.where(lower, me - 2, lax.rem(me + 2, wide))}
    inner_of = {"wide": jnp.where(lower, me + 2, lax.rem(me + wide - 2, wide))}
    end_of = {"wide": jnp.where(at_bottom, me + 2, lax.rem(me + wide - 2, wide))}
    kinds = gradient_kinds(d_model, heads * HEAD_DIM, ff)
    targets = (up_out, down_out, dense_out, qkv_out)
    operands = (
        (norm_hbm.at[1], dpre_hbm),
        (hid_hbm, g_hbm),
        (mixed_hbm, g_hbm),
        (norm_hbm.at[0], dpk_hbm),
    )
    ranges, first = [], 0
    for height, width in kinds:
        count = (height // TILE) * (width // (2 * ACROSS))
        ranges.append((first, first + count, width // (2 * ACROSS)))
        first += count
    steps = first

    def own_at(ring):
        rows_at = pl.ds(pl.multiple_of((ring // RING) * TILE, TILE), TILE)
        return scores.at[
            rows_at, pl.ds(pl.multiple_of(lax.rem(ring, RING) * ACROSS, ACROSS), ACROSS)
        ]

    def guest_at(number):
        cols = pl.ds(pl.multiple_of(lax.rem(number, 4) * ACROSS, ACROSS), ACROSS)
        return xfull.at[number // 4, :, cols]

    def guest_st_at(slot):
        return mixed_st.at[:, pl.ds(pl.multiple_of(slot * ACROSS, ACROSS), ACROSS)]

    def core_st_at(ring):
        return hid_st.at[:, pl.ds(pl.multiple_of(ring * ACROSS, ACROSS), ACROSS)]

    def red_st_at(ring):
        return dpre_st.at[:, pl.ds(pl.multiple_of(ring * ACROSS, ACROSS), ACROSS)]

    def tot_at(slot):
        cols = pl.ds(pl.multiple_of(lax.rem(slot, 4) * ACROSS, ACROSS), ACROSS)
        return norm_st.at[slot // 4, :, cols]

    def left_at(slot):
        return wup.at[:, pl.ds(pl.multiple_of(slot * TILE, TILE), TILE)]

    def right_at(slot):
        return wdown.at[
            pl.ds(pl.multiple_of((slot // 2) * d_model, d_model), d_model),
            pl.ds(pl.multiple_of(lax.rem(slot, 2) * 2 * ACROSS, 2 * ACROSS), 2 * ACROSS),
        ]

    tile_ref = core_r.at[0]

    def by_kind(m, body):
        for kind, (low, high, across) in enumerate(ranges):

            @pl.when((m >= low) & (m < high))
            def _(kind=kind, low=low, across=across):
                at = m - low
                body(kind, at // across, lax.rem(at, across))

    def tile_of(kind, row, col, which):
        return targets[kind].at[
            pl.ds(pl.multiple_of(row * TILE, TILE), TILE),
            pl.ds(pl.multiple_of((2 * col + which) * ACROSS, ACROSS), ACROSS),
        ]

    def fetch(m):
        pl.when(m == ranges[3][0])(lambda: arrived(dpk_st, store_sem.at[7]))

        def body(kind, row, col):
            left, right = operands[kind]
            slot = lax.rem(m, AHEAD + 1)

            @pl.when(col == 0)
            def _():
                pltpu.make_async_copy(
                    left.at[:, pl.ds(pl.multiple_of(row * TILE, TILE), TILE)],
                    left_at(slot),
                    op_sem.at[0, slot],
                ).start()

            pltpu.make_async_copy(
                right.at[:, pl.ds(pl.multiple_of(col * 2 * ACROSS, 2 * ACROSS), 2 * ACROSS)],
                right_at(slot),
                op_sem.at[1, slot],
            ).start()

        by_kind(m, body)

    total_steps = jnp.where(sect == 1, steps + GUESTS, steps)
    chain = jnp.where(sect == 1, steps + GUESTS, steps - GUESTS)
    visit = ranges[2][0]

    def place(m):
        shared = (sect == 0) & (m < 2 * GUESTS)
        away = shared & (lax.rem(m, 2) == 1)
        later = (sect == 1) & (m >= visit)
        visitor = later & (m < visit + GUESTS)
        n = jnp.where(shared, m // 2, jnp.where(sect == 0, m - GUESTS, m))
        number = jnp.where(visitor, m - visit, m // 2)
        tile = jnp.where(visitor, 2 * (m - visit) + 1, jnp.where(later, m - GUESTS, m))
        return away, visitor, n, number, tile

    def is_root(n):
        return middle & (chip == 1 + lax.rem(n, 2))

    def products(step_at, m):
        slot, ring = lax.rem(m, AHEAD + 1), lax.rem(m, RING)

        def body(kind, row, col):
            @pl.when(col == 0)
            def _():
                arrived(left_at(slot), op_sem.at[0, slot])
                turned[...] = left_at(slot)[...].T

        by_kind(m, body)
        arrived(right_at(slot), op_sem.at[1, slot])
        both = dot(turned[...], right_at(slot)[...])
        first, second = both[:, :ACROSS], both[:, ACROSS:]
        own_at(lax.rem(step_at, OWN))[...] = jnp.where(core == 0, first, second)

        @pl.when(m >= RING)
        def _():
            arrived(tile_ref, core_ss.at[ring])
            pl.semaphore_wait(core_free, 1)

        core_st_at(ring)[...] = jnp.where(core == 0, second, first).astype(BF16)
        remote(
            core_st_at(ring), core_r.at[ring], core_ss.at[ring], core_rs.at[ring], partner
        ).start()

    def send_red(m, value, target, sem, dev, free):
        ring = lax.rem(m, RING)

        @pl.when(m >= RING)
        def _():
            pl.semaphore_wait(free, 1)

        red_st_at(ring)[...] = value.astype(BF16)
        remote(red_st_at(ring), target.at[ring], red_ss.at[ring], sem.at[ring], dev).start()

    def chip_sum(m):
        away, visitor, n, number, tile = place(m)
        ring = lax.rem(tile, RING)
        own = own_at(lax.rem(m, OWN))

        @pl.when(visitor)
        def _():
            arrived(tile_ref, guest_rs.at[number])
            own[...] = guest_at(number)[...].astype(F32)

        @pl.when(jnp.logical_not(visitor))
        def _():
            arrived(tile_ref, core_rs.at[ring])
            own[...] = own[...] + core_r[ring].astype(F32)

            @pl.when(tile + RING < steps)
            def _():
                pl.semaphore_signal(core_free, inc=1, device_id=partner, device_id_type=MESH)

        @pl.when(away)
        def _():
            slot = lax.rem(number, 2)
            pl.when(number >= 2)(lambda: arrived(tile_ref, guest_ss.at[slot]))
            guest_st_at(slot)[...] = own[...].astype(BF16)
            remote(
                guest_st_at(slot),
                guest_at(number),
                guest_ss.at[slot],
                guest_rs.at[number],
                x_dev,
            ).start()

        @pl.when(at_end & jnp.logical_not(away))
        def _():
            pl.when(n >= RING)(lambda: arrived(tile_ref, red_ss.at[lax.rem(n, RING)]))
            send_red(n, own[...], outer_r, outer_rs, end_of, outer_free.at[lax.rem(n, 2)])

    def take_outer(m, n):
        ring = lax.rem(n, RING)
        arrived(tile_ref, outer_rs.at[ring])
        total = own_at(lax.rem(m, OWN))[...] + outer_r[ring].astype(F32)

        @pl.when(n + RING < chain)
        def _():
            pl.semaphore_signal(
                outer_free.at[lax.rem(n, 2)], inc=1, device_id=outer_of, device_id_type=MESH
            )

        return total

    def pass_in(m):
        _, _, n, _, _ = place(m)
        total = take_outer(m, n)
        pl.when(n >= RING)(lambda: arrived(tile_ref, red_ss.at[lax.rem(n, RING)]))
        send_red(n, total, inner_r, inner_rs, inner_of, inner_free)

    def finish(m):
        _, visitor, n, number, tile = place(m)
        ring = lax.rem(n, RING)
        slot = lax.rem(n // 2, TOTALS)
        total = take_outer(m, n)
        arrived(tile_ref, inner_rs.at[ring])
        total = total + inner_r[ring].astype(F32)

        @pl.when(n + RING < chain)
        def _():
            pl.semaphore_signal(inner_free, inc=1, device_id=inner_of, device_id_type=MESH)

        @pl.when(n >= 2 * TOTALS)
        def _():
            for k in range(4):
                arrived(tile_ref, tot_ss.at[k, slot])

        tot_at(slot)[...] = total.astype(BF16)

        def send(here):
            remote(tot_at(slot), here, tot_ss.at[0, slot], bc_rs.at[m], outer_of).start()
            remote(tot_at(slot), here, tot_ss.at[1, slot], bc_rs.at[m], inner_of).start()
            pltpu.make_async_copy(tot_at(slot), here, tot_ss.at[3, slot]).start()

        def body(kind, row, col):
            here = tile_of(kind, row, col, core)

            @pl.when(visitor)
            def _():
                send(guest_hbm.at[number])
                remote(tot_at(slot), here, tot_ss.at[2, slot], bc_rs.at[tile], x_dev).start()

            @pl.when(jnp.logical_not(visitor))
            def _():
                send(here)
                remote(
                    tot_at(slot), here, tot_ss.at[2, slot], fin_rs.at[kind], partner
                ).start()

        by_kind(tile, body)

    def hand_on(m):
        _, visitor, _, number, tile = place(m)
        arrived(tile_ref, bc_rs.at[m])

        def body(kind, row, col):
            here = tile_of(kind, row, col, core)

            @pl.when(visitor)
            def _():
                held = guest_hbm.at[number]

                @pl.when(middle)
                def _():
                    remote(held, held, fwd_ss.at[m], bc_rs.at[m], outer_of).start()

                remote(held, here, share_ss.at[m], bc_rs.at[tile], x_dev).start()

            @pl.when(jnp.logical_not(visitor))
            def _():
                @pl.when(middle)
                def _():
                    remote(here, here, fwd_ss.at[m], bc_rs.at[m], outer_of).start()

                remote(here, here, share_ss.at[m], fin_rs.at[kind], partner).start()

        by_kind(tile, body)

    def guest_home(number, carry):
        m = 2 * number + 1
        arrived(tile_ref, bc_rs.at[m])

        def body(kind, row, col):
            here = tile_of(kind, row, col, core)
            remote(here, here, share_ss.at[m], fin_rs.at[kind], partner).start()

        by_kind(m, body)
        return carry

    exchanges = (
        {"tensor": 1 - tens},
        partner,
        {"wide": me + 2 - 4 * lax.rem(chip, 2)},
        {"wide": me + 4 - 8 * (chip // 2)},
    )

    def sums_begin():
        sums[:, 0:d_model] = jnp.concatenate(
            [jnp.sum(small[k], axis=0, keepdims=True) for k in range(5)]
            + [jnp.zeros((3, d_model), F32)],
            axis=0,
        )
        total = jnp.sum(bias_sums[...], axis=0, keepdims=True)
        lines = [total[:, k * COLS : (k + 1) * COLS] for k in range(total.shape[1] // COLS)]
        lines.append(jnp.zeros((8 - len(lines), COLS), F32))
        sums[:, d_model:] = jnp.concatenate(lines, axis=0)

    def exchange_start(k):
        if k == 0:
            sums_begin()
        else:
            arrived(sums, sum_ss.at[0])
        sums_r[0] = sums[...]
        remote(sums_r.at[0], sums_r.at[k + 1], sum_ss.at[0], sum_rs.at[k], exchanges[k]).start()

    def exchange_end(k):
        arrived(sums, sum_rs.at[k])
        if k == 0:
            sums[:, 0:d_model] += sums_r[1, :, 0:d_model]
        else:
            sums[...] += sums_r[k + 1]

    def gradient_step(i, carry):
        _, visits, _, _, here_tile = place(i)
        works = (i < total_steps) & jnp.logical_not(visits)
        pl.when(works & (here_tile + AHEAD < steps))(lambda: fetch(here_tile + AHEAD))
        pl.when(works)(lambda: products(i, here_tile))
        for k in range(4):
            pl.when(i == EARLY + 4 * k + 2)(lambda k=k: exchange_start(k))
            pl.when(i == EARLY + 4 * k + 5)(lambda k=k: exchange_end(k))

        def late(lag, allowed, body):
            m = i - lag
            away, _, n, _, _ = place(m)
            inside = (m >= 0) & (m < total_steps)
            pl.when(inside & allowed(away, n))(lambda: body(m))

        def outside(away, n):
            return middle & jnp.logical_not(away | is_root(n))

        late(LAGS[0], lambda away, n: n >= 0, chip_sum)
        late(LAGS[1], outside, pass_in)
        late(LAGS[2], lambda away, n: is_root(n) & jnp.logical_not(away), finish)
        late(LAGS[3], outside, hand_on)
        late(LAGS[4], lambda away, n: at_end & jnp.logical_not(away), hand_on)
        return carry

    def gradient_begin():
        arrived(norm_st.at[0], store_sem.at[0])
        arrived(norm_st.at[1], store_sem.at[1])
        arrived(hid_st, store_sem.at[2])
        arrived(mixed_st, store_sem.at[3])
        arrived(dpre_st, store_sem.at[6])
        for s in range(micro):
            arrived(gfull.at[s], g_store.at[s])
        for m in range(AHEAD):
            fetch(jnp.int32(m))

    def at(seq, allowed, body):
        pl.when(allowed & (seq >= 0) & (seq < micro))(lambda: body(seq))

    @pl.when(sect == 1)
    def _():
        lax.fori_loop(0, micro, lambda s, carry: (backward(s), carry)[1], 0)

    first = jnp.int32(0)
    pl.when(sect == 1)(lambda: forward_meet(first))
    forward(first)
    forward_ff(first)
    always = sect >= 0

    def step(i, carry):
        f = i
        b = jnp.where(sect == 1, i, i - micro)
        at(b, (sect == 0) & (b == 0), backward_meet)
        at(b, sect == 0, backward)
        at(f + 1, sect == 1, forward_meet)
        at(f, always, forward_attention)
        at(f + 1, always, forward)
        at(b, always, backward_attention)
        at(b - 1, always, backward_norm)
        at(f, always, forward_out)
        at(b, always, backward_ff)
        at(b + 1, (sect == 0) & (b >= 0), backward_meet)
        at(b - 1, always, backward_end)
        at(f, always, forward_end)
        at(f + 1, always, forward_ff)

        starts = jnp.where(sect == 1, i == micro, i == 2 * micro - 1)
        goes_on = (sect == 0) & (i == 2 * micro)
        pl.when(starts)(gradient_begin)
        low = jnp.where(goes_on, EARLY, 0)
        high = jnp.where(
            goes_on | (starts & (sect == 1)),
            total_steps + LAGS[4],
            jnp.where(starts, EARLY, 0),
        )
        lax.fori_loop(low, high, gradient_step, 0)
        return carry

    lax.fori_loop(0, jnp.where(sect == 1, micro + 1, 2 * micro + 1), step, 0)

    for s in range(micro):
        arrived(gfull.at[s, my_rows], yg_s.at[s])
    arrived(out_st, store_sem.at[4])
    arrived(ig_st, store_sem.at[8])
    pl.when(sect == 0)(lambda: arrived(out_st, xs_ss.at[0]))
    pl.when(sect == 1)(lambda: arrived(gx_st, gs_ss.at[0]))

    arrived(sums, sum_ss.at[0])
    for ring in range(RING):
        arrived(tile_ref, core_ss.at[ring])

    @pl.when(sect == 0)
    def _():
        lax.fori_loop(0, GUESTS, guest_home, 0)
        for slot in range(2):
            arrived(tile_ref, guest_ss.at[slot])

    def drain(m, carry):
        away, _, n, _, _ = place(m)
        root = is_root(n)
        stays = jnp.logical_not(away)
        ring = lax.rem(n, RING)
        sends = at_end | (middle & jnp.logical_not(root))
        pl.when(stays & sends & (n + RING >= chain))(lambda: arrived(tile_ref, red_ss.at[ring]))

        @pl.when(stays & root & (n + 2 * TOTALS >= chain))
        def _():
            for k in range(4):
                arrived(tile_ref, tot_ss.at[k, lax.rem(n // 2, TOTALS)])

        @pl.when(stays & middle & jnp.logical_not(root))
        def _():
            arrived(tile_ref, fwd_ss.at[m])

        pl.when(away | jnp.logical_not(root))(lambda: arrived(tile_ref, share_ss.at[m]))
        return carry

    lax.fori_loop(0, total_steps, drain, 0)
    for kind, (height, width) in enumerate(kinds):
        arrived(targets[kind].at[pl.ds(0, height // 2)], fin_rs.at[kind])


def relay(dims, doc_lengths, block_input, cotangent, weights, collective_id):
    micro, rows, group, wide, heads, d_model, ff = dims
    (
        norm_gain,
        norm_bias,
        qkv_weight,
        qkv_bias,
        dense_weight,
        dense_bias,
        up_weight,
        up_bias,
        down_weight,
        down_bias,
    ) = weights
    inner = heads * HEAD_DIM
    per_source = group + group // 2
    anywhere = pl.BlockSpec(memory_space=pl.ANY)
    local = pl.BlockSpec(memory_space=pltpu.VMEM)
    scalars = pl.BlockSpec(memory_space=pltpu.SMEM)
    dma = pltpu.SemaphoreType.DMA
    vmem = pltpu.VMEM
    outs = [
        jax.ShapeDtypeStruct((micro, rows, d_model), BF16),
        jax.ShapeDtypeStruct((micro, rows, d_model), F32),
        jax.ShapeDtypeStruct((2, micro * group, d_model), BF16),
        jax.ShapeDtypeStruct((micro * group, d_model), BF16),
        jax.ShapeDtypeStruct((micro * group, inner), BF16),
        jax.ShapeDtypeStruct((micro * group, ff), BF16),
        jax.ShapeDtypeStruct((micro * group, ff), BF16),
        jax.ShapeDtypeStruct((micro * group, 3 * inner), BF16),
    ]
    kinds = gradient_kinds(d_model, inner, ff)
    steps = sum((height // TILE) * (width // (2 * ACROSS)) for height, width in kinds)
    outs += [jax.ShapeDtypeStruct(kind, BF16) for kind in kinds]
    outs += [jax.ShapeDtypeStruct((GUESTS, TILE, ACROSS), BF16)]
    outs += [jax.ShapeDtypeStruct((8, d_model + COLS), F32)]
    regular = pltpu.SemaphoreType.REGULAR
    scratch = [
        vmem((5, 8, d_model), F32),
        vmem((8, 3 * inner + ff), F32),
        vmem((micro, group, LANES), F32),
        vmem((micro, group, LANES), F32),
        vmem((micro, group, LANES), F32),
        vmem(qkv_weight.shape, BF16),
        vmem(dense_weight.shape, BF16),
        vmem(up_weight.shape, BF16),
        vmem(down_weight.shape, BF16),
        vmem((micro, group, d_model), BF16),
        vmem((micro, group, d_model), BF16),
        vmem((micro, rows, d_model), F32),
        vmem((micro, wide, per_source, LANES), BF16),
        vmem((micro, wide, group // 2, LANES), BF16),
        vmem((micro, wide, group // 2, LANES), BF16),
        vmem((micro, wide, per_source, LANES), BF16),
        vmem((micro, rows, d_model), BF16),
        vmem((micro, rows, d_model), BF16),
        vmem((wide, per_source, LANES), BF16),
        vmem((micro, wide, group // 2, LANES), BF16),
        vmem((micro, wide, group // 2, LANES), BF16),
        vmem((2, wide, per_source, LANES), BF16),
        vmem((rows, d_model), BF16),
        vmem((rows, d_model), BF16),
        vmem((rows, d_model), BF16),
        vmem((rows, d_model), BF16),
        vmem((rows, d_model), F32),
        vmem((2, group, d_model), BF16),
        vmem((group, inner), BF16),
        vmem((group, ff), BF16),
        vmem((group, ff), BF16),
        vmem((group, 3 * inner), BF16),
        vmem((micro, group, ff), BF16),
        vmem((group, d_model), F32),
        vmem((group, d_model), F32),
        vmem((group, d_model), F32),
        vmem((SEQ, LANES), BF16),
        vmem((SEQ, LANES), BF16),
        vmem((SEQ, LANES), BF16),
        vmem((SEQ, LANES), BF16),
        vmem((SEQ, LANES), F32),
        vmem((micro, SEQ // BLOCK, 8, BLOCK), F32),
        vmem((wide, 8, group), F32),
        vmem((BLOCK, SEQ), F32),
        vmem((BLOCK, LANES), F32),
        vmem((BLOCK, LANES), F32),
        dma((4,)),
        dma((micro,)),
        dma((micro,)),
        dma((micro,)),
        dma((micro,)),
        dma((micro,)),
        dma((micro,)),
        dma((1,)),
        dma((micro,)),
        dma((micro,)),
        dma((micro,)),
        dma((micro,)),
        dma((micro,)),
        dma((2,)),
        dma((micro,)),
        dma((1,)),
        dma((micro,)),
        dma((1,)),
        dma((micro,)),
        dma((1,)),
        dma((1,)),
        dma((9,)),
        dma((micro,)),
        vmem((RING, TILE, ACROSS), BF16),
        vmem((RING, TILE, ACROSS), BF16),
        vmem((RING, TILE, ACROSS), BF16),
        vmem((TILE, micro * group), BF16),
        vmem((5, 8, d_model + COLS), F32),
        dma((2, AHEAD + 1)),
        dma((RING,)),
        dma((RING,)),
        dma((RING,)),
        dma((RING,)),
        dma((RING,)),
        dma((steps + GUESTS,)),
        dma((4, TOTALS)),
        dma((steps + GUESTS,)),
        dma((steps + GUESTS,)),
        dma((4,)),
        dma((1,)),
        dma((4,)),
        dma((2,)),
        dma((GUESTS,)),
        regular,
        regular((2,)),
        regular,
    ]
    return pl.pallas_call(
        functools.partial(relay_kernel, dims),
        out_shape=outs,
        in_specs=[scalars, anywhere, anywhere] + [local] * 6 + [anywhere] * 4,
        out_specs=[anywhere] * 13 + [local],
        scratch_shapes=scratch,
        compiler_params=pltpu.CompilerParams(
            collective_id=collective_id, has_side_effects=True, vmem_limit_bytes=63 << 20
        ),
        name="relay",
    )(
        doc_lengths,
        block_input,
        cotangent,
        norm_gain,
        norm_bias,
        qkv_bias[None],
        up_bias[None],
        dense_bias[None],
        down_bias[None],
        qkv_weight,
        dense_weight,
        up_weight,
        down_weight,
    )


WIDEN_STEPS = 8


def widen_kernel(sums, *refs):
    count = (len(refs) - 6) // 2
    sources, targets = refs[:count], refs[count : 2 * count]
    gain, shift, dense_bias, down_bias, qkv_bias, up_bias = refs[2 * count :]
    for source, target in zip(sources, targets):
        target[...] = source[...].astype(target.dtype).reshape(target.shape)
    d_model = gain.shape[2]
    gain[0] = sums[0:2, :d_model]
    shift[0] = sums[2:4, :d_model]
    dense_bias[...] = sums[4:5, :d_model]
    down_bias[...] = sums[4:5, :d_model]
    lines = qkv_bias.shape[1] // COLS
    for k in range(lines):
        qkv_bias[:, k * COLS : (k + 1) * COLS] = sums[k : k + 1, d_model:]
    for k in range(up_bias.shape[1] // COLS):
        up_bias[:, k * COLS : (k + 1) * COLS] = sums[lines + k : lines + k + 1, d_model:]


def widened(rows_out, grads, sums, d_model, qkv_width, ff):
    micro, rows, _ = rows_out[0].shape
    parts = WIDEN_STEPS // micro

    def rows_of(grad):
        return grad.shape[0] // WIDEN_STEPS, grad.shape[1]

    def place(i):
        return i // parts, lax.rem(i, parts), 0

    small = [(1, 2, d_model)] * 2 + [(1, d_model)] * 2 + [(1, qkv_width), (1, ff)]
    return pl.pallas_call(
        widen_kernel,
        grid=(WIDEN_STEPS,),
        out_shape=[jax.ShapeDtypeStruct((1,) + part.shape, part.dtype) for part in rows_out]
        + [jax.ShapeDtypeStruct((1,) + grad.shape, F32) for grad in grads]
        + [jax.ShapeDtypeStruct(shape, F32) for shape in small],
        in_specs=[pl.BlockSpec(sums.shape, lambda i: (0, 0))]
        + [pl.BlockSpec((1, rows // parts, d_model), place) for _ in rows_out]
        + [pl.BlockSpec(rows_of(grad), lambda i: (i, 0)) for grad in grads],
        out_specs=[
            pl.BlockSpec((1, 1, rows // parts, d_model), lambda i: (0,) + place(i))
            for _ in rows_out
        ]
        + [pl.BlockSpec((1,) + rows_of(grad), lambda i: (0, i, 0)) for grad in grads]
        + [pl.BlockSpec(shape, lambda i, zeros=(0,) * len(shape): zeros) for shape in small],
        compiler_params=pltpu.CompilerParams(vmem_limit_bytes=60 << 20),
        name="widened",
    )(sums, *rows_out, *grads)


def relay_shards(
    block_input,
    doc_lengths,
    norm_gain,
    norm_bias,
    qkv_weight,
    qkv_bias,
    dense_weight,
    dense_bias,
    up_weight,
    up_bias,
    down_weight,
    down_bias,
    cotangent,
):
    weights = tuple(
        array[0]
        for array in (
            norm_gain,
            norm_bias,
            qkv_weight,
            qkv_bias,
            dense_weight,
            dense_bias,
            up_weight,
            up_bias,
            down_weight,
            down_bias,
        )
    )
    micro, rows, d_model = block_input.shape
    group = rows * lax.axis_size("tensor")
    wide = lax.axis_size("wide")
    heads = qkv_weight.shape[2] // (3 * HEAD_DIM)
    ff = up_weight.shape[2]
    dims = (micro, rows, group, wide, heads, d_model, ff)
    out, input_grad, *_, up_grad, down_grad, dense_grad, qkv_grad, _, sums = relay(
        dims, doc_lengths, block_input, cotangent, weights, 1
    )
    out, input_grad, up_grad, down_grad, dense_grad, qkv_grad, *small = widened(
        (out, input_grad),
        (up_grad, down_grad, dense_grad, qkv_grad),
        sums,
        d_model,
        qkv_weight.shape[2],
        ff,
    )
    gain, shift, dense_b, down_b, qkv_b, up_b = small
    return (
        out,
        input_grad,
        gain,
        shift,
        qkv_grad,
        qkv_b,
        dense_grad,
        dense_b,
        up_grad,
        up_b,
        down_grad,
        down_b,
    )


def shortened(shard):

    def short(part):
        return part.astype(jnp.bfloat16) if part.dtype == jnp.float32 else part

    return jax.tree.map(short, shard)


def from_behind(block, axis, distance):
    devices = range(lax.axis_size(axis))
    route = [(i - distance, i) for i in devices if i - distance in devices]
    return lax.ppermute(block, axis, route)


def norm_parts(values, gain, shift):
    center = jnp.mean(values, axis=-1, keepdims=True)
    centred = values - center
    spread = jnp.mean(centred * centred, axis=-1, keepdims=True)
    inv_scale = lax.rsqrt(spread + EPSILON)
    normed = centred * inv_scale
    return (normed * gain + shift, normed, inv_scale)


def norm_back(grad, normed, inv_scale, gain):
    scaled = grad * gain
    inner_mean = jnp.mean(scaled, axis=-1, keepdims=True)
    cross_mean = jnp.mean(scaled * normed, axis=-1, keepdims=True)
    return inv_scale * (scaled - inner_mean - normed * cross_mean)


def doc_layout(lengths, tok_index):
    ends = jnp.cumsum(lengths)
    starts = ends - lengths
    doc_ids = jnp.sum((tok_index[:, None] >= ends[None, :]).astype(jnp.int32), axis=1)
    numbers = jnp.arange(lengths.shape[0], dtype=jnp.int32)
    picked = doc_ids[:, None] == numbers[None, :]
    begins = jnp.sum(jnp.where(picked, starts[None, :], 0), axis=1)
    return (doc_ids, tok_index - begins)


def rope_tables(offsets):
    half = ROT // 2
    freqs = ROPE_BASE ** (-2.0 * jnp.arange(half, dtype=jnp.float32) / ROT)
    angle = offsets.astype(jnp.float32)[:, None] * freqs[None, :]
    return (jnp.cos(angle)[:, None, :], jnp.sin(angle)[:, None, :])


def rotate(values, cos_table, sin_table):
    half = ROT // 2
    front = values[..., :half]
    back = values[..., half:ROT]
    turned = [
        front * cos_table - back * sin_table,
        back * cos_table + front * sin_table,
        values[..., ROT:],
    ]
    return jnp.concatenate(turned, axis=-1)


def unrotate(values, cos_table, sin_table):
    half = ROT // 2
    front = values[..., :half]
    back = values[..., half:ROT]
    turned = [
        front * cos_table + back * sin_table,
        back * cos_table - front * sin_table,
        values[..., ROT:],
    ]
    return jnp.concatenate(turned, axis=-1)


def gelu_parts(pre_act):
    cumul = 0.5 * (1.0 + lax.erf(pre_act * (1.0 / math.sqrt(2.0))))
    density = jnp.exp(-0.5 * pre_act * pre_act) * (1.0 / math.sqrt(2.0 * math.pi))
    return (pre_act * cumul, cumul + pre_act * density)


def store_slot(buffer, update, slot_here, is_valid):
    previous = lax.dynamic_index_in_dim(buffer, slot_here, 0, keepdims=False)
    return lax.dynamic_update_index_in_dim(
        buffer, jnp.where(is_valid, update, previous), slot_here, 0
    )


def gather_keys(key_rows, value_rows):
    return (
        lax.all_gather(key_rows, "wide", axis=0, tiled=True),
        lax.all_gather(value_rows, "wide", axis=0, tiled=True),
    )


def forward_parts(inputs, lengths, weights, with_output):
    (
        norm_gain,
        norm_bias,
        qkv_weight,
        qkv_bias,
        dense_weight,
        dense_bias,
        up_weight,
        up_bias,
        down_weight,
        down_bias,
    ) = weights
    seq_len = SEQ
    group = inputs.shape[0] * lax.axis_size("tensor")
    head_count = qkv_weight.shape[1] // (3 * HEAD_DIM)
    factor = 1.0 / math.sqrt(HEAD_DIM)
    values = inputs.astype(jnp.float32)
    norm_first, normed_first, scale_first = norm_parts(values, norm_gain[0], norm_bias[0])
    norm_second, normed_second, scale_second = norm_parts(values, norm_gain[1], norm_bias[1])
    full_first, full_second = (
        lax.all_gather(norm_first.astype(jnp.bfloat16), "tensor", axis=0, tiled=True),
        lax.all_gather(norm_second.astype(jnp.bfloat16), "tensor", axis=0, tiled=True),
    )
    tok_index = lax.axis_index("wide") * group + jnp.arange(group, dtype=jnp.int32)
    doc_ids, offsets = doc_layout(lengths, tok_index)
    all_index = jnp.arange(seq_len, dtype=jnp.int32)
    all_docs = doc_layout(lengths, all_index)[0]
    cos_table, sin_table = rope_tables(offsets)
    packed = jnp.dot(full_first, qkv_weight, preferred_element_type=jnp.float32) + qkv_bias
    packed = packed.reshape(group, head_count, 3, HEAD_DIM)
    queries = rotate(packed[:, :, 0], cos_table, sin_table).astype(jnp.bfloat16)
    key_here = rotate(packed[:, :, 1], cos_table, sin_table).astype(jnp.bfloat16)
    value_here = packed[:, :, 2].astype(jnp.bfloat16)
    key_all, value_all = gather_keys(key_here.reshape(group, -1), value_here.reshape(group, -1))
    key_heads = key_all.reshape(seq_len, head_count, HEAD_DIM)
    value_heads = value_all.reshape(seq_len, head_count, HEAD_DIM)
    allowed = (doc_ids[:, None] == all_docs[None, :]) & (all_index[None, :] <= tok_index[:, None])
    raw_scores = jnp.einsum("qhd,khd->qhk", queries, key_heads, preferred_element_type=jnp.float32)
    scores = jnp.where(allowed[:, None, :], raw_scores * factor, -jnp.inf)
    row_max = jnp.max(scores, axis=-1, keepdims=True)
    log_total = row_max + jnp.log(jnp.sum(jnp.exp(scores - row_max), axis=-1, keepdims=True))
    attn_probs = jnp.exp(scores - log_total)
    probs_low = attn_probs.astype(jnp.bfloat16)
    mixed_out = jnp.einsum(
        "qhk,khd->qhd", probs_low, value_heads, preferred_element_type=jnp.float32
    )
    mixed_out = mixed_out.reshape(group, -1).astype(jnp.bfloat16)
    up_pre = jnp.dot(full_second, up_weight, preferred_element_type=jnp.float32) + up_bias
    up_act, gelu_slope = gelu_parts(up_pre)
    hidden = up_act.astype(jnp.bfloat16)
    output = None
    if with_output:
        partial_value = jnp.dot(mixed_out, dense_weight, preferred_element_type=jnp.float32)
        partial_value = partial_value + jnp.dot(
            hidden, down_weight, preferred_element_type=jnp.float32
        )
        branch = (
            lax.psum_scatter(
                partial_value.astype(jnp.bfloat16), "tensor", scatter_dimension=0, tiled=True
            ).astype(jnp.float32)
            + dense_bias
            + down_bias
        )
        output = (values + branch).astype(jnp.bfloat16)
    return dict(
        output=output,
        normed_first=normed_first,
        scale_first=scale_first,
        normed_second=normed_second,
        scale_second=scale_second,
        full_first=full_first,
        full_second=full_second,
        tok_index=tok_index,
        doc_ids=doc_ids,
        all_index=all_index,
        all_docs=all_docs,
        cos_table=cos_table,
        sin_table=sin_table,
        queries=queries,
        key_here=key_here,
        value_here=value_here,
        key_all=key_all,
        value_all=value_all,
        key_heads=key_heads,
        value_heads=value_heads,
        attn_probs=attn_probs,
        probs_low=probs_low,
        log_total=log_total,
        mixed_out=mixed_out,
        gelu_slope=gelu_slope,
        hidden=hidden,
    )


def backward_parts(inputs, grad_out, lengths, weights):
    (
        norm_gain,
        norm_bias,
        qkv_weight,
        qkv_bias,
        dense_weight,
        dense_bias,
        up_weight,
        up_bias,
        down_weight,
        down_bias,
    ) = weights
    parts = forward_parts(inputs, lengths, weights, False)
    seq_len = SEQ
    group = inputs.shape[0] * lax.axis_size("tensor")
    head_count = qkv_weight.shape[1] // (3 * HEAD_DIM)
    factor = 1.0 / math.sqrt(HEAD_DIM)
    cos_table = parts["cos_table"]
    sin_table = parts["sin_table"]
    grad_low = grad_out.astype(jnp.bfloat16)
    grad_rows = grad_low.astype(jnp.float32)
    grad_full = lax.all_gather(grad_low, "tensor", axis=0, tiled=True)
    dense_grad = jnp.einsum(
        "cf,cd->fd", parts["mixed_out"], grad_full, preferred_element_type=jnp.float32
    )
    down_grad = jnp.einsum(
        "cf,cd->fd", parts["hidden"], grad_full, preferred_element_type=jnp.float32
    )
    hidden_grad = jnp.einsum(
        "cd,fd->cf", grad_full, down_weight, preferred_element_type=jnp.float32
    )
    pre_grad = (hidden_grad * parts["gelu_slope"]).astype(jnp.bfloat16)
    up_grad = jnp.einsum(
        "cd,cf->df", parts["full_second"], pre_grad, preferred_element_type=jnp.float32
    )
    up_bias_grad = jnp.sum(pre_grad.astype(jnp.float32), axis=0)
    second_grad = jnp.einsum("cf,df->cd", pre_grad, up_weight, preferred_element_type=jnp.float32)
    mixed_grad = jnp.einsum(
        "cd,fd->cf", grad_full, dense_weight, preferred_element_type=jnp.float32
    )
    mixed_grad = mixed_grad.astype(jnp.bfloat16).reshape(group, head_count, HEAD_DIM)
    attn_probs = parts["attn_probs"]
    probs_grad = jnp.einsum(
        "qhd,khd->qhk", mixed_grad, parts["value_heads"], preferred_element_type=jnp.float32
    )
    inner = jnp.sum(attn_probs * probs_grad, axis=-1, keepdims=True)
    score_grad = (attn_probs * (probs_grad - inner) * factor).astype(jnp.bfloat16)
    query_grad = jnp.einsum(
        "qhk,khd->qhd", score_grad, parts["key_heads"], preferred_element_type=jnp.float32
    )
    key_sums = jnp.einsum(
        "qhk,qhd->khd", score_grad, parts["queries"], preferred_element_type=jnp.float32
    )
    value_sums = jnp.einsum(
        "qhk,qhd->khd", parts["probs_low"], mixed_grad, preferred_element_type=jnp.float32
    )
    key_flat, value_flat = (
        lax.psum_scatter(
            key_sums.reshape(seq_len, -1).astype(jnp.bfloat16),
            "wide",
            scatter_dimension=0,
            tiled=True,
        ).astype(jnp.float32),
        lax.psum_scatter(
            value_sums.reshape(seq_len, -1).astype(jnp.bfloat16),
            "wide",
            scatter_dimension=0,
            tiled=True,
        ).astype(jnp.float32),
    )
    key_grad = key_flat.reshape(group, head_count, HEAD_DIM)
    value_grad = value_flat.reshape(group, head_count, HEAD_DIM)
    query_back = unrotate(query_grad, cos_table, sin_table)
    key_back = unrotate(key_grad, cos_table, sin_table)
    packed_grad = (
        jnp.stack([query_back, key_back, value_grad], axis=2)
        .reshape(group, -1)
        .astype(jnp.bfloat16)
    )
    qkv_grad = jnp.einsum(
        "cd,cf->df", parts["full_first"], packed_grad, preferred_element_type=jnp.float32
    )
    qkv_bias_grad = jnp.sum(packed_grad.astype(jnp.float32), axis=0)
    first_grad = jnp.einsum(
        "cf,df->cd", packed_grad, qkv_weight, preferred_element_type=jnp.float32
    )
    norm_first_grad, norm_second_grad = (
        lax.psum_scatter(
            first_grad.astype(jnp.bfloat16), "tensor", scatter_dimension=0, tiled=True
        ).astype(jnp.float32),
        lax.psum_scatter(
            second_grad.astype(jnp.bfloat16), "tensor", scatter_dimension=0, tiled=True
        ).astype(jnp.float32),
    )
    gain_grad = jnp.stack(
        [
            jnp.sum(norm_first_grad * parts["normed_first"], axis=0),
            jnp.sum(norm_second_grad * parts["normed_second"], axis=0),
        ]
    )
    shift_grad = jnp.stack([jnp.sum(norm_first_grad, axis=0), jnp.sum(norm_second_grad, axis=0)])
    input_grad = grad_out + norm_back(
        norm_first_grad, parts["normed_first"], parts["scale_first"], norm_gain[0]
    )
    input_grad = input_grad + norm_back(
        norm_second_grad, parts["normed_second"], parts["scale_second"], norm_gain[1]
    )
    bias_rows = jnp.sum(grad_rows, axis=0)
    terms = (
        gain_grad,
        shift_grad,
        qkv_grad,
        qkv_bias_grad,
        dense_grad,
        bias_rows,
        up_grad,
        up_bias_grad,
        down_grad,
        bias_rows,
    )
    return (input_grad, terms)


def general_shards(
    block_input,
    doc_lengths,
    norm_gain,
    norm_bias,
    qkv_weight,
    qkv_bias,
    dense_weight,
    dense_bias,
    up_weight,
    up_bias,
    down_weight,
    down_bias,
    cotangent,
):
    weights = (
        norm_gain[0],
        norm_bias[0],
        qkv_weight[0],
        qkv_bias[0],
        dense_weight[0],
        dense_bias[0],
        up_weight[0],
        up_bias[0],
        down_weight[0],
        down_bias[0],
    )
    section_index = lax.axis_index("section")
    last_section = lax.axis_size("section") - 1
    micro_count = block_input.shape[0]
    row_count = block_input.shape[1]
    tick_count = micro_count + last_section

    def forward_tick(carry, tick_index):
        incoming, kept_inputs, outputs, kept_pairs = carry
        slot_raw = tick_index - section_index
        is_valid = (slot_raw >= 0) & (slot_raw < micro_count)
        slot_here = jnp.clip(slot_raw, 0, micro_count - 1)
        fresh = lax.dynamic_index_in_dim(
            block_input, jnp.clip(tick_index, 0, micro_count - 1), 0, keepdims=False
        )
        inputs = jnp.where(section_index == 0, fresh, incoming)
        lengths = lax.dynamic_index_in_dim(doc_lengths, slot_here, 0, keepdims=False)
        parts = forward_parts(inputs, lengths, weights, True)
        output = parts["output"]
        kept_inputs = store_slot(kept_inputs, inputs, slot_here, is_valid)
        outputs = store_slot(outputs, output, slot_here, is_valid)
        incoming = jax.tree.map(
            lambda part, own: part.astype(own.dtype),
            from_behind(shortened(output), "section", 1),
            output,
        )
        return ((incoming, kept_inputs, outputs, kept_pairs), None)

    pair_init = (jnp.zeros((1,), jnp.bfloat16), jnp.zeros((1,), jnp.bfloat16))
    zero_rows = jnp.zeros((row_count, block_input.shape[2]), jnp.bfloat16)
    zero_stack = jnp.zeros(block_input.shape, jnp.bfloat16)
    forward_init = (zero_rows, zero_stack, zero_stack, pair_init)
    forward_done = lax.scan(forward_tick, forward_init, jnp.arange(tick_count, dtype=jnp.int32))[0]
    kept_inputs = forward_done[1]
    outputs = forward_done[2]
    kept_pairs = forward_done[3]

    def add_masked(total, term, scale_mask):
        return total + scale_mask * term

    def backward_tick(carry, tick_index):
        incoming, grads, input_grads = carry
        slot_raw = tick_index - (last_section - section_index)
        is_valid = (slot_raw >= 0) & (slot_raw < micro_count)
        slot_here = jnp.clip(slot_raw, 0, micro_count - 1)
        top_grad = lax.dynamic_index_in_dim(cotangent, slot_here, 0, keepdims=False)
        grad_out = jnp.where(section_index == last_section, top_grad, incoming)
        inputs = lax.dynamic_index_in_dim(kept_inputs, slot_here, 0, keepdims=False)
        lengths = lax.dynamic_index_in_dim(doc_lengths, slot_here, 0, keepdims=False)
        input_grad, terms = backward_parts(inputs, grad_out, lengths, weights)
        scale_mask = is_valid.astype(jnp.float32)
        grads = tuple((add_masked(total, term, scale_mask) for total, term in zip(grads, terms)))
        input_grads = store_slot(input_grads, input_grad, slot_here, is_valid)
        incoming = from_behind(shortened(input_grad), "section", -1).astype(input_grad.dtype)
        return ((incoming, grads, input_grads), None)

    grad_init = tuple((jnp.zeros(weight.shape, jnp.float32) for weight in weights))
    backward_init = (
        jnp.zeros((row_count, block_input.shape[2]), jnp.float32),
        grad_init,
        jnp.zeros(block_input.shape, jnp.float32),
    )
    backward_done = lax.scan(backward_tick, backward_init, jnp.arange(tick_count, dtype=jnp.int32))[
        0
    ]
    grads = backward_done[1]
    input_grads = backward_done[2]
    wide_sums = (
        lax.psum(grads[2].astype(jnp.bfloat16), "wide").astype(jnp.float32),
        lax.psum(grads[3].astype(jnp.bfloat16), "wide").astype(jnp.float32),
        lax.psum(grads[4].astype(jnp.bfloat16), "wide").astype(jnp.float32),
        lax.psum(grads[6].astype(jnp.bfloat16), "wide").astype(jnp.float32),
        lax.psum(grads[7].astype(jnp.bfloat16), "wide").astype(jnp.float32),
        lax.psum(grads[8].astype(jnp.bfloat16), "wide").astype(jnp.float32),
    )
    shared = lax.psum((grads[0], grads[1], grads[5], grads[9]), ("tensor", "wide"))
    return (
        outputs[None],
        input_grads[None],
        shared[0][None],
        shared[1][None],
        wide_sums[0][None],
        wide_sums[1][None],
        wide_sums[2][None],
        shared[2][None],
        wide_sums[3][None],
        wide_sums[4][None],
        wide_sums[5][None],
        shared[3][None],
    )


def solution(mesh):
    placed = (
        P(None, ("wide", "tensor"), None),
        P(),
        P("section", None, None),
        P("section", None, None),
        P("section", None, "tensor"),
        P("section", "tensor"),
        P("section", "tensor", None),
        P("section", None),
        P("section", None, "tensor"),
        P("section", "tensor"),
        P("section", "tensor", None),
        P("section", None),
        P(None, ("wide", "tensor"), None),
    )
    results = (
        P("section", None, ("wide", "tensor"), None),
        P("section", None, ("wide", "tensor"), None),
        P("section", None, None),
        P("section", None, None),
        P("section", None, "tensor"),
        P("section", "tensor"),
        P("section", "tensor", None),
        P("section", None),
        P("section", None, "tensor"),
        P("section", "tensor"),
        P("section", "tensor", None),
        P("section", None),
    )

    def program(*args):
        heads = args[4].shape[2] // (3 * HEAD_DIM * mesh.shape["tensor"])
        micro, seq_len, d_model = args[0].shape
        group = seq_len // mesh.shape["wide"]
        fits = heads == mesh.shape["wide"] == 8
        fits = fits and mesh.shape["section"] == 2 and mesh.shape["tensor"] == 2
        fits = fits and micro * group == d_model and args[8].shape[2] == 4 * d_model
        body = relay_shards if fits and group == TILE else general_shards
        return jax.shard_map(
            body, mesh=mesh, in_specs=placed, out_specs=results, check_vma=False
        )(*args)

    return program
```

```python
import functools
import math

import jax
import jax.numpy as jnp
from jax import lax
from jax.experimental import pallas as pl
from jax.experimental.pallas import tpu as pltpu
from jax.sharding import PartitionSpec as P

HEAD_DIM = 64
ROT = 16
SEQ = 2048


EPSILON = 1e-05
ROPE_BASE = 10000.0

MESH = pl.DeviceIdType.MESH
F32 = jnp.float32
BF16 = jnp.bfloat16
LANES = 128
BLOCK = 512
COLS = 512
NEG = -1e30
SCORE_SCALE = math.log2(math.e) / math.sqrt(HEAD_DIM)


TILE = 256
ACROSS = 256
AHEAD = 3
RING = 8
TOTALS = 8
LAGS = (2, 5, 8, 12, 15)
OWN = 16
GUESTS = 12
EARLY = 24


def gradient_kinds(d_model, inner, ff):
    return ((d_model, ff), (ff, d_model), (inner, d_model), (d_model, 3 * inner))


def dot(a, b):
    return jnp.dot(a, b, preferred_element_type=F32)


def dot_t(a, b):
    return lax.dot_general(a, b, (((1,), (1,)), ((), ())), preferred_element_type=F32)


def t_dot(a, b):
    return lax.dot_general(a, b, (((0,), (0,)), ((), ())), preferred_element_type=F32)


def lane_low(rows):
    return lax.broadcasted_iota(jnp.int32, (rows, LANES), 1) < HEAD_DIM


def turn(values):
    return pltpu.roll(values, HEAD_DIM, 1)


def rotary(values, cos_ref, front_ref, back_ref, seq, sign):
    cos, front, back = cos_ref[seq], front_ref[seq], back_ref[seq]
    ahead = pltpu.roll(values, LANES - ROT // 2, 1)
    behind = pltpu.roll(values, ROT // 2, 1)
    return values * cos + sign * (ahead * front + behind * back)


def pair_up(first, second, low):
    return jnp.where(low, first, turn(second)), jnp.where(low, turn(first), second)


def relay_kernel(
    dims,
    lengths,
    x_hbm,
    cot_hbm,
    gain,
    shift,
    qkv_b,
    up_b,
    dense_b,
    down_b,
    wqkv_hbm,
    wdense_hbm,
    wup_hbm,
    wdown_hbm,
    out_hbm,
    ig_hbm,
    norm_hbm,
    g_hbm,
    mixed_hbm,
    hid_hbm,
    dpre_hbm,
    dpk_hbm,
    up_out,
    down_out,
    dense_out,
    qkv_out,
    guest_hbm,
    sums,
    small,
    bias_sums,
    cos,
    front,
    back,
    wqkv,
    wdense,
    wup,
    wdown,
    xfull,
    gfull,
    cot,
    qkv_r,
    mix_r,
    do_r,
    dqkv_r,
    rsf_r,
    rsb_r,
    qkv_st,
    o_st,
    do_st,
    dqkv_st,
    rsf_st,
    rsb_st,
    out_st,
    gx_st,
    ig_st,
    norm_st,
    mixed_st,
    hid_st,
    dpre_st,
    dpk_st,
    slope,
    part,
    part_b,
    dn1,
    qm,
    kr,
    vx,
    dox,
    dq,
    lse,
    delta,
    scores,
    peak,
    acc,
    wsem,
    ownx_sem,
    yx_s,
    yx_r,
    owng_sem,
    yg_s,
    yg_r,
    qkv_ss,
    qkv_rs,
    o_ss,
    o_rs,
    do_ss,
    do_rs,
    dqkv_ss,
    dqkv_rs,
    rsf_ss,
    rsf_rs,
    rsb_ss,
    rsb_rs,
    xs_ss,
    gs_ss,
    store_sem,
    g_store,
    core_r,
    outer_r,
    inner_r,
    turned,
    sums_r,
    op_sem,
    core_ss,
    core_rs,
    outer_rs,
    inner_rs,
    red_ss,
    bc_rs,
    tot_ss,
    fwd_ss,
    share_ss,
    fin_rs,
    sum_ss,
    sum_rs,
    guest_ss,
    guest_rs,
    core_free,
    outer_free,
    inner_free,
):
    micro, rows, group, wide, heads, d_model, ff = dims
    sect = lax.axis_index("section")
    tens = lax.axis_index("tensor")
    me = lax.axis_index("wide")
    pairs = heads // 2
    per_source = group + group // 2
    half = group // 2
    q_blocks = SEQ // BLOCK
    sources = BLOCK // group
    my_rows = pl.ds(pl.multiple_of(tens * rows, rows), rows)
    his_rows = pl.ds(pl.multiple_of((1 - tens) * rows, rows), rows)
    x_dev = {"section": 1 - sect}
    y_dev = {"tensor": 1 - tens}
    low_half = lane_low(half)
    low_group = lane_low(group)

    def remote(src, dst, ss, rs, dev):
        return pltpu.make_async_remote_copy(
            src_ref=src, dst_ref=dst, send_sem=ss, recv_sem=rs, device_id=dev, device_id_type=MESH
        )

    def arrived(ref, sem):
        pltpu.make_async_copy(ref, ref, sem).wait()

    def tokens_of(s):
        return pl.ds(pl.multiple_of(s * group, group), group)

    def y_send_x(s):
        own = xfull.at[s, my_rows]
        return remote(own, own, yx_s.at[s], yx_r.at[s], y_dev)

    def y_send_g(s):
        own = gfull.at[s, my_rows]
        return remote(own, own, yg_s.at[s], yg_r.at[s], y_dev)

    def spread(stage, target, seq, dest, ss, rs):
        @pl.when(dest == me)
        def _():
            pltpu.make_async_copy(stage, target.at[seq, me], rs).start()

        @pl.when(dest != me)
        def _():
            remote(stage, target.at[seq, me], ss, rs, {"wide": dest}).start()

    loads = [
        pltpu.make_async_copy(source, target, wsem.at[i])
        for i, (source, target) in enumerate(
            ((wqkv_hbm, wqkv), (wup_hbm, wup), (wdown_hbm, wdown), (wdense_hbm, wdense))
        )
    ]

    barrier = pltpu.get_barrier_semaphore()
    for dev in [x_dev, y_dev] + [{"wide": lax.rem(me + k, wide)} for k in range(1, wide)]:
        pl.semaphore_signal(barrier, inc=1, device_id=dev, device_id_type=MESH)

    @pl.when(sect == 0)
    def _():
        for s in range(micro):
            pltpu.make_async_copy(x_hbm.at[s], xfull.at[s, my_rows], ownx_sem.at[s]).start()

    for load in loads:
        load.start()

    @pl.when(sect == 1)
    def _():
        for s in range(micro):
            pltpu.make_async_copy(cot_hbm.at[s], cot.at[s], owng_sem.at[s]).start()

    def starts_of(s, tokens):
        found = jnp.zeros_like(tokens)
        end = jnp.int32(0)
        for j in range(lengths.shape[1]):
            end = end + lengths[s, j]
            found = jnp.where(tokens >= end, end, found)
        return found

    lane = lax.rem(lax.broadcasted_iota(jnp.int32, (8, LANES), 1), HEAD_DIM)
    number = lax.rem(lane, ROT // 2)
    freq = jnp.zeros((8, LANES), F32)
    for k in range(ROT // 2):
        freq = jnp.where(number == k, ROPE_BASE ** (-2.0 * k / ROT), freq)
    lane, freq = lane[0:1, :], freq[0:1, :]

    def table_step(s, carry):
        tokens = me * group + lax.broadcasted_iota(jnp.int32, (group, LANES), 0)
        angle = (tokens - starts_of(s, tokens)).astype(F32) * freq
        sine = jnp.sin(angle)
        cos[s] = jnp.where(lane < ROT, jnp.cos(angle), 1.0)
        front[s] = jnp.where(lane < ROT // 2, -sine, 0.0)
        back[s] = jnp.where((lane >= ROT // 2) & (lane < ROT), sine, 0.0)
        return carry

    lax.fori_loop(0, micro, table_step, 0)
    small[...] = jnp.zeros_like(small)
    bias_sums[...] = jnp.zeros_like(bias_sums)
    pl.semaphore_wait(barrier, wide + 1)

    @pl.when(sect == 0)
    def _():
        for s in range(micro):
            remote(x_hbm.at[s], xfull.at[s, my_rows], yx_s.at[s], yx_r.at[s], y_dev).start()
        for s in range(micro):
            arrived(xfull.at[s, my_rows], ownx_sem.at[s])

    @pl.when(sect == 1)
    def _():
        for s in range(micro):
            arrived(cot.at[s], owng_sem.at[s])

            def chunk(i, carry, s=s):
                at = pl.ds(pl.multiple_of(i * 32, 32), 32)
                there = pl.ds(pl.multiple_of(tens * rows + i * 32, 32), 32)
                gfull[s, there, :] = cot[s, at, :].astype(BF16)
                return carry

            lax.fori_loop(0, rows // 32, chunk, 0)
            y_send_g(s).start()

    def fold(values):
        total = values[0:8]
        for k in range(1, values.shape[0] // 8):
            total = total + values[k * 8 : (k + 1) * 8]
        return total

    def normed_rows(values):
        center = jnp.mean(values, axis=-1, keepdims=True)
        centred = values - center
        spread_of = jnp.mean(centred * centred, axis=-1, keepdims=True)
        inv = lax.rsqrt(spread_of + EPSILON)
        return centred * inv, inv

    def unpack_heads(s):
        def step(src, carry):
            qk = qkv_r[s, src, 0:group, :].astype(F32)
            at = pl.multiple_of(src * group, group)
            qm[pl.ds(at, group), :] = jnp.where(low_group, qk, 0.0).astype(BF16)
            kr[pl.ds(at, group), :] = turn(qk).astype(BF16)
            packed_v = qkv_r[s, src, group:per_source, :].astype(F32)
            ones = jnp.where(
                lax.broadcasted_iota(jnp.int32, (half, LANES), 1) == HEAD_DIM, 1.0, 0.0
            )
            vx[pl.ds(at, half), :] = jnp.where(low_half, packed_v, ones).astype(BF16)
            vx[pl.ds(pl.multiple_of(at + half, half), half), :] = jnp.where(
                low_half, turn(packed_v), ones
            ).astype(BF16)
            return carry

        lax.fori_loop(0, wide, step, 0, unroll=True)

    def forward_meet(s):
        arrived(xfull.at[s, my_rows], ownx_sem.at[s])
        y_send_x(s).start()

    def backward_meet(s):
        arrived(gfull.at[s, my_rows], owng_sem.at[s])
        y_send_g(s).start()

    def forward(s):
        arrived(xfull.at[s, his_rows], yx_r.at[s])

        def norm_step(i, carry):
            at = pl.ds(pl.multiple_of(i * 32, 32), 32)
            a, _ = normed_rows(xfull[s, at, :].astype(F32))
            norm_st[0, at, :] = (a * gain[0:1, :] + shift[0:1, :]).astype(BF16)
            norm_st[1, at, :] = (a * gain[1:2, :] + shift[1:2, :]).astype(BF16)
            return carry

        @pl.when(s > 0)
        def _():
            arrived(norm_st.at[0], store_sem.at[0])
            arrived(norm_st.at[1], store_sem.at[1])

        lax.fori_loop(0, group // 32, norm_step, 0, unroll=True)
        pltpu.make_async_copy(norm_st.at[0], norm_hbm.at[0, tokens_of(s)], store_sem.at[0]).start()
        pltpu.make_async_copy(norm_st.at[1], norm_hbm.at[1, tokens_of(s)], store_sem.at[1]).start()

        def qkv_step(k, carry):
            pair = lax.rem(me // 2 + 1 + k, pairs)
            cols = pl.ds(pl.multiple_of(pair * 3 * LANES, LANES), 3 * LANES)
            packed = dot(norm_st[0], wqkv[:, cols]) + qkv_b[:, cols]
            first, middle, last = (packed[:, i * LANES : (i + 1) * LANES] for i in range(3))
            qk0 = rotary(first, cos, front, back, s, 1.0)
            qk1 = rotary(
                turn(jnp.where(low_group, last, middle)), cos, front, back, s, 1.0
            )
            vv = jnp.where(low_group, middle, last)
            v0 = jnp.where(low_half, vv[:half], turn(vv[half:]))
            v1 = jnp.where(low_half, turn(vv[:half]), vv[half:])
            for i, (qk, v) in enumerate(((qk0, v0), (qk1, v1))):
                qkv_st[2 * pair + i, 0:group, :] = qk.astype(BF16)
                qkv_st[2 * pair + i, group:per_source, :] = v.astype(BF16)
            for i in range(2):
                dest = 2 * pair + i
                spread(qkv_st.at[dest], qkv_r, s, dest, qkv_ss.at[0], qkv_rs.at[s])
            return carry

        pl.when(s == 0)(loads[0].wait)
        lax.fori_loop(0, pairs, qkv_step, 0, unroll=True)

    def forward_ff(s):
        @pl.when(s == 0)
        def _():
            loads[1].wait()
            loads[2].wait()

        @pl.when(s > 0)
        def _():
            arrived(hid_st, store_sem.at[2])

        def ff_step(j, carry):
            cols = pl.ds(pl.multiple_of(j * COLS, COLS), COLS)
            pre = dot(norm_st[1], wup[:, cols]) + up_b[:, cols]
            cumul = 0.5 * (1.0 + lax.erf(pre * (1.0 / math.sqrt(2.0))))
            density = jnp.exp(-0.5 * pre * pre) * (1.0 / math.sqrt(2.0 * math.pi))
            hid = (pre * cumul).astype(BF16)
            hid_st[:, cols] = hid
            slope[s, :, cols] = (cumul + pre * density).astype(BF16)
            term = dot(hid, wdown[cols, :])

            @pl.when(j == 0)
            def _():
                part[...] = term

            @pl.when(j > 0)
            def _():
                part[...] += term

            return carry

        lax.fori_loop(0, ff // COLS, ff_step, 0, unroll=True)
        pltpu.make_async_copy(hid_st, hid_hbm.at[tokens_of(s)], store_sem.at[2]).start()

    def forward_attention(s):
        arrived(qkv_r.at[s], qkv_rs.at[s])
        arrived(qkv_st.at[pl.ds(0, wide - 1)], qkv_ss.at[0])
        unpack_heads(s)

        for i in range(q_blocks):
            q_at = slice(i * BLOCK, (i + 1) * BLOCK)
            tokens = i * BLOCK + lax.broadcasted_iota(jnp.int32, (BLOCK, LANES), 0)
            begin = starts_of(s, tokens)[:, 0:1]
            best = jnp.full((BLOCK, LANES), NEG, F32)
            for j in range(i + 1):
                k_at = slice(j * BLOCK, (j + 1) * BLOCK)
                raw = dot_t(qm[q_at, :], kr[k_at, :])
                u = j * BLOCK + lax.broadcasted_iota(jnp.int32, (BLOCK, BLOCK), 1)
                seen = u >= begin
                if i == j:
                    seen = seen & (u <= tokens[:, 0:1])
                raw = jnp.where(seen, raw, NEG)
                scores[:, k_at] = raw
                for k in range(BLOCK // LANES):
                    best = jnp.maximum(best, raw[:, k * LANES : (k + 1) * LANES])
            top = jnp.max(best, axis=1, keepdims=True) * SCORE_SCALE
            out = jnp.zeros((BLOCK, LANES), F32)
            for j in range(i + 1):
                k_at = slice(j * BLOCK, (j + 1) * BLOCK)
                probs = jnp.exp2(scores[:, k_at] * SCORE_SCALE - top)
                out = out + dot(probs.astype(BF16), vx[k_at, :])
            total = out[:, HEAD_DIM : HEAD_DIM + 1]
            out = out / total
            log_total = top + jnp.log2(total)
            lse[s, i] = jnp.broadcast_to(log_total, (BLOCK, LANES)).T[0:8, :]
            for k in range(sources):
                first = out[k * group : k * group + half]
                second = out[k * group + half : (k + 1) * group]
                source = i * sources + k
                o_st[s, source] = jnp.where(low_half, first, turn(second)).astype(BF16)
                spread(o_st.at[s, source], mix_r, s, source, o_ss.at[s], o_rs.at[s])

    def forward_out(s):
        arrived(mix_r.at[s], o_rs.at[s])
        arrived(o_st.at[s, pl.ds(0, wide - 1)], o_ss.at[s])
        pl.when((s == 0) & (sect == 0))(loads[3].wait)
        pl.when(s > 0)(lambda: arrived(mixed_st, store_sem.at[3]))
        for pair in range(pairs):
            top, bottom = pair_up(
                mix_r[s, 2 * pair].astype(F32), mix_r[s, 2 * pair + 1].astype(F32), low_half
            )
            mixed_st[0:half, pair * LANES : (pair + 1) * LANES] = top.astype(BF16)
            mixed_st[half:group, pair * LANES : (pair + 1) * LANES] = bottom.astype(BF16)
        pltpu.make_async_copy(mixed_st, mixed_hbm.at[tokens_of(s)], store_sem.at[3]).start()
        part[...] += dot(mixed_st[...], wdense[...])
        rsf_st[...] = part[his_rows, :].astype(BF16)
        remote(rsf_st, rsf_r.at[s], rsf_ss.at[0], rsf_rs.at[s], y_dev).start()

    def forward_end(s):
        arrived(rsf_r.at[s], rsf_rs.at[s])
        arrived(rsf_st, rsf_ss.at[0])

        @pl.when(s > 0)
        def _():
            arrived(out_st, store_sem.at[4])
            pl.when(sect == 0)(lambda: arrived(out_st, xs_ss.at[0]))

        def out_step(i, carry):
            at = pl.ds(pl.multiple_of(i * 32, 32), 32)
            there = pl.ds(pl.multiple_of(tens * rows + i * 32, 32), 32)
            branch = part[there, :] + rsf_r[s, at, :].astype(F32) + (dense_b[...] + down_b[...])
            out_st[at, :] = (xfull[s, there, :].astype(F32) + branch).astype(BF16)
            return carry

        lax.fori_loop(0, rows // 32, out_step, 0, unroll=True)

        @pl.when(sect == 0)
        def _():
            remote(out_st, xfull.at[s, my_rows], xs_ss.at[0], ownx_sem.at[s], x_dev).start()

        pltpu.make_async_copy(out_st, out_hbm.at[s], store_sem.at[4]).start()

    def backward(s):
        arrived(gfull.at[s, his_rows], yg_r.at[s])
        pl.when((s == 0) & (sect == 1))(loads[3].wait)
        pltpu.make_async_copy(gfull.at[s], g_hbm.at[tokens_of(s)], g_store.at[s]).start()

        def mixed_step(k, carry):
            pair = lax.rem(me // 2 + 1 + k, pairs)
            at = pl.ds(pl.multiple_of(pair * LANES, LANES), LANES)
            both = dot_t(gfull[s], wdense[at, :])
            first = jnp.where(low_half, both[:half], turn(both[half:]))
            second = jnp.where(low_half, turn(both[:half]), both[half:])
            do_st[s, 2 * pair] = first.astype(BF16)
            do_st[s, 2 * pair + 1] = second.astype(BF16)
            for i in range(2):
                dest = 2 * pair + i
                spread(do_st.at[s, dest], do_r, s, dest, do_ss.at[s], do_rs.at[s])
            return carry

        lax.fori_loop(0, pairs, mixed_step, 0, unroll=True)

    def backward_ff(s):
        pl.when(s > 0)(lambda: arrived(dpre_st, store_sem.at[6]))

        def ff_step(j, carry):
            cols = pl.ds(pl.multiple_of(j * COLS, COLS), COLS)
            grad = dot_t(gfull[s], wdown[cols, :])
            grad = (grad * slope[s, :, cols].astype(F32)).astype(BF16)
            dpre_st[:, cols] = grad
            sums_at = pl.ds(pl.multiple_of(3 * heads * HEAD_DIM + j * COLS, COLS), COLS)
            bias_sums[:, sums_at] += fold(grad.astype(F32))
            term = dot_t(grad, wup[:, cols])

            @pl.when(j == 0)
            def _():
                dn1[...] = term

            @pl.when(j > 0)
            def _():
                dn1[...] += term

            return carry

        lax.fori_loop(0, ff // COLS, ff_step, 0, unroll=True)
        pltpu.make_async_copy(dpre_st, dpre_hbm.at[tokens_of(s)], store_sem.at[6]).start()

    def backward_attention(s):
        arrived(do_r.at[s], do_rs.at[s])
        arrived(do_st.at[s, pl.ds(0, wide - 1)], do_ss.at[s])
        pl.when(sect == 0)(lambda: unpack_heads(s))

        def unpack_step(src, carry):
            at = pl.multiple_of(src * group, group)
            grad = do_r[s, src].astype(F32)
            dox[pl.ds(at, half), :] = jnp.where(low_half, grad, 0.0).astype(BF16)
            dox[pl.ds(pl.multiple_of(at + half, half), half), :] = jnp.where(
                low_half, turn(grad), 0.0
            ).astype(BF16)
            product = grad * o_st[s, src].astype(F32)
            left = jnp.sum(jnp.where(low_half, product, 0.0), axis=1, keepdims=True)
            right = jnp.sum(jnp.where(low_half, 0.0, product), axis=1, keepdims=True)
            delta[src, :, 0:half] = jnp.broadcast_to(left, (half, LANES)).T[0:8, :]
            delta[src, :, half:group] = jnp.broadcast_to(right, (half, LANES)).T[0:8, :]
            return carry

        lax.fori_loop(0, wide, unpack_step, 0, unroll=True)
        slot = lax.rem(s, 2)
        rows_of = []
        for i in range(q_blocks):
            tokens = i * BLOCK + lax.broadcasted_iota(jnp.int32, (8, BLOCK), 1)
            inner_sum = jnp.concatenate(
                [delta[i * sources + k, 0:1, :] for k in range(sources)], axis=1
            )
            rows_of.append((starts_of(s, tokens)[0:1, :], tokens[0:1, :], inner_sum))
        for j in range(q_blocks):
            k_at = slice(j * BLOCK, (j + 1) * BLOCK)
            for i in range(j, q_blocks):
                q_at = slice(i * BLOCK, (i + 1) * BLOCK)
                begin, token, inner_sum = rows_of[i]
                raw = dot_t(kr[k_at, :], qm[q_at, :])
                u = j * BLOCK + lax.broadcasted_iota(jnp.int32, (BLOCK, BLOCK), 0)
                probs = jnp.exp2(raw * SCORE_SCALE - lse[s, i, 0:1, :])
                seen = u >= begin
                if i == j:
                    seen = seen & (u <= token)
                probs = jnp.where(seen, probs, 0.0)
                probs_grad = dot_t(vx[k_at, :], dox[q_at, :])
                score_grad = (probs * (probs_grad - inner_sum)).astype(BF16)
                value_term = dot(probs.astype(BF16), dox[q_at, :])
                key_term = dot(score_grad, kr[q_at, :])
                query_term = t_dot(score_grad, kr[k_at, :])
                if i == j:
                    acc[...] = value_term
                    peak[...] = key_term
                else:
                    acc[...] += value_term
                    peak[...] += key_term
                if j == 0:
                    dq[q_at, :] = query_term
                else:
                    dq[q_at, :] += query_term
            for k in range(sources):
                source = j * sources + k
                mine = slice(k * group, (k + 1) * group)
                at = slice(source * group, (source + 1) * group)
                both = jnp.where(low_group, dq[at, :], peak[mine, :])
                both = both * (1.0 / math.sqrt(HEAD_DIM))
                value = acc[mine, :]
                value = jnp.where(low_half, value[:half], turn(value[half:]))
                dqkv_st[slot, source, 0:group, :] = both.astype(BF16)
                dqkv_st[slot, source, group:per_source, :] = value.astype(BF16)
                spread(
                    dqkv_st.at[slot, source], dqkv_r, s, source, dqkv_ss.at[slot], dqkv_rs.at[s]
                )

    def backward_norm(s):
        arrived(dqkv_r.at[s], dqkv_rs.at[s])
        slot = lax.rem(s, 2)
        arrived(dqkv_st.at[slot, pl.ds(0, wide - 1)], dqkv_ss.at[slot])
        pl.when(s > 0)(lambda: arrived(dpk_st, store_sem.at[7]))

        def pair_step(pair, carry):
            qk0 = rotary(
                dqkv_r[s, 2 * pair, 0:group, :].astype(F32), cos, front, back, s, -1.0
            )
            qk1 = turn(
                rotary(
                    dqkv_r[s, 2 * pair + 1, 0:group, :].astype(F32), cos, front, back, s, -1.0
                )
            )
            top, bottom = pair_up(
                dqkv_r[s, 2 * pair, group:per_source, :].astype(F32),
                dqkv_r[s, 2 * pair + 1, group:per_source, :].astype(F32),
                low_half,
            )
            vv = jnp.concatenate([top, bottom], axis=0)
            columns = (qk0, jnp.where(low_group, vv, qk1), jnp.where(low_group, qk1, vv))
            for k, column in enumerate(columns):
                at = pl.ds(pl.multiple_of((pair * 3 + k) * LANES, LANES), LANES)
                column = column.astype(BF16)
                dpk_st[:, at] = column
                bias_sums[:, at] += fold(column.astype(F32))
            return carry

        lax.fori_loop(0, pairs, pair_step, 0, unroll=True)
        pltpu.make_async_copy(dpk_st, dpk_hbm.at[tokens_of(s)], store_sem.at[7]).start()
        part_b[...] = dot_t(dpk_st[...], wqkv[...])

        def e_step(i, carry):
            at = pl.ds(pl.multiple_of(i * 32, 32), 32)
            a, _ = normed_rows(xfull[s, at, :].astype(F32))
            first = part_b[at, :]
            second = dn1[at, :]
            small[0] += fold(first * a)
            small[1] += fold(second * a)
            small[2] += fold(first)
            small[3] += fold(second)
            part_b[at, :] = first * gain[0:1, :] + second * gain[1:2, :]
            return carry

        lax.fori_loop(0, group // 32, e_step, 0, unroll=True)
        rsb_st[...] = part_b[his_rows, :].astype(BF16)
        remote(rsb_st, rsb_r.at[s], rsb_ss.at[0], rsb_rs.at[s], y_dev).start()

    def backward_end(s):
        arrived(rsb_r.at[s], rsb_rs.at[s])
        arrived(rsb_st, rsb_ss.at[0])

        @pl.when(s > 0)
        def _():
            arrived(ig_st, store_sem.at[8])
            pl.when(sect == 1)(lambda: arrived(gx_st, gs_ss.at[0]))

        def in_step(i, carry):
            at = pl.ds(pl.multiple_of(i * 32, 32), 32)
            there = pl.ds(pl.multiple_of(tens * rows + i * 32, 32), 32)
            a, inv = normed_rows(xfull[s, there, :].astype(F32))
            e = part_b[there, :] + rsb_r[s, at, :].astype(F32)
            mean_e = jnp.mean(e, axis=-1, keepdims=True)
            cross = jnp.mean(e * a, axis=-1, keepdims=True)
            g_low = gfull[s, there, :].astype(F32)
            small[4] += fold(g_low)
            g = jnp.where(sect == 1, cot[s, at, :], g_low)
            grad = g + inv * (e - mean_e - a * cross)
            ig_st[at, :] = grad
            gx_st[at, :] = grad.astype(BF16)
            return carry

        lax.fori_loop(0, rows // 32, in_step, 0, unroll=True)

        @pl.when(s == micro - 1)
        def _():
            for k in range(micro):
                arrived(xfull.at[k, my_rows], yx_s.at[k])

        @pl.when(sect == 1)
        def _():
            remote(gx_st, gfull.at[s, my_rows], gs_ss.at[0], owng_sem.at[s], x_dev).start()

        pltpu.make_async_copy(ig_st, ig_hbm.at[s], store_sem.at[8]).start()

    chip, core = me // 2, lax.rem(me, 2)
    partner = {"wide": me + 1 - 2 * core}
    up_dev = {"wide": lax.rem(me + 2, wide)}
    down_dev = {"wide": lax.rem(me + wide - 2, wide)}
    at_bottom, at_top = chip == 0, chip == wide // 2 - 1
    at_end = at_bottom | at_top
    middle = jnp.logical_not(at_end)
    lower = chip == 1
    outer_of = {"wide": jnp.where(lower, me - 2, lax.rem(me + 2, wide))}
    inner_of = {"wide": jnp.where(lower, me + 2, lax.rem(me + wide - 2, wide))}
    end_of = {"wide": jnp.where(at_bottom, me + 2, lax.rem(me + wide - 2, wide))}
    kinds = gradient_kinds(d_model, heads * HEAD_DIM, ff)
    targets = (up_out, down_out, dense_out, qkv_out)
    operands = (
        (norm_hbm.at[1], dpre_hbm),
        (hid_hbm, g_hbm),
        (mixed_hbm, g_hbm),
        (norm_hbm.at[0], dpk_hbm),
    )
    ranges, first = [], 0
    for height, width in kinds:
        count = (height // TILE) * (width // (2 * ACROSS))
        ranges.append((first, first + count, width // (2 * ACROSS)))
        first += count
    steps = first

    def own_at(ring):
        rows_at = pl.ds(pl.multiple_of((ring // RING) * TILE, TILE), TILE)
        return scores.at[
            rows_at, pl.ds(pl.multiple_of(lax.rem(ring, RING) * ACROSS, ACROSS), ACROSS)
        ]

    def guest_at(number):
        cols = pl.ds(pl.multiple_of(lax.rem(number, 4) * ACROSS, ACROSS), ACROSS)
        return xfull.at[number // 4, :, cols]

    def guest_st_at(slot):
        return mixed_st.at[:, pl.ds(pl.multiple_of(slot * ACROSS, ACROSS), ACROSS)]

    def core_st_at(ring):
        return hid_st.at[:, pl.ds(pl.multiple_of(ring * ACROSS, ACROSS), ACROSS)]

    def red_st_at(ring):
        return dpre_st.at[:, pl.ds(pl.multiple_of(ring * ACROSS, ACROSS), ACROSS)]

    def tot_at(slot):
        cols = pl.ds(pl.multiple_of(lax.rem(slot, 4) * ACROSS, ACROSS), ACROSS)
        return norm_st.at[slot // 4, :, cols]

    def left_at(slot):
        return wup.at[:, pl.ds(pl.multiple_of(slot * TILE, TILE), TILE)]

    def right_at(slot):
        return wdown.at[
            pl.ds(pl.multiple_of((slot // 2) * d_model, d_model), d_model),
            pl.ds(pl.multiple_of(lax.rem(slot, 2) * 2 * ACROSS, 2 * ACROSS), 2 * ACROSS),
        ]

    tile_ref = core_r.at[0]

    def by_kind(m, body):
        for kind, (low, high, across) in enumerate(ranges):

            @pl.when((m >= low) & (m < high))
            def _(kind=kind, low=low, across=across):
                at = m - low
                body(kind, at // across, lax.rem(at, across))

    def tile_of(kind, row, col, which):
        return targets[kind].at[
            pl.ds(pl.multiple_of(row * TILE, TILE), TILE),
            pl.ds(pl.multiple_of((2 * col + which) * ACROSS, ACROSS), ACROSS),
        ]

    def fetch(m):
        pl.when(m == ranges[3][0])(lambda: arrived(dpk_st, store_sem.at[7]))

        def body(kind, row, col):
            left, right = operands[kind]
            slot = lax.rem(m, AHEAD + 1)

            @pl.when(col == 0)
            def _():
                pltpu.make_async_copy(
                    left.at[:, pl.ds(pl.multiple_of(row * TILE, TILE), TILE)],
                    left_at(slot),
                    op_sem.at[0, slot],
                ).start()

            pltpu.make_async_copy(
                right.at[:, pl.ds(pl.multiple_of(col * 2 * ACROSS, 2 * ACROSS), 2 * ACROSS)],
                right_at(slot),
                op_sem.at[1, slot],
            ).start()

        by_kind(m, body)

    total_steps = jnp.where(sect == 1, steps + GUESTS, steps)
    chain = jnp.where(sect == 1, steps + GUESTS, steps - GUESTS)
    visit = ranges[2][0]

    def place(m):
        shared = (sect == 0) & (m < 2 * GUESTS)
        away = shared & (lax.rem(m, 2) == 1)
        later = (sect == 1) & (m >= visit)
        visitor = later & (m < visit + GUESTS)
        n = jnp.where(shared, m // 2, jnp.where(sect == 0, m - GUESTS, m))
        number = jnp.where(visitor, m - visit, m // 2)
        tile = jnp.where(visitor, 2 * (m - visit) + 1, jnp.where(later, m - GUESTS, m))
        return away, visitor, n, number, tile

    def is_root(n):
        return middle & (chip == 1 + lax.rem(n, 2))

    def products(step_at, m):
        slot, ring = lax.rem(m, AHEAD + 1), lax.rem(m, RING)

        def body(kind, row, col):
            @pl.when(col == 0)
            def _():
                arrived(left_at(slot), op_sem.at[0, slot])
                turned[...] = left_at(slot)[...].T

        by_kind(m, body)
        arrived(right_at(slot), op_sem.at[1, slot])
        both = dot(turned[...], right_at(slot)[...])
        first, second = both[:, :ACROSS], both[:, ACROSS:]
        own_at(lax.rem(step_at, OWN))[...] = jnp.where(core == 0, first, second)

        @pl.when(m >= RING)
        def _():
            arrived(tile_ref, core_ss.at[ring])
            pl.semaphore_wait(core_free, 1)

        core_st_at(ring)[...] = jnp.where(core == 0, second, first).astype(BF16)
        remote(
            core_st_at(ring), core_r.at[ring], core_ss.at[ring], core_rs.at[ring], partner
        ).start()

    def send_red(m, value, target, sem, dev, free):
        ring = lax.rem(m, RING)

        @pl.when(m >= RING)
        def _():
            pl.semaphore_wait(free, 1)

        red_st_at(ring)[...] = value.astype(BF16)
        remote(red_st_at(ring), target.at[ring], red_ss.at[ring], sem.at[ring], dev).start()

    def chip_sum(m):
        away, visitor, n, number, tile = place(m)
        ring = lax.rem(tile, RING)
        own = own_at(lax.rem(m, OWN))

        @pl.when(visitor)
        def _():
            arrived(tile_ref, guest_rs.at[number])
            own[...] = guest_at(number)[...].astype(F32)

        @pl.when(jnp.logical_not(visitor))
        def _():
            arrived(tile_ref, core_rs.at[ring])
            own[...] = own[...] + core_r[ring].astype(F32)

            @pl.when(tile + RING < steps)
            def _():
                pl.semaphore_signal(core_free, inc=1, device_id=partner, device_id_type=MESH)

        @pl.when(away)
        def _():
            slot = lax.rem(number, 2)
            pl.when(number >= 2)(lambda: arrived(tile_ref, guest_ss.at[slot]))
            guest_st_at(slot)[...] = own[...].astype(BF16)
            remote(
                guest_st_at(slot),
                guest_at(number),
                guest_ss.at[slot],
                guest_rs.at[number],
                x_dev,
            ).start()

        @pl.when(at_end & jnp.logical_not(away))
        def _():
            pl.when(n >= RING)(lambda: arrived(tile_ref, red_ss.at[lax.rem(n, RING)]))
            send_red(n, own[...], outer_r, outer_rs, end_of, outer_free.at[lax.rem(n, 2)])

    def take_outer(m, n):
        ring = lax.rem(n, RING)
        arrived(tile_ref, outer_rs.at[ring])
        total = own_at(lax.rem(m, OWN))[...] + outer_r[ring].astype(F32)

        @pl.when(n + RING < chain)
        def _():
            pl.semaphore_signal(
                outer_free.at[lax.rem(n, 2)], inc=1, device_id=outer_of, device_id_type=MESH
            )

        return total

    def pass_in(m):
        _, _, n, _, _ = place(m)
        total = take_outer(m, n)
        pl.when(n >= RING)(lambda: arrived(tile_ref, red_ss.at[lax.rem(n, RING)]))
        send_red(n, total, inner_r, inner_rs, inner_of, inner_free)

    def finish(m):
        _, visitor, n, number, tile = place(m)
        ring = lax.rem(n, RING)
        slot = lax.rem(n // 2, TOTALS)
        total = take_outer(m, n)
        arrived(tile_ref, inner_rs.at[ring])
        total = total + inner_r[ring].astype(F32)

        @pl.when(n + RING < chain)
        def _():
            pl.semaphore_signal(inner_free, inc=1, device_id=inner_of, device_id_type=MESH)

        @pl.when(n >= 2 * TOTALS)
        def _():
            for k in range(4):
                arrived(tile_ref, tot_ss.at[k, slot])

        tot_at(slot)[...] = total.astype(BF16)

        def send(here):
            remote(tot_at(slot), here, tot_ss.at[0, slot], bc_rs.at[m], outer_of).start()
            remote(tot_at(slot), here, tot_ss.at[1, slot], bc_rs.at[m], inner_of).start()
            pltpu.make_async_copy(tot_at(slot), here, tot_ss.at[3, slot]).start()

        def body(kind, row, col):
            here = tile_of(kind, row, col, core)

            @pl.when(visitor)
            def _():
                send(guest_hbm.at[number])
                remote(tot_at(slot), here, tot_ss.at[2, slot], bc_rs.at[tile], x_dev).start()

            @pl.when(jnp.logical_not(visitor))
            def _():
                send(here)
                remote(
                    tot_at(slot), here, tot_ss.at[2, slot], fin_rs.at[kind], partner
                ).start()

        by_kind(tile, body)

    def hand_on(m):
        _, visitor, _, number, tile = place(m)
        arrived(tile_ref, bc_rs.at[m])

        def body(kind, row, col):
            here = tile_of(kind, row, col, core)

            @pl.when(visitor)
            def _():
                held = guest_hbm.at[number]

                @pl.when(middle)
                def _():
                    remote(held, held, fwd_ss.at[m], bc_rs.at[m], outer_of).start()

                remote(held, here, share_ss.at[m], bc_rs.at[tile], x_dev).start()

            @pl.when(jnp.logical_not(visitor))
            def _():
                @pl.when(middle)
                def _():
                    remote(here, here, fwd_ss.at[m], bc_rs.at[m], outer_of).start()

                remote(here, here, share_ss.at[m], fin_rs.at[kind], partner).start()

        by_kind(tile, body)

    def guest_home(number, carry):
        m = 2 * number + 1
        arrived(tile_ref, bc_rs.at[m])

        def body(kind, row, col):
            here = tile_of(kind, row, col, core)
            remote(here, here, share_ss.at[m], fin_rs.at[kind], partner).start()

        by_kind(m, body)
        return carry

    exchanges = (
        {"tensor": 1 - tens},
        partner,
        {"wide": me + 2 - 4 * lax.rem(chip, 2)},
        {"wide": me + 4 - 8 * (chip // 2)},
    )

    def sums_begin():
        sums[:, 0:d_model] = jnp.concatenate(
            [jnp.sum(small[k], axis=0, keepdims=True) for k in range(5)]
            + [jnp.zeros((3, d_model), F32)],
            axis=0,
        )
        total = jnp.sum(bias_sums[...], axis=0, keepdims=True)
        lines = [total[:, k * COLS : (k + 1) * COLS] for k in range(total.shape[1] // COLS)]
        lines.append(jnp.zeros((8 - len(lines), COLS), F32))
        sums[:, d_model:] = jnp.concatenate(lines, axis=0)

    def exchange_start(k):
        if k == 0:
            sums_begin()
        else:
            arrived(sums, sum_ss.at[0])
        sums_r[0] = sums[...]
        remote(sums_r.at[0], sums_r.at[k + 1], sum_ss.at[0], sum_rs.at[k], exchanges[k]).start()

    def exchange_end(k):
        arrived(sums, sum_rs.at[k])
        if k == 0:
            sums[:, 0:d_model] += sums_r[1, :, 0:d_model]
        else:
            sums[...] += sums_r[k + 1]

    def gradient_step(i, carry):
        _, visits, _, _, here_tile = place(i)
        works = (i < total_steps) & jnp.logical_not(visits)
        pl.when(works & (here_tile + AHEAD < steps))(lambda: fetch(here_tile + AHEAD))
        pl.when(works)(lambda: products(i, here_tile))
        for k in range(4):
            pl.when(i == EARLY + 4 * k + 2)(lambda k=k: exchange_start(k))
            pl.when(i == EARLY + 4 * k + 5)(lambda k=k: exchange_end(k))

        def late(lag, allowed, body):
            m = i - lag
            away, _, n, _, _ = place(m)
            inside = (m >= 0) & (m < total_steps)
            pl.when(inside & allowed(away, n))(lambda: body(m))

        def outside(away, n):
            return middle & jnp.logical_not(away | is_root(n))

        late(LAGS[0], lambda away, n: n >= 0, chip_sum)
        late(LAGS[1], outside, pass_in)
        late(LAGS[2], lambda away, n: is_root(n) & jnp.logical_not(away), finish)
        late(LAGS[3], outside, hand_on)
        late(LAGS[4], lambda away, n: at_end & jnp.logical_not(away), hand_on)
        return carry

    def gradient_begin():
        arrived(norm_st.at[0], store_sem.at[0])
        arrived(norm_st.at[1], store_sem.at[1])
        arrived(hid_st, store_sem.at[2])
        arrived(mixed_st, store_sem.at[3])
        arrived(dpre_st, store_sem.at[6])
        for s in range(micro):
            arrived(gfull.at[s], g_store.at[s])
        for m in range(AHEAD):
            fetch(jnp.int32(m))

    def at(seq, allowed, body):
        pl.when(allowed & (seq >= 0) & (seq < micro))(lambda: body(seq))

    @pl.when(sect == 1)
    def _():
        lax.fori_loop(0, micro, lambda s, carry: (backward(s), carry)[1], 0)

    first = jnp.int32(0)
    pl.when(sect == 1)(lambda: forward_meet(first))
    forward(first)
    forward_ff(first)
    always = sect >= 0

    def step(i, carry):
        f = i
        b = jnp.where(sect == 1, i, i - micro)
        at(b, (sect == 0) & (b == 0), backward_meet)
        at(b, sect == 0, backward)
        at(f + 1, sect == 1, forward_meet)
        at(f, always, forward_attention)
        at(f + 1, always, forward)
        at(b, always, backward_attention)
        at(b - 1, always, backward_norm)
        at(f, always, forward_out)
        at(b, always, backward_ff)
        at(b + 1, (sect == 0) & (b >= 0), backward_meet)
        at(b - 1, always, backward_end)
        at(f, always, forward_end)
        at(f + 1, always, forward_ff)

        starts = jnp.where(sect == 1, i == micro, i == 2 * micro - 1)
        goes_on = (sect == 0) & (i == 2 * micro)
        pl.when(starts)(gradient_begin)
        low = jnp.where(goes_on, EARLY, 0)
        high = jnp.where(
            goes_on | (starts & (sect == 1)),
            total_steps + LAGS[4],
            jnp.where(starts, EARLY, 0),
        )
        lax.fori_loop(low, high, gradient_step, 0)
        return carry

    lax.fori_loop(0, jnp.where(sect == 1, micro + 1, 2 * micro + 1), step, 0)

    for s in range(micro):
        arrived(gfull.at[s, my_rows], yg_s.at[s])
    arrived(out_st, store_sem.at[4])
    arrived(ig_st, store_sem.at[8])
    pl.when(sect == 0)(lambda: arrived(out_st, xs_ss.at[0]))
    pl.when(sect == 1)(lambda: arrived(gx_st, gs_ss.at[0]))

    arrived(sums, sum_ss.at[0])
    for ring in range(RING):
        arrived(tile_ref, core_ss.at[ring])

    @pl.when(sect == 0)
    def _():
        lax.fori_loop(0, GUESTS, guest_home, 0)
        for slot in range(2):
            arrived(tile_ref, guest_ss.at[slot])

    def drain(m, carry):
        away, _, n, _, _ = place(m)
        root = is_root(n)
        stays = jnp.logical_not(away)
        ring = lax.rem(n, RING)
        sends = at_end | (middle & jnp.logical_not(root))
        pl.when(stays & sends & (n + RING >= chain))(lambda: arrived(tile_ref, red_ss.at[ring]))

        @pl.when(stays & root & (n + 2 * TOTALS >= chain))
        def _():
            for k in range(4):
                arrived(tile_ref, tot_ss.at[k, lax.rem(n // 2, TOTALS)])

        @pl.when(stays & middle & jnp.logical_not(root))
        def _():
            arrived(tile_ref, fwd_ss.at[m])

        pl.when(away | jnp.logical_not(root))(lambda: arrived(tile_ref, share_ss.at[m]))
        return carry

    lax.fori_loop(0, total_steps, drain, 0)
    for kind, (height, width) in enumerate(kinds):
        arrived(targets[kind].at[pl.ds(0, height // 2)], fin_rs.at[kind])


def relay(dims, doc_lengths, block_input, cotangent, weights, collective_id):
    micro, rows, group, wide, heads, d_model, ff = dims
    (
        norm_gain,
        norm_bias,
        qkv_weight,
        qkv_bias,
        dense_weight,
        dense_bias,
        up_weight,
        up_bias,
        down_weight,
        down_bias,
    ) = weights
    inner = heads * HEAD_DIM
    per_source = group + group // 2
    anywhere = pl.BlockSpec(memory_space=pl.ANY)
    local = pl.BlockSpec(memory_space=pltpu.VMEM)
    scalars = pl.BlockSpec(memory_space=pltpu.SMEM)
    dma = pltpu.SemaphoreType.DMA
    vmem = pltpu.VMEM
    outs = [
        jax.ShapeDtypeStruct((micro, rows, d_model), BF16),
        jax.ShapeDtypeStruct((micro, rows, d_model), F32),
        jax.ShapeDtypeStruct((2, micro * group, d_model), BF16),
        jax.ShapeDtypeStruct((micro * group, d_model), BF16),
        jax.ShapeDtypeStruct((micro * group, inner), BF16),
        jax.ShapeDtypeStruct((micro * group, ff), BF16),
        jax.ShapeDtypeStruct((micro * group, ff), BF16),
        jax.ShapeDtypeStruct((micro * group, 3 * inner), BF16),
    ]
    kinds = gradient_kinds(d_model, inner, ff)
    steps = sum((height // TILE) * (width // (2 * ACROSS)) for height, width in kinds)
    outs += [jax.ShapeDtypeStruct(kind, BF16) for kind in kinds]
    outs += [jax.ShapeDtypeStruct((GUESTS, TILE, ACROSS), BF16)]
    outs += [jax.ShapeDtypeStruct((8, d_model + COLS), F32)]
    regular = pltpu.SemaphoreType.REGULAR
    scratch = [
        vmem((5, 8, d_model), F32),
        vmem((8, 3 * inner + ff), F32),
        vmem((micro, group, LANES), F32),
        vmem((micro, group, LANES), F32),
        vmem((micro, group, LANES), F32),
        vmem(qkv_weight.shape, BF16),
        vmem(dense_weight.shape, BF16),
        vmem(up_weight.shape, BF16),
        vmem(down_weight.shape, BF16),
        vmem((micro, group, d_model), BF16),
        vmem((micro, group, d_model), BF16),
        vmem((micro, rows, d_model), F32),
        vmem((micro, wide, per_source, LANES), BF16),
        vmem((micro, wide, group // 2, LANES), BF16),
        vmem((micro, wide, group // 2, LANES), BF16),
        vmem((micro, wide, per_source, LANES), BF16),
        vmem((micro, rows, d_model), BF16),
        vmem((micro, rows, d_model), BF16),
        vmem((wide, per_source, LANES), BF16),
        vmem((micro, wide, group // 2, LANES), BF16),
        vmem((micro, wide, group // 2, LANES), BF16),
        vmem((2, wide, per_source, LANES), BF16),
        vmem((rows, d_model), BF16),
        vmem((rows, d_model), BF16),
        vmem((rows, d_model), BF16),
        vmem((rows, d_model), BF16),
        vmem((rows, d_model), F32),
        vmem((2, group, d_model), BF16),
        vmem((group, inner), BF16),
        vmem((group, ff), BF16),
        vmem((group, ff), BF16),
        vmem((group, 3 * inner), BF16),
        vmem((micro, group, ff), BF16),
        vmem((group, d_model), F32),
        vmem((group, d_model), F32),
        vmem((group, d_model), F32),
        vmem((SEQ, LANES), BF16),
        vmem((SEQ, LANES), BF16),
        vmem((SEQ, LANES), BF16),
        vmem((SEQ, LANES), BF16),
        vmem((SEQ, LANES), F32),
        vmem((micro, SEQ // BLOCK, 8, BLOCK), F32),
        vmem((wide, 8, group), F32),
        vmem((BLOCK, SEQ), F32),
        vmem((BLOCK, LANES), F32),
        vmem((BLOCK, LANES), F32),
        dma((4,)),
        dma((micro,)),
        dma((micro,)),
        dma((micro,)),
        dma((micro,)),
        dma((micro,)),
        dma((micro,)),
        dma((1,)),
        dma((micro,)),
        dma((micro,)),
        dma((micro,)),
        dma((micro,)),
        dma((micro,)),
        dma((2,)),
        dma((micro,)),
        dma((1,)),
        dma((micro,)),
        dma((1,)),
        dma((micro,)),
        dma((1,)),
        dma((1,)),
        dma((9,)),
        dma((micro,)),
        vmem((RING, TILE, ACROSS), BF16),
        vmem((RING, TILE, ACROSS), BF16),
        vmem((RING, TILE, ACROSS), BF16),
        vmem((TILE, micro * group), BF16),
        vmem((5, 8, d_model + COLS), F32),
        dma((2, AHEAD + 1)),
        dma((RING,)),
        dma((RING,)),
        dma((RING,)),
        dma((RING,)),
        dma((RING,)),
        dma((steps + GUESTS,)),
        dma((4, TOTALS)),
        dma((steps + GUESTS,)),
        dma((steps + GUESTS,)),
        dma((4,)),
        dma((1,)),
        dma((4,)),
        dma((2,)),
        dma((GUESTS,)),
        regular,
        regular((2,)),
        regular,
    ]
    return pl.pallas_call(
        functools.partial(relay_kernel, dims),
        out_shape=outs,
        in_specs=[scalars, anywhere, anywhere] + [local] * 6 + [anywhere] * 4,
        out_specs=[anywhere] * 13 + [local],
        scratch_shapes=scratch,
        compiler_params=pltpu.CompilerParams(
            collective_id=collective_id, has_side_effects=True, vmem_limit_bytes=63 << 20
        ),
        name="relay",
    )(
        doc_lengths,
        block_input,
        cotangent,
        norm_gain,
        norm_bias,
        qkv_bias[None],
        up_bias[None],
        dense_bias[None],
        down_bias[None],
        qkv_weight,
        dense_weight,
        up_weight,
        down_weight,
    )


WIDEN_STEPS = 8


def widen_kernel(sums, *refs):
    count = (len(refs) - 6) // 2
    sources, targets = refs[:count], refs[count : 2 * count]
    gain, shift, dense_bias, down_bias, qkv_bias, up_bias = refs[2 * count :]
    for source, target in zip(sources, targets):
        target[...] = source[...].astype(target.dtype).reshape(target.shape)
    d_model = gain.shape[2]
    gain[0] = sums[0:2, :d_model]
    shift[0] = sums[2:4, :d_model]
    dense_bias[...] = sums[4:5, :d_model]
    down_bias[...] = sums[4:5, :d_model]
    lines = qkv_bias.shape[1] // COLS
    for k in range(lines):
        qkv_bias[:, k * COLS : (k + 1) * COLS] = sums[k : k + 1, d_model:]
    for k in range(up_bias.shape[1] // COLS):
        up_bias[:, k * COLS : (k + 1) * COLS] = sums[lines + k : lines + k + 1, d_model:]


def widened(rows_out, grads, sums, d_model, qkv_width, ff):
    micro, rows, _ = rows_out[0].shape
    parts = WIDEN_STEPS // micro

    def rows_of(grad):
        return grad.shape[0] // WIDEN_STEPS, grad.shape[1]

    def place(i):
        return i // parts, lax.rem(i, parts), 0

    small = [(1, 2, d_model)] * 2 + [(1, d_model)] * 2 + [(1, qkv_width), (1, ff)]
    return pl.pallas_call(
        widen_kernel,
        grid=(WIDEN_STEPS,),
        out_shape=[jax.ShapeDtypeStruct((1,) + part.shape, part.dtype) for part in rows_out]
        + [jax.ShapeDtypeStruct((1,) + grad.shape, F32) for grad in grads]
        + [jax.ShapeDtypeStruct(shape, F32) for shape in small],
        in_specs=[pl.BlockSpec(sums.shape, lambda i: (0, 0))]
        + [pl.BlockSpec((1, rows // parts, d_model), place) for _ in rows_out]
        + [pl.BlockSpec(rows_of(grad), lambda i: (i, 0)) for grad in grads],
        out_specs=[
            pl.BlockSpec((1, 1, rows // parts, d_model), lambda i: (0,) + place(i))
            for _ in rows_out
        ]
        + [pl.BlockSpec((1,) + rows_of(grad), lambda i: (0, i, 0)) for grad in grads]
        + [pl.BlockSpec(shape, lambda i, zeros=(0,) * len(shape): zeros) for shape in small],
        compiler_params=pltpu.CompilerParams(vmem_limit_bytes=60 << 20),
        name="widened",
    )(sums, *rows_out, *grads)


def relay_shards(
    block_input,
    doc_lengths,
    norm_gain,
    norm_bias,
    qkv_weight,
    qkv_bias,
    dense_weight,
    dense_bias,
    up_weight,
    up_bias,
    down_weight,
    down_bias,
    cotangent,
):
    weights = tuple(
        array[0]
        for array in (
            norm_gain,
            norm_bias,
            qkv_weight,
            qkv_bias,
            dense_weight,
            dense_bias,
            up_weight,
            up_bias,
            down_weight,
            down_bias,
        )
    )
    micro, rows, d_model = block_input.shape
    group = rows * lax.axis_size("tensor")
    wide = lax.axis_size("wide")
    heads = qkv_weight.shape[2] // (3 * HEAD_DIM)
    ff = up_weight.shape[2]
    dims = (micro, rows, group, wide, heads, d_model, ff)
    out, input_grad, *_, up_grad, down_grad, dense_grad, qkv_grad, _, sums = relay(
        dims, doc_lengths, block_input, cotangent, weights, 1
    )
    out, input_grad, up_grad, down_grad, dense_grad, qkv_grad, *small = widened(
        (out, input_grad),
        (up_grad, down_grad, dense_grad, qkv_grad),
        sums,
        d_model,
        qkv_weight.shape[2],
        ff,
    )
    gain, shift, dense_b, down_b, qkv_b, up_b = small
    return (
        out,
        input_grad,
        gain,
        shift,
        qkv_grad,
        qkv_b,
        dense_grad,
        dense_b,
        up_grad,
        up_b,
        down_grad,
        down_b,
    )


def shortened(shard):

    def short(part):
        return part.astype(jnp.bfloat16) if part.dtype == jnp.float32 else part

    return jax.tree.map(short, shard)


def from_behind(block, axis, distance):
    devices = range(lax.axis_size(axis))
    route = [(i - distance, i) for i in devices if i - distance in devices]
    return lax.ppermute(block, axis, route)


def norm_parts(values, gain, shift):
    center = jnp.mean(values, axis=-1, keepdims=True)
    centred = values - center
    spread = jnp.mean(centred * centred, axis=-1, keepdims=True)
    inv_scale = lax.rsqrt(spread + EPSILON)
    normed = centred * inv_scale
    return (normed * gain + shift, normed, inv_scale)


def norm_back(grad, normed, inv_scale, gain):
    scaled = grad * gain
    inner_mean = jnp.mean(scaled, axis=-1, keepdims=True)
    cross_mean = jnp.mean(scaled * normed, axis=-1, keepdims=True)
    return inv_scale * (scaled - inner_mean - normed * cross_mean)


def doc_layout(lengths, tok_index):
    ends = jnp.cumsum(lengths)
    starts = ends - lengths
    doc_ids = jnp.sum((tok_index[:, None] >= ends[None, :]).astype(jnp.int32), axis=1)
    numbers = jnp.arange(lengths.shape[0], dtype=jnp.int32)
    picked = doc_ids[:, None] == numbers[None, :]
    begins = jnp.sum(jnp.where(picked, starts[None, :], 0), axis=1)
    return (doc_ids, tok_index - begins)


def rope_tables(offsets):
    half = ROT // 2
    freqs = ROPE_BASE ** (-2.0 * jnp.arange(half, dtype=jnp.float32) / ROT)
    angle = offsets.astype(jnp.float32)[:, None] * freqs[None, :]
    return (jnp.cos(angle)[:, None, :], jnp.sin(angle)[:, None, :])


def rotate(values, cos_table, sin_table):
    half = ROT // 2
    front = values[..., :half]
    back = values[..., half:ROT]
    turned = [
        front * cos_table - back * sin_table,
        back * cos_table + front * sin_table,
        values[..., ROT:],
    ]
    return jnp.concatenate(turned, axis=-1)


def unrotate(values, cos_table, sin_table):
    half = ROT // 2
    front = values[..., :half]
    back = values[..., half:ROT]
    turned = [
        front * cos_table + back * sin_table,
        back * cos_table - front * sin_table,
        values[..., ROT:],
    ]
    return jnp.concatenate(turned, axis=-1)


def gelu_parts(pre_act):
    cumul = 0.5 * (1.0 + lax.erf(pre_act * (1.0 / math.sqrt(2.0))))
    density = jnp.exp(-0.5 * pre_act * pre_act) * (1.0 / math.sqrt(2.0 * math.pi))
    return (pre_act * cumul, cumul + pre_act * density)


def store_slot(buffer, update, slot_here, is_valid):
    previous = lax.dynamic_index_in_dim(buffer, slot_here, 0, keepdims=False)
    return lax.dynamic_update_index_in_dim(
        buffer, jnp.where(is_valid, update, previous), slot_here, 0
    )


def gather_keys(key_rows, value_rows):
    return (
        lax.all_gather(key_rows, "wide", axis=0, tiled=True),
        lax.all_gather(value_rows, "wide", axis=0, tiled=True),
    )


def forward_parts(inputs, lengths, weights, with_output):
    (
        norm_gain,
        norm_bias,
        qkv_weight,
        qkv_bias,
        dense_weight,
        dense_bias,
        up_weight,
        up_bias,
        down_weight,
        down_bias,
    ) = weights
    seq_len = SEQ
    group = inputs.shape[0] * lax.axis_size("tensor")
    head_count = qkv_weight.shape[1] // (3 * HEAD_DIM)
    factor = 1.0 / math.sqrt(HEAD_DIM)
    values = inputs.astype(jnp.float32)
    norm_first, normed_first, scale_first = norm_parts(values, norm_gain[0], norm_bias[0])
    norm_second, normed_second, scale_second = norm_parts(values, norm_gain[1], norm_bias[1])
    full_first, full_second = (
        lax.all_gather(norm_first.astype(jnp.bfloat16), "tensor", axis=0, tiled=True),
        lax.all_gather(norm_second.astype(jnp.bfloat16), "tensor", axis=0, tiled=True),
    )
    tok_index = lax.axis_index("wide") * group + jnp.arange(group, dtype=jnp.int32)
    doc_ids, offsets = doc_layout(lengths, tok_index)
    all_index = jnp.arange(seq_len, dtype=jnp.int32)
    all_docs = doc_layout(lengths, all_index)[0]
    cos_table, sin_table = rope_tables(offsets)
    packed = jnp.dot(full_first, qkv_weight, preferred_element_type=jnp.float32) + qkv_bias
    packed = packed.reshape(group, head_count, 3, HEAD_DIM)
    queries = rotate(packed[:, :, 0], cos_table, sin_table).astype(jnp.bfloat16)
    key_here = rotate(packed[:, :, 1], cos_table, sin_table).astype(jnp.bfloat16)
    value_here = packed[:, :, 2].astype(jnp.bfloat16)
    key_all, value_all = gather_keys(key_here.reshape(group, -1), value_here.reshape(group, -1))
    key_heads = key_all.reshape(seq_len, head_count, HEAD_DIM)
    value_heads = value_all.reshape(seq_len, head_count, HEAD_DIM)
    allowed = (doc_ids[:, None] == all_docs[None, :]) & (all_index[None, :] <= tok_index[:, None])
    raw_scores = jnp.einsum("qhd,khd->qhk", queries, key_heads, preferred_element_type=jnp.float32)
    scores = jnp.where(allowed[:, None, :], raw_scores * factor, -jnp.inf)
    row_max = jnp.max(scores, axis=-1, keepdims=True)
    log_total = row_max + jnp.log(jnp.sum(jnp.exp(scores - row_max), axis=-1, keepdims=True))
    attn_probs = jnp.exp(scores - log_total)
    probs_low = attn_probs.astype(jnp.bfloat16)
    mixed_out = jnp.einsum(
        "qhk,khd->qhd", probs_low, value_heads, preferred_element_type=jnp.float32
    )
    mixed_out = mixed_out.reshape(group, -1).astype(jnp.bfloat16)
    up_pre = jnp.dot(full_second, up_weight, preferred_element_type=jnp.float32) + up_bias
    up_act, gelu_slope = gelu_parts(up_pre)
    hidden = up_act.astype(jnp.bfloat16)
    output = None
    if with_output:
        partial_value = jnp.dot(mixed_out, dense_weight, preferred_element_type=jnp.float32)
        partial_value = partial_value + jnp.dot(
            hidden, down_weight, preferred_element_type=jnp.float32
        )
        branch = (
            lax.psum_scatter(
                partial_value.astype(jnp.bfloat16), "tensor", scatter_dimension=0, tiled=True
            ).astype(jnp.float32)
            + dense_bias
            + down_bias
        )
        output = (values + branch).astype(jnp.bfloat16)
    return dict(
        output=output,
        normed_first=normed_first,
        scale_first=scale_first,
        normed_second=normed_second,
        scale_second=scale_second,
        full_first=full_first,
        full_second=full_second,
        tok_index=tok_index,
        doc_ids=doc_ids,
        all_index=all_index,
        all_docs=all_docs,
        cos_table=cos_table,
        sin_table=sin_table,
        queries=queries,
        key_here=key_here,
        value_here=value_here,
        key_all=key_all,
        value_all=value_all,
        key_heads=key_heads,
        value_heads=value_heads,
        attn_probs=attn_probs,
        probs_low=probs_low,
        log_total=log_total,
        mixed_out=mixed_out,
        gelu_slope=gelu_slope,
        hidden=hidden,
    )


def backward_parts(inputs, grad_out, lengths, weights):
    (
        norm_gain,
        norm_bias,
        qkv_weight,
        qkv_bias,
        dense_weight,
        dense_bias,
        up_weight,
        up_bias,
        down_weight,
        down_bias,
    ) = weights
    parts = forward_parts(inputs, lengths, weights, False)
    seq_len = SEQ
    group = inputs.shape[0] * lax.axis_size("tensor")
    head_count = qkv_weight.shape[1] // (3 * HEAD_DIM)
    factor = 1.0 / math.sqrt(HEAD_DIM)
    cos_table = parts["cos_table"]
    sin_table = parts["sin_table"]
    grad_low = grad_out.astype(jnp.bfloat16)
    grad_rows = grad_low.astype(jnp.float32)
    grad_full = lax.all_gather(grad_low, "tensor", axis=0, tiled=True)
    dense_grad = jnp.einsum(
        "cf,cd->fd", parts["mixed_out"], grad_full, preferred_element_type=jnp.float32
    )
    down_grad = jnp.einsum(
        "cf,cd->fd", parts["hidden"], grad_full, preferred_element_type=jnp.float32
    )
    hidden_grad = jnp.einsum(
        "cd,fd->cf", grad_full, down_weight, preferred_element_type=jnp.float32
    )
    pre_grad = (hidden_grad * parts["gelu_slope"]).astype(jnp.bfloat16)
    up_grad = jnp.einsum(
        "cd,cf->df", parts["full_second"], pre_grad, preferred_element_type=jnp.float32
    )
    up_bias_grad = jnp.sum(pre_grad.astype(jnp.float32), axis=0)
    second_grad = jnp.einsum("cf,df->cd", pre_grad, up_weight, preferred_element_type=jnp.float32)
    mixed_grad = jnp.einsum(
        "cd,fd->cf", grad_full, dense_weight, preferred_element_type=jnp.float32
    )
    mixed_grad = mixed_grad.astype(jnp.bfloat16).reshape(group, head_count, HEAD_DIM)
    attn_probs = parts["attn_probs"]
    probs_grad = jnp.einsum(
        "qhd,khd->qhk", mixed_grad, parts["value_heads"], preferred_element_type=jnp.float32
    )
    inner = jnp.sum(attn_probs * probs_grad, axis=-1, keepdims=True)
    score_grad = (attn_probs * (probs_grad - inner) * factor).astype(jnp.bfloat16)
    query_grad = jnp.einsum(
        "qhk,khd->qhd", score_grad, parts["key_heads"], preferred_element_type=jnp.float32
    )
    key_sums = jnp.einsum(
        "qhk,qhd->khd", score_grad, parts["queries"], preferred_element_type=jnp.float32
    )
    value_sums = jnp.einsum(
        "qhk,qhd->khd", parts["probs_low"], mixed_grad, preferred_element_type=jnp.float32
    )
    key_flat, value_flat = (
        lax.psum_scatter(
            key_sums.reshape(seq_len, -1).astype(jnp.bfloat16),
            "wide",
            scatter_dimension=0,
            tiled=True,
        ).astype(jnp.float32),
        lax.psum_scatter(
            value_sums.reshape(seq_len, -1).astype(jnp.bfloat16),
            "wide",
            scatter_dimension=0,
            tiled=True,
        ).astype(jnp.float32),
    )
    key_grad = key_flat.reshape(group, head_count, HEAD_DIM)
    value_grad = value_flat.reshape(group, head_count, HEAD_DIM)
    query_back = unrotate(query_grad, cos_table, sin_table)
    key_back = unrotate(key_grad, cos_table, sin_table)
    packed_grad = (
        jnp.stack([query_back, key_back, value_grad], axis=2)
        .reshape(group, -1)
        .astype(jnp.bfloat16)
    )
    qkv_grad = jnp.einsum(
        "cd,cf->df", parts["full_first"], packed_grad, preferred_element_type=jnp.float32
    )
    qkv_bias_grad = jnp.sum(packed_grad.astype(jnp.float32), axis=0)
    first_grad = jnp.einsum(
        "cf,df->cd", packed_grad, qkv_weight, preferred_element_type=jnp.float32
    )
    norm_first_grad, norm_second_grad = (
        lax.psum_scatter(
            first_grad.astype(jnp.bfloat16), "tensor", scatter_dimension=0, tiled=True
        ).astype(jnp.float32),
        lax.psum_scatter(
            second_grad.astype(jnp.bfloat16), "tensor", scatter_dimension=0, tiled=True
        ).astype(jnp.float32),
    )
    gain_grad = jnp.stack(
        [
            jnp.sum(norm_first_grad * parts["normed_first"], axis=0),
            jnp.sum(norm_second_grad * parts["normed_second"], axis=0),
        ]
    )
    shift_grad = jnp.stack([jnp.sum(norm_first_grad, axis=0), jnp.sum(norm_second_grad, axis=0)])
    input_grad = grad_out + norm_back(
        norm_first_grad, parts["normed_first"], parts["scale_first"], norm_gain[0]
    )
    input_grad = input_grad + norm_back(
        norm_second_grad, parts["normed_second"], parts["scale_second"], norm_gain[1]
    )
    bias_rows = jnp.sum(grad_rows, axis=0)
    terms = (
        gain_grad,
        shift_grad,
        qkv_grad,
        qkv_bias_grad,
        dense_grad,
        bias_rows,
        up_grad,
        up_bias_grad,
        down_grad,
        bias_rows,
    )
    return (input_grad, terms)


def general_shards(
    block_input,
    doc_lengths,
    norm_gain,
    norm_bias,
    qkv_weight,
    qkv_bias,
    dense_weight,
    dense_bias,
    up_weight,
    up_bias,
    down_weight,
    down_bias,
    cotangent,
):
    weights = (
        norm_gain[0],
        norm_bias[0],
        qkv_weight[0],
        qkv_bias[0],
        dense_weight[0],
        dense_bias[0],
        up_weight[0],
        up_bias[0],
        down_weight[0],
        down_bias[0],
    )
    section_index = lax.axis_index("section")
    last_section = lax.axis_size("section") - 1
    micro_count = block_input.shape[0]
    row_count = block_input.shape[1]
    tick_count = micro_count + last_section

    def forward_tick(carry, tick_index):
        incoming, kept_inputs, outputs, kept_pairs = carry
        slot_raw = tick_index - section_index
        is_valid = (slot_raw >= 0) & (slot_raw < micro_count)
        slot_here = jnp.clip(slot_raw, 0, micro_count - 1)
        fresh = lax.dynamic_index_in_dim(
            block_input, jnp.clip(tick_index, 0, micro_count - 1), 0, keepdims=False
        )
        inputs = jnp.where(section_index == 0, fresh, incoming)
        lengths = lax.dynamic_index_in_dim(doc_lengths, slot_here, 0, keepdims=False)
        parts = forward_parts(inputs, lengths, weights, True)
        output = parts["output"]
        kept_inputs = store_slot(kept_inputs, inputs, slot_here, is_valid)
        outputs = store_slot(outputs, output, slot_here, is_valid)
        incoming = jax.tree.map(
            lambda part, own: part.astype(own.dtype),
            from_behind(shortened(output), "section", 1),
            output,
        )
        return ((incoming, kept_inputs, outputs, kept_pairs), None)

    pair_init = (jnp.zeros((1,), jnp.bfloat16), jnp.zeros((1,), jnp.bfloat16))
    zero_rows = jnp.zeros((row_count, block_input.shape[2]), jnp.bfloat16)
    zero_stack = jnp.zeros(block_input.shape, jnp.bfloat16)
    forward_init = (zero_rows, zero_stack, zero_stack, pair_init)
    forward_done = lax.scan(forward_tick, forward_init, jnp.arange(tick_count, dtype=jnp.int32))[0]
    kept_inputs = forward_done[1]
    outputs = forward_done[2]
    kept_pairs = forward_done[3]

    def add_masked(total, term, scale_mask):
        return total + scale_mask * term

    def backward_tick(carry, tick_index):
        incoming, grads, input_grads = carry
        slot_raw = tick_index - (last_section - section_index)
        is_valid = (slot_raw >= 0) & (slot_raw < micro_count)
        slot_here = jnp.clip(slot_raw, 0, micro_count - 1)
        top_grad = lax.dynamic_index_in_dim(cotangent, slot_here, 0, keepdims=False)
        grad_out = jnp.where(section_index == last_section, top_grad, incoming)
        inputs = lax.dynamic_index_in_dim(kept_inputs, slot_here, 0, keepdims=False)
        lengths = lax.dynamic_index_in_dim(doc_lengths, slot_here, 0, keepdims=False)
        input_grad, terms = backward_parts(inputs, grad_out, lengths, weights)
        scale_mask = is_valid.astype(jnp.float32)
        grads = tuple((add_masked(total, term, scale_mask) for total, term in zip(grads, terms)))
        input_grads = store_slot(input_grads, input_grad, slot_here, is_valid)
        incoming = from_behind(shortened(input_grad), "section", -1).astype(input_grad.dtype)
        return ((incoming, grads, input_grads), None)

    grad_init = tuple((jnp.zeros(weight.shape, jnp.float32) for weight in weights))
    backward_init = (
        jnp.zeros((row_count, block_input.shape[2]), jnp.float32),
        grad_init,
        jnp.zeros(block_input.shape, jnp.float32),
    )
    backward_done = lax.scan(backward_tick, backward_init, jnp.arange(tick_count, dtype=jnp.int32))[
        0
    ]
    grads = backward_done[1]
    input_grads = backward_done[2]
    wide_sums = (
        lax.psum(grads[2].astype(jnp.bfloat16), "wide").astype(jnp.float32),
        lax.psum(grads[3].astype(jnp.bfloat16), "wide").astype(jnp.float32),
        lax.psum(grads[4].astype(jnp.bfloat16), "wide").astype(jnp.float32),
        lax.psum(grads[6].astype(jnp.bfloat16), "wide").astype(jnp.float32),
        lax.psum(grads[7].astype(jnp.bfloat16), "wide").astype(jnp.float32),
        lax.psum(grads[8].astype(jnp.bfloat16), "wide").astype(jnp.float32),
    )
    shared = lax.psum((grads[0], grads[1], grads[5], grads[9]), ("tensor", "wide"))
    return (
        outputs[None],
        input_grads[None],
        shared[0][None],
        shared[1][None],
        wide_sums[0][None],
        wide_sums[1][None],
        wide_sums[2][None],
        shared[2][None],
        wide_sums[3][None],
        wide_sums[4][None],
        wide_sums[5][None],
        shared[3][None],
    )


def solution(mesh):
    placed = (
        P(None, ("wide", "tensor"), None),
        P(),
        P("section", None, None),
        P("section", None, None),
        P("section", None, "tensor"),
        P("section", "tensor"),
        P("section", "tensor", None),
        P("section", None),
        P("section", None, "tensor"),
        P("section", "tensor"),
        P("section", "tensor", None),
        P("section", None),
        P(None, ("wide", "tensor"), None),
    )
    results = (
        P("section", None, ("wide", "tensor"), None),
        P("section", None, ("wide", "tensor"), None),
        P("section", None, None),
        P("section", None, None),
        P("section", None, "tensor"),
        P("section", "tensor"),
        P("section", "tensor", None),
        P("section", None),
        P("section", None, "tensor"),
        P("section", "tensor"),
        P("section", "tensor", None),
        P("section", None),
    )

    def program(*args):
        heads = args[4].shape[2] // (3 * HEAD_DIM * mesh.shape["tensor"])
        micro, seq_len, d_model = args[0].shape
        group = seq_len // mesh.shape["wide"]
        fits = heads == mesh.shape["wide"] == 8
        fits = fits and mesh.shape["section"] == 2 and mesh.shape["tensor"] == 2
        fits = fits and micro * group == d_model and args[8].shape[2] == 4 * d_model
        body = relay_shards if fits and group == TILE else general_shards
        return jax.shard_map(
            body, mesh=mesh, in_specs=placed, out_specs=results, check_vma=False
        )(*args)

    return program
```
